32 devices in a mesh: dp: 8 (over z, x), mp: 4 (over y, core).
Axes of the slice: x: 2, y: 2, z: 4, core: 2. Of those that a mesh axis runs over, the one named last changes fastest.
Arguments:
- hidden: bfloat16 [8192, 1536], P('dp'), may hold values from -6 to 6
- segments: int32 [8, 1024], P('dp'), may hold values from 0 to 15, never falling along the last dimension, each value on 1 to 512 neighbouring positions
- cotangent: bfloat16 [8192, 1536], P('dp', 'mp'), may hold values from -6 to 6
- in_weight: float32 [1536, 2, 3072], P('dp', None, 'mp'), may hold values from -0.15625 to 0.15625
- in_moment: float32 [1536, 2, 3072], P('dp', None, 'mp'), may hold values from -192 to 192
- bc_weight: float32 [1536, 256], P('dp'), may hold values from -0.15625 to 0.15625
- bc_moment: float32 [1536, 256], P('dp'), may hold values from -192 to 192
- step_weight: float32 [1536, 48], P('dp', 'mp'), may hold values from -0.15625 to 0.15625
- step_moment: float32 [1536, 48], P('dp', 'mp'), may hold values from -384 to 384
- out_weight: float32 [3072, 1536], P('mp', 'dp'), may hold values from -0.109375 to 0.109375
- out_moment: float32 [3072, 1536], P('mp', 'dp'), may hold values from -384 to 384
- conv_table: float32 [6, 3072], P(None, 'mp'), may hold values from -0.6 to 1.5
- conv_moment: float32 [6, 3072], P(None, 'mp'), may hold values from -192 to 192
- bc_table: float32 [5, 256], replicated, may hold values from -0.6 to 0.6
- bc_table_moment: float32 [5, 256], replicated, may hold values from -192 to 192
- head_table: float32 [3, 48], P(None, 'mp'), may hold values from -7 to 3
- head_moment: float32 [3, 48], P(None, 'mp'), may hold values from -1536 to 1536
- norm_gain: float32 [1536], replicated, may hold values from 0.5 to 1.5
- gain_moment: float32 [1536], replicated, may hold values from -192 to 192
Outputs:
- output: bfloat16 [8192, 1536], P('dp', 'mp')
- input_grad: bfloat16 [8192, 1536], P('dp')
- in_moment_next: float32 [1536, 2, 3072], P('dp', None, 'mp')
- in_weight_next: float32 [1536, 2, 3072], P('dp', None, 'mp')
- bc_moment_next: float32 [1536, 256], P('dp')
- bc_weight_next: float32 [1536, 256], P('dp')
- step_moment_next: float32 [1536, 48], P('dp', 'mp')
- step_weight_next: float32 [1536, 48], P('dp', 'mp')
- out_moment_next: float32 [3072, 1536], P('mp', 'dp')
- out_weight_next: float32 [3072, 1536], P('mp', 'dp')
- conv_moment_next: float32 [6, 3072], P(None, 'mp')
- bc_table_moment_next: float32 [5, 256], replicated
- head_moment_next: float32 [3, 48], P(None, 'mp')
- gain_moment_next: float32 [1536], replicated
The draws below stay inside these ranges and needn't reach their ends.
Inputs may be any that keep to these rules, and one draw needn't show every extreme that they name: `segments`: within each sequence segment numbers never fall; a document spans 1 to 512 tokens and one spans exactly 512.
All inputs are finite; a program needn't handle non-finite values.
Results may differ from the reference program's by a relative error of at most 0.01.
Values may be sent and summed in bfloat16 or wider, within the bound.
No kernel may reach another device: no remote copies, remote signals or barrier semaphores. Data moves between devices by JAX's collectives and lax.ppermute only.
A program may use at most 128 MiB of HBM per device.

```python
import math
import jax
import jax.numpy as jnp
import numpy as np
from jax import lax

D = 1536
HEADS = 48
STATE = 128
CONV = 4
STRETCH = 256
LENGTH = 1024
DOCS = 16
INNER = 3072
MOST_DOC = 512
SEQS = 8
TOKENS = 8192


def draw_conv_table(key, part):
    key = jax.random.fold_in(key, 11)
    first, second, third = jax.random.split(key, 3)
    taps = jax.random.uniform(first, (CONV, INNER), jnp.float32, -0.6, 0.6)
    offset = jax.random.uniform(second, (1, INNER), jnp.float32, -0.3, 0.3)
    gains = jax.random.uniform(third, (1, INNER), jnp.float32, 0.5, 1.5)
    return jnp.concatenate([taps, offset, gains], axis=0)


def draw_bc_table(key, part):
    key = jax.random.fold_in(key, 23)
    first, second = jax.random.split(key, 2)
    taps = jax.random.uniform(first, (CONV, 2 * STATE), jnp.float32, -0.6, 0.6)
    offset = jax.random.uniform(second, (1, 2 * STATE), jnp.float32, -0.3, 0.3)
    return jnp.concatenate([taps, offset], axis=0)


def draw_head_table(key, part):
    key = jax.random.fold_in(key, 37)
    first, second, third = jax.random.split(key, 3)
    steps = jnp.exp(jax.random.uniform(first, (1, HEADS), jnp.float32, jnp.log(0.001), jnp.log(0.1)))
    step_bias = jnp.log(jnp.expm1(steps))
    rate_log = jnp.log(jax.random.uniform(second, (1, HEADS), jnp.float32, 1.0, 16.0))
    skip = jax.random.uniform(third, (1, HEADS), jnp.float32, 0.5, 1.5)
    return jnp.concatenate([step_bias, rate_log, skip], axis=0)


def block_levels(own_key, dims, cuts, low, largest):
    loudness, own = 1.0, jax.random.fold_in(own_key, 6)
    for axis_at, shards_of in cuts:
        draws = jnp.exp(jax.random.uniform(jax.random.fold_in(own, axis_at), (shards_of,), jnp.float32, low / len(cuts), largest / len(cuts)))
        loudness = loudness * jnp.repeat(draws, dims[axis_at] // shards_of).reshape([-1 if axis == axis_at else 1 for axis in range(len(dims))])
    return loudness


def profile(amount, total, most, lean):
    loads = [(1 << 20) // math.isqrt(rank ** lean) + 1 for rank in range(2, amount + 1)]
    rest, given = total - most - (amount - 1), [1] * (amount - 1)
    while rest > 0:
        free = [i for i in range(amount - 1) if given[i] < most]
        mass, budget = sum([loads[i] for i in free]), rest
        for i in free:
            more = min(most - given[i], max(1, budget * loads[i] // mass), rest)
            given[i] = given[i] + more
            rest = rest - more
    return np.array([most] + given)


def uneven_parts(stream_key, amount, total, bound, lean):
    if amount == 2:
        one = jax.random.randint(stream_key, (), max(1, total - bound), min(bound, total - 1) + 1)
        return jnp.stack([one, total - one])
    lengths = jnp.asarray(profile(amount, total, bound, lean), jnp.int32)
    pairs = (amount - 1) // 2
    giver, receiver = lengths[1:1 + 2 * pairs:2], lengths[2:2 + 2 * pairs:2]
    slack = jnp.minimum(giver - 1, bound - receiver)
    moved = jax.random.randint(jax.random.fold_in(stream_key, 1), (pairs,), 0, 1 << 20) % (slack + 1)
    lengths = lengths.at[1:1 + 2 * pairs:2].set(giver - moved).at[2:2 + 2 * pairs:2].set(receiver + moved)
    return lengths[jax.random.permutation(jax.random.fold_in(stream_key, 2), amount)]


def scatter_about(rng, dims, deviation, most, cuts=(), kind=jnp.bfloat16):
    values = jax.random.normal(rng, dims, jnp.float32) * deviation
    if len(cuts) > 0:
        values = block_levels(rng, dims, cuts, -0.22, 0.18) * values
    return jnp.clip(values, min=-most, max=most).astype(kind)


def setup_inputs(seed: int = 0) -> dict:
    arg_keys = jax.random.split(jax.random.key(seed), 20)
    return {
        "hidden": scatter_about(arg_keys[0], (TOKENS, D), 1.0, 6.0, ((0, 8),)),
        "segments": jax.vmap(lambda own: jnp.searchsorted(jnp.cumsum(uneven_parts(own, DOCS, LENGTH, MOST_DOC, 2)), jnp.arange(LENGTH), side="right"))(jax.random.split(arg_keys[1], SEQS)).reshape((SEQS, LENGTH)).astype(jnp.int32),
        "cotangent": scatter_about(arg_keys[2], (TOKENS, D), 1.0, 6.0, ((0, 8), (1, 4))),
        "in_weight": scatter_about(arg_keys[3], (D, 2, INNER), D ** -0.5, 0.15625, ((0, 8), (2, 4)), jnp.float32),
        "in_moment": scatter_about(arg_keys[4], (D, 2, INNER), (TOKENS // 256), 192.0, ((0, 8), (2, 4)), jnp.float32),
        "bc_weight": scatter_about(arg_keys[5], (D, 2 * STATE), D ** -0.5, 0.15625, ((0, 8),), jnp.float32),
        "bc_moment": scatter_about(arg_keys[6], (D, 2 * STATE), (TOKENS // 256), 192.0, ((0, 8),), jnp.float32),
        "step_weight": scatter_about(arg_keys[7], (D, HEADS), D ** -0.5, 0.15625, ((0, 8), (1, 4)), jnp.float32),
        "step_moment": scatter_about(arg_keys[8], (D, HEADS), (TOKENS // 128), 384.0, ((0, 8), (1, 4)), jnp.float32),
        "out_weight": scatter_about(arg_keys[9], (INNER, D), INNER ** -0.5, 0.109375, ((0, 4), (1, 8)), jnp.float32),
        "out_moment": scatter_about(arg_keys[10], (INNER, D), (TOKENS // 128), 384.0, ((0, 4), (1, 8)), jnp.float32),
        "conv_table": draw_conv_table(jax.random.fold_in(arg_keys[19], 71), 0),
        "conv_moment": scatter_about(arg_keys[12], (CONV + 2, INNER), (TOKENS // 256), 192.0, ((1, 4),), jnp.float32),
        "bc_table": draw_bc_table(jax.random.fold_in(arg_keys[19], 71), 0),
        "bc_table_moment": scatter_about(arg_keys[14], (CONV + 1, 2 * STATE), (TOKENS // 256), 192.0, (), jnp.float32),
        "head_table": draw_head_table(jax.random.fold_in(arg_keys[19], 71), 0),
        "head_moment": scatter_about(arg_keys[16], (3, HEADS), (TOKENS // 32), 1536.0, ((1, 4),), jnp.float32),
        "norm_gain": jnp.clip(1.0 + 0.1 * jax.random.normal(arg_keys[17], (D,), jnp.float32), 0.5, 1.5),
        "gain_moment": scatter_about(arg_keys[18], (D,), (TOKENS // 256), 192.0, (), jnp.float32),
    }


epsilon = 1e-05
learn_rate = 0.0001
decay_rate = 0.1
highest = lax.Precision.HIGHEST

@jax.custom_vjp
def low(v):
    return lax.optimization_barrier(v.astype(jnp.bfloat16)).astype(jnp.float32)

@jax.custom_vjp
def low_back(v):
    return v

def low_keep(v):
    return (low(v), None)

def low_pass(kept, grad):
    return (grad,)

def back_keep(v):
    return (v, None)

def back_low(kept, grad):
    return (low(grad),)
low.defvjp(low_keep, low_pass)
low_back.defvjp(back_keep, back_low)

def causal_conv(values, taps, offset, seg):
    total = offset + taps[0] * values
    for lag in range(1, taps.shape[0]):
        moved = jnp.pad(values[:, :-lag], ((0, 0), (lag, 0), (0, 0)))
        seg_moved = jnp.pad(seg[:, :-lag], ((0, 0), (lag, 0)), constant_values=-1)
        keep = (seg_moved == seg).astype(values.dtype)
        total = total + taps[lag] * moved * keep[..., None]
    return total

def ssd_scan(x_act, steps, b_mat, c_mat, a_log, skip, seg):
    batch_seqs, seq_len, head_count, head_width = x_act.shape
    count = seq_len // STRETCH
    rates = -jnp.exp(a_log)
    dtype = x_act.dtype

    def split(array):
        return jnp.moveaxis(array.reshape((batch_seqs, count, STRETCH) + array.shape[2:]), 1, 0)
    order = jnp.arange(STRETCH)
    causal = order[:, None] >= order[None, :]

    def block(carry, pieces):
        state, last_seg = carry
        x_block, step_block, b_block, c_block, seg_block = pieces
        cum = jnp.cumsum(step_block * rates, axis=1)
        mask = causal[None] & (seg_block[:, :, None] == seg_block[:, None, :])
        diff = cum[:, :, None, :] - cum[:, None, :, :]
        decay = jnp.where(mask[..., None], jnp.exp(jnp.where(mask[..., None], diff, 0.0)), 0.0)
        scores = jnp.einsum('stn,sun->stu', c_block, b_block, precision=highest)
        weights = scores[..., None] * decay * step_block[:, None, :, :]
        inner_part = jnp.einsum('stuh,suhp->sthp', weights, x_block, precision=highest)
        carried = (seg_block == last_seg[:, None]).astype(dtype)
        entry = jnp.exp(cum) * carried[..., None]
        state_part = jnp.einsum('stn,shpn->sthp', c_block, state, precision=highest) * entry[..., None]
        tail = cum[:, -1, :]
        final_seg = seg_block[:, -1]
        same_end = (seg_block == final_seg[:, None]).astype(dtype)
        to_end = jnp.exp(tail[:, None, :] - cum) * same_end[..., None] * step_block
        kept = jnp.exp(tail) * (final_seg == last_seg).astype(dtype)[:, None]
        new_state = state * kept[:, :, None, None] + jnp.einsum('suh,suhp,sun->shpn', to_end, x_block, b_block, precision=highest)
        result = inner_part + state_part + skip[None, None, :, None] * x_block
        return ((new_state, final_seg), result)
    start = (jnp.zeros((batch_seqs, head_count, head_width, b_mat.shape[-1]), dtype), jnp.full((batch_seqs,), -1, seg.dtype))
    final_carry, blocks = lax.scan(jax.checkpoint(block), start, (split(x_act), split(steps), split(b_mat), split(c_mat), split(seg)))
    return jnp.moveaxis(blocks, 0, 1).reshape(batch_seqs, seq_len, head_count, head_width)

def local_mix(x_pre, bc_pre, step_pre, conv_x, conv_bc, heads, seg):
    batch_seqs, seq_len = seg.shape
    x_act = jax.nn.silu(causal_conv(x_pre.reshape(batch_seqs, seq_len, -1), conv_x[:-1], conv_x[-1], seg))
    bc_act = jax.nn.silu(causal_conv(bc_pre.reshape(batch_seqs, seq_len, -1), conv_bc[:-1], conv_bc[-1], seg))
    half = bc_act.shape[-1] // 2
    steps = jax.nn.softplus(step_pre.reshape(batch_seqs, seq_len, -1) + heads[0])
    head_count = steps.shape[-1]
    head_width = x_act.shape[-1] // head_count
    mixed = ssd_scan(x_act.reshape(batch_seqs, seq_len, head_count, head_width), steps, bc_act[..., :half], bc_act[..., half:], heads[1], heads[2], seg)
    return mixed.reshape(batch_seqs * seq_len, head_count * head_width)

def momentum(moment, grad):
    return 0.5 * moment + 0.5 * grad

def advance(weight, moment, grad):
    fresh = momentum(moment, grad)
    return (fresh, weight - learn_rate * fresh - learn_rate * decay_rate * weight)

def reference(hidden, segments, cotangent, in_weight, in_moment, bc_weight, bc_moment, step_weight, step_moment, out_weight, out_moment, conv_table, conv_moment, bc_table, bc_table_moment, head_table, head_moment, norm_gain, gain_moment):

    def forward(inputs, in_w, bc_w, step_w, out_w, conv_t, bc_t, head_t, gain):
        in_low = low(in_w)
        bc_low = low(bc_w)
        step_low = low(step_w)
        out_low = low(out_w)

        def one_sequence(pair):
            rows, seg_row = pair
            inv_rms = lax.rsqrt(lax.optimization_barrier(jnp.mean(rows * rows, axis=-1, keepdims=True)) + epsilon)
            normed_low = low(rows * inv_rms * gain)
            both = low_back(jnp.einsum('td,dkc->tkc', normed_low, in_low, precision=highest))
            bc_pre = low_back(jnp.dot(normed_low, bc_low, precision=highest, preferred_element_type=jnp.float32))
            step_pre = low_back(jnp.dot(normed_low, step_low, precision=highest, preferred_element_type=jnp.float32))
            mixed = local_mix(both[:, 1], bc_pre, step_pre, conv_t[:CONV + 1], bc_t, head_t, seg_row[None])
            gated = mixed * jax.nn.silu(both[:, 0])
            scale_row = lax.rsqrt(lax.optimization_barrier(jnp.mean(gated * gated, axis=-1, keepdims=True)) + epsilon)
            gated_out = low(gated * scale_row * conv_t[CONV + 1])
            return rows + jnp.dot(gated_out, out_low, precision=highest, preferred_element_type=jnp.float32)
        results = lax.map(jax.checkpoint(one_sequence), (inputs.reshape(SEQS, LENGTH, D), segments))
        return results.reshape(TOKENS, D)
    inputs = hidden.astype(jnp.float32)
    result, pullback = jax.vjp(forward, inputs, in_weight, bc_weight, step_weight, out_weight, conv_table, bc_table, head_table, norm_gain)
    grads = pullback(cotangent.astype(jnp.float32))
    in_m, in_w = advance(in_weight, in_moment, grads[1])
    bc_m, bc_w = advance(bc_weight, bc_moment, grads[2])
    step_m, step_w = advance(step_weight, step_moment, grads[3])
    out_m, out_w = advance(out_weight, out_moment, grads[4])
    conv_m = momentum(conv_moment, grads[5])
    bct_m = momentum(bc_table_moment, grads[6])
    head_m = momentum(head_moment, grads[7])
    gain_m = momentum(gain_moment, grads[8])
    return (result.astype(jnp.bfloat16), grads[0].astype(jnp.bfloat16), in_m, in_w, bc_m, bc_w, step_m, step_w, out_m, out_w, conv_m, bct_m, head_m, gain_m)
```

```python
import functools

import jax
import jax.numpy as jnp
from jax import lax
from jax.experimental import pallas as pl
from jax.experimental.pallas import tpu as pltpu
from jax.sharding import PartitionSpec as P

CHUNK = 128
EPSILON = 1e-05
LEARN_RATE = 0.0001
DECAY_RATE = 0.1
WIDTH = 64
LANES = 128
HALO = 8
bf16 = jnp.bfloat16
f32 = jnp.float32
VMEM_LIMIT = 56 * 1024 * 1024


def dot_nn(a, b):
    return lax.dot_general(a, b, (((1,), (0,)), ((), ())), preferred_element_type=f32)


def dot_nt(a, b):
    return lax.dot_general(a, b, (((1,), (1,)), ((), ())), preferred_element_type=f32)


def dot_tn(a, b):
    return lax.dot_general(a, b, (((0,), (0,)), ((), ())), preferred_element_type=f32)


def split3(v):
    high = v.astype(bf16)
    rest = v - high.astype(f32)
    mid = rest.astype(bf16)
    low = (rest - mid.astype(f32)).astype(bf16)
    return high, mid, low


def exact_left(ones, v):
    high, mid, low = split3(v)
    return dot_nn(ones, high) + dot_nn(ones, mid) + dot_nn(ones, low)


def spread(v, expand):
    high, mid, low = split3(v)
    return dot_nn(high, expand) + dot_nn(mid, expand) + dot_nn(low, expand)


def gather_heads(v, expand):
    high = v.astype(bf16)
    mid = (v - high.astype(f32)).astype(bf16)
    return dot_nt(high, expand) + dot_nt(mid, expand)


def sigmoid(v):
    return 1.0 / (1.0 + jnp.exp(-v))


def conv_block(scratch, before, now, taps, keep):
    rows = now.shape[0]
    scratch[0:HALO, :] = before
    scratch[HALO:HALO + rows, :] = now
    total = taps[4:5, :] + taps[0:1, :] * now
    for lag in (1, 2, 3):
        moved = scratch[HALO - lag:HALO - lag + rows, :]
        total = total + taps[lag:lag + 1, :] * (moved * keep[:, lag - 1:lag])
    return total


def step_parts(step_pre, heads):
    raw = step_pre + heads[0:1, :]
    steps = jnp.maximum(raw, 0.0) + jnp.log1p(jnp.exp(-jnp.abs(raw)))
    rates = -jnp.exp(heads[1:2, :])
    return raw, steps, rates


def triangle(lower):
    row = lax.broadcasted_iota(jnp.int32, (CHUNK, CHUNK), 0)
    col = lax.broadcasted_iota(jnp.int32, (CHUNK, CHUNK), 1)
    return row >= col if lower else row <= col


def ssd_forward_kernel(
    x_ref, xb_ref, bc_ref, bcb_ref, st_ref, aux_ref, seg_ref, conv_ref, bct_ref, heads_ref, expand_ref,
    mixed_ref, state_ref, state, xs_scr, bc_scr,
):
    chunk = pl.program_id(0)

    @pl.when(chunk == 0)
    def _():
        state[...] = jnp.zeros_like(state)

    channels = x_ref.shape[1]
    aux = aux_ref[...]
    expand = expand_ref[...]
    u = conv_block(xs_scr, xb_ref[...], x_ref[...], conv_ref, aux)
    x_act = u * sigmoid(u)
    ubc = conv_block(bc_scr, bcb_ref[...], bc_ref[...], bct_ref, aux)
    bc_act = (ubc * sigmoid(ubc)).astype(bf16)
    b_mat, c_mat = bc_act[:, :LANES], bc_act[:, LANES:]
    _, steps, rates = step_parts(st_ref[...], heads_ref)
    lower = triangle(True)
    cum = exact_left(lower.astype(bf16), steps * rates)
    cum_t = cum.T
    tail = cum[CHUNK - 1:CHUNK, :]
    entry = jnp.exp(cum) * aux[:, 6:7]
    to_end = jnp.exp(tail - cum) * aux[:, 7:8]
    wide = spread(jnp.concatenate([steps, entry, to_end], axis=0), expand)
    step_e, entry_e, to_end_e = wide[:CHUNK], wide[CHUNK:2 * CHUNK], wide[2 * CHUNK:]
    skip_e = spread(jnp.broadcast_to(heads_ref[2:3, :], (8, LANES)), expand)[0:1, :]
    mask = lower & (aux[:, 8:9] == seg_ref[...])
    scores = jnp.where(mask, dot_nt(c_mat, b_mat), 0.0)
    xs = x_act * step_e
    xs_low = xs.astype(bf16)
    held = state[...]
    held_low = held.astype(bf16)
    state_ref[...] = held_low
    out = dot_nn(c_mat, held_low) * entry_e + skip_e * x_act
    state[...] = held * entry_e[CHUNK - 1:CHUNK, :] + dot_tn(b_mat, (xs * to_end_e).astype(bf16))
    first = lax.broadcasted_iota(jnp.int32, (CHUNK, LANES), 1) < WIDTH
    zero = jnp.zeros((CHUNK, LANES), bf16)
    for pair in range(channels // LANES):
        span = slice(pair * LANES, (pair + 1) * LANES)
        parts = []
        for head in (2 * pair, 2 * pair + 1):
            diff = cum[:, head:head + 1] - cum_t[head:head + 1, :]
            parts.append((scores * jnp.exp(jnp.minimum(diff, 0.0))).astype(bf16))
        own = xs_low[:, span]
        both = jnp.concatenate([jnp.where(first, own, zero), jnp.where(first, zero, own)], axis=0)
        mixed_ref[:, span] = out[:, span] + dot_nn(jnp.concatenate(parts, axis=1), both)


def ssd_backward_kernel(
    x_ref, xb_ref, bc_ref, bcb_ref, st_ref, aux_ref, seg_ref, conv_ref, bct_ref, heads_ref, expand_ref,
    mixed_ref, dy_ref, state_ref,
    dx_ref, dbc_ref, dst_ref, dconv_ref, dbct_ref, dheads_ref,
    dstate, xs_scr, bc_scr, du_scr, dubc_scr,
):
    at = pl.program_id(0)

    @pl.when(at == 0)
    def _():
        dstate[...] = jnp.zeros_like(dstate)
        du_scr[...] = jnp.zeros_like(du_scr)
        dubc_scr[...] = jnp.zeros_like(dubc_scr)
        dconv_ref[...] = jnp.zeros_like(dconv_ref)
        dbct_ref[...] = jnp.zeros_like(dbct_ref)
        dheads_ref[...] = jnp.zeros_like(dheads_ref)

    channels = x_ref.shape[1]
    aux = aux_ref[...]
    expand = expand_ref[...]
    x_now, bc_now = x_ref[...], bc_ref[...]
    u = conv_block(xs_scr, xb_ref[...], x_now, conv_ref, aux)
    sg = sigmoid(u)
    x_act = u * sg
    ubc = conv_block(bc_scr, bcb_ref[...], bc_now, bct_ref, aux)
    sgbc = sigmoid(ubc)
    bc_act = (ubc * sgbc).astype(bf16)
    b_mat, c_mat = bc_act[:, :LANES], bc_act[:, LANES:]
    raw, steps, rates = step_parts(st_ref[...], heads_ref)
    lower = triangle(True)
    cum = exact_left(lower.astype(bf16), steps * rates)
    cum_t = cum.T
    tail = cum[CHUNK - 1:CHUNK, :]
    entry = jnp.exp(cum) * aux[:, 6:7]
    to_end = jnp.exp(tail - cum) * aux[:, 7:8]
    wide = spread(jnp.concatenate([steps, entry, to_end], axis=0), expand)
    step_e, entry_e, to_end_e = wide[:CHUNK], wide[CHUNK:2 * CHUNK], wide[2 * CHUNK:]
    skip_e = spread(jnp.broadcast_to(heads_ref[2:3, :], (8, LANES)), expand)[0:1, :]
    upper = triangle(False)
    mask = upper & (aux[:, 8:9] == seg_ref[...])
    scores = jnp.where(mask, dot_nt(b_mat, c_mat), 0.0)
    xs = x_act * step_e
    xs_low = xs.astype(bf16)
    dy_low = dy_ref[...]
    dy = dy_low.astype(f32)
    held_low = state_ref[...]
    grad = dstate[...]
    grad_low = grad.astype(bf16)
    entry_dy = (entry_e * dy).astype(bf16)
    kept_e = entry_e[CHUNK - 1:CHUNK, :]
    dstate[...] = grad * kept_e + dot_tn(c_mat, entry_dy)
    dc = dot_nt(entry_dy, held_low)
    db = dot_nt((xs * to_end_e).astype(bf16), grad_low)
    q_state = dot_nn(b_mat, grad_low) * to_end_e
    first = lax.broadcasted_iota(jnp.int32, (CHUNK, LANES), 1) < WIDTH
    zero = jnp.zeros((CHUNK, LANES), bf16)
    dscores = jnp.zeros((CHUNK, CHUNK), f32)
    q_parts = []
    for pair in range(channels // LANES):
        span = slice(pair * LANES, (pair + 1) * LANES)
        own = dy_low[:, span]
        both = jnp.concatenate([jnp.where(first, own, zero), jnp.where(first, zero, own)], axis=0)
        dweights = dot_nt(xs_low[:, span], both)
        parts = []
        for i, head in enumerate((2 * pair, 2 * pair + 1)):
            diff = cum_t[head:head + 1, :] - cum[:, head:head + 1]
            decay = jnp.exp(jnp.minimum(diff, 0.0))
            parts.append((scores * decay).astype(bf16))
            dscores = dscores + dweights[:, i * LANES:(i + 1) * LANES] * decay
        q_parts.append(dot_nn(jnp.concatenate(parts, axis=1), both))
    q = jnp.concatenate(q_parts, axis=1) + q_state
    dscores_low = jnp.where(mask, dscores, 0.0).astype(bf16)
    db = db + dot_nn(dscores_low, c_mat)
    dc = dc + dot_tn(dscores_low, b_mat)
    xs_round = xs_low.astype(f32)
    rows = gather_heads(
        jnp.concatenate(
            [
                dy * (mixed_ref[...] - skip_e * x_act) - xs_round * q,
                x_act * q,
            ],
            axis=0,
        ),
        expand,
    )
    flow, dstep = rows[:CHUNK], rows[CHUNK:]
    sums = jnp.concatenate(
        [
            jnp.sum(xs_round * q_state + kept_e * (held_low.astype(f32) * grad), axis=0, keepdims=True),
            jnp.sum(dy * x_act, axis=0, keepdims=True),
            jnp.zeros((6, channels), f32),
        ],
        axis=0,
    )
    sums = gather_heads(sums, expand)
    dlog = exact_left(upper.astype(bf16), flow) + sums[0:1, :]
    dstep = dstep + rates * dlog
    draw = dstep * sigmoid(raw)
    dst_ref[...] = draw
    dheads_ref[0:1, :] += jnp.sum(draw, axis=0, keepdims=True)
    dheads_ref[1:2, :] += rates * jnp.sum(dlog * steps, axis=0, keepdims=True)
    dheads_ref[2:3, :] += sums[1:2, :]

    def conv_back(scratch, du, now, taps, dtaps):
        scratch[0:CHUNK, :] = du
        total = taps[0:1, :] * du
        dtaps[0:1, :] += jnp.sum(now * du, axis=0, keepdims=True)
        dtaps[4:5, :] += jnp.sum(du, axis=0, keepdims=True)
        for lag in (1, 2, 3):
            moved = scratch[lag:lag + CHUNK, :] * aux[:, 2 + lag:3 + lag]
            total = total + taps[lag:lag + 1, :] * moved
            dtaps[lag:lag + 1, :] += jnp.sum(now * moved, axis=0, keepdims=True)
        scratch[CHUNK:CHUNK + HALO, :] = du[0:HALO, :]
        return total

    du = (skip_e * dy + step_e * q) * (sg * (1.0 + u * (1.0 - sg)))
    dx_ref[...] = conv_back(du_scr, du, x_now, conv_ref, dconv_ref).astype(dx_ref.dtype)
    dubc = jnp.concatenate([db, dc], axis=1) * (sgbc * (1.0 + ubc * (1.0 - sgbc)))
    dbc_ref[...] = conv_back(dubc_scr, dubc, bc_now, bct_ref, dbct_ref)


def common_specs(place, channels):
    before = lambda i: (jnp.maximum(place(i) * (CHUNK // HALO) - 1, 0), 0)
    now = lambda i: (place(i), 0)
    whole = lambda i: (0, 0)
    return [
        pl.BlockSpec((CHUNK, channels), now),
        pl.BlockSpec((HALO, channels), before),
        pl.BlockSpec((CHUNK, 2 * LANES), now),
        pl.BlockSpec((HALO, 2 * LANES), before),
        pl.BlockSpec((CHUNK, LANES), now),
        pl.BlockSpec((CHUNK, 16), now),
        pl.BlockSpec((1, CHUNK), lambda i: (0, place(i))),
        pl.BlockSpec((8, channels), whole),
        pl.BlockSpec((8, 2 * LANES), whole),
        pl.BlockSpec((8, LANES), whole),
        pl.BlockSpec((LANES, channels), whole),
    ]


def ssd_forward(x_pre, bc_pre, step_pre, aux, seg_row, conv_rows, bc_rows, head_rows, expand):
    tokens, channels = x_pre.shape
    count = tokens // CHUNK
    now = lambda i: (i, 0)
    return pl.pallas_call(
        ssd_forward_kernel,
        grid=(count,),
        in_specs=common_specs(lambda i: i, channels),
        out_specs=[
            pl.BlockSpec((CHUNK, channels), now),
            pl.BlockSpec((None, LANES, channels), lambda i: (i, 0, 0)),
        ],
        out_shape=[
            jax.ShapeDtypeStruct((tokens, channels), f32),
            jax.ShapeDtypeStruct((count, LANES, channels), bf16),
        ],
        scratch_shapes=[
            pltpu.VMEM((LANES, channels), f32),
            pltpu.VMEM((HALO + CHUNK, channels), f32),
            pltpu.VMEM((HALO + CHUNK, 2 * LANES), f32),
        ],
        compiler_params=pltpu.CompilerParams(vmem_limit_bytes=VMEM_LIMIT),
        name="ssd_forward",
    )(x_pre, x_pre, bc_pre, bc_pre, step_pre, aux, seg_row, conv_rows, bc_rows, head_rows, expand)


def ssd_backward(x_pre, bc_pre, step_pre, aux, seg_row, conv_rows, bc_rows, head_rows, expand, mixed, dy, states):
    tokens, channels = x_pre.shape
    count = tokens // CHUNK
    place = lambda i: count - 1 - i
    now = lambda i: (place(i), 0)
    whole = lambda i: (0, 0)
    return pl.pallas_call(
        ssd_backward_kernel,
        grid=(count,),
        in_specs=common_specs(place, channels) + [
            pl.BlockSpec((CHUNK, channels), now),
            pl.BlockSpec((CHUNK, channels), now),
            pl.BlockSpec((None, LANES, channels), lambda i: (place(i), 0, 0)),
        ],
        out_specs=[
            pl.BlockSpec((CHUNK, channels), now),
            pl.BlockSpec((CHUNK, 2 * LANES), now),
            pl.BlockSpec((CHUNK, LANES), now),
            pl.BlockSpec((8, channels), whole),
            pl.BlockSpec((8, 2 * LANES), whole),
            pl.BlockSpec((8, LANES), whole),
        ],
        out_shape=[
            jax.ShapeDtypeStruct((tokens, channels), bf16),
            jax.ShapeDtypeStruct((tokens, 2 * LANES), f32),
            jax.ShapeDtypeStruct((tokens, LANES), f32),
            jax.ShapeDtypeStruct((8, channels), f32),
            jax.ShapeDtypeStruct((8, 2 * LANES), f32),
            jax.ShapeDtypeStruct((8, LANES), f32),
        ],
        scratch_shapes=[
            pltpu.VMEM((LANES, channels), f32),
            pltpu.VMEM((HALO + CHUNK, channels), f32),
            pltpu.VMEM((HALO + CHUNK, 2 * LANES), f32),
            pltpu.VMEM((HALO + CHUNK, channels), f32),
            pltpu.VMEM((HALO + CHUNK, 2 * LANES), f32),
        ],
        compiler_params=pltpu.CompilerParams(vmem_limit_bytes=VMEM_LIMIT),
        name="ssd_backward",
    )(x_pre, x_pre, bc_pre, bc_pre, step_pre, aux, seg_row, conv_rows, bc_rows, head_rows, expand, mixed, dy, states)


def segment_facts(seg):
    row = seg[0]
    tokens = row.shape[0]
    cols = []
    for lag in (1, 2, 3):
        cols.append(jnp.pad(row[:-lag], (lag, 0), constant_values=-1) == row)
    for lag in (1, 2, 3):
        cols.append(jnp.pad(row[lag:], (0, lag), constant_values=-1) == row)
    blocks = row.reshape(tokens // CHUNK, CHUNK)
    ends = blocks[:, -1:]
    before = jnp.concatenate([jnp.full((1, 1), -1, row.dtype), ends[:-1]], axis=0)
    cols.append((blocks == before).reshape(-1))
    cols.append((blocks == ends).reshape(-1))
    cols.append(row)
    facts = jnp.stack([c.astype(f32) for c in cols], axis=1)
    return jnp.pad(facts, ((0, 0), (0, 16 - facts.shape[1]))), seg.astype(f32)


def pad_rows(table, rows=8):
    return jnp.pad(table, ((0, rows - table.shape[0]), (0, 0)))


def pad_lanes(table, lanes=LANES):
    return jnp.pad(table, ((0, 0), (0, lanes - table.shape[1])))


def head_expand(channels):
    head = jnp.arange(LANES)[:, None]
    return (head == (jnp.arange(channels) // WIDTH)[None, :]).astype(bf16)


def place_kernel(idx_ref, lhs_ref, *refs, widths, count):
    groups = len(widths)
    pieces = refs[: groups * count]
    outs = refs[groups * count: groups * count + groups]
    weights = refs[groups * count + groups:]

    @pl.when(pl.program_id(0) == 0)
    def _():
        for g in range(groups):
            for s in range(count):
                piece = pieces[g * count + s]
                rows = piece.shape[0]
                weights[g][pl.ds(pl.multiple_of(idx_ref[s] * rows, rows), rows), :] = piece[...]

    lhs = lhs_ref[...]
    for g in range(groups):
        outs[g][...] = dot_nn(lhs, weights[g][...])


TILE = 256


def project(lhs, groups, idx):
    tokens, depth = lhs.shape
    count = len(groups[0])
    widths = tuple(g[0].shape[1] for g in groups)
    whole = lambda i: (0, 0)
    flat = [p for g in groups for p in g]
    return pl.pallas_call(
        functools.partial(place_kernel, widths=widths, count=count),
        grid=(tokens // TILE,),
        in_specs=[pl.BlockSpec(memory_space=pltpu.SMEM), pl.BlockSpec((TILE, depth), lambda i: (i, 0))]
        + [pl.BlockSpec(p.shape, whole) for p in flat],
        out_specs=[pl.BlockSpec((TILE, w), lambda i: (i, 0)) for w in widths]
        + [pl.BlockSpec((depth, w), whole) for w in widths],
        out_shape=[jax.ShapeDtypeStruct((tokens, w), f32) for w in widths]
        + [jax.ShapeDtypeStruct((depth, w), bf16) for w in widths],
        compiler_params=pltpu.CompilerParams(vmem_limit_bytes=VMEM_LIMIT),
        cost_estimate=pl.CostEstimate(
            flops=2 * tokens * depth * sum(widths), bytes_accessed=6 * depth * sum(widths), transcendentals=0
        ),
        name="project",
    )(idx, lhs, *flat)


def column_to_row(col):
    return jnp.broadcast_to(col, (col.shape[0], LANES)).T[0:1, :]


def row_to_column(row):
    return jnp.broadcast_to(row, (LANES, row.shape[1])).T[:, 0:1]


def gate_kernel(idx_ref, lhs_ref, cot_ref, mixed_ref, conv_ref, *refs, count):
    gate_pieces, out_pieces = refs[:count], refs[count: 2 * count]
    gate_ref, gout_ref, sums_ref, wg_ref, wo_ref = refs[2 * count:]

    @pl.when(pl.program_id(0) == 0)
    def _():
        for dest, source in ((wg_ref, gate_pieces), (wo_ref, out_pieces)):
            for s in range(count):
                rows = source[s].shape[0]
                dest[pl.ds(pl.multiple_of(idx_ref[s] * rows, rows), rows), :] = source[s][...]

    gate = dot_nn(lhs_ref[...], wg_ref[...])
    gout = dot_nn(cot_ref[...], wo_ref[...])
    gate_ref[...] = gate
    gout_ref[...] = gout
    gated = mixed_ref[...] * (gate * sigmoid(gate))
    square = jnp.sum(gated * gated, axis=1, keepdims=True)
    inner = jnp.sum(gout * conv_ref[5:6, :] * gated, axis=1, keepdims=True)
    sums_ref[...] = jnp.concatenate(
        [column_to_row(square), column_to_row(inner), jnp.zeros((6, square.shape[0]), f32)], axis=0
    )


def gate_forward(lhs, cot, mixed, conv_rows, gate_pieces, out_pieces, idx):
    tokens, depth = lhs.shape
    channels = mixed.shape[1]
    count = len(gate_pieces)
    whole = lambda i: (0, 0)
    now = lambda i: (i, 0)
    return pl.pallas_call(
        functools.partial(gate_kernel, count=count),
        grid=(tokens // TILE,),
        in_specs=[
            pl.BlockSpec(memory_space=pltpu.SMEM),
            pl.BlockSpec((TILE, depth), now),
            pl.BlockSpec((TILE, depth), now),
            pl.BlockSpec((TILE, channels), now),
            pl.BlockSpec((8, channels), whole),
        ]
        + [pl.BlockSpec(p.shape, whole) for p in (*gate_pieces, *out_pieces)],
        out_specs=[
            pl.BlockSpec((TILE, channels), now),
            pl.BlockSpec((TILE, channels), now),
            pl.BlockSpec((8, TILE), lambda i: (0, i)),
            pl.BlockSpec((depth, channels), whole),
            pl.BlockSpec((depth, channels), whole),
        ],
        out_shape=[
            jax.ShapeDtypeStruct((tokens, channels), f32),
            jax.ShapeDtypeStruct((tokens, channels), f32),
            jax.ShapeDtypeStruct((8, tokens), f32),
            jax.ShapeDtypeStruct((depth, channels), bf16),
            jax.ShapeDtypeStruct((depth, channels), bf16),
        ],
        compiler_params=pltpu.CompilerParams(vmem_limit_bytes=VMEM_LIMIT),
        cost_estimate=pl.CostEstimate(
            flops=4 * tokens * depth * channels, bytes_accessed=8 * depth * channels, transcendentals=0
        ),
        name="gate_forward",
    )(idx, lhs, cot, mixed, conv_rows, *gate_pieces, *out_pieces)


def gate_back_kernel(gate_ref, gout_ref, mixed_ref, sums_ref, conv_ref, gated_out_ref, dmixed_ref, dgate_ref, dgain_ref, *, inner_total):
    gate, gout, mixed = gate_ref[...], gout_ref[...], mixed_ref[...]
    gain = conv_ref[5:6, :]
    square, inner = row_to_column(sums_ref[0:1, :]), row_to_column(sums_ref[1:2, :])
    scale = lax.rsqrt(square / inner_total + EPSILON)
    sg = sigmoid(gate)
    act = gate * sg
    gated = mixed * act
    normal = gated * scale
    gated_out_ref[...] = (normal * gain).astype(bf16)
    dgated = scale * (gain * gout) - gated * (scale * scale * scale * inner / inner_total)
    dmixed_ref[...] = (dgated * act).astype(bf16)
    dgate_ref[...] = (dgated * mixed * sg * (1.0 + gate * (1.0 - sg))).astype(bf16)

    @pl.when(pl.program_id(0) == 0)
    def _():
        dgain_ref[...] = jnp.zeros_like(dgain_ref)

    dgain_ref[0:1, :] += jnp.sum(gout * normal, axis=0, keepdims=True)


def gate_backward(gate, gout, mixed, sums, conv_rows, inner_total):
    tokens, channels = gate.shape
    whole = lambda i: (0, 0)
    now = lambda i: (i, 0)
    block = pl.BlockSpec((TILE, channels), now)
    return pl.pallas_call(
        functools.partial(gate_back_kernel, inner_total=inner_total),
        grid=(tokens // TILE,),
        in_specs=[block, block, block, pl.BlockSpec((8, TILE), lambda i: (0, i)), pl.BlockSpec((8, channels), whole)],
        out_specs=[block, block, block, pl.BlockSpec((8, channels), whole)],
        out_shape=[
            jax.ShapeDtypeStruct((tokens, channels), bf16),
            jax.ShapeDtypeStruct((tokens, channels), bf16),
            jax.ShapeDtypeStruct((tokens, channels), bf16),
            jax.ShapeDtypeStruct((8, channels), f32),
        ],
        compiler_params=pltpu.CompilerParams(vmem_limit_bytes=VMEM_LIMIT),
        name="gate_backward",
    )(gate, gout, mixed, sums, conv_rows)


def weight_grad_kernel(slot_ref, lhs_ref, rhs_ref, out_ref, *, rows):
    per = TILE_D // rows
    product = dot_tn(lhs_ref[...], rhs_ref[...])
    for p in range(per):
        block = pl.program_id(0) * per + p
        out_ref[slot_ref[block]] = product[p * rows:(p + 1) * rows, :].astype(out_ref.dtype)


TILE_D = 384


def weight_grad(lhs, rhs, slots):
    tokens, depth = lhs.shape
    width = rhs.shape[1]
    count = slots.shape[0]
    rows = depth // count
    return pl.pallas_call(
        functools.partial(weight_grad_kernel, rows=rows),
        grid=(depth // TILE_D,),
        in_specs=[
            pl.BlockSpec(memory_space=pltpu.SMEM),
            pl.BlockSpec((tokens, TILE_D), lambda i: (0, i)),
            pl.BlockSpec((tokens, width), lambda i: (0, 0)),
        ],
        out_specs=pl.BlockSpec((count, rows, width), lambda i: (0, 0, 0)),
        out_shape=jax.ShapeDtypeStruct((count, rows, width), bf16),
        compiler_params=pltpu.CompilerParams(vmem_limit_bytes=VMEM_LIMIT),
        cost_estimate=pl.CostEstimate(flops=2 * tokens * depth * width, bytes_accessed=4 * depth * width, transcendentals=0),
        name="weight_grad",
    )(slots, lhs, rhs)


def out_kernel(rank_ref, lhs_ref, w_ref, *outs):
    lhs = lhs_ref[...]
    width = outs[0].shape[1]
    for r, out in enumerate(outs):
        start = pl.multiple_of((rank_ref[0] ^ r) * width, width)
        out[...] = dot_nt(lhs, w_ref[pl.ds(start, width), :]).astype(out.dtype)


def out_partial(gated_out, w_out, rank, ranks):
    tokens, channels = gated_out.shape
    depth = w_out.shape[0]
    width = depth // ranks
    now = lambda i: (i, 0)
    return pl.pallas_call(
        out_kernel,
        grid=(tokens // TILE,),
        in_specs=[
            pl.BlockSpec(memory_space=pltpu.SMEM),
            pl.BlockSpec((TILE, channels), now),
            pl.BlockSpec((depth, channels), lambda i: (0, 0)),
        ],
        out_specs=[pl.BlockSpec((TILE, width), now)] * ranks,
        out_shape=[jax.ShapeDtypeStruct((tokens, width), bf16)] * ranks,
        compiler_params=pltpu.CompilerParams(vmem_limit_bytes=VMEM_LIMIT),
        cost_estimate=pl.CostEstimate(flops=2 * tokens * depth * channels, bytes_accessed=4 * depth * channels, transcendentals=0),
        name="out_partial",
    )(rank, gated_out, w_out)


def term_kernel(rank_ref, gx_ref, wx_ref, gg_ref, wg_ref, gs_ref, ws_ref, gb_ref, wb_ref, out_ref):
    total = dot_nt(gx_ref[...], wx_ref[...]) + dot_nt(gg_ref[...], wg_ref[...])
    total = total + dot_nt(gs_ref[...], ws_ref[...]) + dot_nt(gb_ref[...], wb_ref[...])
    out_ref[...] = total.astype(out_ref.dtype)


def normed_term(pairs, rank, ranks):
    tokens = pairs[0][0].shape[0]
    depth = pairs[0][1].shape[0]
    rows = tokens // ranks
    specs, flat = [], []
    for g, w in pairs:
        specs.append(pl.BlockSpec((rows, g.shape[1]), lambda i, rank_ref: (i ^ rank_ref[0], 0)))
        specs.append(pl.BlockSpec(w.shape, lambda i, rank_ref: (0, 0)))
        flat += [g, w]
    return pl.pallas_call(
        term_kernel,
        grid_spec=pltpu.PrefetchScalarGridSpec(
            num_scalar_prefetch=1,
            grid=(ranks,),
            in_specs=specs,
            out_specs=pl.BlockSpec((None, rows, depth), lambda i, rank_ref: (i, 0, 0)),
        ),
        out_shape=jax.ShapeDtypeStruct((ranks, rows, depth), bf16),
        compiler_params=pltpu.CompilerParams(vmem_limit_bytes=VMEM_LIMIT),
        cost_estimate=pl.CostEstimate(flops=4 * tokens * depth * 800, bytes_accessed=8 * depth * 768, transcendentals=0),
        name="normed_term",
    )(rank, *flat)


def norm_back_kernel(rank_ref, a_ref, b_ref, hidden_ref, cot_ref, gain_ref, out_ref, dgain_ref):
    grad = a_ref[...].astype(f32) + b_ref[...].astype(f32)
    inputs = hidden_ref[...].astype(f32)
    inv_rms = lax.rsqrt(jnp.mean(inputs * inputs, axis=1, keepdims=True) + EPSILON)
    normed = inputs * inv_rms
    scaled = grad * gain_ref[0:1, :]
    mean = jnp.mean(scaled * normed, axis=1, keepdims=True)
    out_ref[...] = (inv_rms * (scaled - normed * mean) + cot_ref[...].astype(f32)).astype(out_ref.dtype)
    dgain_ref[...] = jnp.broadcast_to(jnp.sum(grad * normed, axis=0, keepdims=True), dgain_ref.shape)


def norm_backward(a, b, hidden, cot, gain_rows, rank):
    rows, depth = a.shape
    mine = lambda i, rank_ref: (rank_ref[0], 0)
    whole = lambda i, rank_ref: (0, 0)
    return pl.pallas_call(
        norm_back_kernel,
        grid_spec=pltpu.PrefetchScalarGridSpec(
            num_scalar_prefetch=1,
            grid=(1,),
            in_specs=[
                pl.BlockSpec((rows, depth), whole),
                pl.BlockSpec((rows, depth), whole),
                pl.BlockSpec((rows, depth), mine),
                pl.BlockSpec((rows, depth), mine),
                pl.BlockSpec((8, depth), whole),
            ],
            out_specs=[pl.BlockSpec((rows, depth), whole), pl.BlockSpec((8, depth), whole)],
        ),
        out_shape=[jax.ShapeDtypeStruct((rows, depth), bf16), jax.ShapeDtypeStruct((8, depth), f32)],
        compiler_params=pltpu.CompilerParams(vmem_limit_bytes=VMEM_LIMIT),
        name="norm_backward",
    )(rank, a, b, hidden, cot, gain_rows)


def outer_from(v, k):
    size = lax.axis_size("dp")
    n = size // 2
    return lax.ppermute(v, "dp", [(((o + k) % n) * 2 + x, o * 2 + x) for o in range(n) for x in range(2)])


def outer_flip(v, bit):
    n = lax.axis_size("dp") // 2
    return lax.ppermute(v, "dp", [((o ^ bit) * 2 + x, o * 2 + x) for o in range(n) for x in range(2)])


def inner_flip(v):
    return lax.ppermute(v, "dp", [(d ^ 1, d) for d in range(lax.axis_size("dp"))])


def rank_flip(v, bit):
    return lax.ppermute(v, "mp", [(m ^ bit, m) for m in range(lax.axis_size("mp"))])


def dp_pieces(piece):
    n = lax.axis_size("dp") // 2
    found = []
    for k in range(n):
        here = piece if k == 0 else outer_from(piece, k)
        found += [here, inner_flip(here)]
    return found


def dp_scatter(blocks):
    n = lax.axis_size("dp") // 2
    total = None
    for k in list(range(1, n)) + [0]:
        here = blocks[2 * k].astype(f32) + inner_flip(blocks[2 * k + 1]).astype(f32)
        if k > 0:
            here = outer_from(here.astype(bf16), -k).astype(f32)
        total = here if total is None else total + here
    return total


def dp_sum(v):
    v = v + inner_flip(v)
    bit = 1
    while bit < lax.axis_size("dp") // 2:
        v = v + outer_flip(v, bit)
        bit *= 2
    return v


def mp_sum(v):
    v = v + rank_flip(v, 1)
    return v + rank_flip(v, 2)


def mp_reduce(blocks):
    near = blocks[0].astype(f32) + rank_flip(blocks[1], 1).astype(f32)
    far = blocks[2].astype(f32) + rank_flip(blocks[3], 1).astype(f32)
    return near, rank_flip(far.astype(bf16), 2)


def mp_pieces(v):
    far = rank_flip(v, 2)
    return [v, rank_flip(v, 1), far, rank_flip(far, 1)]


def in_rank_order(pieces, rank, axis):
    width = pieces[0].shape[axis]
    shape = list(pieces[0].shape)
    shape[axis] = width * len(pieces)
    full = jnp.zeros(shape, pieces[0].dtype)
    for r, piece in enumerate(pieces):
        full = lax.dynamic_update_slice_in_dim(full, piece, (rank ^ r) * width, axis)
    return full


def momentum(moment, grad):
    return 0.5 * moment + 0.5 * grad


def advance(weight, moment, grad):
    fresh = momentum(moment, grad)
    return (fresh, weight - LEARN_RATE * fresh - LEARN_RATE * DECAY_RATE * weight)


def body(
    hidden, segments, cotangent, in_weight, in_moment, bc_weight, bc_moment, step_weight, step_moment,
    out_weight, out_moment, conv_table, conv_moment, bc_table, bc_table_moment, head_table, head_moment,
    norm_gain, gain_moment,
):
    size = lax.axis_size("dp")
    ranks = lax.axis_size("mp")
    n = size // 2
    place, rank = lax.axis_index("dp"), lax.axis_index("mp")
    outer, inner = place // 2, place % 2
    slot = jnp.arange(size)
    idx = (((outer + slot // 2) % n) * 2 + (inner ^ (slot % 2))).astype(jnp.int32)
    slots = ((((slot // 2) - outer) % n) * 2 + (inner ^ (slot % 2))).astype(jnp.int32)
    rank1 = rank.reshape(1).astype(jnp.int32)
    channels = in_weight.shape[2]
    heads = head_table.shape[1]
    tokens, depth = hidden.shape

    x_pieces = dp_pieces(in_weight[:, 1].astype(bf16))
    bc_pieces = dp_pieces(bc_weight.astype(bf16))
    gate_pieces = dp_pieces(in_weight[:, 0].astype(bf16))
    out_pieces = dp_pieces(out_weight.T.astype(bf16))
    w_step = lax.all_gather(step_weight.astype(bf16), "dp", axis=0, tiled=True)
    w_step = pad_lanes(w_step)
    cot = in_rank_order(mp_pieces(cotangent), rank, 1)

    inputs = hidden.astype(f32)
    inv_rms = lax.rsqrt(jnp.mean(inputs * inputs, axis=-1, keepdims=True) + EPSILON)
    normed_low = (inputs * inv_rms * norm_gain).astype(bf16)
    aux, seg_row = segment_facts(segments)
    conv_rows, bc_rows = pad_rows(conv_table), pad_rows(bc_table)
    head_rows = pad_lanes(pad_rows(head_table))
    expand = head_expand(channels)

    x_pre, bc_pre, w_x, w_bc = project(normed_low, [x_pieces, bc_pieces], idx)
    step_pre = dot_nn(normed_low, w_step)
    facts = (aux, seg_row, conv_rows, bc_rows, head_rows, expand)
    mixed, states = ssd_forward(x_pre, bc_pre, step_pre, *facts)
    gate_pre, gout, sums, w_gate, w_out = gate_forward(
        normed_low, cot, mixed, conv_rows, gate_pieces, out_pieces, idx
    )
    sums = mp_sum(sums)
    gated_out, dmixed, dgate, dgain = gate_backward(gate_pre, gout, mixed, sums, conv_rows, channels * ranks)

    grad_out = weight_grad(cot, gated_out, slots)
    grad_gate = weight_grad(normed_low, dgate, slots)
    shard_out = dp_scatter(grad_out)
    shard_gate = dp_scatter(grad_gate)
    near, far = mp_reduce(out_partial(gated_out, w_out, rank1, ranks))
    width = depth // ranks
    resid = lax.dynamic_slice_in_dim(hidden, rank * width, width, 1).astype(f32)
    output = (resid + near + far.astype(f32)).astype(bf16)

    dx, dbc_part, dstep, dconv, dbct_part, dheads = ssd_backward(
        x_pre, bc_pre, step_pre, *facts, mixed, dmixed, states
    )
    grad_x = weight_grad(normed_low, dx, slots)
    shard_x = dp_scatter(grad_x)
    dstep_low = dstep.astype(bf16)
    grad_step = dot_tn(normed_low, dstep_low[:, :heads])
    shard_step = lax.psum_scatter(grad_step, "dp", scatter_dimension=0, tiled=True)

    share = dbc_part.shape[1] // ranks
    dbc_low_part = dbc_part.astype(bf16)
    parts = [lax.dynamic_slice_in_dim(dbc_low_part, (rank ^ r) * share, share, 1) for r in range(ranks)]
    near, far = mp_reduce(parts)
    dbc_low = (near + far.astype(f32)).astype(bf16)
    wb_share = lax.dynamic_slice_in_dim(w_bc, rank * share, share, 1)
    grad_bc = dot_tn(normed_low, dbc_low)
    shard_bc_mine = lax.psum_scatter(grad_bc, "dp", scatter_dimension=0, tiled=True)
    shard_bc = in_rank_order(mp_pieces(shard_bc_mine), rank, 1)

    term = normed_term([(dx, w_x), (dgate, w_gate), (dstep_low, w_step), (dbc_low, wb_share)], rank1, ranks)
    near, far = mp_reduce([term[r] for r in range(ranks)])
    mine, dgain_mine = norm_backward(near, far, hidden, cot, pad_rows(norm_gain[None]), rank1)
    input_grad = in_rank_order(mp_pieces(mine), rank, 0)

    dconv_all = jnp.concatenate([dconv[:5], dgain[:1]], axis=0)
    shared = mp_sum(jnp.concatenate([dbct_part[:5].reshape(-1, LANES), dgain_mine[:1].reshape(-1, LANES)], axis=0))
    packed = jnp.concatenate([shared, dconv_all.reshape(-1, LANES), dheads], axis=0)
    packed = dp_sum(packed)
    cut1 = 5 * 2
    cut2 = cut1 + depth // LANES
    cut3 = cut2 + 6 * channels // LANES
    total_bct = packed[:cut1].reshape(5, 2 * LANES)
    total_gain = packed[cut1:cut2].reshape(-1)
    total_conv = packed[cut2:cut3].reshape(6, channels)
    total_head = packed[cut3:cut3 + 3, :heads]

    in_m, in_w = advance(in_weight, in_moment, jnp.stack([shard_gate, shard_x], axis=1))
    bc_m, bc_w = advance(bc_weight, bc_moment, shard_bc)
    step_m, step_w = advance(step_weight, step_moment, shard_step)
    out_m, out_w = advance(out_weight, out_moment, shard_out.T)
    return (
        output, input_grad, in_m, in_w, bc_m, bc_w, step_m, step_w, out_m, out_w,
        momentum(conv_moment, total_conv),
        momentum(bc_table_moment, total_bct),
        momentum(head_moment, total_head),
        momentum(gain_moment, total_gain),
    )


def solution(mesh):
    placed = (
        P("dp", None),
        P("dp", None),
        P("dp", "mp"),
        P("dp", None, "mp"),
        P("dp", None, "mp"),
        P("dp", None),
        P("dp", None),
        P("dp", "mp"),
        P("dp", "mp"),
        P("mp", "dp"),
        P("mp", "dp"),
        P(None, "mp"),
        P(None, "mp"),
        P(),
        P(),
        P(None, "mp"),
        P(None, "mp"),
        P(),
        P(),
    )
    return jax.shard_map(
        body,
        mesh=mesh,
        in_specs=placed,
        out_specs=(
            P("dp", "mp"),
            P("dp", None),
            P("dp", None, "mp"),
            P("dp", None, "mp"),
            P("dp", None),
            P("dp", None),
            P("dp", "mp"),
            P("dp", "mp"),
            P("mp", "dp"),
            P("mp", "dp"),
            P(None, "mp"),
            P(),
            P(None, "mp"),
            P(),
        ),
        check_vma=False,
    )
```

```python
import functools

import jax
import jax.numpy as jnp
from jax import lax
from jax.experimental import pallas as pl
from jax.experimental.pallas import tpu as pltpu
from jax.sharding import PartitionSpec as P

CHUNK = 128
EPSILON = 1e-05
LEARN_RATE = 0.0001
DECAY_RATE = 0.1
WIDTH = 64
LANES = 128
HALO = 8
bf16 = jnp.bfloat16
f32 = jnp.float32
VMEM_LIMIT = 56 * 1024 * 1024


def dot_nn(a, b):
    return lax.dot_general(a, b, (((1,), (0,)), ((), ())), preferred_element_type=f32)


def dot_nt(a, b):
    return lax.dot_general(a, b, (((1,), (1,)), ((), ())), preferred_element_type=f32)


def dot_tn(a, b):
    return lax.dot_general(a, b, (((0,), (0,)), ((), ())), preferred_element_type=f32)


def split3(v):
    high = v.astype(bf16)
    rest = v - high.astype(f32)
    mid = rest.astype(bf16)
    low = (rest - mid.astype(f32)).astype(bf16)
    return high, mid, low


def exact_left(ones, v):
    high, mid, low = split3(v)
    return dot_nn(ones, high) + dot_nn(ones, mid) + dot_nn(ones, low)


def spread(v, expand):
    high, mid, low = split3(v)
    return dot_nn(high, expand) + dot_nn(mid, expand) + dot_nn(low, expand)


def gather_heads(v, expand):
    high = v.astype(bf16)
    mid = (v - high.astype(f32)).astype(bf16)
    return dot_nt(high, expand) + dot_nt(mid, expand)


def sigmoid(v):
    return 1.0 / (1.0 + jnp.exp(-v))


def conv_block(scratch, before, now, taps, keep):
    rows = now.shape[0]
    scratch[0:HALO, :] = before
    scratch[HALO:HALO + rows, :] = now
    total = taps[4:5, :] + taps[0:1, :] * now
    for lag in (1, 2, 3):
        moved = scratch[HALO - lag:HALO - lag + rows, :]
        total = total + taps[lag:lag + 1, :] * (moved * keep[:, lag - 1:lag])
    return total


def step_parts(step_pre, heads):
    raw = step_pre + heads[0:1, :]
    steps = jnp.maximum(raw, 0.0) + jnp.log1p(jnp.exp(-jnp.abs(raw)))
    rates = -jnp.exp(heads[1:2, :])
    return raw, steps, rates


def triangle(lower):
    row = lax.broadcasted_iota(jnp.int32, (CHUNK, CHUNK), 0)
    col = lax.broadcasted_iota(jnp.int32, (CHUNK, CHUNK), 1)
    return row >= col if lower else row <= col


def ssd_forward_kernel(
    x_ref, xb_ref, bc_ref, bcb_ref, st_ref, aux_ref, seg_ref, conv_ref, bct_ref, heads_ref, expand_ref,
    mixed_ref, state_ref, state, xs_scr, bc_scr,
):
    chunk = pl.program_id(0)

    @pl.when(chunk == 0)
    def _():
        state[...] = jnp.zeros_like(state)

    channels = x_ref.shape[1]
    aux = aux_ref[...]
    expand = expand_ref[...]
    u = conv_block(xs_scr, xb_ref[...], x_ref[...], conv_ref, aux)
    x_act = u * sigmoid(u)
    ubc = conv_block(bc_scr, bcb_ref[...], bc_ref[...], bct_ref, aux)
    bc_act = (ubc * sigmoid(ubc)).astype(bf16)
    b_mat, c_mat = bc_act[:, :LANES], bc_act[:, LANES:]
    _, steps, rates = step_parts(st_ref[...], heads_ref)
    lower = triangle(True)
    cum = exact_left(lower.astype(bf16), steps * rates)
    cum_t = cum.T
    tail = cum[CHUNK - 1:CHUNK, :]
    entry = jnp.exp(cum) * aux[:, 6:7]
    to_end = jnp.exp(tail - cum) * aux[:, 7:8]
    wide = spread(jnp.concatenate([steps, entry, to_end], axis=0), expand)
    step_e, entry_e, to_end_e = wide[:CHUNK], wide[CHUNK:2 * CHUNK], wide[2 * CHUNK:]
    skip_e = spread(jnp.broadcast_to(heads_ref[2:3, :], (8, LANES)), expand)[0:1, :]
    mask = lower & (aux[:, 8:9] == seg_ref[...])
    scores = jnp.where(mask, dot_nt(c_mat, b_mat), 0.0)
    xs = x_act * step_e
    xs_low = xs.astype(bf16)
    held = state[...]
    held_low = held.astype(bf16)
    state_ref[...] = held_low
    out = dot_nn(c_mat, held_low) * entry_e + skip_e * x_act
    state[...] = held * entry_e[CHUNK - 1:CHUNK, :] + dot_tn(b_mat, (xs * to_end_e).astype(bf16))
    first = lax.broadcasted_iota(jnp.int32, (CHUNK, LANES), 1) < WIDTH
    zero = jnp.zeros((CHUNK, LANES), bf16)
    for pair in range(channels // LANES):
        span = slice(pair * LANES, (pair + 1) * LANES)
        parts = []
        for head in (2 * pair, 2 * pair + 1):
            diff = cum[:, head:head + 1] - cum_t[head:head + 1, :]
            parts.append((scores * jnp.exp(jnp.minimum(diff, 0.0))).astype(bf16))
        own = xs_low[:, span]
        both = jnp.concatenate([jnp.where(first, own, zero), jnp.where(first, zero, own)], axis=0)
        mixed_ref[:, span] = out[:, span] + dot_nn(jnp.concatenate(parts, axis=1), both)


def ssd_backward_kernel(
    x_ref, xb_ref, bc_ref, bcb_ref, st_ref, aux_ref, seg_ref, conv_ref, bct_ref, heads_ref, expand_ref,
    mixed_ref, dy_ref, state_ref,
    dx_ref, dbc_ref, dst_ref, dconv_ref, dbct_ref, dheads_ref,
    dstate, xs_scr, bc_scr, du_scr, dubc_scr,
):
    at = pl.program_id(0)

    @pl.when(at == 0)
    def _():
        dstate[...] = jnp.zeros_like(dstate)
        du_scr[...] = jnp.zeros_like(du_scr)
        dubc_scr[...] = jnp.zeros_like(dubc_scr)
        dconv_ref[...] = jnp.zeros_like(dconv_ref)
        dbct_ref[...] = jnp.zeros_like(dbct_ref)
        dheads_ref[...] = jnp.zeros_like(dheads_ref)

    channels = x_ref.shape[1]
    aux = aux_ref[...]
    expand = expand_ref[...]
    x_now, bc_now = x_ref[...], bc_ref[...]
    u = conv_block(xs_scr, xb_ref[...], x_now, conv_ref, aux)
    sg = sigmoid(u)
    x_act = u * sg
    ubc = conv_block(bc_scr, bcb_ref[...], bc_now, bct_ref, aux)
    sgbc = sigmoid(ubc)
    bc_act = (ubc * sgbc).astype(bf16)
    b_mat, c_mat = bc_act[:, :LANES], bc_act[:, LANES:]
    raw, steps, rates = step_parts(st_ref[...], heads_ref)
    lower = triangle(True)
    cum = exact_left(lower.astype(bf16), steps * rates)
    cum_t = cum.T
    tail = cum[CHUNK - 1:CHUNK, :]
    entry = jnp.exp(cum) * aux[:, 6:7]
    to_end = jnp.exp(tail - cum) * aux[:, 7:8]
    wide = spread(jnp.concatenate([steps, entry, to_end], axis=0), expand)
    step_e, entry_e, to_end_e = wide[:CHUNK], wide[CHUNK:2 * CHUNK], wide[2 * CHUNK:]
    skip_e = spread(jnp.broadcast_to(heads_ref[2:3, :], (8, LANES)), expand)[0:1, :]
    upper = triangle(False)
    mask = upper & (aux[:, 8:9] == seg_ref[...])
    scores = jnp.where(mask, dot_nt(b_mat, c_mat), 0.0)
    xs = x_act * step_e
    xs_low = xs.astype(bf16)
    dy_low = dy_ref[...]
    dy = dy_low.astype(f32)
    held_low = state_ref[...]
    grad = dstate[...]
    grad_low = grad.astype(bf16)
    entry_dy = (entry_e * dy).astype(bf16)
    kept_e = entry_e[CHUNK - 1:CHUNK, :]
    dstate[...] = grad * kept_e + dot_tn(c_mat, entry_dy)
    dc = dot_nt(entry_dy, held_low)
    db = dot_nt((xs * to_end_e).astype(bf16), grad_low)
    q_state = dot_nn(b_mat, grad_low) * to_end_e
    first = lax.broadcasted_iota(jnp.int32, (CHUNK, LANES), 1) < WIDTH
    zero = jnp.zeros((CHUNK, LANES), bf16)
    dscores = jnp.zeros((CHUNK, CHUNK), f32)
    q_parts = []
    for pair in range(channels // LANES):
        span = slice(pair * LANES, (pair + 1) * LANES)
        own = dy_low[:, span]
        both = jnp.concatenate([jnp.where(first, own, zero), jnp.where(first, zero, own)], axis=0)
        dweights = dot_nt(xs_low[:, span], both)
        parts = []
        for i, head in enumerate((2 * pair, 2 * pair + 1)):
            diff = cum_t[head:head + 1, :] - cum[:, head:head + 1]
            decay = jnp.exp(jnp.minimum(diff, 0.0))
            parts.append((scores * decay).astype(bf16))
            dscores = dscores + dweights[:, i * LANES:(i + 1) * LANES] * decay
        q_parts.append(dot_nn(jnp.concatenate(parts, axis=1), both))
    q = jnp.concatenate(q_parts, axis=1) + q_state
    dscores_low = jnp.where(mask, dscores, 0.0).astype(bf16)
    db = db + dot_nn(dscores_low, c_mat)
    dc = dc + dot_tn(dscores_low, b_mat)
    xs_round = xs_low.astype(f32)
    rows = gather_heads(
        jnp.concatenate(
            [
                dy * (mixed_ref[...] - skip_e * x_act) - xs_round * q,
                x_act * q,
            ],
            axis=0,
        ),
        expand,
    )
    flow, dstep = rows[:CHUNK], rows[CHUNK:]
    sums = jnp.concatenate(
        [
            jnp.sum(xs_round * q_state + kept_e * (held_low.astype(f32) * grad), axis=0, keepdims=True),
            jnp.sum(dy * x_act, axis=0, keepdims=True),
            jnp.zeros((6, channels), f32),
        ],
        axis=0,
    )
    sums = gather_heads(sums, expand)
    dlog = exact_left(upper.astype(bf16), flow) + sums[0:1, :]
    dstep = dstep + rates * dlog
    draw = dstep * sigmoid(raw)
    dst_ref[...] = draw
    dheads_ref[0:1, :] += jnp.sum(draw, axis=0, keepdims=True)
    dheads_ref[1:2, :] += rates * jnp.sum(dlog * steps, axis=0, keepdims=True)
    dheads_ref[2:3, :] += sums[1:2, :]

    def conv_back(scratch, du, now, taps, dtaps):
        scratch[0:CHUNK, :] = du
        total = taps[0:1, :] * du
        dtaps[0:1, :] += jnp.sum(now * du, axis=0, keepdims=True)
        dtaps[4:5, :] += jnp.sum(du, axis=0, keepdims=True)
        for lag in (1, 2, 3):
            moved = scratch[lag:lag + CHUNK, :] * aux[:, 2 + lag:3 + lag]
            total = total + taps[lag:lag + 1, :] * moved
            dtaps[lag:lag + 1, :] += jnp.sum(now * moved, axis=0, keepdims=True)
        scratch[CHUNK:CHUNK + HALO, :] = du[0:HALO, :]
        return total

    du = (skip_e * dy + step_e * q) * (sg * (1.0 + u * (1.0 - sg)))
    dx_ref[...] = conv_back(du_scr, du, x_now, conv_ref, dconv_ref).astype(dx_ref.dtype)
    dubc = jnp.concatenate([db, dc], axis=1) * (sgbc * (1.0 + ubc * (1.0 - sgbc)))
    dbc_ref[...] = conv_back(dubc_scr, dubc, bc_now, bct_ref, dbct_ref)


def common_specs(place, channels):
    before = lambda i: (jnp.maximum(place(i) * (CHUNK // HALO) - 1, 0), 0)
    now = lambda i: (place(i), 0)
    whole = lambda i: (0, 0)
    return [
        pl.BlockSpec((CHUNK, channels), now),
        pl.BlockSpec((HALO, channels), before),
        pl.BlockSpec((CHUNK, 2 * LANES), now),
        pl.BlockSpec((HALO, 2 * LANES), before),
        pl.BlockSpec((CHUNK, LANES), now),
        pl.BlockSpec((CHUNK, 16), now),
        pl.BlockSpec((1, CHUNK), lambda i: (0, place(i))),
        pl.BlockSpec((8, channels), whole),
        pl.BlockSpec((8, 2 * LANES), whole),
        pl.BlockSpec((8, LANES), whole),
        pl.BlockSpec((LANES, channels), whole),
    ]


def ssd_forward(x_pre, bc_pre, step_pre, aux, seg_row, conv_rows, bc_rows, head_rows, expand):
    tokens, channels = x_pre.shape
    count = tokens // CHUNK
    now = lambda i: (i, 0)
    return pl.pallas_call(
        ssd_forward_kernel,
        grid=(count,),
        in_specs=common_specs(lambda i: i, channels),
        out_specs=[
            pl.BlockSpec((CHUNK, channels), now),
            pl.BlockSpec((None, LANES, channels), lambda i: (i, 0, 0)),
        ],
        out_shape=[
            jax.ShapeDtypeStruct((tokens, channels), f32),
            jax.ShapeDtypeStruct((count, LANES, channels), bf16),
        ],
        scratch_shapes=[
            pltpu.VMEM((LANES, channels), f32),
            pltpu.VMEM((HALO + CHUNK, channels), f32),
            pltpu.VMEM((HALO + CHUNK, 2 * LANES), f32),
        ],
        compiler_params=pltpu.CompilerParams(vmem_limit_bytes=VMEM_LIMIT),
        name="ssd_forward",
    )(x_pre, x_pre, bc_pre, bc_pre, step_pre, aux, seg_row, conv_rows, bc_rows, head_rows, expand)


def ssd_backward(x_pre, bc_pre, step_pre, aux, seg_row, conv_rows, bc_rows, head_rows, expand, mixed, dy, states):
    tokens, channels = x_pre.shape
    count = tokens // CHUNK
    place = lambda i: count - 1 - i
    now = lambda i: (place(i), 0)
    whole = lambda i: (0, 0)
    return pl.pallas_call(
        ssd_backward_kernel,
        grid=(count,),
        in_specs=common_specs(place, channels) + [
            pl.BlockSpec((CHUNK, channels), now),
            pl.BlockSpec((CHUNK, channels), now),
            pl.BlockSpec((None, LANES, channels), lambda i: (place(i), 0, 0)),
        ],
        out_specs=[
            pl.BlockSpec((CHUNK, channels), now),
            pl.BlockSpec((CHUNK, 2 * LANES), now),
            pl.BlockSpec((CHUNK, LANES), now),
            pl.BlockSpec((8, channels), whole),
            pl.BlockSpec((8, 2 * LANES), whole),
            pl.BlockSpec((8, LANES), whole),
        ],
        out_shape=[
            jax.ShapeDtypeStruct((tokens, channels), bf16),
            jax.ShapeDtypeStruct((tokens, 2 * LANES), f32),
            jax.ShapeDtypeStruct((tokens, LANES), f32),
            jax.ShapeDtypeStruct((8, channels), f32),
            jax.ShapeDtypeStruct((8, 2 * LANES), f32),
            jax.ShapeDtypeStruct((8, LANES), f32),
        ],
        scratch_shapes=[
            pltpu.VMEM((LANES, channels), f32),
            pltpu.VMEM((HALO + CHUNK, channels), f32),
            pltpu.VMEM((HALO + CHUNK, 2 * LANES), f32),
            pltpu.VMEM((HALO + CHUNK, channels), f32),
            pltpu.VMEM((HALO + CHUNK, 2 * LANES), f32),
        ],
        compiler_params=pltpu.CompilerParams(vmem_limit_bytes=VMEM_LIMIT),
        name="ssd_backward",
    )(x_pre, x_pre, bc_pre, bc_pre, step_pre, aux, seg_row, conv_rows, bc_rows, head_rows, expand, mixed, dy, states)


def segment_facts(seg):
    row = seg[0]
    tokens = row.shape[0]
    cols = []
    for lag in (1, 2, 3):
        cols.append(jnp.pad(row[:-lag], (lag, 0), constant_values=-1) == row)
    for lag in (1, 2, 3):
        cols.append(jnp.pad(row[lag:], (0, lag), constant_values=-1) == row)
    blocks = row.reshape(tokens // CHUNK, CHUNK)
    ends = blocks[:, -1:]
    before = jnp.concatenate([jnp.full((1, 1), -1, row.dtype), ends[:-1]], axis=0)
    cols.append((blocks == before).reshape(-1))
    cols.append((blocks == ends).reshape(-1))
    cols.append(row)
    facts = jnp.stack([c.astype(f32) for c in cols], axis=1)
    return jnp.pad(facts, ((0, 0), (0, 16 - facts.shape[1]))), seg.astype(f32)


def pad_rows(table, rows=8):
    return jnp.pad(table, ((0, rows - table.shape[0]), (0, 0)))


def pad_lanes(table, lanes=LANES):
    return jnp.pad(table, ((0, 0), (0, lanes - table.shape[1])))


def head_expand(channels):
    head = jnp.arange(LANES)[:, None]
    return (head == (jnp.arange(channels) // WIDTH)[None, :]).astype(bf16)


TILE = 256
TILE_D = 384


def fill(dest, pieces, idx_ref):
    for s, piece in enumerate(pieces):
        rows = piece.shape[0]
        dest[pl.ds(pl.multiple_of(idx_ref[s] * rows, rows), rows), :] = piece[...]


def params():
    return pltpu.CompilerParams(vmem_limit_bytes=VMEM_LIMIT)


def cost(flops, moved):
    return pl.CostEstimate(flops=int(flops), bytes_accessed=int(moved), transcendentals=0)


def prepare_kernel(hidden_ref, gain_ref, cot_ref, low_ref, low_t_ref, cot_t_ref):
    inputs = hidden_ref[...].astype(f32)
    inv_rms = lax.rsqrt(jnp.mean(inputs * inputs, axis=1, keepdims=True) + EPSILON)
    low = (inputs * inv_rms * gain_ref[0:1, :]).astype(bf16)
    low_ref[...] = low
    low_t_ref[...] = low.T
    cot_t_ref[...] = cot_ref[...].T


def prepare(hidden, gain_rows, cot):
    tokens, depth = hidden.shape
    block = pl.BlockSpec((TILE, depth), lambda i: (i, 0))
    turned = pl.BlockSpec((depth, TILE), lambda i: (0, i))
    return pl.pallas_call(
        prepare_kernel,
        grid=(tokens // TILE,),
        in_specs=[block, pl.BlockSpec((8, depth), lambda i: (0, 0)), block],
        out_specs=[block, turned, turned],
        out_shape=[
            jax.ShapeDtypeStruct((tokens, depth), bf16),
            jax.ShapeDtypeStruct((depth, tokens), bf16),
            jax.ShapeDtypeStruct((depth, tokens), bf16),
        ],
        compiler_params=params(),
        name="prepare",
    )(hidden, gain_rows, cot)


def project_kernel(idx_ref, lhs_ref, *refs, count):
    pieces, (x_ref, small_ref, w_ref) = refs[:count], refs[count:]

    @pl.when(pl.program_id(0) == 0)
    def _():
        fill(w_ref, pieces, idx_ref)

    product = dot_nn(lhs_ref[...], w_ref[...])
    channels = x_ref.shape[1]
    x_ref[...] = product[:, :channels]
    small_ref[...] = product[:, channels:].T


def project(lhs, pieces, idx, channels):
    tokens, depth = lhs.shape
    count, width = len(pieces), pieces[0].shape[1]
    whole = lambda i: (0, 0)
    return pl.pallas_call(
        functools.partial(project_kernel, count=count),
        grid=(tokens // TILE,),
        in_specs=[pl.BlockSpec(memory_space=pltpu.SMEM), pl.BlockSpec((TILE, depth), lambda i: (i, 0))]
        + [pl.BlockSpec(p.shape, whole) for p in pieces],
        out_specs=[
            pl.BlockSpec((TILE, channels), lambda i: (i, 0)),
            pl.BlockSpec((width - channels, TILE), lambda i: (0, i)),
            pl.BlockSpec((depth, width), whole),
        ],
        out_shape=[
            jax.ShapeDtypeStruct((tokens, channels), f32),
            jax.ShapeDtypeStruct((width - channels, tokens), f32),
            jax.ShapeDtypeStruct((depth, width), bf16),
        ],
        compiler_params=params(),
        cost_estimate=cost(2 * tokens * depth * width, 6 * depth * width),
        name="project",
    )(idx, lhs, *pieces)


def column_to_row(col):
    return jnp.broadcast_to(col, (col.shape[0], LANES)).T[0:8, :]


def row_to_column(row):
    return jnp.broadcast_to(row, (LANES, row.shape[1])).T[:, 0:1]


def gate_kernel(idx_ref, lhs_ref, mixed_ref, *refs, count):
    pieces, (gate_ref, sums_ref, w_ref) = refs[:count], refs[count:]

    @pl.when(pl.program_id(0) == 0)
    def _():
        fill(w_ref, pieces, idx_ref)

    gate = dot_nn(lhs_ref[...], w_ref[...])
    gate_ref[...] = gate
    gated = mixed_ref[...] * (gate * sigmoid(gate))
    sums_ref[...] = column_to_row(jnp.sum(gated * gated, axis=1, keepdims=True))


def gate_forward(lhs, mixed, pieces, idx):
    tokens, depth = lhs.shape
    channels = mixed.shape[1]
    whole = lambda i: (0, 0)
    now = lambda i: (i, 0)
    return pl.pallas_call(
        functools.partial(gate_kernel, count=len(pieces)),
        grid=(tokens // TILE,),
        in_specs=[
            pl.BlockSpec(memory_space=pltpu.SMEM),
            pl.BlockSpec((TILE, depth), now),
            pl.BlockSpec((TILE, channels), now),
        ]
        + [pl.BlockSpec(p.shape, whole) for p in pieces],
        out_specs=[
            pl.BlockSpec((TILE, channels), now),
            pl.BlockSpec((8, TILE), lambda i: (0, i)),
            pl.BlockSpec((depth, channels), whole),
        ],
        out_shape=[
            jax.ShapeDtypeStruct((tokens, channels), f32),
            jax.ShapeDtypeStruct((8, tokens), f32),
            jax.ShapeDtypeStruct((depth, channels), bf16),
        ],
        compiler_params=params(),
        cost_estimate=cost(2 * tokens * depth * channels, 8 * depth * channels),
        name="gate_forward",
    )(idx, lhs, mixed, *pieces)


def gated_kernel(gate_ref, mixed_ref, square_ref, conv_ref, out_ref, *, inner_total):
    gate = gate_ref[...]
    scale = lax.rsqrt(row_to_column(square_ref[0:1, :]) / inner_total + EPSILON)
    gated = mixed_ref[...] * (gate * sigmoid(gate))
    out_ref[...] = (gated * scale * conv_ref[5:6, :]).astype(bf16)


def gated_norm(gate, mixed, square, conv_rows, inner_total):
    tokens, channels = gate.shape
    block = pl.BlockSpec((TILE, channels), lambda i: (i, 0))
    return pl.pallas_call(
        functools.partial(gated_kernel, inner_total=inner_total),
        grid=(tokens // TILE,),
        in_specs=[block, block, pl.BlockSpec((8, TILE), lambda i: (0, i)), pl.BlockSpec((8, channels), lambda i: (0, 0))],
        out_specs=block,
        out_shape=jax.ShapeDtypeStruct((tokens, channels), bf16),
        compiler_params=params(),
        cost_estimate=cost(20 * tokens * channels, 10 * tokens * channels),
        name="gated_norm",
    )(gate, mixed, square, conv_rows)


def gout_kernel(idx_ref, cot_ref, gate_ref, mixed_ref, conv_ref, *refs, count):
    pieces, (gout_ref, sums_ref, w_ref) = refs[:count], refs[count:]

    @pl.when(pl.program_id(0) == 0)
    def _():
        fill(w_ref, pieces, idx_ref)

    gout = dot_nn(cot_ref[...], w_ref[...])
    gout_ref[...] = gout
    gate = gate_ref[...]
    gated = mixed_ref[...] * (gate * sigmoid(gate))
    sums_ref[...] = column_to_row(jnp.sum(gout * conv_ref[5:6, :] * gated, axis=1, keepdims=True))


def grad_gout(cot, gate, mixed, conv_rows, pieces, idx):
    tokens, depth = cot.shape
    channels = mixed.shape[1]
    whole = lambda i: (0, 0)
    now = lambda i: (i, 0)
    return pl.pallas_call(
        functools.partial(gout_kernel, count=len(pieces)),
        grid=(tokens // TILE,),
        in_specs=[
            pl.BlockSpec(memory_space=pltpu.SMEM),
            pl.BlockSpec((TILE, depth), now),
            pl.BlockSpec((TILE, channels), now),
            pl.BlockSpec((TILE, channels), now),
            pl.BlockSpec((8, channels), whole),
        ]
        + [pl.BlockSpec(p.shape, whole) for p in pieces],
        out_specs=[
            pl.BlockSpec((TILE, channels), now),
            pl.BlockSpec((8, TILE), lambda i: (0, i)),
            pl.BlockSpec((depth, channels), whole),
        ],
        out_shape=[
            jax.ShapeDtypeStruct((tokens, channels), f32),
            jax.ShapeDtypeStruct((8, tokens), f32),
            jax.ShapeDtypeStruct((depth, channels), bf16),
        ],
        compiler_params=params(),
        cost_estimate=cost(2 * tokens * depth * channels, 8 * depth * channels),
        name="grad_gout",
    )(idx, cot, gate, mixed, conv_rows, *pieces)


def gate_back_kernel(gate_ref, gout_ref, mixed_ref, square_ref, inner_ref, conv_ref, dmixed_ref, dgate_ref, dgain_ref, *, inner_total):
    gate, gout, mixed = gate_ref[...], gout_ref[...], mixed_ref[...]
    gain = conv_ref[5:6, :]
    square, inner = row_to_column(square_ref[0:1, :]), row_to_column(inner_ref[0:1, :])
    scale = lax.rsqrt(square / inner_total + EPSILON)
    sg = sigmoid(gate)
    act = gate * sg
    gated = mixed * act
    dgated = scale * (gain * gout) - gated * (scale * scale * scale * inner / inner_total)
    dmixed_ref[...] = (dgated * act).astype(bf16)
    dgate_ref[...] = (dgated * mixed * sg * (1.0 + gate * (1.0 - sg))).astype(bf16)

    @pl.when(pl.program_id(0) == 0)
    def _():
        dgain_ref[...] = jnp.zeros_like(dgain_ref)

    dgain_ref[0:1, :] += jnp.sum(gout * gated * scale, axis=0, keepdims=True)


def gate_backward(gate, gout, mixed, square, inner, conv_rows, inner_total):
    tokens, channels = gate.shape
    whole = lambda i: (0, 0)
    block = pl.BlockSpec((TILE, channels), lambda i: (i, 0))
    row = pl.BlockSpec((8, TILE), lambda i: (0, i))
    return pl.pallas_call(
        functools.partial(gate_back_kernel, inner_total=inner_total),
        grid=(tokens // TILE,),
        in_specs=[block, block, block, row, row, pl.BlockSpec((8, channels), whole)],
        out_specs=[block, block, pl.BlockSpec((8, channels), whole)],
        out_shape=[
            jax.ShapeDtypeStruct((tokens, channels), bf16),
            jax.ShapeDtypeStruct((tokens, channels), bf16),
            jax.ShapeDtypeStruct((8, channels), f32),
        ],
        compiler_params=params(),
        cost_estimate=cost(30 * tokens * channels, 16 * tokens * channels),
        name="gate_backward",
    )(gate, gout, mixed, square, inner, conv_rows)


def weight_grad_kernel(idx_ref, lhs_ref, *refs, count, parts):
    rhs, outs, scratch = refs[:parts], refs[parts:parts + count], refs[parts + count]
    at = pl.program_id(0)
    start = 0
    for part in rhs:
        width = part.shape[1]
        scratch[pl.ds(pl.multiple_of(at * TILE_D, TILE_D), TILE_D), start:start + width] = dot_nn(lhs_ref[...], part[...]).astype(bf16)
        start += width

    @pl.when(at == pl.num_programs(0) - 1)
    def _():
        for s, out in enumerate(outs):
            rows = out.shape[0]
            out[...] = scratch[pl.ds(pl.multiple_of(idx_ref[s] * rows, rows), rows), :]


def weight_grad(lhs_t, rhs, idx):
    depth, tokens = lhs_t.shape
    width = sum(r.shape[1] for r in rhs)
    count = idx.shape[0]
    rows = depth // count
    whole = lambda i: (0, 0)
    return pl.pallas_call(
        functools.partial(weight_grad_kernel, count=count, parts=len(rhs)),
        grid=(depth // TILE_D,),
        in_specs=[pl.BlockSpec(memory_space=pltpu.SMEM), pl.BlockSpec((TILE_D, tokens), lambda i: (i, 0))]
        + [pl.BlockSpec(r.shape, whole) for r in rhs],
        out_specs=[pl.BlockSpec((rows, width), whole)] * count,
        out_shape=[jax.ShapeDtypeStruct((rows, width), bf16)] * count,
        scratch_shapes=[pltpu.VMEM((depth, width), bf16)],
        compiler_params=params(),
        cost_estimate=cost(2 * tokens * depth * width, 4 * depth * width),
        name="weight_grad",
    )(idx, lhs_t, *rhs)


def out_kernel(rank_ref, lhs_ref, w_ref, *outs):
    product = dot_nt(lhs_ref[...], w_ref[...]).astype(bf16)
    for r, out in enumerate(outs):
        @pl.when(pl.program_id(0) == r)
        def _():
            out[...] = product


def out_partial(gated_out, w_out, rank, ranks):
    tokens, channels = gated_out.shape
    depth = w_out.shape[0]
    width = depth // ranks
    whole = lambda i, rank_ref: (0, 0)
    return pl.pallas_call(
        out_kernel,
        grid_spec=pltpu.PrefetchScalarGridSpec(
            num_scalar_prefetch=1,
            grid=(ranks,),
            in_specs=[
                pl.BlockSpec((tokens, channels), whole),
                pl.BlockSpec((width, channels), lambda i, rank_ref: (i ^ rank_ref[0], 0)),
            ],
            out_specs=[pl.BlockSpec((tokens, width), whole)] * ranks,
        ),
        out_shape=[jax.ShapeDtypeStruct((tokens, width), bf16)] * ranks,
        compiler_params=params(),
        cost_estimate=cost(2 * tokens * depth * channels, 4 * depth * channels),
        name="out_partial",
    )(rank, gated_out, w_out)


def term_kernel(rank_ref, *refs, parts, ranks):
    pairs, outs, scratch = refs[:2 * parts], refs[2 * parts:2 * parts + ranks], refs[2 * parts + ranks]
    total = None
    for p in range(parts):
        product = dot_nt(pairs[2 * p][...], pairs[2 * p + 1][...])
        total = product if total is None else total + product
    scratch[...] = total.astype(bf16)
    for r, out in enumerate(outs):
        rows = out.shape[0]
        out[...] = scratch[pl.ds(pl.multiple_of((rank_ref[0] ^ r) * rows, rows), rows), :]


def normed_term(pairs, rank, ranks):
    tokens = pairs[0][0].shape[0]
    depth = pairs[0][1].shape[0]
    rows = tokens // ranks
    specs, flat, inner = [], [], 0
    for g, w in pairs:
        specs.append(pl.BlockSpec(g.shape, lambda i: (0, 0)))
        specs.append(pl.BlockSpec((TILE_D, w.shape[1]), lambda i: (i, 0)))
        flat += [g, w]
        inner += w.shape[1]
    return pl.pallas_call(
        functools.partial(term_kernel, parts=len(pairs), ranks=ranks),
        grid=(depth // TILE_D,),
        in_specs=[pl.BlockSpec(memory_space=pltpu.SMEM)] + specs,
        out_specs=[pl.BlockSpec((rows, TILE_D), lambda i: (0, i))] * ranks,
        out_shape=[jax.ShapeDtypeStruct((rows, depth), bf16)] * ranks,
        scratch_shapes=[pltpu.VMEM((tokens, TILE_D), bf16)],
        compiler_params=params(),
        cost_estimate=cost(2 * tokens * depth * inner, 4 * depth * inner),
        name="normed_term",
    )(rank, *flat)


def norm_back_kernel(rank_ref, a_ref, b_ref, hidden_ref, cot_ref, gain_ref, out_ref, dgain_ref):
    grad = a_ref[...].astype(f32) + b_ref[...].astype(f32)
    inputs = hidden_ref[...].astype(f32)
    inv_rms = lax.rsqrt(jnp.mean(inputs * inputs, axis=1, keepdims=True) + EPSILON)
    normed = inputs * inv_rms
    scaled = grad * gain_ref[0:1, :]
    mean = jnp.mean(scaled * normed, axis=1, keepdims=True)
    out_ref[...] = (inv_rms * (scaled - normed * mean) + cot_ref[...].astype(f32)).astype(out_ref.dtype)
    dgain_ref[...] = jnp.broadcast_to(jnp.sum(grad * normed, axis=0, keepdims=True), dgain_ref.shape)


def norm_backward(a, b, hidden, cot, gain_rows, rank):
    rows, depth = a.shape
    mine = lambda i, rank_ref: (rank_ref[0], 0)
    whole = lambda i, rank_ref: (0, 0)
    return pl.pallas_call(
        norm_back_kernel,
        grid_spec=pltpu.PrefetchScalarGridSpec(
            num_scalar_prefetch=1,
            grid=(1,),
            in_specs=[
                pl.BlockSpec((rows, depth), whole),
                pl.BlockSpec((rows, depth), whole),
                pl.BlockSpec((rows, depth), mine),
                pl.BlockSpec((rows, depth), mine),
                pl.BlockSpec((8, depth), whole),
            ],
            out_specs=[pl.BlockSpec((rows, depth), whole), pl.BlockSpec((8, depth), whole)],
        ),
        out_shape=[jax.ShapeDtypeStruct((rows, depth), bf16), jax.ShapeDtypeStruct((8, depth), f32)],
        compiler_params=params(),
        name="norm_backward",
    )(rank, a, b, hidden, cot, gain_rows)


def after(v, *done):
    return lax.optimization_barrier((v, *done))[0]


def outer_from(v, k):
    n = lax.axis_size("dp") // 2
    return lax.ppermute(v, "dp", [(((o + k) % n) * 2 + x, o * 2 + x) for o in range(n) for x in range(2)])


def outer_flip(v, bit):
    n = lax.axis_size("dp") // 2
    return lax.ppermute(v, "dp", [((o ^ bit) * 2 + x, o * 2 + x) for o in range(n) for x in range(2)])


def inner_flip(v):
    return lax.ppermute(v, "dp", [(d ^ 1, d) for d in range(lax.axis_size("dp"))])


def rank_flip(v, bit):
    return lax.ppermute(v, "mp", [(m ^ bit, m) for m in range(lax.axis_size("mp"))])


def hops(n):
    order = []
    for k in range(1, n // 2 + 1):
        order.append(k)
        if n - k != k:
            order.append(n - k)
    return order


def dp_pieces(piece, ready=None):
    n = lax.axis_size("dp") // 2
    found = [None] * (2 * n)
    start = piece if ready is None else after(piece, ready)
    arrived = {0: start}
    for k in hops(n):
        arrived[k] = outer_from(start, k)
    for k in [0] + hops(n):
        found[2 * k], found[2 * k + 1] = arrived[k], inner_flip(arrived[k])
    return found, arrived[hops(n)[-1]]


def dp_scatter(blocks, ready=None):
    n = lax.axis_size("dp") // 2
    total, last = None, ready
    for k in hops(n)[::-1] + [0]:
        send = blocks[2 * k + 1] if last is None else after(blocks[2 * k + 1], last)
        last = inner_flip(send)
        here = blocks[2 * k].astype(f32) + last.astype(f32)
        if k > 0:
            here = outer_from(here.astype(bf16), n - k).astype(f32)
        total = here if total is None else total + here
    return total, last


def dp_sum(v):
    v = v + inner_flip(v)
    bit = 1
    while bit < lax.axis_size("dp") // 2:
        v = v + outer_flip(v, bit)
        bit *= 2
    return v


def mp_sum(v):
    v = v + rank_flip(v, 1)
    return v + rank_flip(v, 2)


def mp_sum_direct(v):
    return (v + rank_flip(v, 1)) + (rank_flip(v, 2) + rank_flip(v, 3))


def mp_reduce(blocks):
    far = blocks[2].astype(f32) + rank_flip(blocks[3], 1).astype(f32)
    near = blocks[0].astype(f32) + rank_flip(blocks[1], 1).astype(f32)
    return near, rank_flip(far.astype(bf16), 2)


def mp_pieces(v):
    far = rank_flip(v, 2)
    return [v, rank_flip(v, 1), far, rank_flip(far, 1)]


def in_rank_order(pieces, rank, axis):
    width = pieces[0].shape[axis]
    shape = list(pieces[0].shape)
    shape[axis] = width * len(pieces)
    full = jnp.zeros(shape, pieces[0].dtype)
    for r, piece in enumerate(pieces):
        full = lax.dynamic_update_slice_in_dim(full, piece, (rank ^ r) * width, axis)
    return full


def momentum(moment, grad):
    return 0.5 * moment + 0.5 * grad


def advance(weight, moment, grad):
    fresh = momentum(moment, grad)
    return (fresh, weight - LEARN_RATE * fresh - LEARN_RATE * DECAY_RATE * weight)


def body(
    hidden, segments, cotangent, in_weight, in_moment, bc_weight, bc_moment, step_weight, step_moment,
    out_weight, out_moment, conv_table, conv_moment, bc_table, bc_table_moment, head_table, head_moment,
    norm_gain, gain_moment,
):
    size = lax.axis_size("dp")
    ranks = lax.axis_size("mp")
    n = size // 2
    place, rank = lax.axis_index("dp"), lax.axis_index("mp")
    outer, inner = place // 2, place % 2
    slot = jnp.arange(size)
    idx = (((outer + slot // 2) % n) * 2 + (inner ^ (slot % 2))).astype(jnp.int32)
    rank1 = rank.reshape(1).astype(jnp.int32)
    rows, _, channels = in_weight.shape
    heads = head_table.shape[1]
    tokens, depth = hidden.shape
    share = bc_weight.shape[1] // ranks
    spare = LANES - share - heads

    own_bc = lax.dynamic_slice_in_dim(bc_weight, rank * share, share, 1)
    set_a = jnp.concatenate([in_weight[:, 1], own_bc, step_weight, jnp.zeros((rows, spare), f32)], axis=1)
    a_pieces, a_last = dp_pieces(set_a.astype(bf16))
    b_pieces, b_last = dp_pieces(in_weight[:, 0].astype(bf16), a_last)
    c_pieces, _ = dp_pieces(out_weight.T.astype(bf16), b_last)
    cot = in_rank_order(mp_pieces(cotangent), rank, 1)

    gain_rows = pad_rows(norm_gain[None])
    normed_low, normed_t, cot_t = prepare(hidden, gain_rows, cot)
    aux, seg_row = segment_facts(segments)
    conv_rows, bc_rows = pad_rows(conv_table), pad_rows(bc_table)
    head_rows = pad_lanes(pad_rows(head_table))
    expand = head_expand(channels)

    x_pre, small, w_a = project(normed_low, a_pieces, idx, channels)
    bc_pre = in_rank_order(mp_pieces(small[:share].astype(bf16)), rank, 0).T.astype(f32)
    step_pre = pad_lanes(small[share:share + heads].T)
    facts = (aux, seg_row, conv_rows, bc_rows, head_rows, expand)
    mixed, states = ssd_forward(x_pre, bc_pre, step_pre, *facts)
    gate_pre, square, w_b = gate_forward(normed_low, mixed, b_pieces, idx)
    square = mp_sum_direct(square)
    gated_out = gated_norm(gate_pre, mixed, square, conv_rows, channels * ranks)
    shard_c, c_flip = dp_scatter(weight_grad(cot_t, [gated_out], idx))

    gout, inner_dot, w_c = grad_gout(cot, gate_pre, mixed, conv_rows, c_pieces, idx)
    inner_dot = mp_sum_direct(inner_dot)
    dmixed, dgate, dgain = gate_backward(gate_pre, gout, mixed, square, inner_dot, conv_rows, channels * ranks)
    shard_b, b_flip = dp_scatter(weight_grad(normed_t, [dgate], idx), c_flip)

    near, far = mp_reduce(out_partial(gated_out, w_c, rank1, ranks))
    width = depth // ranks
    resid = lax.dynamic_slice_in_dim(hidden, rank * width, width, 1).astype(f32)
    output = (resid + near + far.astype(f32)).astype(bf16)

    dx, dbc_part, dstep, dconv, dbct_part, dheads = ssd_backward(
        x_pre, bc_pre, step_pre, *facts, mixed, dmixed, states
    )
    dbc_low_part = dbc_part.astype(bf16).T
    parts = [lax.dynamic_slice_in_dim(dbc_low_part, (rank ^ r) * share, share, 0) for r in range(ranks)]
    near, far = mp_reduce(parts)
    dbc_low = (near + far.astype(f32)).astype(bf16).T
    dsmall = jnp.concatenate([dbc_low, dstep[:, :heads].astype(bf16), jnp.zeros((tokens, spare), bf16)], axis=1)
    shard_a, _ = dp_scatter(weight_grad(normed_t, [dx, dsmall], idx), b_flip)

    term = normed_term([(dx, w_a[:, :channels]), (dsmall, w_a[:, channels:]), (dgate, w_b)], rank1, ranks)
    near, far = mp_reduce(term)
    mine, dgain_mine = norm_backward(near, far, hidden, cot, gain_rows, rank1)
    input_grad = in_rank_order(mp_pieces(mine), rank, 0)

    dconv_all = jnp.concatenate([dconv[:5], dgain[:1]], axis=0)
    packed = jnp.concatenate(
        [mp_sum(dbct_part[:5].reshape(-1, LANES)), dconv_all.reshape(-1, LANES), dheads], axis=0
    )
    packed = dp_sum(packed)
    cut1 = 5 * 2
    cut2 = cut1 + 6 * channels // LANES
    total_bct = packed[:cut1].reshape(5, 2 * LANES)
    total_conv = packed[cut1:cut2].reshape(6, channels)
    total_head = packed[cut2:cut2 + 3, :heads]
    total_gain = dp_sum(mp_sum(dgain_mine[:1].reshape(-1, LANES))).reshape(-1)

    shard_x = shard_a[:, :channels]
    shard_bc = in_rank_order(mp_pieces(shard_a[:, channels:channels + share]), rank, 1)
    shard_step = shard_a[:, channels + share:channels + share + heads]
    in_m, in_w = advance(in_weight, in_moment, jnp.stack([shard_b, shard_x], axis=1))
    bc_m, bc_w = advance(bc_weight, bc_moment, shard_bc)
    step_m, step_w = advance(step_weight, step_moment, shard_step)
    out_m, out_w = advance(out_weight, out_moment, shard_c.T)
    return (
        output, input_grad, in_m, in_w, bc_m, bc_w, step_m, step_w, out_m, out_w,
        momentum(conv_moment, total_conv),
        momentum(bc_table_moment, total_bct),
        momentum(head_moment, total_head),
        momentum(gain_moment, total_gain),
    )


def solution(mesh):
    placed = (
        P("dp", None),
        P("dp", None),
        P("dp", "mp"),
        P("dp", None, "mp"),
        P("dp", None, "mp"),
        P("dp", None),
        P("dp", None),
        P("dp", "mp"),
        P("dp", "mp"),
        P("mp", "dp"),
        P("mp", "dp"),
        P(None, "mp"),
        P(None, "mp"),
        P(),
        P(),
        P(None, "mp"),
        P(None, "mp"),
        P(),
        P(),
    )
    return jax.shard_map(
        body,
        mesh=mesh,
        in_specs=placed,
        out_specs=(
            P("dp", "mp"),
            P("dp", None),
            P("dp", None, "mp"),
            P("dp", None, "mp"),
            P("dp", None),
            P("dp", None),
            P("dp", "mp"),
            P("dp", "mp"),
            P("mp", "dp"),
            P("mp", "dp"),
            P(None, "mp"),
            P(),
            P(None, "mp"),
            P(),
        ),
        check_vma=False,
    )
```

```python
import functools

import jax
import jax.numpy as jnp
from jax import lax
from jax.experimental import pallas as pl
from jax.experimental.pallas import tpu as pltpu
from jax.sharding import PartitionSpec as P

CHUNK = 128
EPSILON = 1e-05
LEARN_RATE = 0.0001
DECAY_RATE = 0.1
WIDTH = 64
LANES = 128
HALO = 8
bf16 = jnp.bfloat16
f32 = jnp.float32
MIB = 1024 * 1024


def dot_nn(a, b):
    return lax.dot_general(a, b, (((1,), (0,)), ((), ())), preferred_element_type=f32)


def dot_nt(a, b):
    return lax.dot_general(a, b, (((1,), (1,)), ((), ())), preferred_element_type=f32)


def dot_tn(a, b):
    return lax.dot_general(a, b, (((0,), (0,)), ((), ())), preferred_element_type=f32)


def split3(v):
    high = v.astype(bf16)
    rest = v - high.astype(f32)
    mid = rest.astype(bf16)
    low = (rest - mid.astype(f32)).astype(bf16)
    return high, mid, low


def exact_left(ones, v):
    high, mid, low = split3(v)
    return dot_nn(ones, high) + dot_nn(ones, mid) + dot_nn(ones, low)


def spread(v, expand):
    high, mid, low = split3(v)
    return dot_nn(high, expand) + dot_nn(mid, expand) + dot_nn(low, expand)


def gather_heads(v, expand):
    high = v.astype(bf16)
    mid = (v - high.astype(f32)).astype(bf16)
    return dot_nt(high, expand) + dot_nt(mid, expand)


def sigmoid(v):
    return 1.0 / (1.0 + jnp.exp(-v))


def conv_block(scratch, before, now, taps, keep):
    rows = now.shape[0]
    scratch[0:HALO, :] = before
    scratch[HALO:HALO + rows, :] = now
    total = taps[4:5, :] + taps[0:1, :] * now
    for lag in (1, 2, 3):
        moved = scratch[HALO - lag:HALO - lag + rows, :]
        total = total + taps[lag:lag + 1, :] * (moved * keep[:, lag - 1:lag])
    return total


def step_parts(step_pre, heads):
    raw = step_pre + heads[0:1, :]
    steps = jnp.maximum(raw, 0.0) + jnp.log1p(jnp.exp(-jnp.abs(raw)))
    rates = -jnp.exp(heads[1:2, :])
    return raw, steps, rates


def triangle(lower):
    row = lax.broadcasted_iota(jnp.int32, (CHUNK, CHUNK), 0)
    col = lax.broadcasted_iota(jnp.int32, (CHUNK, CHUNK), 1)
    return row >= col if lower else row <= col


def ssd_forward_kernel(
    x_ref, xb_ref, bc_ref, bcb_ref, st_ref, aux_ref, seg_ref, conv_ref, bct_ref, heads_ref, expand_ref,
    mixed_ref, state_ref, state, xs_scr, bc_scr,
):
    chunk = pl.program_id(0)

    @pl.when(chunk == 0)
    def _():
        state[...] = jnp.zeros_like(state)

    channels = x_ref.shape[1]
    aux = aux_ref[...]
    expand = expand_ref[...]
    u = conv_block(xs_scr, xb_ref[...], x_ref[...], conv_ref, aux)
    x_act = u * sigmoid(u)
    ubc = conv_block(bc_scr, bcb_ref[...], bc_ref[...], bct_ref, aux)
    bc_act = (ubc * sigmoid(ubc)).astype(bf16)
    b_mat, c_mat = bc_act[:, :LANES], bc_act[:, LANES:]
    _, steps, rates = step_parts(st_ref[...], heads_ref)
    lower = triangle(True)
    cum = exact_left(lower.astype(bf16), steps * rates)
    cum_t = cum.T
    tail = cum[CHUNK - 1:CHUNK, :]
    entry = jnp.exp(cum) * aux[:, 6:7]
    to_end = jnp.exp(tail - cum) * aux[:, 7:8]
    wide = spread(jnp.concatenate([steps, entry, to_end], axis=0), expand)
    step_e, entry_e, to_end_e = wide[:CHUNK], wide[CHUNK:2 * CHUNK], wide[2 * CHUNK:]
    skip_e = spread(jnp.broadcast_to(heads_ref[2:3, :], (8, LANES)), expand)[0:1, :]
    mask = lower & (aux[:, 8:9] == seg_ref[...])
    scores = jnp.where(mask, dot_nt(c_mat, b_mat), 0.0)
    xs = x_act * step_e
    xs_low = xs.astype(bf16)
    held = state[...]
    held_low = held.astype(bf16)
    state_ref[...] = held_low
    out = dot_nn(c_mat, held_low) * entry_e + skip_e * x_act
    state[...] = held * entry_e[CHUNK - 1:CHUNK, :] + dot_tn(b_mat, (xs * to_end_e).astype(bf16))
    first = lax.broadcasted_iota(jnp.int32, (CHUNK, LANES), 1) < WIDTH
    zero = jnp.zeros((CHUNK, LANES), bf16)
    for pair in range(channels // LANES):
        span = slice(pair * LANES, (pair + 1) * LANES)
        parts = []
        for head in (2 * pair, 2 * pair + 1):
            diff = cum[:, head:head + 1] - cum_t[head:head + 1, :]
            parts.append((scores * jnp.exp(jnp.minimum(diff, 0.0))).astype(bf16))
        own = xs_low[:, span]
        both = jnp.concatenate([jnp.where(first, own, zero), jnp.where(first, zero, own)], axis=0)
        mixed_ref[:, span] = out[:, span] + dot_nn(jnp.concatenate(parts, axis=1), both)


def ssd_backward_kernel(
    x_ref, xb_ref, bc_ref, bcb_ref, st_ref, aux_ref, seg_ref, conv_ref, bct_ref, heads_ref, expand_ref,
    mixed_ref, dy_ref, state_ref,
    dx_ref, dbc_ref, dbc_t_ref, dst_ref, dst_t_ref, dconv_ref, dbct_ref, dheads_ref,
    dstate, xs_scr, bc_scr, du_scr, dubc_scr,
):
    at = pl.program_id(0)

    @pl.when(at == 0)
    def _():
        dstate[...] = jnp.zeros_like(dstate)
        du_scr[...] = jnp.zeros_like(du_scr)
        dubc_scr[...] = jnp.zeros_like(dubc_scr)
        dconv_ref[...] = jnp.zeros_like(dconv_ref)
        dbct_ref[...] = jnp.zeros_like(dbct_ref)
        dheads_ref[...] = jnp.zeros_like(dheads_ref)

    channels = x_ref.shape[1]
    aux = aux_ref[...]
    expand = expand_ref[...]
    x_now, bc_now = x_ref[...], bc_ref[...]
    u = conv_block(xs_scr, xb_ref[...], x_now, conv_ref, aux)
    sg = sigmoid(u)
    x_act = u * sg
    ubc = conv_block(bc_scr, bcb_ref[...], bc_now, bct_ref, aux)
    sgbc = sigmoid(ubc)
    bc_act = (ubc * sgbc).astype(bf16)
    b_mat, c_mat = bc_act[:, :LANES], bc_act[:, LANES:]
    raw, steps, rates = step_parts(st_ref[...], heads_ref)
    lower = triangle(True)
    cum = exact_left(lower.astype(bf16), steps * rates)
    cum_t = cum.T
    tail = cum[CHUNK - 1:CHUNK, :]
    entry = jnp.exp(cum) * aux[:, 6:7]
    to_end = jnp.exp(tail - cum) * aux[:, 7:8]
    wide = spread(jnp.concatenate([steps, entry, to_end], axis=0), expand)
    step_e, entry_e, to_end_e = wide[:CHUNK], wide[CHUNK:2 * CHUNK], wide[2 * CHUNK:]
    skip_e = spread(jnp.broadcast_to(heads_ref[2:3, :], (8, LANES)), expand)[0:1, :]
    upper = triangle(False)
    mask = upper & (aux[:, 8:9] == seg_ref[...])
    scores = jnp.where(mask, dot_nt(b_mat, c_mat), 0.0)
    xs = x_act * step_e
    xs_low = xs.astype(bf16)
    dy_low = dy_ref[...]
    dy = dy_low.astype(f32)
    held_low = state_ref[...]
    grad = dstate[...]
    grad_low = grad.astype(bf16)
    entry_dy = (entry_e * dy).astype(bf16)
    kept_e = entry_e[CHUNK - 1:CHUNK, :]
    dstate[...] = grad * kept_e + dot_tn(c_mat, entry_dy)
    dc = dot_nt(entry_dy, held_low)
    db = dot_nt((xs * to_end_e).astype(bf16), grad_low)
    q_state = dot_nn(b_mat, grad_low) * to_end_e
    first = lax.broadcasted_iota(jnp.int32, (CHUNK, LANES), 1) < WIDTH
    zero = jnp.zeros((CHUNK, LANES), bf16)
    dscores = jnp.zeros((CHUNK, CHUNK), f32)
    q_parts = []
    for pair in range(channels // LANES):
        span = slice(pair * LANES, (pair + 1) * LANES)
        own = dy_low[:, span]
        both = jnp.concatenate([jnp.where(first, own, zero), jnp.where(first, zero, own)], axis=0)
        dweights = dot_nt(xs_low[:, span], both)
        parts = []
        for i, head in enumerate((2 * pair, 2 * pair + 1)):
            diff = cum_t[head:head + 1, :] - cum[:, head:head + 1]
            decay = jnp.exp(jnp.minimum(diff, 0.0))
            parts.append((scores * decay).astype(bf16))
            dscores = dscores + dweights[:, i * LANES:(i + 1) * LANES] * decay
        q_parts.append(dot_nn(jnp.concatenate(parts, axis=1), both))
    q = jnp.concatenate(q_parts, axis=1) + q_state
    dscores_low = jnp.where(mask, dscores, 0.0).astype(bf16)
    db = db + dot_nn(dscores_low, c_mat)
    dc = dc + dot_tn(dscores_low, b_mat)
    xs_round = xs_low.astype(f32)
    rows = gather_heads(
        jnp.concatenate(
            [
                dy * (mixed_ref[...] - skip_e * x_act) - xs_round * q,
                x_act * q,
            ],
            axis=0,
        ),
        expand,
    )
    flow, dstep = rows[:CHUNK], rows[CHUNK:]
    sums = jnp.concatenate(
        [
            jnp.sum(xs_round * q_state + kept_e * (held_low.astype(f32) * grad), axis=0, keepdims=True),
            jnp.sum(dy * x_act, axis=0, keepdims=True),
            jnp.zeros((6, channels), f32),
        ],
        axis=0,
    )
    sums = gather_heads(sums, expand)
    dlog = exact_left(upper.astype(bf16), flow) + sums[0:1, :]
    dstep = dstep + rates * dlog
    draw = dstep * sigmoid(raw)
    dst_ref[...] = pltpu.roll(draw, WIDTH, 1).astype(bf16)
    dst_t_ref[...] = draw.T[0:16, :].astype(bf16)
    dheads_ref[0:1, :] += jnp.sum(draw, axis=0, keepdims=True)
    dheads_ref[1:2, :] += rates * jnp.sum(dlog * steps, axis=0, keepdims=True)
    dheads_ref[2:3, :] += sums[1:2, :]

    def conv_back(scratch, du, now, taps, dtaps):
        scratch[0:CHUNK, :] = du
        total = taps[0:1, :] * du
        dtaps[0:1, :] += jnp.sum(now * du, axis=0, keepdims=True)
        dtaps[4:5, :] += jnp.sum(du, axis=0, keepdims=True)
        for lag in (1, 2, 3):
            moved = scratch[lag:lag + CHUNK, :] * aux[:, 2 + lag:3 + lag]
            total = total + taps[lag:lag + 1, :] * moved
            dtaps[lag:lag + 1, :] += jnp.sum(now * moved, axis=0, keepdims=True)
        scratch[CHUNK:CHUNK + HALO, :] = du[0:HALO, :]
        return total

    du = (skip_e * dy + step_e * q) * (sg * (1.0 + u * (1.0 - sg)))
    dx_ref[...] = conv_back(du_scr, du, x_now, conv_ref, dconv_ref).astype(dx_ref.dtype)
    dubc = jnp.concatenate([db, dc], axis=1) * (sgbc * (1.0 + ubc * (1.0 - sgbc)))
    dbc = conv_back(dubc_scr, dubc, bc_now, bct_ref, dbct_ref).astype(bf16)
    dbc_ref[...] = dbc
    dbc_t_ref[...] = dbc.T


def common_specs(place, channels):
    before = lambda i: (jnp.maximum(place(i) * (CHUNK // HALO) - 1, 0), 0)
    now = lambda i: (place(i), 0)
    whole = lambda i: (0, 0)
    return [
        pl.BlockSpec((CHUNK, channels), now),
        pl.BlockSpec((HALO, channels), before),
        pl.BlockSpec((CHUNK, 2 * LANES), now),
        pl.BlockSpec((HALO, 2 * LANES), before),
        pl.BlockSpec((CHUNK, LANES), now),
        pl.BlockSpec((CHUNK, 16), now),
        pl.BlockSpec((1, CHUNK), lambda i: (0, place(i))),
        pl.BlockSpec((8, channels), whole),
        pl.BlockSpec((8, 2 * LANES), whole),
        pl.BlockSpec((8, LANES), whole),
        pl.BlockSpec((LANES, channels), whole),
    ]


def ssd_forward(x_pre, bc_pre, step_pre, aux, seg_row, conv_rows, bc_rows, head_rows, expand):
    tokens, channels = x_pre.shape
    count = tokens // CHUNK
    now = lambda i: (i, 0)
    return pl.pallas_call(
        ssd_forward_kernel,
        grid=(count,),
        in_specs=common_specs(lambda i: i, channels),
        out_specs=[
            pl.BlockSpec((CHUNK, channels), now),
            pl.BlockSpec((None, LANES, channels), lambda i: (i, 0, 0)),
        ],
        out_shape=[
            jax.ShapeDtypeStruct((tokens, channels), f32),
            jax.ShapeDtypeStruct((count, LANES, channels), bf16),
        ],
        scratch_shapes=[
            pltpu.VMEM((LANES, channels), f32),
            pltpu.VMEM((HALO + CHUNK, channels), f32),
            pltpu.VMEM((HALO + CHUNK, 2 * LANES), f32),
        ],
        compiler_params=pltpu.CompilerParams(vmem_limit_bytes=32 * MIB),
        cost_estimate=pl.CostEstimate(flops=14 * 10**9, bytes_accessed=40 * 10**6, transcendentals=0),
        name="ssd_forward",
    )(x_pre, x_pre, bc_pre, bc_pre, step_pre, aux, seg_row, conv_rows, bc_rows, head_rows, expand)


def ssd_backward(x_pre, bc_pre, step_pre, aux, seg_row, conv_rows, bc_rows, head_rows, expand, mixed, dy, states):
    tokens, channels = x_pre.shape
    count = tokens // CHUNK
    place = lambda i: count - 1 - i
    now = lambda i: (place(i), 0)
    whole = lambda i: (0, 0)
    return pl.pallas_call(
        ssd_backward_kernel,
        grid=(count,),
        in_specs=common_specs(place, channels) + [
            pl.BlockSpec((CHUNK, channels), now),
            pl.BlockSpec((CHUNK, channels), now),
            pl.BlockSpec((None, LANES, channels), lambda i: (place(i), 0, 0)),
        ],
        out_specs=[
            pl.BlockSpec((CHUNK, channels), now),
            pl.BlockSpec((CHUNK, 2 * LANES), now),
            pl.BlockSpec((2 * LANES, CHUNK), lambda i: (0, place(i))),
            pl.BlockSpec((CHUNK, LANES), now),
            pl.BlockSpec((16, CHUNK), lambda i: (0, place(i))),
            pl.BlockSpec((8, channels), whole),
            pl.BlockSpec((8, 2 * LANES), whole),
            pl.BlockSpec((8, LANES), whole),
        ],
        out_shape=[
            jax.ShapeDtypeStruct((tokens, channels), bf16),
            jax.ShapeDtypeStruct((tokens, 2 * LANES), bf16),
            jax.ShapeDtypeStruct((2 * LANES, tokens), bf16),
            jax.ShapeDtypeStruct((tokens, LANES), bf16),
            jax.ShapeDtypeStruct((16, tokens), bf16),
            jax.ShapeDtypeStruct((8, channels), f32),
            jax.ShapeDtypeStruct((8, 2 * LANES), f32),
            jax.ShapeDtypeStruct((8, LANES), f32),
        ],
        scratch_shapes=[
            pltpu.VMEM((LANES, channels), f32),
            pltpu.VMEM((HALO + CHUNK, channels), f32),
            pltpu.VMEM((HALO + CHUNK, 2 * LANES), f32),
            pltpu.VMEM((HALO + CHUNK, channels), f32),
            pltpu.VMEM((HALO + CHUNK, 2 * LANES), f32),
        ],
        compiler_params=pltpu.CompilerParams(vmem_limit_bytes=32 * MIB),
        cost_estimate=pl.CostEstimate(flops=28 * 10**9, bytes_accessed=80 * 10**6, transcendentals=0),
        name="ssd_backward",
    )(x_pre, x_pre, bc_pre, bc_pre, step_pre, aux, seg_row, conv_rows, bc_rows, head_rows, expand, mixed, dy, states)


def segment_facts(seg):
    row = seg[0]
    tokens = row.shape[0]
    cols = []
    for lag in (1, 2, 3):
        cols.append(jnp.pad(row[:-lag], (lag, 0), constant_values=-1) == row)
    for lag in (1, 2, 3):
        cols.append(jnp.pad(row[lag:], (0, lag), constant_values=-1) == row)
    blocks = row.reshape(tokens // CHUNK, CHUNK)
    ends = blocks[:, -1:]
    before = jnp.concatenate([jnp.full((1, 1), -1, row.dtype), ends[:-1]], axis=0)
    cols.append((blocks == before).reshape(-1))
    cols.append((blocks == ends).reshape(-1))
    cols.append(row)
    facts = jnp.stack([c.astype(f32) for c in cols], axis=1)
    return jnp.pad(facts, ((0, 0), (0, 16 - facts.shape[1]))), seg.astype(f32)


def pad_rows(table, rows=8):
    return jnp.pad(table, ((0, rows - table.shape[0]), (0, 0)))


def pad_lanes(table, lanes=LANES):
    return jnp.pad(table, ((0, 0), (0, lanes - table.shape[1])))


def head_expand(channels):
    head = jnp.arange(LANES)[:, None]
    return (head == (jnp.arange(channels) // WIDTH)[None, :]).astype(bf16)


TILE = 256
TILE_D = 384


def fill(dest, pieces, idx_ref):
    rows = pieces[0].shape[0]
    s = 0
    for piece in pieces:
        for b in range(piece.shape[0] // rows):
            start = pl.multiple_of(idx_ref[s] * rows, rows)
            dest[pl.ds(start, rows), :] = piece[b * rows:(b + 1) * rows, :]
            s += 1


def params(mib=24):
    return pltpu.CompilerParams(vmem_limit_bytes=mib * MIB)


def cost(flops, moved):
    return pl.CostEstimate(flops=int(flops), bytes_accessed=int(moved), transcendentals=0)


def prepare_kernel(hidden_ref, gain_ref, low_ref, low_t_ref):
    inputs = hidden_ref[...].astype(f32)
    inv_rms = lax.rsqrt(jnp.mean(inputs * inputs, axis=1, keepdims=True) + EPSILON)
    low = (inputs * inv_rms * gain_ref[0:1, :]).astype(bf16)
    low_ref[...] = low
    low_t_ref[...] = low.T


def prepare(hidden, gain_rows):
    tokens, depth = hidden.shape
    block = pl.BlockSpec((TILE, depth), lambda i: (i, 0))
    return pl.pallas_call(
        prepare_kernel,
        grid=(tokens // TILE,),
        in_specs=[block, pl.BlockSpec((8, depth), lambda i: (0, 0))],
        out_specs=[block, pl.BlockSpec((depth, TILE), lambda i: (0, i))],
        out_shape=[jax.ShapeDtypeStruct((tokens, depth), bf16), jax.ShapeDtypeStruct((depth, tokens), bf16)],
        compiler_params=params(),
        cost_estimate=cost(6 * 10**9, 20 * 10**6),
        name="prepare",
    )(hidden, gain_rows)


def columns_kernel(rank_ref, *refs, count):
    pieces, (full_ref, full_t_ref) = refs[:count], refs[count:]
    for r, piece in enumerate(pieces):
        width = piece.shape[1]
        start = pl.multiple_of((rank_ref[0] ^ r) * width, LANES)
        value = piece[...]
        full_ref[:, pl.ds(start, width)] = value
        full_t_ref[pl.ds(start, width), :] = value.T


def join_columns(pieces, rank):
    tokens, width = pieces[0].shape
    depth = width * len(pieces)
    return pl.pallas_call(
        functools.partial(columns_kernel, count=len(pieces)),
        grid=(tokens // TILE,),
        in_specs=[pl.BlockSpec(memory_space=pltpu.SMEM)] + [pl.BlockSpec((TILE, width), lambda i: (i, 0))] * len(pieces),
        out_specs=[pl.BlockSpec((TILE, depth), lambda i: (i, 0)), pl.BlockSpec((depth, TILE), lambda i: (0, i))],
        out_shape=[jax.ShapeDtypeStruct((tokens, depth), bf16), jax.ShapeDtypeStruct((depth, tokens), bf16)],
        compiler_params=params(),
        cost_estimate=cost(4 * 10**9, 16 * 10**6),
        name="join_columns",
    )(rank, *pieces)


def rows_kernel(rank_ref, *refs, count):
    pieces, full_ref = refs[:count], refs[count]
    for r, piece in enumerate(pieces):
        rows = piece.shape[0]
        full_ref[pl.ds(pl.multiple_of((rank_ref[0] ^ r) * rows, rows), rows), :] = piece[...]


def join_rows(pieces, rank):
    rows, width = pieces[0].shape
    shape = (rows * len(pieces), width)
    return pl.pallas_call(
        functools.partial(rows_kernel, count=len(pieces)),
        in_specs=[pl.BlockSpec(memory_space=pltpu.SMEM)] + [pl.BlockSpec(memory_space=pltpu.VMEM)] * len(pieces),
        out_specs=pl.BlockSpec(memory_space=pltpu.VMEM),
        out_shape=jax.ShapeDtypeStruct(shape, pieces[0].dtype),
        compiler_params=params(),
        cost_estimate=cost(10**9, 4 * shape[0] * shape[1]),
        name="join_rows",
    )(rank, *pieces)


def small_kernel(rank_ref, *refs, count):
    pieces, (small_ref, bc_ref, step_ref, scratch) = refs[:count], refs[count:]
    share = pieces[0].shape[0]
    for r, piece in enumerate(pieces):
        scratch[pl.ds(pl.multiple_of((rank_ref[0] ^ r) * share, share), share), :] = piece[...].astype(f32)
    bc_ref[...] = scratch[...].T
    turned = small_ref[...].T
    lane = lax.broadcasted_iota(jnp.int32, turned.shape, 1)
    step_ref[...] = jnp.where(lane < LANES - share, pltpu.roll(turned, LANES - share, 1), 0.0)


def join_small(pieces, small, rank):
    share, tokens = pieces[0].shape
    width = share * len(pieces)
    return pl.pallas_call(
        functools.partial(small_kernel, count=len(pieces)),
        grid=(tokens // TILE,),
        in_specs=[pl.BlockSpec(memory_space=pltpu.SMEM)]
        + [pl.BlockSpec((share, TILE), lambda i: (0, i))] * len(pieces)
        + [pl.BlockSpec((LANES, TILE), lambda i: (0, i))],
        out_specs=[pl.BlockSpec((TILE, width), lambda i: (i, 0)), pl.BlockSpec((TILE, LANES), lambda i: (i, 0))],
        out_shape=[jax.ShapeDtypeStruct((tokens, width), f32), jax.ShapeDtypeStruct((tokens, LANES), f32)],
        scratch_shapes=[pltpu.VMEM((width, TILE), f32)],
        compiler_params=params(),
        cost_estimate=cost(2 * 10**9, 4 * 10**6),
        name="join_small",
    )(rank, *pieces, small)


def project_kernel(idx_ref, lhs_ref, *refs, count):
    pieces, (x_ref, small_ref, share_ref, w_ref, wt_ref) = refs[:count], refs[count:]
    channels = x_ref.shape[1]

    @pl.when(pl.program_id(0) == 0)
    def _():
        fill(w_ref, pieces, idx_ref)
        wt_ref[...] = w_ref[:, channels:].T[0:wt_ref.shape[0], :]

    product = dot_nn(lhs_ref[...], w_ref[...])
    x_ref[...] = product[:, :channels]
    small = product[:, channels:].T
    small_ref[...] = small
    share_ref[...] = small[0:share_ref.shape[0], :].astype(bf16)


def project(lhs, pieces, idx, channels, share):
    tokens, depth = lhs.shape
    count, width = len(pieces), pieces[0].shape[1]
    whole = lambda i: (0, 0)
    return pl.pallas_call(
        functools.partial(project_kernel, count=count),
        grid=(tokens // TILE,),
        in_specs=[pl.BlockSpec(memory_space=pltpu.SMEM), pl.BlockSpec((TILE, depth), lambda i: (i, 0))]
        + [pl.BlockSpec(p.shape, whole) for p in pieces],
        out_specs=[
            pl.BlockSpec((TILE, channels), lambda i: (i, 0)),
            pl.BlockSpec((width - channels, TILE), lambda i: (0, i)),
            pl.BlockSpec((share, TILE), lambda i: (0, i)),
            pl.BlockSpec((depth, width), whole),
            pl.BlockSpec((share, depth), whole),
        ],
        out_shape=[
            jax.ShapeDtypeStruct((tokens, channels), f32),
            jax.ShapeDtypeStruct((width - channels, tokens), f32),
            jax.ShapeDtypeStruct((share, tokens), bf16),
            jax.ShapeDtypeStruct((depth, width), bf16),
            jax.ShapeDtypeStruct((share, depth), bf16),
        ],
        compiler_params=params(),
        cost_estimate=cost(2 * tokens * depth * width, 6 * depth * width),
        name="project",
    )(idx, lhs, *pieces)


def column_to_row(col):
    return jnp.broadcast_to(col, (col.shape[0], LANES)).T[0:8, :]


def row_to_column(row):
    return jnp.broadcast_to(row, (LANES, row.shape[1])).T[:, 0:1]


def gate_kernel(idx_ref, lhs_ref, mixed_ref, *refs, count):
    pieces, (gate_ref, sums_ref, w_ref) = refs[:count], refs[count:]

    @pl.when(pl.program_id(0) == 0)
    def _():
        fill(w_ref, pieces, idx_ref)

    gate = dot_nn(lhs_ref[...], w_ref[...])
    gate_ref[...] = gate
    gated = mixed_ref[...] * (gate * sigmoid(gate))
    sums_ref[...] = column_to_row(jnp.sum(gated * gated, axis=1, keepdims=True))


def gate_forward(lhs, mixed, pieces, idx):
    tokens, depth = lhs.shape
    channels = mixed.shape[1]
    whole = lambda i: (0, 0)
    now = lambda i: (i, 0)
    return pl.pallas_call(
        functools.partial(gate_kernel, count=len(pieces)),
        grid=(tokens // TILE,),
        in_specs=[
            pl.BlockSpec(memory_space=pltpu.SMEM),
            pl.BlockSpec((TILE, depth), now),
            pl.BlockSpec((TILE, channels), now),
        ]
        + [pl.BlockSpec(p.shape, whole) for p in pieces],
        out_specs=[
            pl.BlockSpec((TILE, channels), now),
            pl.BlockSpec((8, TILE), lambda i: (0, i)),
            pl.BlockSpec((depth, channels), whole),
        ],
        out_shape=[
            jax.ShapeDtypeStruct((tokens, channels), f32),
            jax.ShapeDtypeStruct((8, tokens), f32),
            jax.ShapeDtypeStruct((depth, channels), bf16),
        ],
        compiler_params=params(),
        cost_estimate=cost(2 * tokens * depth * channels, 8 * depth * channels),
        name="gate_forward",
    )(idx, lhs, mixed, *pieces)


def gated_kernel(gate_ref, mixed_ref, square_ref, conv_ref, out_ref, *, inner_total):
    gate = gate_ref[...]
    scale = lax.rsqrt(row_to_column(square_ref[0:1, :]) / inner_total + EPSILON)
    gated = mixed_ref[...] * (gate * sigmoid(gate))
    out_ref[...] = (gated * scale * conv_ref[5:6, :]).astype(bf16)


def gated_norm(gate, mixed, square, conv_rows, inner_total):
    tokens, channels = gate.shape
    block = pl.BlockSpec((TILE, channels), lambda i: (i, 0))
    return pl.pallas_call(
        functools.partial(gated_kernel, inner_total=inner_total),
        grid=(tokens // TILE,),
        in_specs=[block, block, pl.BlockSpec((8, TILE), lambda i: (0, i)), pl.BlockSpec((8, channels), lambda i: (0, 0))],
        out_specs=block,
        out_shape=jax.ShapeDtypeStruct((tokens, channels), bf16),
        compiler_params=params(),
        cost_estimate=cost(20 * tokens * channels, 10 * tokens * channels),
        name="gated_norm",
    )(gate, mixed, square, conv_rows)


def gout_kernel(idx_ref, cot_ref, gate_ref, mixed_ref, conv_ref, *refs, count):
    pieces, (gout_ref, sums_ref, w_ref) = refs[:count], refs[count:]

    @pl.when(pl.program_id(0) == 0)
    def _():
        fill(w_ref, pieces, idx_ref)

    gout = dot_nn(cot_ref[...], w_ref[...])
    gout_ref[...] = gout
    gate = gate_ref[...]
    gated = mixed_ref[...] * (gate * sigmoid(gate))
    sums_ref[...] = column_to_row(jnp.sum(gout * conv_ref[5:6, :] * gated, axis=1, keepdims=True))


def grad_gout(cot, gate, mixed, conv_rows, pieces, idx):
    tokens, depth = cot.shape
    channels = mixed.shape[1]
    whole = lambda i: (0, 0)
    now = lambda i: (i, 0)
    return pl.pallas_call(
        functools.partial(gout_kernel, count=len(pieces)),
        grid=(tokens // TILE,),
        in_specs=[
            pl.BlockSpec(memory_space=pltpu.SMEM),
            pl.BlockSpec((TILE, depth), now),
            pl.BlockSpec((TILE, channels), now),
            pl.BlockSpec((TILE, channels), now),
            pl.BlockSpec((8, channels), whole),
        ]
        + [pl.BlockSpec(p.shape, whole) for p in pieces],
        out_specs=[
            pl.BlockSpec((TILE, channels), now),
            pl.BlockSpec((8, TILE), lambda i: (0, i)),
            pl.BlockSpec((depth, channels), whole),
        ],
        out_shape=[
            jax.ShapeDtypeStruct((tokens, channels), f32),
            jax.ShapeDtypeStruct((8, tokens), f32),
            jax.ShapeDtypeStruct((depth, channels), bf16),
        ],
        compiler_params=params(),
        cost_estimate=cost(2 * tokens * depth * channels, 8 * depth * channels),
        name="grad_gout",
    )(idx, cot, gate, mixed, conv_rows, *pieces)


def gate_back_kernel(gate_ref, gout_ref, mixed_ref, square_ref, inner_ref, conv_ref, dmixed_ref, dgate_ref, dgain_ref, *, inner_total):
    gate, gout, mixed = gate_ref[...], gout_ref[...], mixed_ref[...]
    gain = conv_ref[5:6, :]
    square, inner = row_to_column(square_ref[0:1, :]), row_to_column(inner_ref[0:1, :])
    scale = lax.rsqrt(square / inner_total + EPSILON)
    sg = sigmoid(gate)
    act = gate * sg
    gated = mixed * act
    dgated = scale * (gain * gout) - gated * (scale * scale * scale * inner / inner_total)
    dmixed_ref[...] = (dgated * act).astype(bf16)
    dgate_ref[...] = (dgated * mixed * sg * (1.0 + gate * (1.0 - sg))).astype(bf16)

    @pl.when(pl.program_id(0) == 0)
    def _():
        dgain_ref[...] = jnp.zeros_like(dgain_ref)

    dgain_ref[5:6, :] += jnp.sum(gout * gated * scale, axis=0, keepdims=True)


def gate_backward(gate, gout, mixed, square, inner, conv_rows, inner_total):
    tokens, channels = gate.shape
    whole = lambda i: (0, 0)
    block = pl.BlockSpec((TILE, channels), lambda i: (i, 0))
    row = pl.BlockSpec((8, TILE), lambda i: (0, i))
    return pl.pallas_call(
        functools.partial(gate_back_kernel, inner_total=inner_total),
        grid=(tokens // TILE,),
        in_specs=[block, block, block, row, row, pl.BlockSpec((8, channels), whole)],
        out_specs=[block, block, pl.BlockSpec((8, channels), whole)],
        out_shape=[
            jax.ShapeDtypeStruct((tokens, channels), bf16),
            jax.ShapeDtypeStruct((tokens, channels), bf16),
            jax.ShapeDtypeStruct((8, channels), f32),
        ],
        compiler_params=params(),
        cost_estimate=cost(30 * tokens * channels, 16 * tokens * channels),
        name="gate_backward",
    )(gate, gout, mixed, square, inner, conv_rows)


def weight_grad_kernel(idx_ref, lhs_ref, rhs_ref, *refs, rows, turned):
    outs, scratch = refs[:-1], refs[-1]
    at = pl.program_id(0)
    scratch[pl.ds(pl.multiple_of(at * TILE_D, TILE_D), TILE_D), :] = (dot_nt if turned else dot_nn)(
        lhs_ref[...], rhs_ref[...]
    ).astype(bf16)

    @pl.when(at == pl.num_programs(0) - 1)
    def _():
        s = 0
        for out in outs:
            for b in range(out.shape[0] // rows):
                start = pl.multiple_of(idx_ref[s] * rows, rows)
                out[b * rows:(b + 1) * rows, :] = scratch[pl.ds(start, rows), :]
                s += 1


def weight_grad(lhs_t, rhs, idx, sizes, turned=False):
    depth, tokens = lhs_t.shape
    width = rhs.shape[0 if turned else 1]
    rows = depth // idx.shape[0]
    whole = lambda i: (0, 0)
    return pl.pallas_call(
        functools.partial(weight_grad_kernel, rows=rows, turned=turned),
        grid=(depth // TILE_D,),
        in_specs=[
            pl.BlockSpec(memory_space=pltpu.SMEM),
            pl.BlockSpec((TILE_D, tokens), lambda i: (i, 0)),
            pl.BlockSpec(rhs.shape, whole),
        ],
        out_specs=[pl.BlockSpec((size * rows, width), whole) for size in sizes],
        out_shape=[jax.ShapeDtypeStruct((size * rows, width), bf16) for size in sizes],
        scratch_shapes=[pltpu.VMEM((depth, width), bf16)],
        compiler_params=params(),
        cost_estimate=cost(2 * tokens * depth * width, 4 * depth * width),
        name="weight_grad",
    )(idx, lhs_t, rhs)


def out_kernel(rank_ref, lhs_ref, w_ref, *outs):
    product = dot_nt(lhs_ref[...], w_ref[...]).astype(bf16)
    for r, out in enumerate(outs):
        @pl.when(pl.program_id(0) == r)
        def _():
            out[...] = product


def out_partial(gated_out, w_out, rank, ranks):
    tokens, channels = gated_out.shape
    depth = w_out.shape[0]
    width = depth // ranks
    whole = lambda i, rank_ref: (0, 0)
    return pl.pallas_call(
        out_kernel,
        grid_spec=pltpu.PrefetchScalarGridSpec(
            num_scalar_prefetch=1,
            grid=(ranks,),
            in_specs=[
                pl.BlockSpec((tokens, channels), whole),
                pl.BlockSpec((width, channels), lambda i, rank_ref: (i ^ rank_ref[0], 0)),
            ],
            out_specs=[pl.BlockSpec((tokens, width), whole)] * ranks,
        ),
        out_shape=[jax.ShapeDtypeStruct((tokens, width), bf16)] * ranks,
        compiler_params=params(),
        cost_estimate=cost(2 * tokens * depth * channels, 4 * depth * channels),
        name="out_partial",
    )(rank, gated_out, w_out)


def term_kernel(rank_ref, gx_ref, wx_ref, gg_ref, wg_ref, gs_ref, ws_ref, gb_ref, wbt_ref, *refs):
    outs, scratch = refs[:-1], refs[-1]
    total = dot_nt(gx_ref[...], wx_ref[...]) + dot_nt(gg_ref[...], wg_ref[...])
    total = total + dot_nt(gs_ref[...], ws_ref[...]) + dot_nn(gb_ref[...], wbt_ref[...])
    scratch[...] = total.astype(bf16)
    for r, out in enumerate(outs):
        rows = out.shape[0]
        out[...] = scratch[pl.ds(pl.multiple_of((rank_ref[0] ^ r) * rows, rows), rows), :]


def normed_term(dx, dgate, dstep, dbc, w_a, w_b, w_bct, rank, ranks):
    tokens, channels = dx.shape
    depth = w_a.shape[0]
    rows = tokens // ranks
    whole = lambda i: (0, 0)
    return pl.pallas_call(
        term_kernel,
        grid=(depth // TILE_D,),
        in_specs=[
            pl.BlockSpec(memory_space=pltpu.SMEM),
            pl.BlockSpec(dx.shape, whole),
            pl.BlockSpec((TILE_D, channels), lambda i: (i, 0)),
            pl.BlockSpec(dgate.shape, whole),
            pl.BlockSpec((TILE_D, channels), lambda i: (i, 0)),
            pl.BlockSpec(dstep.shape, whole),
            pl.BlockSpec((TILE_D, LANES), lambda i: (i, channels // LANES)),
            pl.BlockSpec(dbc.shape, whole),
            pl.BlockSpec((w_bct.shape[0], TILE_D), lambda i: (0, i)),
        ],
        out_specs=[pl.BlockSpec((rows, TILE_D), lambda i: (0, i))] * ranks,
        out_shape=[jax.ShapeDtypeStruct((rows, depth), bf16)] * ranks,
        scratch_shapes=[pltpu.VMEM((tokens, TILE_D), bf16)],
        compiler_params=params(32),
        cost_estimate=cost(2 * tokens * depth * 1920, 4 * depth * 1920),
        name="normed_term",
    )(rank, dx, w_a, dgate, w_b, dstep, w_a, dbc, w_bct)


def norm_back_kernel(rank_ref, a_ref, b_ref, hidden_ref, cot_ref, gain_ref, out_ref, dgain_ref):
    grad = a_ref[...].astype(f32) + b_ref[...].astype(f32)
    inputs = hidden_ref[...].astype(f32)
    inv_rms = lax.rsqrt(jnp.mean(inputs * inputs, axis=1, keepdims=True) + EPSILON)
    normed = inputs * inv_rms
    scaled = grad * gain_ref[0:1, :]
    mean = jnp.mean(scaled * normed, axis=1, keepdims=True)
    out_ref[...] = (inv_rms * (scaled - normed * mean) + cot_ref[...].astype(f32)).astype(out_ref.dtype)
    dgain_ref[...] = jnp.broadcast_to(jnp.sum(grad * normed, axis=0, keepdims=True), dgain_ref.shape)


def norm_backward(a, b, hidden, cot, gain_rows, rank):
    rows, depth = a.shape
    mine = lambda i, rank_ref: (rank_ref[0], 0)
    whole = lambda i, rank_ref: (0, 0)
    return pl.pallas_call(
        norm_back_kernel,
        grid_spec=pltpu.PrefetchScalarGridSpec(
            num_scalar_prefetch=1,
            grid=(1,),
            in_specs=[
                pl.BlockSpec((rows, depth), whole),
                pl.BlockSpec((rows, depth), whole),
                pl.BlockSpec((rows, depth), mine),
                pl.BlockSpec((rows, depth), mine),
                pl.BlockSpec((8, depth), whole),
            ],
            out_specs=[pl.BlockSpec((rows, depth), whole), pl.BlockSpec((8, depth), whole)],
        ),
        out_shape=[jax.ShapeDtypeStruct((rows, depth), bf16), jax.ShapeDtypeStruct((8, depth), f32)],
        compiler_params=params(),
        cost_estimate=cost(4 * 10**9, 12 * 10**6),
        name="norm_backward",
    )(rank, a, b, hidden, cot, gain_rows)


def fence(*values):
    leaves, tree = jax.tree.flatten(values)
    return jax.tree.unflatten(tree, lax.optimization_barrier(leaves))


def outer_from(v, k):
    n = lax.axis_size("dp") // 2
    return lax.ppermute(v, "dp", [(((o + k) % n) * 2 + x, o * 2 + x) for o in range(n) for x in range(2)])


def outer_flip(v, bit):
    n = lax.axis_size("dp") // 2
    return lax.ppermute(v, "dp", [((o ^ bit) * 2 + x, o * 2 + x) for o in range(n) for x in range(2)])


def inner_flip(v):
    return lax.ppermute(v, "dp", [(d ^ 1, d) for d in range(lax.axis_size("dp"))])


def rank_flip(v, bit):
    return lax.ppermute(v, "mp", [(m ^ bit, m) for m in range(lax.axis_size("mp"))])


def hops(n):
    order = []
    for k in range(1, n // 2 + 1):
        order.append(k)
        if n - k != k:
            order.append(n - k)
    return order


def outer_blocks(own, here, back, ks):
    rows = own.shape[0]
    return [
        (here[i * rows:(i + 1) * rows].astype(f32) + back[i * rows:(i + 1) * rows].astype(f32)).astype(bf16)
        for i in range(len(ks))
    ]


def outer_send(blocks, ks):
    n = lax.axis_size("dp") // 2
    return [outer_from(block, n - k) for block, k in zip(blocks, ks)]


def dp_sum(v):
    v = v + inner_flip(v)
    bit = 1
    while bit < lax.axis_size("dp") // 2:
        v = v + outer_flip(v, bit)
        bit *= 2
    return v


def mp_sum(v):
    v = v + rank_flip(v, 1)
    return v + rank_flip(v, 2)


def mp_sum_direct(v):
    return (v + rank_flip(v, 1)) + (rank_flip(v, 2) + rank_flip(v, 3))


def mp_reduce(blocks):
    far = blocks[2].astype(f32) + rank_flip(blocks[3], 1).astype(f32)
    near = blocks[0].astype(f32) + rank_flip(blocks[1], 1).astype(f32)
    return near, rank_flip(far.astype(bf16), 2)


def mp_pieces(v):
    far = rank_flip(v, 2)
    return [v, rank_flip(v, 1), far, rank_flip(far, 1)]


def in_rank_order(pieces, rank, axis):
    width = pieces[0].shape[axis]
    shape = list(pieces[0].shape)
    shape[axis] = width * len(pieces)
    full = jnp.zeros(shape, pieces[0].dtype)
    for r, piece in enumerate(pieces):
        full = lax.dynamic_update_slice_in_dim(full, piece, (rank ^ r) * width, axis)
    return full


def momentum(moment, grad):
    return 0.5 * moment + 0.5 * grad


def advance(weight, moment, grad):
    fresh = momentum(moment, grad)
    return (fresh, weight - LEARN_RATE * fresh - LEARN_RATE * DECAY_RATE * weight)


def body(
    hidden, segments, cotangent, in_weight, in_moment, bc_weight, bc_moment, step_weight, step_moment,
    out_weight, out_moment, conv_table, conv_moment, bc_table, bc_table_moment, head_table, head_moment,
    norm_gain, gain_moment,
):
    size = lax.axis_size("dp")
    ranks = lax.axis_size("mp")
    n = size // 2
    place, rank = lax.axis_index("dp"), lax.axis_index("mp")
    outer, inner = place // 2, place % 2
    rank1 = rank.reshape(1).astype(jnp.int32)
    rows, _, channels = in_weight.shape
    heads = head_table.shape[1]
    tokens, depth = hidden.shape
    share = bc_weight.shape[1] // ranks
    spare = LANES - share - heads

    ks = hops(n)
    near_ks, far_k = ks[:-1], ks[-1]

    def members(order):
        return jnp.stack([((outer + k) % n) * 2 + (inner ^ j) for k, j in order]).astype(jnp.int32)

    first = [(0, 0), (0, 1)]
    idx = members(first + [(k, 0) for k in ks] + [(k, 1) for k in ks])
    idx_c = members(first + [(k, j) for j in (0, 1) for k in near_ks] + [(far_k, 0), (far_k, 1)])
    sizes = (1, 1, n - 1, n - 1)
    width = depth // ranks

    own_bc = lax.dynamic_slice_in_dim(bc_weight, rank * share, share, 1)
    set_a = jnp.concatenate([in_weight[:, 1], own_bc, step_weight, jnp.zeros((rows, spare), f32)], axis=1).astype(bf16)
    set_b = in_weight[:, 0].astype(bf16)
    set_c = out_weight.T.astype(bf16)
    wide_a = set_a.shape[1]

    a_z = [outer_from(set_a, k) for k in ks]
    own_x = inner_flip(jnp.concatenate([set_a, set_b, set_c], axis=1))
    cot_far = rank_flip(cotangent, 2)
    gain_rows = pad_rows(norm_gain[None])
    normed_low, normed_t = prepare(hidden, gain_rows)
    aux, seg_row = segment_facts(segments)
    head_rows = pad_lanes(pad_rows(head_table))
    facts = (aux, seg_row, pad_rows(conv_table), pad_rows(bc_table), head_rows, head_expand(channels))
    set_a, set_b, set_c, a_z, own_x, cot_far, normed_low, normed_t, facts = fence(
        set_a, set_b, set_c, a_z, own_x, cot_far, normed_low, normed_t, facts
    )
    a_own, b_own, c_own = own_x[:, :wide_a], own_x[:, wide_a:wide_a + channels], own_x[:, wide_a + channels:]

    b_z = [outer_from(set_b, k) for k in ks]
    a_z = jnp.concatenate(a_z, axis=0)
    a_x = inner_flip(a_z)
    cot, cot_t = join_columns([cotangent, rank_flip(cotangent, 1), cot_far, rank_flip(cot_far, 1)], rank1)
    set_c, b_z, a_z, a_x, a_own, b_own, c_own, cot, cot_t, normed_low = fence(
        set_c, b_z, a_z, a_x, a_own, b_own, c_own, cot, cot_t, normed_low
    )

    c_near = [outer_from(set_c, k) for k in near_ks]
    b_z = jnp.concatenate(b_z, axis=0)
    b_x = inner_flip(b_z)
    x_pre, small, bc_share, w_a, w_bct_share = project(normed_low, [set_a, a_own, a_z, a_x], idx, channels, share)
    bc_pre, step_pre = join_small([bc_share] + [rank_flip(bc_share, r) for r in (1, 2, 3)], small, rank1)
    set_c, c_near, b_z, b_x, x_pre, bc_pre, step_pre, w_bct_share = fence(
        set_c, c_near, b_z, b_x, x_pre, bc_pre, step_pre, w_bct_share
    )

    c_far = outer_from(set_c, far_k)
    c_near = jnp.concatenate(c_near, axis=0)
    c_near_x = inner_flip(c_near)
    mixed, states = ssd_forward(x_pre, bc_pre, step_pre, *facts)
    c_far, c_near, c_near_x, mixed, states, w_bct_share = fence(c_far, c_near, c_near_x, mixed, states, w_bct_share)

    c_far_x = inner_flip(c_far)
    w_bct = [w_bct_share] + [rank_flip(w_bct_share, r) for r in (1, 2, 3)]
    gate_pre, square, w_b = gate_forward(normed_low, mixed, [set_b, b_own, b_z, b_x], idx)
    c_far_x, w_bct, gate_pre, square, mixed = fence(c_far_x, w_bct, gate_pre, square, mixed)

    conv_rows = facts[2]
    square = mp_sum_direct(square)
    gout, inner_dot, w_c = grad_gout(
        cot, gate_pre, mixed, conv_rows, [set_c, c_own, c_near, c_near_x, c_far, c_far_x], idx_c
    )
    square, gout, inner_dot, w_c = fence(square, gout, inner_dot, w_c)

    inner_dot = mp_sum_direct(inner_dot)
    gated_out = gated_norm(gate_pre, mixed, square, conv_rows, channels * ranks)
    gc_own, gc_own1, gc_here, gc_send = weight_grad(cot_t, gated_out, idx, sizes)
    inner_dot, gated_out, gc_own, gc_own1, gc_here, gc_send = fence(
        inner_dot, gated_out, gc_own, gc_own1, gc_here, gc_send
    )

    gc_back = inner_flip(gc_send)
    dmixed, dgate, dgain = gate_backward(gate_pre, gout, mixed, square, inner_dot, conv_rows, channels * ranks)
    dmixed, dgate, dgain, w_c, w_bct = fence(dmixed, dgate, dgain, w_c, w_bct)
    gb_own, gb_own1, gb_here, gb_send = weight_grad(normed_t, dgate, idx, sizes)
    partial = out_partial(gated_out, w_c, rank1, ranks)
    w_bct = join_rows(w_bct, rank1)
    gc_back, gb_own, gb_own1, gb_here, gb_send, partial, dmixed, w_bct = fence(
        gc_back, gb_own, gb_own1, gb_here, gb_send, partial, dmixed, w_bct
    )
    out_far = (partial[2].astype(f32) + rank_flip(partial[3], 1).astype(f32)).astype(bf16)
    out_near = partial[0].astype(f32) + rank_flip(partial[1], 1).astype(f32)
    gc_send_z = outer_blocks(gc_own, gc_here, gc_back, ks)
    out_far, out_near, gc_send_z, gb_send, dmixed, w_bct = fence(out_far, out_near, gc_send_z, gb_send, dmixed, w_bct)

    c_got = outer_send(gc_send_z, ks)
    gb_back = inner_flip(gb_send)
    out_got = rank_flip(out_far, 2)
    dx, dbc, dbc_t, dstep, dstep_t, dconv, dbct_part, dheads = ssd_backward(
        x_pre, bc_pre, step_pre, *facts, mixed, dmixed, states
    )
    c_got, gb_back, out_got, dx, dbc, dbc_t, dstep, dstep_t, dconv, dbct_part, dheads, gc_own1, gb_own1 = fence(
        c_got, gb_back, out_got, dx, dbc, dbc_t, dstep, dstep_t, dconv, dbct_part, dheads, gc_own1, gb_own1
    )

    b_got = outer_send(outer_blocks(gb_own, gb_here, gb_back, ks), ks)
    c_own_got = inner_flip(gc_own1)
    ga_own, ga_own1, ga_here, ga_send = weight_grad(normed_t, dx, idx, sizes)
    ga_own, ga_own1, ga_here, ga_send, dx, dbc_t = fence(ga_own, ga_own1, ga_here, ga_send, dx, dbc_t)
    ga_back = inner_flip(ga_send)
    term = normed_term(dx, dgate, dstep, dbc, w_a, w_b, w_bct, rank1, ranks)
    term, dbc_t = fence(term, dbc_t)
    near, far = mp_reduce(term)
    parts = lax.all_to_all(dbc_t.reshape(ranks, share, tokens), "mp", 0, 0)
    dbc_share = jnp.sum(parts.astype(f32), axis=0).astype(bf16)
    dsmall_t = jnp.concatenate([dbc_share, dstep_t, jnp.zeros((LANES - share - 16, tokens), bf16)], axis=0)
    gs_own, gs_own1, gs_here, gs_send = weight_grad(normed_t, dsmall_t, idx, sizes, turned=True)
    b_got, c_own_got, ga_back, near, far, gs_own, gs_own1, gs_here, gs_send = fence(
        b_got, c_own_got, ga_back, near, far, gs_own, gs_own1, gs_here, gs_send
    )

    def total(own, own_got, got):
        value = own.astype(f32) + own_got.astype(f32)
        for part in got:
            value = value + part.astype(f32)
        return value

    a_got = outer_send(outer_blocks(ga_own, ga_here, ga_back, ks), ks)
    mine, dgain_mine = norm_backward(near, far, hidden, cot, gain_rows, rank1)
    a_own_got, b_own_got = inner_flip(ga_own1), inner_flip(gb_own1)
    gs_back, s_own_got = inner_flip(gs_send), inner_flip(gs_own1)
    s_got = outer_send(outer_blocks(gs_own, gs_here, gs_back, ks), ks)
    input_grad = join_rows(mp_pieces(mine), rank1)
    resid = lax.dynamic_slice_in_dim(hidden, rank * width, width, 1).astype(f32)
    output = (resid + out_near + out_got.astype(f32)).astype(bf16)
    shard_c = total(gc_own, c_own_got, c_got)
    shard_b = total(gb_own, b_own_got, b_got)
    shard_a = total(ga_own, a_own_got, a_got)
    shard_s = total(gs_own, s_own_got, s_got)

    packed = dp_sum(jnp.concatenate([dconv + dgain, mp_sum(dbct_part), dheads], axis=1))
    total_conv = packed[:6, :channels]
    total_bct = packed[:5, channels:channels + 2 * LANES]
    total_head = packed[:3, channels + 2 * LANES:channels + 2 * LANES + heads]
    total_gain = dp_sum(mp_sum(dgain_mine))[0]

    shard_bc = in_rank_order(mp_pieces(shard_s[:, :share]), rank, 1)
    shard_step = shard_s[:, share:share + heads]
    in_m, in_w = advance(in_weight, in_moment, jnp.stack([shard_b, shard_a], axis=1))
    bc_m, bc_w = advance(bc_weight, bc_moment, shard_bc)
    step_m, step_w = advance(step_weight, step_moment, shard_step)
    out_m, out_w = advance(out_weight, out_moment, shard_c.T)
    return (
        output, input_grad, in_m, in_w, bc_m, bc_w, step_m, step_w, out_m, out_w,
        momentum(conv_moment, total_conv),
        momentum(bc_table_moment, total_bct),
        momentum(head_moment, total_head),
        momentum(gain_moment, total_gain),
    )


def solution(mesh):
    placed = (
        P("dp", None),
        P("dp", None),
        P("dp", "mp"),
        P("dp", None, "mp"),
        P("dp", None, "mp"),
        P("dp", None),
        P("dp", None),
        P("dp", "mp"),
        P("dp", "mp"),
        P("mp", "dp"),
        P("mp", "dp"),
        P(None, "mp"),
        P(None, "mp"),
        P(),
        P(),
        P(None, "mp"),
        P(None, "mp"),
        P(),
        P(),
    )
    return jax.shard_map(
        body,
        mesh=mesh,
        in_specs=placed,
        out_specs=(
            P("dp", "mp"),
            P("dp", None),
            P("dp", None, "mp"),
            P("dp", None, "mp"),
            P("dp", None),
            P("dp", None),
            P("dp", "mp"),
            P("dp", "mp"),
            P("mp", "dp"),
            P("mp", "dp"),
            P(None, "mp"),
            P(),
            P(None, "mp"),
            P(),
        ),
        check_vma=False,
    )
```

```python
import functools

import jax
import jax.numpy as jnp
from jax import lax
from jax.experimental import pallas as pl
from jax.experimental.pallas import tpu as pltpu
from jax.sharding import PartitionSpec as P

CHUNK = 128
EPSILON = 1e-05
LEARN_RATE = 0.0001
DECAY_RATE = 0.1
WIDTH = 64
LANES = 128
HALO = 8
bf16 = jnp.bfloat16
f32 = jnp.float32
MIB = 1024 * 1024


def dot_nn(a, b):
    return lax.dot_general(a, b, (((1,), (0,)), ((), ())), preferred_element_type=f32)


def dot_nt(a, b):
    return lax.dot_general(a, b, (((1,), (1,)), ((), ())), preferred_element_type=f32)


def dot_tn(a, b):
    return lax.dot_general(a, b, (((0,), (0,)), ((), ())), preferred_element_type=f32)


def split3(v):
    high = v.astype(bf16)
    rest = v - high.astype(f32)
    mid = rest.astype(bf16)
    low = (rest - mid.astype(f32)).astype(bf16)
    return high, mid, low


def exact_left(ones, v):
    high, mid, low = split3(v)
    return dot_nn(ones, high) + dot_nn(ones, mid) + dot_nn(ones, low)


def spread(v, expand):
    high, mid, low = split3(v)
    return dot_nn(high, expand) + dot_nn(mid, expand) + dot_nn(low, expand)


def gather_heads(v, expand):
    high = v.astype(bf16)
    mid = (v - high.astype(f32)).astype(bf16)
    return dot_nt(high, expand) + dot_nt(mid, expand)


def sigmoid(v):
    return 1.0 / (1.0 + jnp.exp(-v))


def conv_block(scratch, before, now, taps, keep):
    rows = now.shape[0]
    scratch[0:HALO, :] = before
    scratch[HALO:HALO + rows, :] = now
    total = taps[4:5, :] + taps[0:1, :] * now
    for lag in (1, 2, 3):
        moved = scratch[HALO - lag:HALO - lag + rows, :]
        total = total + taps[lag:lag + 1, :] * (moved * keep[:, lag - 1:lag])
    return total


def step_parts(step_pre, heads):
    raw = step_pre + heads[0:1, :]
    steps = jnp.maximum(raw, 0.0) + jnp.log1p(jnp.exp(-jnp.abs(raw)))
    rates = -jnp.exp(heads[1:2, :])
    return raw, steps, rates


def triangle(lower):
    row = lax.broadcasted_iota(jnp.int32, (CHUNK, CHUNK), 0)
    col = lax.broadcasted_iota(jnp.int32, (CHUNK, CHUNK), 1)
    return row >= col if lower else row <= col


def ssd_forward_kernel(
    x_ref, xb_ref, bc_ref, bcb_ref, st_ref, aux_ref, seg_ref, conv_ref, bct_ref, heads_ref, expand_ref,
    mixed_ref, state_ref, state, xs_scr, bc_scr,
):
    chunk = pl.program_id(0)

    @pl.when(chunk == 0)
    def _():
        state[...] = jnp.zeros_like(state)

    channels = x_ref.shape[1]
    aux = aux_ref[...]
    expand = expand_ref[...]
    u = conv_block(xs_scr, xb_ref[...], x_ref[...], conv_ref, aux)
    x_act = u * sigmoid(u)
    ubc = conv_block(bc_scr, bcb_ref[...], bc_ref[...], bct_ref, aux)
    bc_act = (ubc * sigmoid(ubc)).astype(bf16)
    b_mat, c_mat = bc_act[:, :LANES], bc_act[:, LANES:]
    _, steps, rates = step_parts(st_ref[...], heads_ref)
    lower = triangle(True)
    cum = exact_left(lower.astype(bf16), steps * rates)
    cum_t = cum.T
    tail = cum[CHUNK - 1:CHUNK, :]
    entry = jnp.exp(cum) * aux[:, 6:7]
    to_end = jnp.exp(tail - cum) * aux[:, 7:8]
    wide = spread(jnp.concatenate([steps, entry, to_end], axis=0), expand)
    step_e, entry_e, to_end_e = wide[:CHUNK], wide[CHUNK:2 * CHUNK], wide[2 * CHUNK:]
    skip_e = spread(jnp.broadcast_to(heads_ref[2:3, :], (8, LANES)), expand)[0:1, :]
    mask = lower & (aux[:, 8:9] == seg_ref[...])
    scores = jnp.where(mask, dot_nt(c_mat, b_mat), 0.0)
    xs = x_act * step_e
    xs_low = xs.astype(bf16)
    held = state[...]
    held_low = held.astype(bf16)
    state_ref[...] = held_low
    out = dot_nn(c_mat, held_low) * entry_e + skip_e * x_act
    state[...] = held * entry_e[CHUNK - 1:CHUNK, :] + dot_tn(b_mat, (xs * to_end_e).astype(bf16))
    first = lax.broadcasted_iota(jnp.int32, (CHUNK, LANES), 1) < WIDTH
    zero = jnp.zeros((CHUNK, LANES), bf16)
    for pair in range(channels // LANES):
        span = slice(pair * LANES, (pair + 1) * LANES)
        parts = []
        for head in (2 * pair, 2 * pair + 1):
            diff = cum[:, head:head + 1] - cum_t[head:head + 1, :]
            parts.append((scores * jnp.exp(jnp.minimum(diff, 0.0))).astype(bf16))
        own = xs_low[:, span]
        both = jnp.concatenate([jnp.where(first, own, zero), jnp.where(first, zero, own)], axis=0)
        mixed_ref[:, span] = out[:, span] + dot_nn(jnp.concatenate(parts, axis=1), both)


def ssd_backward_kernel(
    rank_ref, x_ref, xb_ref, bc_ref, bcb_ref, st_ref, aux_ref, seg_ref, conv_ref, bct_ref, heads_ref, expand_ref,
    mixed_ref, dy_ref, state_ref,
    dx_ref, dbc_ref, keep_ref, send_ref, dst_ref, dst_t_ref, dconv_ref, dbct_ref, dheads_ref,
    dstate, xs_scr, bc_scr, du_scr, dubc_scr, share_scr,
):
    at = pl.program_id(0)

    @pl.when(at == 0)
    def _():
        dstate[...] = jnp.zeros_like(dstate)
        du_scr[...] = jnp.zeros_like(du_scr)
        dubc_scr[...] = jnp.zeros_like(dubc_scr)
        dconv_ref[...] = jnp.zeros_like(dconv_ref)
        dbct_ref[...] = jnp.zeros_like(dbct_ref)
        dheads_ref[...] = jnp.zeros_like(dheads_ref)

    channels = x_ref.shape[1]
    aux = aux_ref[...]
    expand = expand_ref[...]
    x_now, bc_now = x_ref[...], bc_ref[...]
    u = conv_block(xs_scr, xb_ref[...], x_now, conv_ref, aux)
    sg = sigmoid(u)
    x_act = u * sg
    ubc = conv_block(bc_scr, bcb_ref[...], bc_now, bct_ref, aux)
    sgbc = sigmoid(ubc)
    bc_act = (ubc * sgbc).astype(bf16)
    b_mat, c_mat = bc_act[:, :LANES], bc_act[:, LANES:]
    raw, steps, rates = step_parts(st_ref[...], heads_ref)
    lower = triangle(True)
    cum = exact_left(lower.astype(bf16), steps * rates)
    cum_t = cum.T
    tail = cum[CHUNK - 1:CHUNK, :]
    entry = jnp.exp(cum) * aux[:, 6:7]
    to_end = jnp.exp(tail - cum) * aux[:, 7:8]
    wide = spread(jnp.concatenate([steps, entry, to_end], axis=0), expand)
    step_e, entry_e, to_end_e = wide[:CHUNK], wide[CHUNK:2 * CHUNK], wide[2 * CHUNK:]
    skip_e = spread(jnp.broadcast_to(heads_ref[2:3, :], (8, LANES)), expand)[0:1, :]
    upper = triangle(False)
    mask = upper & (aux[:, 8:9] == seg_ref[...])
    scores = jnp.where(mask, dot_nt(b_mat, c_mat), 0.0)
    xs = x_act * step_e
    xs_low = xs.astype(bf16)
    dy_low = dy_ref[...]
    dy = dy_low.astype(f32)
    held_low = state_ref[...]
    grad = dstate[...]
    grad_low = grad.astype(bf16)
    entry_dy = (entry_e * dy).astype(bf16)
    kept_e = entry_e[CHUNK - 1:CHUNK, :]
    dstate[...] = grad * kept_e + dot_tn(c_mat, entry_dy)
    dc = dot_nt(entry_dy, held_low)
    db = dot_nt((xs * to_end_e).astype(bf16), grad_low)
    q_state = dot_nn(b_mat, grad_low) * to_end_e
    first = lax.broadcasted_iota(jnp.int32, (CHUNK, LANES), 1) < WIDTH
    zero = jnp.zeros((CHUNK, LANES), bf16)
    dscores = jnp.zeros((CHUNK, CHUNK), f32)
    q_parts = []
    for pair in range(channels // LANES):
        span = slice(pair * LANES, (pair + 1) * LANES)
        own = dy_low[:, span]
        both = jnp.concatenate([jnp.where(first, own, zero), jnp.where(first, zero, own)], axis=0)
        dweights = dot_nt(xs_low[:, span], both)
        parts = []
        for i, head in enumerate((2 * pair, 2 * pair + 1)):
            diff = cum_t[head:head + 1, :] - cum[:, head:head + 1]
            decay = jnp.exp(jnp.minimum(diff, 0.0))
            parts.append((scores * decay).astype(bf16))
            dscores = dscores + dweights[:, i * LANES:(i + 1) * LANES] * decay
        q_parts.append(dot_nn(jnp.concatenate(parts, axis=1), both))
    q = jnp.concatenate(q_parts, axis=1) + q_state
    dscores_low = jnp.where(mask, dscores, 0.0).astype(bf16)
    db = db + dot_nn(dscores_low, c_mat)
    dc = dc + dot_tn(dscores_low, b_mat)
    xs_round = xs_low.astype(f32)
    rows = gather_heads(
        jnp.concatenate(
            [
                dy * (mixed_ref[...] - skip_e * x_act) - xs_round * q,
                x_act * q,
            ],
            axis=0,
        ),
        expand,
    )
    flow, dstep = rows[:CHUNK], rows[CHUNK:]
    sums = jnp.concatenate(
        [
            jnp.sum(xs_round * q_state + kept_e * (held_low.astype(f32) * grad), axis=0, keepdims=True),
            jnp.sum(dy * x_act, axis=0, keepdims=True),
            jnp.zeros((6, channels), f32),
        ],
        axis=0,
    )
    sums = gather_heads(sums, expand)
    dlog = exact_left(upper.astype(bf16), flow) + sums[0:1, :]
    dstep = dstep + rates * dlog
    draw = dstep * sigmoid(raw)
    dst_ref[...] = pltpu.roll(draw, WIDTH, 1).astype(bf16)
    dst_t_ref[...] = draw.T[0:16, :].astype(bf16)
    dheads_ref[0:1, :] += jnp.sum(draw, axis=0, keepdims=True)
    dheads_ref[1:2, :] += rates * jnp.sum(dlog * steps, axis=0, keepdims=True)
    dheads_ref[2:3, :] += sums[1:2, :]

    def conv_back(scratch, du, now, taps, dtaps):
        scratch[0:CHUNK, :] = du
        total = taps[0:1, :] * du
        dtaps[0:1, :] += jnp.sum(now * du, axis=0, keepdims=True)
        dtaps[4:5, :] += jnp.sum(du, axis=0, keepdims=True)
        for lag in (1, 2, 3):
            moved = scratch[lag:lag + CHUNK, :] * aux[:, 2 + lag:3 + lag]
            total = total + taps[lag:lag + 1, :] * moved
            dtaps[lag:lag + 1, :] += jnp.sum(now * moved, axis=0, keepdims=True)
        scratch[CHUNK:CHUNK + HALO, :] = du[0:HALO, :]
        return total

    du = (skip_e * dy + step_e * q) * (sg * (1.0 + u * (1.0 - sg)))
    dx_ref[...] = conv_back(du_scr, du, x_now, conv_ref, dconv_ref).astype(dx_ref.dtype)
    dubc = jnp.concatenate([db, dc], axis=1) * (sgbc * (1.0 + ubc * (1.0 - sgbc)))
    dbc = conv_back(dubc_scr, dubc, bc_now, bct_ref, dbct_ref).astype(bf16)
    dbc_ref[...] = dbc
    share = 2 * LANES // 4
    turned = dbc.T
    for member in range(4):
        apart = member ^ rank_ref[0]
        start = pl.multiple_of((apart & 1) * 2 * share + (apart >> 1) * share, share)
        share_scr[pl.ds(start, share), :] = turned[member * share:(member + 1) * share, :]
    keep_ref[...] = share_scr[0:2 * share, :]
    send_ref[...] = share_scr[2 * share:4 * share, :]


def common_specs(place, channels):
    before = lambda i: (jnp.maximum(place(i) * (CHUNK // HALO) - 1, 0), 0)
    now = lambda i: (place(i), 0)
    whole = lambda i: (0, 0)
    return [
        pl.BlockSpec((CHUNK, channels), now),
        pl.BlockSpec((HALO, channels), before),
        pl.BlockSpec((CHUNK, 2 * LANES), now),
        pl.BlockSpec((HALO, 2 * LANES), before),
        pl.BlockSpec((CHUNK, LANES), now),
        pl.BlockSpec((CHUNK, 16), now),
        pl.BlockSpec((1, CHUNK), lambda i: (0, place(i))),
        pl.BlockSpec((8, channels), whole),
        pl.BlockSpec((8, 2 * LANES), whole),
        pl.BlockSpec((8, LANES), whole),
        pl.BlockSpec((LANES, channels), whole),
    ]


def ssd_forward(x_pre, bc_pre, step_pre, aux, seg_row, conv_rows, bc_rows, head_rows, expand):
    tokens, channels = x_pre.shape
    count = tokens // CHUNK
    now = lambda i: (i, 0)
    return pl.pallas_call(
        ssd_forward_kernel,
        grid=(count,),
        in_specs=common_specs(lambda i: i, channels),
        out_specs=[
            pl.BlockSpec((CHUNK, channels), now),
            pl.BlockSpec((None, LANES, channels), lambda i: (i, 0, 0)),
        ],
        out_shape=[
            jax.ShapeDtypeStruct((tokens, channels), f32),
            jax.ShapeDtypeStruct((count, LANES, channels), bf16),
        ],
        scratch_shapes=[
            pltpu.VMEM((LANES, channels), f32),
            pltpu.VMEM((HALO + CHUNK, channels), f32),
            pltpu.VMEM((HALO + CHUNK, 2 * LANES), f32),
        ],
        compiler_params=pltpu.CompilerParams(vmem_limit_bytes=14 * MIB),
        cost_estimate=pl.CostEstimate(flops=14 * 10**9, bytes_accessed=40 * 10**6, transcendentals=0),
        name="ssd_forward",
    )(x_pre, x_pre, bc_pre, bc_pre, step_pre, aux, seg_row, conv_rows, bc_rows, head_rows, expand)


def ssd_backward(rank, x_pre, bc_pre, step_pre, aux, seg_row, conv_rows, bc_rows, head_rows, expand, mixed, dy, states):
    tokens, channels = x_pre.shape
    count = tokens // CHUNK
    place = lambda i: count - 1 - i
    now = lambda i: (place(i), 0)
    whole = lambda i: (0, 0)
    return pl.pallas_call(
        ssd_backward_kernel,
        grid=(count,),
        in_specs=[pl.BlockSpec(memory_space=pltpu.SMEM)] + common_specs(place, channels) + [
            pl.BlockSpec((CHUNK, channels), now),
            pl.BlockSpec((CHUNK, channels), now),
            pl.BlockSpec((None, LANES, channels), lambda i: (place(i), 0, 0)),
        ],
        out_specs=[
            pl.BlockSpec((CHUNK, channels), now),
            pl.BlockSpec((CHUNK, 2 * LANES), now),
            pl.BlockSpec((LANES, CHUNK), lambda i: (0, place(i))),
            pl.BlockSpec((LANES, CHUNK), lambda i: (0, place(i))),
            pl.BlockSpec((CHUNK, LANES), now),
            pl.BlockSpec((16, CHUNK), lambda i: (0, place(i))),
            pl.BlockSpec((8, channels), whole),
            pl.BlockSpec((8, 2 * LANES), whole),
            pl.BlockSpec((8, LANES), whole),
        ],
        out_shape=[
            jax.ShapeDtypeStruct((tokens, channels), bf16),
            jax.ShapeDtypeStruct((tokens, 2 * LANES), bf16),
            jax.ShapeDtypeStruct((LANES, tokens), bf16),
            jax.ShapeDtypeStruct((LANES, tokens), bf16),
            jax.ShapeDtypeStruct((tokens, LANES), bf16),
            jax.ShapeDtypeStruct((16, tokens), bf16),
            jax.ShapeDtypeStruct((8, channels), f32),
            jax.ShapeDtypeStruct((8, 2 * LANES), f32),
            jax.ShapeDtypeStruct((8, LANES), f32),
        ],
        scratch_shapes=[
            pltpu.VMEM((LANES, channels), f32),
            pltpu.VMEM((HALO + CHUNK, channels), f32),
            pltpu.VMEM((HALO + CHUNK, 2 * LANES), f32),
            pltpu.VMEM((HALO + CHUNK, channels), f32),
            pltpu.VMEM((HALO + CHUNK, 2 * LANES), f32),
            pltpu.VMEM((2 * LANES, CHUNK), bf16),
        ],
        compiler_params=pltpu.CompilerParams(vmem_limit_bytes=14 * MIB),
        cost_estimate=pl.CostEstimate(flops=28 * 10**9, bytes_accessed=80 * 10**6, transcendentals=0),
        name="ssd_backward",
    )(rank, x_pre, x_pre, bc_pre, bc_pre, step_pre, aux, seg_row, conv_rows, bc_rows, head_rows, expand, mixed, dy, states)


def segment_facts(seg):
    row = seg[0]
    tokens = row.shape[0]
    cols = []
    for lag in (1, 2, 3):
        cols.append(jnp.pad(row[:-lag], (lag, 0), constant_values=-1) == row)
    for lag in (1, 2, 3):
        cols.append(jnp.pad(row[lag:], (0, lag), constant_values=-1) == row)
    blocks = row.reshape(tokens // CHUNK, CHUNK)
    ends = blocks[:, -1:]
    before = jnp.concatenate([jnp.full((1, 1), -1, row.dtype), ends[:-1]], axis=0)
    cols.append((blocks == before).reshape(-1))
    cols.append((blocks == ends).reshape(-1))
    cols.append(row)
    facts = jnp.stack([c.astype(f32) for c in cols], axis=1)
    return jnp.pad(facts, ((0, 0), (0, 16 - facts.shape[1]))), seg.astype(f32)


def pad_rows(table, rows=8):
    return jnp.pad(table, ((0, rows - table.shape[0]), (0, 0)))


def pad_lanes(table, lanes=LANES):
    return jnp.pad(table, ((0, 0), (0, lanes - table.shape[1])))


def head_expand(channels):
    head = jnp.arange(LANES)[:, None]
    return (head == (jnp.arange(channels) // WIDTH)[None, :]).astype(bf16)


TILE = 256
TILE_D = 384


def fill(dest, pieces, idx_ref):
    rows = pieces[0].shape[0]
    s = 0
    for piece in pieces:
        for b in range(piece.shape[0] // rows):
            start = pl.multiple_of(idx_ref[s] * rows, rows)
            dest[pl.ds(start, rows), :] = piece[b * rows:(b + 1) * rows, :]
            s += 1


def params(mib=18):
    return pltpu.CompilerParams(vmem_limit_bytes=mib * MIB)


def cost(us):
    return pl.CostEstimate(flops=int(us * 10**9), bytes_accessed=int(us * 2 * 10**6), transcendentals=0)


def prepare_kernel(hidden_ref, gain_ref, low_ref, low_t_ref, inv_ref):
    inputs = hidden_ref[...].astype(f32)
    inv_rms = lax.rsqrt(jnp.mean(inputs * inputs, axis=1, keepdims=True) + EPSILON)
    low = (inputs * inv_rms * gain_ref[0:1, :]).astype(bf16)
    low_ref[...] = low
    low_t_ref[...] = low.T
    inv_ref[...] = column_to_row(inv_rms)


def prepare(hidden, gain_rows):
    tokens, depth = hidden.shape
    block = pl.BlockSpec((TILE, depth), lambda i: (i, 0))
    return pl.pallas_call(
        prepare_kernel,
        grid=(tokens // TILE,),
        in_specs=[block, pl.BlockSpec((8, depth), lambda i: (0, 0))],
        out_specs=[block, pl.BlockSpec((depth, TILE), lambda i: (0, i)), pl.BlockSpec((8, TILE), lambda i: (0, i))],
        out_shape=[
            jax.ShapeDtypeStruct((tokens, depth), bf16),
            jax.ShapeDtypeStruct((depth, tokens), bf16),
            jax.ShapeDtypeStruct((8, tokens), f32),
        ],
        compiler_params=params(),
        cost_estimate=cost(12),
        name="prepare",
    )(hidden, gain_rows)


def pack_kernel(rank_ref, in_ref, bc_ref, step_ref, a_ref, b_ref, scratch):
    channels = b_ref.shape[1]
    rows, width = bc_ref.shape
    share = width // 4
    heads = step_ref.shape[0]
    b_ref[...] = in_ref[:, 0, :].astype(bf16)
    a_ref[:, :channels] = in_ref[:, 1, :].astype(bf16)
    scratch[...] = jnp.zeros_like(scratch)
    scratch[share:share + heads, 0:rows] = step_ref[...]
    step = scratch[...].T[0:rows, :]
    own = bc_ref[:, 0:LANES]
    for member in range(1, 4):
        moved = pltpu.roll(bc_ref[...], width - member * share, 1)[:, 0:LANES]
        own = jnp.where(rank_ref[0] == member, moved, own)
    lane = lax.broadcasted_iota(jnp.int32, (rows, LANES), 1)
    a_ref[:, channels:] = jnp.where(lane < share, own, step).astype(bf16)


def pack(in_weight, bc_weight, step_t, rank):
    rows, _, channels = in_weight.shape
    vmem = pl.BlockSpec(memory_space=pltpu.VMEM)
    return pl.pallas_call(
        pack_kernel,
        in_specs=[pl.BlockSpec(memory_space=pltpu.SMEM), vmem, vmem, vmem],
        out_specs=[vmem, vmem],
        out_shape=[
            jax.ShapeDtypeStruct((rows, channels + LANES), bf16),
            jax.ShapeDtypeStruct((rows, channels), bf16),
        ],
        scratch_shapes=[pltpu.VMEM((LANES, 2 * LANES), f32)],
        compiler_params=params(),
        cost_estimate=cost(2),
        name="pack",
    )(rank, in_weight, bc_weight, step_t)


def columns_kernel(rank_ref, *refs, count):
    pieces, (full_ref, full_t_ref) = refs[:count], refs[count:]
    for r, piece in enumerate(pieces):
        width = piece.shape[1]
        start = pl.multiple_of((rank_ref[0] ^ r) * width, LANES)
        value = piece[...]
        full_ref[:, pl.ds(start, width)] = value
        full_t_ref[pl.ds(start, width), :] = value.T


def join_columns(pieces, rank):
    tokens, width = pieces[0].shape
    depth = width * len(pieces)
    return pl.pallas_call(
        functools.partial(columns_kernel, count=len(pieces)),
        grid=(tokens // TILE,),
        in_specs=[pl.BlockSpec(memory_space=pltpu.SMEM)] + [pl.BlockSpec((TILE, width), lambda i: (i, 0))] * len(pieces),
        out_specs=[pl.BlockSpec((TILE, depth), lambda i: (i, 0)), pl.BlockSpec((depth, TILE), lambda i: (0, i))],
        out_shape=[jax.ShapeDtypeStruct((tokens, depth), bf16), jax.ShapeDtypeStruct((depth, tokens), bf16)],
        compiler_params=params(),
        cost_estimate=cost(12),
        name="join_columns",
    )(rank, *pieces)


def rows_kernel(rank_ref, *refs, count):
    pieces, full_ref = refs[:count], refs[count]
    for r, piece in enumerate(pieces):
        rows = piece.shape[0]
        full_ref[pl.ds(pl.multiple_of((rank_ref[0] ^ r) * rows, rows), rows), :] = piece[...]


def join_rows(pieces, rank):
    rows, width = pieces[0].shape
    shape = (rows * len(pieces), width)
    return pl.pallas_call(
        functools.partial(rows_kernel, count=len(pieces)),
        in_specs=[pl.BlockSpec(memory_space=pltpu.SMEM)] + [pl.BlockSpec(memory_space=pltpu.VMEM)] * len(pieces),
        out_specs=pl.BlockSpec(memory_space=pltpu.VMEM),
        out_shape=jax.ShapeDtypeStruct(shape, pieces[0].dtype),
        compiler_params=params(),
        cost_estimate=cost(0.1),
        name="join_rows",
    )(rank, *pieces)


def small_kernel(rank_ref, *refs, count):
    pieces, (small_ref, bc_ref, step_ref, scratch) = refs[:count], refs[count:]
    share = pieces[0].shape[0]
    for r, piece in enumerate(pieces):
        scratch[pl.ds(pl.multiple_of((rank_ref[0] ^ r) * share, share), share), :] = piece[...].astype(f32)
    bc_ref[...] = scratch[...].T
    turned = small_ref[...].T
    lane = lax.broadcasted_iota(jnp.int32, turned.shape, 1)
    step_ref[...] = jnp.where(lane < LANES - share, pltpu.roll(turned, LANES - share, 1), 0.0)


def join_small(pieces, small, rank):
    share, tokens = pieces[0].shape
    width = share * len(pieces)
    return pl.pallas_call(
        functools.partial(small_kernel, count=len(pieces)),
        grid=(tokens // TILE,),
        in_specs=[pl.BlockSpec(memory_space=pltpu.SMEM)]
        + [pl.BlockSpec((share, TILE), lambda i: (0, i))] * len(pieces)
        + [pl.BlockSpec((LANES, TILE), lambda i: (0, i))],
        out_specs=[pl.BlockSpec((TILE, width), lambda i: (i, 0)), pl.BlockSpec((TILE, LANES), lambda i: (i, 0))],
        out_shape=[jax.ShapeDtypeStruct((tokens, width), f32), jax.ShapeDtypeStruct((tokens, LANES), f32)],
        scratch_shapes=[pltpu.VMEM((width, TILE), f32)],
        compiler_params=params(),
        cost_estimate=cost(0.1),
        name="join_small",
    )(rank, *pieces, small)


def project_small_kernel(idx_ref, lhs_ref, *refs, count):
    pieces, (small_ref, share_ref, w_ref, wt_ref) = refs[:count], refs[count:]

    @pl.when(pl.program_id(0) == 0)
    def _():
        fill(w_ref, pieces, idx_ref)
        wt_ref[...] = w_ref[...].T[0:wt_ref.shape[0], :]

    small = dot_nn(lhs_ref[...], w_ref[...]).T
    small_ref[...] = small
    share_ref[...] = small[0:share_ref.shape[0], :].astype(bf16)


def project_small(lhs, pieces, idx, share):
    tokens, depth = lhs.shape
    count, last = len(pieces), pieces[0].shape[1] // LANES - 1
    whole = lambda i: (0, 0)
    return pl.pallas_call(
        functools.partial(project_small_kernel, count=count),
        grid=(tokens // TILE,),
        in_specs=[pl.BlockSpec(memory_space=pltpu.SMEM), pl.BlockSpec((TILE, depth), lambda i: (i, 0))]
        + [pl.BlockSpec((p.shape[0], LANES), lambda i: (0, last)) for p in pieces],
        out_specs=[
            pl.BlockSpec((LANES, TILE), lambda i: (0, i)),
            pl.BlockSpec((share, TILE), lambda i: (0, i)),
            pl.BlockSpec((depth, LANES), whole),
            pl.BlockSpec((share, depth), whole),
        ],
        out_shape=[
            jax.ShapeDtypeStruct((LANES, tokens), f32),
            jax.ShapeDtypeStruct((share, tokens), bf16),
            jax.ShapeDtypeStruct((depth, LANES), bf16),
            jax.ShapeDtypeStruct((share, depth), bf16),
        ],
        compiler_params=params(),
        cost_estimate=cost(0.1),
        name="project_small",
    )(idx, lhs, *pieces)


def project_kernel(idx_ref, lhs_ref, *refs, count):
    pieces, (x_ref, w_ref) = refs[:count], refs[count:]

    @pl.when(pl.program_id(0) == 0)
    def _():
        fill(w_ref, pieces, idx_ref)

    x_ref[...] = dot_nn(lhs_ref[...], w_ref[...])


def project(lhs, pieces, idx, channels):
    tokens, depth = lhs.shape
    whole = lambda i: (0, 0)
    return pl.pallas_call(
        functools.partial(project_kernel, count=len(pieces)),
        grid=(tokens // TILE,),
        in_specs=[pl.BlockSpec(memory_space=pltpu.SMEM), pl.BlockSpec((TILE, depth), lambda i: (i, 0))]
        + [pl.BlockSpec((p.shape[0], channels), whole) for p in pieces],
        out_specs=[pl.BlockSpec((TILE, channels), lambda i: (i, 0)), pl.BlockSpec((depth, channels), whole)],
        out_shape=[
            jax.ShapeDtypeStruct((tokens, channels), f32),
            jax.ShapeDtypeStruct((depth, channels), bf16),
        ],
        compiler_params=params(),
        cost_estimate=cost(20),
        name="project",
    )(idx, lhs, *pieces)


def column_to_row(col):
    return jnp.broadcast_to(col, (col.shape[0], LANES)).T[0:8, :]


def row_to_column(row):
    return jnp.broadcast_to(row, (LANES, row.shape[1])).T[:, 0:1]


def gate_kernel(idx_ref, lhs_ref, mixed_ref, *refs, count):
    pieces, (gate_ref, sums_ref, w_ref) = refs[:count], refs[count:]

    @pl.when(pl.program_id(0) == 0)
    def _():
        fill(w_ref, pieces, idx_ref)

    gate = dot_nn(lhs_ref[...], w_ref[...])
    gate_ref[...] = gate
    gated = mixed_ref[...] * (gate * sigmoid(gate))
    sums_ref[...] = column_to_row(jnp.sum(gated * gated, axis=1, keepdims=True))


def gate_forward(lhs, mixed, pieces, idx):
    tokens, depth = lhs.shape
    channels = mixed.shape[1]
    whole = lambda i: (0, 0)
    now = lambda i: (i, 0)
    return pl.pallas_call(
        functools.partial(gate_kernel, count=len(pieces)),
        grid=(tokens // TILE,),
        in_specs=[
            pl.BlockSpec(memory_space=pltpu.SMEM),
            pl.BlockSpec((TILE, depth), now),
            pl.BlockSpec((TILE, channels), now),
        ]
        + [pl.BlockSpec(p.shape, whole) for p in pieces],
        out_specs=[
            pl.BlockSpec((TILE, channels), now),
            pl.BlockSpec((8, TILE), lambda i: (0, i)),
            pl.BlockSpec((depth, channels), whole),
        ],
        out_shape=[
            jax.ShapeDtypeStruct((tokens, channels), f32),
            jax.ShapeDtypeStruct((8, tokens), f32),
            jax.ShapeDtypeStruct((depth, channels), bf16),
        ],
        compiler_params=params(),
        cost_estimate=cost(0.1),
        name="gate_forward",
    )(idx, lhs, mixed, *pieces)


def gated_kernel(gate_ref, mixed_ref, square_ref, conv_ref, out_ref, *, inner_total):
    gate = gate_ref[...]
    scale = lax.rsqrt(row_to_column(square_ref[0:1, :]) / inner_total + EPSILON)
    gated = mixed_ref[...] * (gate * sigmoid(gate))
    out_ref[...] = (gated * scale * conv_ref[5:6, :]).astype(bf16)


def gated_norm(gate, mixed, square, conv_rows, inner_total):
    tokens, channels = gate.shape
    block = pl.BlockSpec((TILE, channels), lambda i: (i, 0))
    return pl.pallas_call(
        functools.partial(gated_kernel, inner_total=inner_total),
        grid=(tokens // TILE,),
        in_specs=[block, block, pl.BlockSpec((8, TILE), lambda i: (0, i)), pl.BlockSpec((8, channels), lambda i: (0, 0))],
        out_specs=block,
        out_shape=jax.ShapeDtypeStruct((tokens, channels), bf16),
        compiler_params=params(),
        cost_estimate=cost(0.1),
        name="gated_norm",
    )(gate, mixed, square, conv_rows)


def gout_kernel(idx_ref, cot_ref, gate_ref, mixed_ref, conv_ref, *refs, count):
    pieces, (gout_ref, sums_ref, w_ref) = refs[:count], refs[count:]

    @pl.when(pl.program_id(0) == 0)
    def _():
        fill(w_ref, pieces, idx_ref)

    gout = dot_nn(cot_ref[...], w_ref[...])
    gout_ref[...] = gout
    gate = gate_ref[...]
    gated = mixed_ref[...] * (gate * sigmoid(gate))
    sums_ref[...] = column_to_row(jnp.sum(gout * conv_ref[5:6, :] * gated, axis=1, keepdims=True))


def grad_gout(cot, gate, mixed, conv_rows, pieces, idx):
    tokens, depth = cot.shape
    channels = mixed.shape[1]
    whole = lambda i: (0, 0)
    now = lambda i: (i, 0)
    return pl.pallas_call(
        functools.partial(gout_kernel, count=len(pieces)),
        grid=(tokens // TILE,),
        in_specs=[
            pl.BlockSpec(memory_space=pltpu.SMEM),
            pl.BlockSpec((TILE, depth), now),
            pl.BlockSpec((TILE, channels), now),
            pl.BlockSpec((TILE, channels), now),
            pl.BlockSpec((8, channels), whole),
        ]
        + [pl.BlockSpec(p.shape, whole) for p in pieces],
        out_specs=[
            pl.BlockSpec((TILE, channels), now),
            pl.BlockSpec((8, TILE), lambda i: (0, i)),
            pl.BlockSpec((depth, channels), whole),
        ],
        out_shape=[
            jax.ShapeDtypeStruct((tokens, channels), f32),
            jax.ShapeDtypeStruct((8, tokens), f32),
            jax.ShapeDtypeStruct((depth, channels), bf16),
        ],
        compiler_params=params(),
        cost_estimate=cost(20),
        name="grad_gout",
    )(idx, cot, gate, mixed, conv_rows, *pieces)


def gate_back_kernel(gate_ref, gout_ref, mixed_ref, square_ref, inner_ref, conv_ref, dmixed_ref, dgate_ref, dgain_ref, *, inner_total):
    gate, gout, mixed = gate_ref[...], gout_ref[...], mixed_ref[...]
    gain = conv_ref[5:6, :]
    square, inner = row_to_column(square_ref[0:1, :]), row_to_column(inner_ref[0:1, :])
    scale = lax.rsqrt(square / inner_total + EPSILON)
    sg = sigmoid(gate)
    act = gate * sg
    gated = mixed * act
    dgated = scale * (gain * gout) - gated * (scale * scale * scale * inner / inner_total)
    dmixed_ref[...] = (dgated * act).astype(bf16)
    dgate_ref[...] = (dgated * mixed * sg * (1.0 + gate * (1.0 - sg))).astype(bf16)

    @pl.when(pl.program_id(0) == 0)
    def _():
        dgain_ref[...] = jnp.zeros_like(dgain_ref)

    dgain_ref[5:6, :] += jnp.sum(gout * gated * scale, axis=0, keepdims=True)


def gate_backward(gate, gout, mixed, square, inner, conv_rows, inner_total):
    tokens, channels = gate.shape
    whole = lambda i: (0, 0)
    block = pl.BlockSpec((TILE, channels), lambda i: (i, 0))
    row = pl.BlockSpec((8, TILE), lambda i: (0, i))
    return pl.pallas_call(
        functools.partial(gate_back_kernel, inner_total=inner_total),
        grid=(tokens // TILE,),
        in_specs=[block, block, block, row, row, pl.BlockSpec((8, channels), whole)],
        out_specs=[block, block, pl.BlockSpec((8, channels), whole)],
        out_shape=[
            jax.ShapeDtypeStruct((tokens, channels), bf16),
            jax.ShapeDtypeStruct((tokens, channels), bf16),
            jax.ShapeDtypeStruct((8, channels), f32),
        ],
        compiler_params=params(),
        cost_estimate=cost(0.1),
        name="gate_backward",
    )(gate, gout, mixed, square, inner, conv_rows)


def weight_grad_kernel(idx_ref, lhs_ref, rhs_ref, *refs, rows, turned):
    outs, scratch = refs[:-1], refs[-1]
    at = pl.program_id(0)
    scratch[pl.ds(pl.multiple_of(at * TILE_D, TILE_D), TILE_D), :] = (dot_nt if turned else dot_nn)(
        lhs_ref[...], rhs_ref[...]
    ).astype(bf16)

    @pl.when(at == pl.num_programs(0) - 1)
    def _():
        s = 0
        for out in outs:
            for b in range(out.shape[0] // rows):
                start = pl.multiple_of(idx_ref[s] * rows, rows)
                out[b * rows:(b + 1) * rows, :] = scratch[pl.ds(start, rows), :]
                s += 1


def weight_grad(lhs_t, rhs, idx, sizes, us=0.1, turned=False):
    depth, tokens = lhs_t.shape
    width = rhs.shape[0 if turned else 1]
    rows = depth // idx.shape[0]
    whole = lambda i: (0, 0)
    return pl.pallas_call(
        functools.partial(weight_grad_kernel, rows=rows, turned=turned),
        grid=(depth // TILE_D,),
        in_specs=[
            pl.BlockSpec(memory_space=pltpu.SMEM),
            pl.BlockSpec((TILE_D, tokens), lambda i: (i, 0)),
            pl.BlockSpec(rhs.shape, whole),
        ],
        out_specs=[pl.BlockSpec((size * rows, width), whole) for size in sizes],
        out_shape=[jax.ShapeDtypeStruct((size * rows, width), bf16) for size in sizes],
        scratch_shapes=[pltpu.VMEM((depth, width), bf16)],
        compiler_params=params(),
        cost_estimate=cost(us),
        name="weight_grad",
    )(idx, lhs_t, rhs)


def out_kernel(rank_ref, lhs_ref, w_ref, *outs):
    product = dot_nt(lhs_ref[...], w_ref[...]).astype(bf16)
    for r, out in enumerate(outs):
        @pl.when(pl.program_id(0) == r)
        def _():
            out[...] = product


def out_partial(gated_out, w_out, rank, ranks):
    tokens, channels = gated_out.shape
    depth = w_out.shape[0]
    width = depth // ranks
    whole = lambda i, rank_ref: (0, 0)
    return pl.pallas_call(
        out_kernel,
        grid_spec=pltpu.PrefetchScalarGridSpec(
            num_scalar_prefetch=1,
            grid=(ranks,),
            in_specs=[
                pl.BlockSpec((tokens, channels), whole),
                pl.BlockSpec((width, channels), lambda i, rank_ref: (i ^ rank_ref[0], 0)),
            ],
            out_specs=[pl.BlockSpec((tokens, width), whole)] * ranks,
        ),
        out_shape=[jax.ShapeDtypeStruct((tokens, width), bf16)] * ranks,
        compiler_params=params(),
        cost_estimate=cost(0.1),
        name="out_partial",
    )(rank, gated_out, w_out)


def term_kernel(rank_ref, gx_ref, wx_ref, gg_ref, wg_ref, gs_ref, ws_ref, gb_ref, wbt_ref, hidden_ref, inv_ref, *refs):
    outs, dgain_ref, scratch = refs[:-2], refs[-2], refs[-1]
    total = dot_nt(gx_ref[...], wx_ref[...]) + dot_nt(gg_ref[...], wg_ref[...])
    total = total + dot_nt(gs_ref[...], ws_ref[...]) + dot_nn(gb_ref[...], wbt_ref[...])
    scratch[...] = total.astype(bf16)
    normed = hidden_ref[...].astype(f32) * row_to_column(inv_ref[0:1, :])
    dgain_ref[...] = jnp.broadcast_to(jnp.sum(total * normed, axis=0, keepdims=True), dgain_ref.shape)
    for r, out in enumerate(outs):
        rows = out.shape[0]
        out[...] = scratch[pl.ds(pl.multiple_of((rank_ref[0] ^ r) * rows, rows), rows), :]


def normed_term(dx, dgate, dstep, dbc, w_a, w_b, w_s, w_bct, hidden, inv_rms, rank, ranks):
    tokens, channels = dx.shape
    depth = w_a.shape[0]
    rows = tokens // ranks
    whole = lambda i: (0, 0)
    return pl.pallas_call(
        term_kernel,
        grid=(depth // TILE_D,),
        in_specs=[
            pl.BlockSpec(memory_space=pltpu.SMEM),
            pl.BlockSpec(dx.shape, whole),
            pl.BlockSpec((TILE_D, channels), lambda i: (i, 0)),
            pl.BlockSpec(dgate.shape, whole),
            pl.BlockSpec((TILE_D, channels), lambda i: (i, 0)),
            pl.BlockSpec(dstep.shape, whole),
            pl.BlockSpec((TILE_D, LANES), lambda i: (i, 0)),
            pl.BlockSpec(dbc.shape, whole),
            pl.BlockSpec((w_bct.shape[0], TILE_D), lambda i: (0, i)),
            pl.BlockSpec((tokens, TILE_D), lambda i: (0, i)),
            pl.BlockSpec(inv_rms.shape, whole),
        ],
        out_specs=[pl.BlockSpec((rows, TILE_D), lambda i: (0, i))] * ranks + [pl.BlockSpec((8, TILE_D), lambda i: (0, i))],
        out_shape=[jax.ShapeDtypeStruct((rows, depth), bf16)] * ranks + [jax.ShapeDtypeStruct((8, depth), f32)],
        scratch_shapes=[pltpu.VMEM((tokens, TILE_D), bf16)],
        compiler_params=params(32),
        cost_estimate=cost(0.1),
        name="normed_term",
    )(rank, dx, w_a, dgate, w_b, dstep, w_s, dbc, w_bct, hidden, inv_rms)


def norm_back_kernel(rank_ref, a_ref, b_ref, hidden_ref, cot_ref, gain_ref, out_ref):
    grad = a_ref[...].astype(f32) + b_ref[...].astype(f32)
    inputs = hidden_ref[...].astype(f32)
    inv_rms = lax.rsqrt(jnp.mean(inputs * inputs, axis=1, keepdims=True) + EPSILON)
    normed = inputs * inv_rms
    scaled = grad * gain_ref[0:1, :]
    mean = jnp.mean(scaled * normed, axis=1, keepdims=True)
    out_ref[...] = (inv_rms * (scaled - normed * mean) + cot_ref[...].astype(f32)).astype(out_ref.dtype)


def norm_backward(a, b, hidden, cot, gain_rows, rank):
    rows, depth = a.shape
    mine = lambda i, rank_ref: (rank_ref[0], 0)
    whole = lambda i, rank_ref: (0, 0)
    return pl.pallas_call(
        norm_back_kernel,
        grid_spec=pltpu.PrefetchScalarGridSpec(
            num_scalar_prefetch=1,
            grid=(1,),
            in_specs=[
                pl.BlockSpec((rows, depth), whole),
                pl.BlockSpec((rows, depth), whole),
                pl.BlockSpec((rows, depth), mine),
                pl.BlockSpec((rows, depth), mine),
                pl.BlockSpec((8, depth), whole),
            ],
            out_specs=pl.BlockSpec((rows, depth), whole),
        ),
        out_shape=jax.ShapeDtypeStruct((rows, depth), bf16),
        compiler_params=params(),
        cost_estimate=cost(0.1),
        name="norm_backward",
    )(rank, a, b, hidden, cot, gain_rows)


def fence(*values):
    leaves, tree = jax.tree.flatten(values)
    return jax.tree.unflatten(tree, lax.optimization_barrier(leaves))


def outer_from(v, k):
    n = lax.axis_size("dp") // 2
    return lax.ppermute(v, "dp", [(((o + k) % n) * 2 + x, o * 2 + x) for o in range(n) for x in range(2)])


def outer_flip(v, bit):
    n = lax.axis_size("dp") // 2
    return lax.ppermute(v, "dp", [((o ^ bit) * 2 + x, o * 2 + x) for o in range(n) for x in range(2)])


def inner_flip(v):
    return lax.ppermute(v, "dp", [(d ^ 1, d) for d in range(lax.axis_size("dp"))])


def rank_flip(v, bit):
    return lax.ppermute(v, "mp", [(m ^ bit, m) for m in range(lax.axis_size("mp"))])


def hops(n):
    order = []
    for k in range(1, n // 2 + 1):
        order.append(k)
        if n - k != k:
            order.append(n - k)
    return order


def pair_sum(a, b):
    return (a.astype(f32) + b.astype(f32)).astype(bf16)


def outer_blocks(own, here, back, ks):
    rows = own.shape[0]
    back = [part[i:i + rows] for part in back for i in range(0, part.shape[0], rows)]
    return [
        (here[i * rows:(i + 1) * rows].astype(f32) + back[i].astype(f32)).astype(bf16) for i in range(len(ks))
    ]


def outer_send(blocks, ks):
    n = lax.axis_size("dp") // 2
    return [outer_from(block, n - k) for block, k in zip(blocks, ks)]


def outer_sum(v):
    bit = 1
    while bit < lax.axis_size("dp") // 2:
        v = v + outer_flip(v, bit)
        bit *= 2
    return v


def mp_sum(v):
    v = v + rank_flip(v, 1)
    return v + rank_flip(v, 2)


def mp_sum_direct(v):
    return (v + rank_flip(v, 1)) + (rank_flip(v, 2) + rank_flip(v, 3))


def mp_reduce(blocks):
    far = blocks[2].astype(f32) + rank_flip(blocks[3], 1).astype(f32)
    near = blocks[0].astype(f32) + rank_flip(blocks[1], 1).astype(f32)
    return near, rank_flip(far.astype(bf16), 2)


def mp_pieces(v):
    far = rank_flip(v, 2)
    return [v, rank_flip(v, 1), far, rank_flip(far, 1)]


def in_rank_order(pieces, rank, axis):
    odd, high = (rank & 1) == 1, (rank & 2) == 2
    join = lambda a, b: jnp.concatenate([a, b], axis=axis)
    low = jnp.where(odd, join(pieces[1], pieces[0]), join(pieces[0], pieces[1]))
    far = jnp.where(odd, join(pieces[3], pieces[2]), join(pieces[2], pieces[3]))
    return jnp.where(high, join(far, low), join(low, far))


def momentum(moment, grad):
    return 0.5 * moment + 0.5 * grad


def advance(weight, moment, grad):
    fresh = momentum(moment, grad)
    return (fresh, weight - LEARN_RATE * fresh - LEARN_RATE * DECAY_RATE * weight)


def body(
    hidden, segments, cotangent, in_weight, in_moment, bc_weight, bc_moment, step_weight, step_moment,
    out_weight, out_moment, conv_table, conv_moment, bc_table, bc_table_moment, head_table, head_moment,
    norm_gain, gain_moment,
):
    size = lax.axis_size("dp")
    ranks = lax.axis_size("mp")
    n = size // 2
    place, rank = lax.axis_index("dp"), lax.axis_index("mp")
    outer, inner = place // 2, place % 2
    rank1 = rank.reshape(1).astype(jnp.int32)
    rows, _, channels = in_weight.shape
    heads = head_table.shape[1]
    tokens, depth = hidden.shape
    share = bc_weight.shape[1] // ranks

    ks = hops(n)
    near_ks, far_k = ks[:-1], ks[-1]

    def members(order):
        return jnp.stack([((outer + k) % n) * 2 + (inner ^ j) for k, j in order]).astype(jnp.int32)

    first = [(0, 0), (0, 1)]
    idx = members(first + [(k, 0) for k in ks] + [(k, 1) for k in ks])
    idx_s = members([(0, 0)] + [(k, 0) for k in ks] + [(0, 1)] + [(k, 1) for k in ks])
    sizes = (1, 1, n - 1, n - 1)
    split_sizes = (1, 1, n - 1, n - 2, 1)
    width = depth // ranks

    set_a, set_b = pack(in_weight, bc_weight, step_weight.T, rank1)
    set_c = out_weight.T.astype(bf16)

    def blocks(own, z, x):
        return [own, x[0]] + [z[k] for k in ks] + [x[k] for k in ks]

    def block(v, i):
        return v[i * rows:(i + 1) * rows]

    def blocks(own, z, x):
        return [own, x[0]] + [z[k] for k in ks] + [x[k] for k in ks]

    def block(v, i):
        return v[i * rows:(i + 1) * rows]

    def outer_all(v, some):
        return {k: outer_from(v, k) for k in some}

    def flip_all(z, some):
        return {k: inner_flip(z[k]) for k in some}

    a_z = outer_all(set_a, ks)
    a_x = {0: inner_flip(set_a)}
    cot_far = rank_flip(cotangent, 2)
    gain_rows = pad_rows(norm_gain[None])
    normed_low, normed_t, inv_rms = prepare(hidden, gain_rows)
    a_x.update(flip_all(a_z, near_ks))
    aux, seg_row = segment_facts(segments)
    head_rows = pad_lanes(pad_rows(head_table))
    facts = (aux, seg_row, pad_rows(conv_table), pad_rows(bc_table), head_rows, head_expand(channels))
    set_a, set_b, set_c, a_z, a_x, cot_far, normed_low, normed_t, inv_rms, facts = fence(
        set_a, set_b, set_c, a_z, a_x, cot_far, normed_low, normed_t, inv_rms, facts
    )

    a_x[far_k] = inner_flip(a_z[far_k])
    b_z = outer_all(set_b, near_ks)
    cot, cot_t = join_columns([cotangent, rank_flip(cotangent, 1), cot_far, rank_flip(cot_far, 1)], rank1)
    set_b, set_c, b_z, a_z, a_x, cot, cot_t, normed_low = fence(set_b, set_c, b_z, a_z, a_x, cot, cot_t, normed_low)

    b_z[far_k] = outer_from(set_b, far_k)
    b_x = {0: inner_flip(set_b), **flip_all(b_z, near_ks[:1])}
    a_blocks = blocks(set_a, a_z, a_x)
    small, bc_share, w_s, w_bct_share = project_small(normed_low, a_blocks, idx, share)
    bc_pieces = mp_pieces(bc_share)
    x_pre, w_a = project(normed_low, a_blocks, idx, channels)
    bc_pieces, x_pre, small, set_c, w_bct_share, w_s = fence(bc_pieces, x_pre, small, set_c, w_bct_share, w_s)
    bc_pre, step_pre = join_small(bc_pieces, small, rank1)
    set_c, b_z, b_x, x_pre, bc_pre, step_pre, w_bct_share = fence(
        set_c, b_z, b_x, x_pre, bc_pre, step_pre, w_bct_share
    )

    c_z = outer_all(set_c, near_ks)
    c_x = {0: inner_flip(set_c)}
    b_x.update(flip_all(b_z, ks[1:]))
    mixed, states = ssd_forward(x_pre, bc_pre, step_pre, *facts)
    mixed, states, b_x, b_z, c_z, c_x, w_bct_share, set_c = fence(mixed, states, b_x, b_z, c_z, c_x, w_bct_share, set_c)

    c_z[far_k] = outer_from(set_c, far_k)
    c_x.update(flip_all(c_z, near_ks))
    gate_pre, square, w_b = gate_forward(normed_low, mixed, blocks(set_b, b_z, b_x), idx)
    mixed, gate_pre, square, w_b, w_bct_share = fence(mixed, gate_pre, square, w_b, w_bct_share)
    conv_rows = facts[2]
    square = mp_sum_direct(square)
    gated_out = gated_norm(gate_pre, mixed, square, conv_rows, channels * ranks)
    gc_own, gc_own1, gc_here, gc_near, gc_far = weight_grad(cot_t, gated_out, idx, split_sizes)
    square, c_z, c_x, gated_out, gc_own, gc_own1, gc_here, gc_near, gc_far, w_bct_share = fence(
        square, c_z, c_x, gated_out, gc_own, gc_own1, gc_here, gc_near, gc_far, w_bct_share
    )
    c_x[far_k] = inner_flip(c_z[far_k])
    c_x, gc_far, gc_near = fence(c_x, gc_far, gc_near)

    gc_far_back, gc_near_back = inner_flip(gc_far), inner_flip(gc_near)
    gout, inner_dot, w_c = grad_gout(cot, gate_pre, mixed, conv_rows, blocks(set_c, c_z, c_x), idx)
    inner_dot = mp_sum_direct(inner_dot)
    gc_far_back, inner_dot, gout, w_c, w_bct_share = fence(gc_far_back, inner_dot, gout, w_c, w_bct_share)
    w_bct = [w_bct_share] + [rank_flip(w_bct_share, r) for r in (1, 2, 3)]
    dmixed, dgate, dgain = gate_backward(gate_pre, gout, mixed, square, inner_dot, conv_rows, channels * ranks)
    gb_own, gb_own1, gb_here, gb_send = weight_grad(normed_t, dgate, idx, sizes)
    partial = out_partial(gated_out, w_c, rank1, ranks)
    gc_near_back, gc_far_back, w_bct, gb_own, gb_own1, gb_here, gb_send, partial, dmixed, dgain = fence(
        gc_near_back, gc_far_back, w_bct, gb_own, gb_own1, gb_here, gb_send, partial, dmixed, dgain
    )
    out_far = pair_sum(partial[2], rank_flip(partial[3], 1))
    out_near = partial[0].astype(f32) + rank_flip(partial[1], 1).astype(f32)
    gc_blocks = [pair_sum(block(gc_here, i), block(gc_near_back, i)) for i in range(n - 2)]
    gc_blocks.append(pair_sum(block(gc_here, n - 2), gc_far_back))
    out_far, out_near, gc_blocks, gb_send, dmixed = fence(out_far, out_near, gc_blocks, gb_send, dmixed)

    c_got = dict(zip(ks, outer_send(gc_blocks, ks)))
    gb_back = inner_flip(gb_send)
    out_got = rank_flip(out_far, 2)
    dx, dbc, dbc_keep, dbc_send, dstep, dstep_t, dconv, dbct_part, dheads = ssd_backward(
        rank1, x_pre, bc_pre, step_pre, *facts, mixed, dmixed, states
    )
    c_got, gb_back, out_got, dx, dbc, dbc_keep, dbc_send, dstep, dstep_t, dconv, dbct_part, dheads, gc_own1, gb_own1 = fence(
        c_got, gb_back, out_got, dx, dbc, dbc_keep, dbc_send, dstep, dstep_t, dconv, dbct_part, dheads, gc_own1, gb_own1
    )

    b_blocks = [pair_sum(block(gb_here, i), block(gb_back, i)) for i in range(n - 1)]
    b_got = outer_send(b_blocks[:-1], near_ks)
    own_got = inner_flip(jnp.concatenate([gc_own1, gb_own1], axis=1))
    dbc_back = rank_flip(dbc_send, 1)
    *term, dgain_norm = normed_term(
        dx, dgate, dstep, dbc, w_a, w_b, w_s, join_rows(w_bct, rank1), hidden, inv_rms, rank1, ranks
    )
    term, dgain_norm, b_got, own_got, far_block, dx, dbc_back = fence(
        term, dgain_norm, b_got, own_got, b_blocks[-1], dx, dbc_back
    )

    b_got = b_got + outer_send([far_block], [far_k])
    far = pair_sum(term[2], rank_flip(term[3], 1))
    near = term[0].astype(f32) + rank_flip(term[1], 1).astype(f32)
    dbc_pair = pair_sum(dbc_keep, dbc_back)
    dbc_got = rank_flip(dbc_pair[share:], 2)
    ga_own, ga_own1, ga_here, ga_near, ga_far = weight_grad(normed_t, dx, idx, split_sizes, us=20)
    shared = jnp.concatenate([dbct_part, dgain_norm], axis=1)
    shared = shared + rank_flip(shared, 1)
    far, near, shared, ga_own, ga_own1, ga_here, ga_near, ga_far, dbc_pair, dbc_got = fence(
        far, near, shared, ga_own, ga_own1, ga_here, ga_near, ga_far, dbc_pair, dbc_got
    )

    got = rank_flip(far, 2)
    shared_got = rank_flip(shared, 2)
    ga_far_back, ga_near_back = inner_flip(ga_far), inner_flip(ga_near)
    dbc_share = pair_sum(dbc_pair[:share], dbc_got)
    dsmall_t = jnp.concatenate([dbc_share, dstep_t, jnp.zeros((LANES - share - 16, tokens), bf16)], axis=0)
    gs_own, gs_here, gs_send = weight_grad(normed_t, dsmall_t, idx_s, (1, n - 1, n), turned=True)
    ga_far_back, b_got, a_far, gs_send, shared, shared_got = fence(
        ga_far_back, b_got, block(ga_here, n - 2), gs_send, shared, shared_got
    )
    a_got = {far_k: outer_from(pair_sum(a_far, ga_far_back), n - far_k)}
    gs_back = inner_flip(gs_send)
    packed = jnp.concatenate([dconv + dgain, dheads, shared + shared_got], axis=1)
    packed_got = inner_flip(packed)
    a_blocks = [pair_sum(block(ga_here, i), block(ga_near_back, i)) for i in range(n - 2)]
    got, near, gs_back, a_blocks, packed, packed_got, ga_own1 = fence(
        got, near, gs_back, a_blocks, packed, packed_got, ga_own1
    )

    mine = norm_backward(near, got, hidden, cot, gain_rows, rank1)
    mine, a_blocks, packed, packed_got, gs_back, ga_own1 = fence(mine, a_blocks, packed, packed_got, gs_back, ga_own1)
    mine_far = rank_flip(mine, 2)
    for k, a_block in zip(near_ks, a_blocks):
        a_got[k] = outer_from(a_block, n - k)
    a_own_got = inner_flip(ga_own1)
    packed = packed + packed_got
    a_got, a_own_got, packed, gs_back = fence(a_got, a_own_got, packed, gs_back)
    s_got = outer_send(outer_blocks(gs_own, gs_here, [gs_back[rows:]], ks), ks)
    packed = outer_sum(packed)
    mine_far, s_got, packed = fence(mine_far, s_got, packed)
    input_grad = join_rows([mine, rank_flip(mine, 1), mine_far, rank_flip(mine_far, 1)], rank1)

    def total(own, own_got, got):
        value = own.astype(f32) + own_got.astype(f32)
        for part in got:
            value = value + part.astype(f32)
        return value

    resid = lax.dynamic_slice_in_dim(hidden, rank * width, width, 1).astype(f32)
    output = (resid + out_near + out_got.astype(f32)).astype(bf16)
    shard_c = total(gc_own, own_got[:, :channels], [c_got[k] for k in ks])
    shard_b = total(gb_own, own_got[:, channels:], b_got)
    shard_a = total(ga_own, a_own_got, [a_got[k] for k in ks])
    shard_s = total(gs_own, gs_back[:rows], s_got)

    cut = channels + LANES
    total_conv = packed[:6, :channels]
    total_head = packed[:3, channels:channels + heads]
    total_bct = packed[:5, cut:cut + 2 * LANES]
    total_gain = packed[0, cut + 2 * LANES:]

    shard_bc = in_rank_order(mp_pieces(shard_s[:, :share]), rank, 1)
    shard_step = shard_s[:, share:share + heads]
    in_m, in_w = advance(in_weight, in_moment, jnp.stack([shard_b, shard_a], axis=1))
    bc_m, bc_w = advance(bc_weight, bc_moment, shard_bc)
    step_m, step_w = advance(step_weight, step_moment, shard_step)
    out_m, out_w = advance(out_weight, out_moment, shard_c.T)
    return (
        output, input_grad, in_m, in_w, bc_m, bc_w, step_m, step_w, out_m, out_w,
        momentum(conv_moment, total_conv),
        momentum(bc_table_moment, total_bct),
        momentum(head_moment, total_head),
        momentum(gain_moment, total_gain),
    )


def solution(mesh):
    placed = (
        P("dp", None),
        P("dp", None),
        P("dp", "mp"),
        P("dp", None, "mp"),
        P("dp", None, "mp"),
        P("dp", None),
        P("dp", None),
        P("dp", "mp"),
        P("dp", "mp"),
        P("mp", "dp"),
        P("mp", "dp"),
        P(None, "mp"),
        P(None, "mp"),
        P(),
        P(),
        P(None, "mp"),
        P(None, "mp"),
        P(),
        P(),
    )
    return jax.shard_map(
        body,
        mesh=mesh,
        in_specs=placed,
        out_specs=(
            P("dp", "mp"),
            P("dp", None),
            P("dp", None, "mp"),
            P("dp", None, "mp"),
            P("dp", None),
            P("dp", None),
            P("dp", "mp"),
            P("dp", "mp"),
            P("mp", "dp"),
            P("mp", "dp"),
            P(None, "mp"),
            P(),
            P(None, "mp"),
            P(),
        ),
        check_vma=False,
    )
```

```python
import functools

import jax
import jax.numpy as jnp
from jax import lax
from jax.experimental import pallas as pl
from jax.experimental.pallas import tpu as pltpu
from jax.sharding import PartitionSpec as P

CHUNK = 128
EPSILON = 1e-05
LEARN_RATE = 0.0001
DECAY_RATE = 0.1
WIDTH = 64
LANES = 128
HALO = 8
bf16 = jnp.bfloat16
f32 = jnp.float32
MIB = 1024 * 1024


def hbm(shape, dtype):
    return pltpu.HBM(shape, dtype)


def from_hbm(v):
    return pltpu.with_memory_space_constraint(v, pltpu.HBM)


def dot_nn(a, b):
    return lax.dot_general(a, b, (((1,), (0,)), ((), ())), preferred_element_type=f32)


def dot_nt(a, b):
    return lax.dot_general(a, b, (((1,), (1,)), ((), ())), preferred_element_type=f32)


def dot_tn(a, b):
    return lax.dot_general(a, b, (((0,), (0,)), ((), ())), preferred_element_type=f32)


def split3(v):
    high = v.astype(bf16)
    rest = v - high.astype(f32)
    mid = rest.astype(bf16)
    low = (rest - mid.astype(f32)).astype(bf16)
    return high, mid, low


def exact_left(ones, v):
    high, mid, low = split3(v)
    return dot_nn(ones, high) + dot_nn(ones, mid) + dot_nn(ones, low)


def spread(v, expand):
    high, mid, low = split3(v)
    return dot_nn(high, expand) + dot_nn(mid, expand) + dot_nn(low, expand)


def gather_heads(v, expand):
    high = v.astype(bf16)
    mid = (v - high.astype(f32)).astype(bf16)
    return dot_nt(high, expand) + dot_nt(mid, expand)


def sigmoid(v):
    return 1.0 / (1.0 + jnp.exp(-v))


def conv_block(scratch, before, now, taps, keep):
    rows = now.shape[0]
    scratch[0:HALO, :] = before
    scratch[HALO:HALO + rows, :] = now
    total = taps[4:5, :] + taps[0:1, :] * now
    for lag in (1, 2, 3):
        moved = scratch[HALO - lag:HALO - lag + rows, :]
        total = total + taps[lag:lag + 1, :] * (moved * keep[:, lag - 1:lag])
    return total


def step_parts(step_pre, heads):
    raw = step_pre + heads[0:1, :]
    steps = jnp.maximum(raw, 0.0) + jnp.log1p(jnp.exp(-jnp.abs(raw)))
    rates = -jnp.exp(heads[1:2, :])
    return raw, steps, rates


def triangle(lower):
    row = lax.broadcasted_iota(jnp.int32, (CHUNK, CHUNK), 0)
    col = lax.broadcasted_iota(jnp.int32, (CHUNK, CHUNK), 1)
    return row >= col if lower else row <= col


def ssd_forward_kernel(
    x_ref, xb_ref, bc_ref, bcb_ref, st_ref, aux_ref, seg_ref, conv_ref, bct_ref, heads_ref, expand_ref,
    mixed_ref, state_ref, state, xs_scr, bc_scr,
):
    chunk = pl.program_id(0)

    @pl.when(chunk == 0)
    def _():
        state[...] = jnp.zeros_like(state)

    channels = x_ref.shape[1]
    aux = aux_ref[...]
    expand = expand_ref[...]
    u = conv_block(xs_scr, xb_ref[...], x_ref[...], conv_ref, aux)
    x_act = u * sigmoid(u)
    ubc = conv_block(bc_scr, bcb_ref[...], bc_ref[...], bct_ref, aux)
    bc_act = (ubc * sigmoid(ubc)).astype(bf16)
    b_mat, c_mat = bc_act[:, :LANES], bc_act[:, LANES:]
    _, steps, rates = step_parts(st_ref[...], heads_ref)
    lower = triangle(True)
    cum = exact_left(lower.astype(bf16), steps * rates)
    cum_t = cum.T
    tail = cum[CHUNK - 1:CHUNK, :]
    entry = jnp.exp(cum) * aux[:, 6:7]
    to_end = jnp.exp(tail - cum) * aux[:, 7:8]
    wide = spread(jnp.concatenate([steps, entry, to_end], axis=0), expand)
    step_e, entry_e, to_end_e = wide[:CHUNK], wide[CHUNK:2 * CHUNK], wide[2 * CHUNK:]
    skip_e = spread(jnp.broadcast_to(heads_ref[2:3, :], (8, LANES)), expand)[0:1, :]
    mask = lower & (aux[:, 8:9] == seg_ref[...])
    scores = jnp.where(mask, dot_nt(c_mat, b_mat), 0.0)
    xs = x_act * step_e
    xs_low = xs.astype(bf16)
    held = state[...]
    held_low = held.astype(bf16)
    state_ref[...] = held_low
    out = dot_nn(c_mat, held_low) * entry_e + skip_e * x_act
    state[...] = held * entry_e[CHUNK - 1:CHUNK, :] + dot_tn(b_mat, (xs * to_end_e).astype(bf16))
    first = lax.broadcasted_iota(jnp.int32, (CHUNK, LANES), 1) < WIDTH
    zero = jnp.zeros((CHUNK, LANES), bf16)
    for pair in range(channels // LANES):
        span = slice(pair * LANES, (pair + 1) * LANES)
        parts = []
        for head in (2 * pair, 2 * pair + 1):
            diff = cum[:, head:head + 1] - cum_t[head:head + 1, :]
            parts.append((scores * jnp.exp(jnp.minimum(diff, 0.0))).astype(bf16))
        own = xs_low[:, span]
        both = jnp.concatenate([jnp.where(first, own, zero), jnp.where(first, zero, own)], axis=0)
        mixed_ref[:, span] = out[:, span] + dot_nn(jnp.concatenate(parts, axis=1), both)


def ssd_backward_kernel(
    rank_ref, x_ref, xb_ref, bc_ref, bcb_ref, st_ref, aux_ref, seg_ref, conv_ref, bct_ref, heads_ref, expand_ref,
    mixed_ref, dy_ref, state_ref,
    dx_ref, dbc_ref, keep_ref, send_ref, dst_ref, dst_t_ref, dconv_ref, dbct_ref, dheads_ref,
    dstate, xs_scr, bc_scr, du_scr, dubc_scr, share_scr,
):
    @pl.when(pl.program_id(0) == 0)
    def _():
        for ref in (dstate, du_scr, dubc_scr, dconv_ref, dbct_ref, dheads_ref):
            ref[...] = jnp.zeros_like(ref)

    channels = x_ref.shape[1]
    aux = aux_ref[...]
    expand = expand_ref[...]
    x_now, bc_now = x_ref[...], bc_ref[...]
    u = conv_block(xs_scr, xb_ref[...], x_now, conv_ref, aux)
    sg = sigmoid(u)
    x_act = u * sg
    ubc = conv_block(bc_scr, bcb_ref[...], bc_now, bct_ref, aux)
    sgbc = sigmoid(ubc)
    bc_act = (ubc * sgbc).astype(bf16)
    b_mat, c_mat = bc_act[:, :LANES], bc_act[:, LANES:]
    raw, steps, rates = step_parts(st_ref[...], heads_ref)
    lower = triangle(True)
    cum = exact_left(lower.astype(bf16), steps * rates)
    cum_t = cum.T
    tail = cum[CHUNK - 1:CHUNK, :]
    entry = jnp.exp(cum) * aux[:, 6:7]
    to_end = jnp.exp(tail - cum) * aux[:, 7:8]
    wide = spread(jnp.concatenate([steps, entry, to_end], axis=0), expand)
    step_e, entry_e, to_end_e = wide[:CHUNK], wide[CHUNK:2 * CHUNK], wide[2 * CHUNK:]
    skip_e = spread(jnp.broadcast_to(heads_ref[2:3, :], (8, LANES)), expand)[0:1, :]
    upper = triangle(False)
    mask = upper & (aux[:, 8:9] == seg_ref[...])
    scores = jnp.where(mask, dot_nt(b_mat, c_mat), 0.0)
    xs = x_act * step_e
    xs_low = xs.astype(bf16)
    dy_low = dy_ref[...]
    dy = dy_low.astype(f32)
    held_low = state_ref[...]
    grad = dstate[...]
    grad_low = grad.astype(bf16)
    entry_dy = (entry_e * dy).astype(bf16)
    kept_e = entry_e[CHUNK - 1:CHUNK, :]
    dstate[...] = grad * kept_e + dot_tn(c_mat, entry_dy)
    dc = dot_nt(entry_dy, held_low)
    db = dot_nt((xs * to_end_e).astype(bf16), grad_low)
    q_state = dot_nn(b_mat, grad_low) * to_end_e
    first = lax.broadcasted_iota(jnp.int32, (CHUNK, LANES), 1) < WIDTH
    zero = jnp.zeros((CHUNK, LANES), bf16)
    dscores = jnp.zeros((CHUNK, CHUNK), f32)
    q_parts = []
    for pair in range(channels // LANES):
        span = slice(pair * LANES, (pair + 1) * LANES)
        own = dy_low[:, span]
        both = jnp.concatenate([jnp.where(first, own, zero), jnp.where(first, zero, own)], axis=0)
        dweights = dot_nt(xs_low[:, span], both)
        parts = []
        for i, head in enumerate((2 * pair, 2 * pair + 1)):
            diff = cum_t[head:head + 1, :] - cum[:, head:head + 1]
            decay = jnp.exp(jnp.minimum(diff, 0.0))
            parts.append((scores * decay).astype(bf16))
            dscores = dscores + dweights[:, i * LANES:(i + 1) * LANES] * decay
        q_parts.append(dot_nn(jnp.concatenate(parts, axis=1), both))
    q = jnp.concatenate(q_parts, axis=1) + q_state
    dscores_low = jnp.where(mask, dscores, 0.0).astype(bf16)
    db = db + dot_nn(dscores_low, c_mat)
    dc = dc + dot_tn(dscores_low, b_mat)
    xs_round = xs_low.astype(f32)
    rows = gather_heads(
        jnp.concatenate(
            [
                dy * (mixed_ref[...] - skip_e * x_act) - xs_round * q,
                x_act * q,
            ],
            axis=0,
        ),
        expand,
    )
    flow, dstep = rows[:CHUNK], rows[CHUNK:]
    sums = jnp.concatenate(
        [
            jnp.sum(xs_round * q_state + kept_e * (held_low.astype(f32) * grad), axis=0, keepdims=True),
            jnp.sum(dy * x_act, axis=0, keepdims=True),
            jnp.zeros((6, channels), f32),
        ],
        axis=0,
    )
    sums = gather_heads(sums, expand)
    dlog = exact_left(upper.astype(bf16), flow) + sums[0:1, :]
    dstep = dstep + rates * dlog
    draw = dstep * sigmoid(raw)
    dst_ref[...] = pltpu.roll(draw, WIDTH, 1).astype(bf16)
    dst_t_ref[...] = draw.T[0:16, :].astype(bf16)
    dheads_ref[0:1, :] += jnp.sum(draw, axis=0, keepdims=True)
    dheads_ref[1:2, :] += rates * jnp.sum(dlog * steps, axis=0, keepdims=True)
    dheads_ref[2:3, :] += sums[1:2, :]

    def conv_back(scratch, du, now, taps, dtaps):
        scratch[0:CHUNK, :] = du
        total = taps[0:1, :] * du
        dtaps[0:1, :] += jnp.sum(now * du, axis=0, keepdims=True)
        dtaps[4:5, :] += jnp.sum(du, axis=0, keepdims=True)
        for lag in (1, 2, 3):
            moved = scratch[lag:lag + CHUNK, :] * aux[:, 2 + lag:3 + lag]
            total = total + taps[lag:lag + 1, :] * moved
            dtaps[lag:lag + 1, :] += jnp.sum(now * moved, axis=0, keepdims=True)
        scratch[CHUNK:CHUNK + HALO, :] = du[0:HALO, :]
        return total

    du = (skip_e * dy + step_e * q) * (sg * (1.0 + u * (1.0 - sg)))
    dx_ref[...] = conv_back(du_scr, du, x_now, conv_ref, dconv_ref).astype(dx_ref.dtype)
    dubc = jnp.concatenate([db, dc], axis=1) * (sgbc * (1.0 + ubc * (1.0 - sgbc)))
    dbc = conv_back(dubc_scr, dubc, bc_now, bct_ref, dbct_ref).astype(bf16)
    dbc_ref[...] = dbc
    share = 2 * LANES // 4
    turned = dbc.T
    for member in range(4):
        apart = member ^ rank_ref[0]
        start = pl.multiple_of((apart & 1) * 2 * share + (apart >> 1) * share, share)
        share_scr[pl.ds(start, share), :] = turned[member * share:(member + 1) * share, :]
    keep_ref[...] = share_scr[0:2 * share, :]
    send_ref[...] = share_scr[2 * share:4 * share, :]


def common_specs(place, channels):
    before = lambda i: (jnp.maximum(place(i) * (CHUNK // HALO) - 1, 0), 0)
    now = lambda i: (place(i), 0)
    whole = lambda i: (0, 0)
    return [
        pl.BlockSpec((CHUNK, channels), now),
        pl.BlockSpec((HALO, channels), before),
        pl.BlockSpec((CHUNK, 2 * LANES), now),
        pl.BlockSpec((HALO, 2 * LANES), before),
        pl.BlockSpec((CHUNK, LANES), now),
        pl.BlockSpec((CHUNK, 16), now),
        pl.BlockSpec((1, CHUNK), lambda i: (0, place(i))),
        pl.BlockSpec((8, channels), whole),
        pl.BlockSpec((8, 2 * LANES), whole),
        pl.BlockSpec((8, LANES), whole),
        pl.BlockSpec((LANES, channels), whole),
    ]


def ssd_forward(x_pre, bc_pre, step_pre, aux, seg_row, conv_rows, bc_rows, head_rows, expand):
    tokens, channels = x_pre.shape
    count = tokens // CHUNK
    now = lambda i: (i, 0)
    return pl.pallas_call(
        ssd_forward_kernel,
        grid=(count,),
        in_specs=common_specs(lambda i: i, channels),
        out_specs=[
            pl.BlockSpec((CHUNK, channels), now),
            pl.BlockSpec((None, LANES, channels), lambda i: (i, 0, 0)),
        ],
        out_shape=[
            hbm((tokens, channels), f32),
            hbm((count, LANES, channels), bf16),
        ],
        scratch_shapes=[
            pltpu.VMEM((LANES, channels), f32),
            pltpu.VMEM((HALO + CHUNK, channels), f32),
            pltpu.VMEM((HALO + CHUNK, 2 * LANES), f32),
        ],
        compiler_params=pltpu.CompilerParams(vmem_limit_bytes=14 * MIB),
        cost_estimate=pl.CostEstimate(flops=14 * 10**9, bytes_accessed=40 * 10**6, transcendentals=0),
        name="ssd_forward",
    )(
        from_hbm(x_pre), from_hbm(x_pre), bc_pre, bc_pre, step_pre, aux, seg_row, conv_rows, bc_rows, head_rows, expand
    )


def ssd_backward(rank, x_pre, bc_pre, step_pre, aux, seg_row, conv_rows, bc_rows, head_rows, expand, mixed, dy, states):
    tokens, channels = x_pre.shape
    count = tokens // CHUNK
    place = lambda i: count - 1 - i
    now = lambda i: (place(i), 0)
    whole = lambda i: (0, 0)
    sums = [
        jax.ShapeDtypeStruct((8, channels), f32),
        jax.ShapeDtypeStruct((8, 2 * LANES), f32),
        jax.ShapeDtypeStruct((8, LANES), f32),
    ]
    return pl.pallas_call(
        ssd_backward_kernel,
        grid=(count,),
        in_specs=[pl.BlockSpec(memory_space=pltpu.SMEM)] + common_specs(place, channels) + [
            pl.BlockSpec((CHUNK, channels), now),
            pl.BlockSpec((CHUNK, channels), now),
            pl.BlockSpec((None, LANES, channels), lambda i: (place(i), 0, 0)),
        ],
        out_specs=[
            pl.BlockSpec((CHUNK, channels), now),
            pl.BlockSpec((CHUNK, 2 * LANES), now),
            pl.BlockSpec((LANES, CHUNK), lambda i: (0, place(i))),
            pl.BlockSpec((LANES, CHUNK), lambda i: (0, place(i))),
            pl.BlockSpec((CHUNK, LANES), now),
            pl.BlockSpec((16, CHUNK), lambda i: (0, place(i))),
        ] + [pl.BlockSpec(v.shape, whole) for v in sums],
        out_shape=[
            hbm((tokens, channels), bf16),
            hbm((tokens, 2 * LANES), bf16),
            hbm((LANES, tokens), bf16),
            hbm((LANES, tokens), bf16),
            hbm((tokens, LANES), bf16),
            hbm((16, tokens), bf16),
        ] + sums,
        scratch_shapes=[
            pltpu.VMEM((LANES, channels), f32),
            pltpu.VMEM((HALO + CHUNK, channels), f32),
            pltpu.VMEM((HALO + CHUNK, 2 * LANES), f32),
            pltpu.VMEM((HALO + CHUNK, channels), f32),
            pltpu.VMEM((HALO + CHUNK, 2 * LANES), f32),
            pltpu.VMEM((2 * LANES, CHUNK), bf16),
        ],
        compiler_params=pltpu.CompilerParams(vmem_limit_bytes=16 * MIB),
        cost_estimate=pl.CostEstimate(flops=28 * 10**9, bytes_accessed=40 * 10**6, transcendentals=0),
        name="ssd_backward",
    )(
        rank, from_hbm(x_pre), from_hbm(x_pre), bc_pre, bc_pre, step_pre, aux, seg_row, conv_rows, bc_rows, head_rows,
        expand, from_hbm(mixed), dy, from_hbm(states),
    )


def segment_facts(seg):
    row = seg[0]
    tokens = row.shape[0]
    cols = []
    for lag in (1, 2, 3):
        cols.append(jnp.pad(row[:-lag], (lag, 0), constant_values=-1) == row)
    for lag in (1, 2, 3):
        cols.append(jnp.pad(row[lag:], (0, lag), constant_values=-1) == row)
    blocks = row.reshape(tokens // CHUNK, CHUNK)
    ends = blocks[:, -1:]
    before = jnp.concatenate([jnp.full((1, 1), -1, row.dtype), ends[:-1]], axis=0)
    cols.append((blocks == before).reshape(-1))
    cols.append((blocks == ends).reshape(-1))
    cols.append(row)
    facts = jnp.stack([c.astype(f32) for c in cols], axis=1)
    return jnp.pad(facts, ((0, 0), (0, 16 - facts.shape[1]))), seg.astype(f32)


def pad_rows(table, rows=8):
    return jnp.pad(table, ((0, rows - table.shape[0]), (0, 0)))


def pad_lanes(table, lanes=LANES):
    return jnp.pad(table, ((0, 0), (0, lanes - table.shape[1])))


def head_expand(channels):
    head = jnp.arange(LANES)[:, None]
    return (head == (jnp.arange(channels) // WIDTH)[None, :]).astype(bf16)


TILE = 256
TILE_D = 384


def fill(dest, pieces, idx_ref):
    rows = pieces[0].shape[0]
    s = 0
    for piece in pieces:
        for b in range(piece.shape[0] // rows):
            start = pl.multiple_of(idx_ref[s] * rows, rows)
            dest[pl.ds(start, rows), :] = piece[b * rows:(b + 1) * rows, :]
            s += 1


def params(mib=18):
    return pltpu.CompilerParams(vmem_limit_bytes=mib * MIB)


def cost(us):
    return pl.CostEstimate(flops=int(us * 10**9), bytes_accessed=int(us * 2 * 10**6), transcendentals=0)


def prepare_kernel(hidden_ref, gain_ref, low_ref, low_t_ref, inv_ref):
    inputs = hidden_ref[...].astype(f32)
    inv_rms = lax.rsqrt(jnp.mean(inputs * inputs, axis=1, keepdims=True) + EPSILON)
    low = (inputs * inv_rms * gain_ref[0:1, :]).astype(bf16)
    low_ref[...] = low
    low_t_ref[...] = low.T
    inv_ref[...] = column_to_row(inv_rms)


def prepare(hidden, gain_rows):
    tokens, depth = hidden.shape
    block = pl.BlockSpec((TILE, depth), lambda i: (i, 0))
    return pl.pallas_call(
        prepare_kernel,
        grid=(tokens // TILE,),
        in_specs=[block, pl.BlockSpec((8, depth), lambda i: (0, 0))],
        out_specs=[block, pl.BlockSpec((depth, TILE), lambda i: (0, i)), pl.BlockSpec((8, TILE), lambda i: (0, i))],
        out_shape=[
            hbm((tokens, depth), bf16),
            hbm((depth, tokens), bf16),
            jax.ShapeDtypeStruct((8, tokens), f32),
        ],
        compiler_params=params(),
        cost_estimate=cost(12),
        name="prepare",
    )(hidden, gain_rows)


def pack_kernel(rank_ref, in_ref, bc_ref, step_ref, a_ref, b_ref, scratch):
    channels = b_ref.shape[1]
    rows, width = bc_ref.shape
    share = width // 4
    heads = step_ref.shape[0]
    b_ref[...] = in_ref[:, 0, :].astype(bf16)
    a_ref[:, :channels] = in_ref[:, 1, :].astype(bf16)
    scratch[...] = jnp.zeros_like(scratch)
    scratch[share:share + heads, 0:rows] = step_ref[...]
    step = scratch[...].T[0:rows, :]
    own = bc_ref[:, 0:LANES]
    for member in range(1, 4):
        moved = pltpu.roll(bc_ref[...], width - member * share, 1)[:, 0:LANES]
        own = jnp.where(rank_ref[0] == member, moved, own)
    lane = lax.broadcasted_iota(jnp.int32, (rows, LANES), 1)
    a_ref[:, channels:] = jnp.where(lane < share, own, step).astype(bf16)


def pack(in_weight, bc_weight, step_t, rank):
    rows, _, channels = in_weight.shape
    vmem = pl.BlockSpec(memory_space=pltpu.VMEM)
    return pl.pallas_call(
        pack_kernel,
        in_specs=[pl.BlockSpec(memory_space=pltpu.SMEM), vmem, vmem, vmem],
        out_specs=[vmem, vmem],
        out_shape=[
            jax.ShapeDtypeStruct((rows, channels + LANES), bf16),
            hbm((rows, channels), bf16),
        ],
        scratch_shapes=[pltpu.VMEM((LANES, 2 * LANES), f32)],
        compiler_params=params(),
        cost_estimate=cost(2),
        name="pack",
    )(rank, from_hbm(in_weight), from_hbm(bc_weight), step_t)


def columns_kernel(rank_ref, *refs, count):
    pieces, (full_ref, full_t_ref) = refs[:count], refs[count:]
    for r, piece in enumerate(pieces):
        width = piece.shape[1]
        start = pl.multiple_of((rank_ref[0] ^ r) * width, LANES)
        value = piece[...]
        full_ref[:, pl.ds(start, width)] = value
        full_t_ref[pl.ds(start, width), :] = value.T


def join_columns(pieces, rank):
    tokens, width = pieces[0].shape
    depth = width * len(pieces)
    return pl.pallas_call(
        functools.partial(columns_kernel, count=len(pieces)),
        grid=(tokens // TILE,),
        in_specs=[pl.BlockSpec(memory_space=pltpu.SMEM)] + [pl.BlockSpec((TILE, width), lambda i: (i, 0))] * len(pieces),
        out_specs=[pl.BlockSpec((TILE, depth), lambda i: (i, 0)), pl.BlockSpec((depth, TILE), lambda i: (0, i))],
        out_shape=[jax.ShapeDtypeStruct((tokens, depth), bf16), jax.ShapeDtypeStruct((depth, tokens), bf16)],
        compiler_params=params(),
        cost_estimate=cost(12),
        name="join_columns",
    )(rank, *pieces)


def rows_kernel(rank_ref, *refs, count):
    pieces, full_ref = refs[:count], refs[count]
    for r, piece in enumerate(pieces):
        rows = piece.shape[0]
        full_ref[pl.ds(pl.multiple_of((rank_ref[0] ^ r) * rows, rows), rows), :] = piece[...]


def join_rows(pieces, rank):
    rows, width = pieces[0].shape
    shape = (rows * len(pieces), width)
    return pl.pallas_call(
        functools.partial(rows_kernel, count=len(pieces)),
        in_specs=[pl.BlockSpec(memory_space=pltpu.SMEM)] + [pl.BlockSpec(memory_space=pltpu.VMEM)] * len(pieces),
        out_specs=pl.BlockSpec(memory_space=pltpu.VMEM),
        out_shape=jax.ShapeDtypeStruct(shape, pieces[0].dtype),
        compiler_params=params(),
        cost_estimate=cost(0.1),
        name="join_rows",
    )(rank, *pieces)


def small_kernel(rank_ref, *refs, count):
    pieces, (small_ref, bc_ref, step_ref, scratch) = refs[:count], refs[count:]
    share = pieces[0].shape[0]
    for r, piece in enumerate(pieces):
        scratch[pl.ds(pl.multiple_of((rank_ref[0] ^ r) * share, share), share), :] = piece[...].astype(f32)
    bc_ref[...] = scratch[...].T
    turned = small_ref[...].T
    lane = lax.broadcasted_iota(jnp.int32, turned.shape, 1)
    step_ref[...] = jnp.where(lane < LANES - share, pltpu.roll(turned, LANES - share, 1), 0.0)


def join_small(pieces, small, rank):
    share, tokens = pieces[0].shape
    width = share * len(pieces)
    return pl.pallas_call(
        functools.partial(small_kernel, count=len(pieces)),
        grid=(tokens // TILE,),
        in_specs=[pl.BlockSpec(memory_space=pltpu.SMEM)]
        + [pl.BlockSpec((share, TILE), lambda i: (0, i))] * len(pieces)
        + [pl.BlockSpec((LANES, TILE), lambda i: (0, i))],
        out_specs=[pl.BlockSpec((TILE, width), lambda i: (i, 0)), pl.BlockSpec((TILE, LANES), lambda i: (i, 0))],
        out_shape=[jax.ShapeDtypeStruct((tokens, width), f32), jax.ShapeDtypeStruct((tokens, LANES), f32)],
        scratch_shapes=[pltpu.VMEM((width, TILE), f32)],
        compiler_params=params(),
        cost_estimate=cost(0.1),
        name="join_small",
    )(rank, *pieces, small)


def project_small_kernel(idx_ref, lhs_ref, *refs, count):
    pieces, (small_ref, share_ref, w_ref, wt_ref) = refs[:count], refs[count:]

    @pl.when(pl.program_id(0) == 0)
    def _():
        fill(w_ref, pieces, idx_ref)
        wt_ref[...] = w_ref[...].T[0:wt_ref.shape[0], :]

    small = dot_nn(lhs_ref[...], w_ref[...]).T
    small_ref[...] = small
    share_ref[...] = small[0:share_ref.shape[0], :].astype(bf16)


def project_small(lhs, pieces, idx, share):
    tokens, depth = lhs.shape
    count, last = len(pieces), pieces[0].shape[1] // LANES - 1
    whole = lambda i: (0, 0)
    return pl.pallas_call(
        functools.partial(project_small_kernel, count=count),
        grid=(tokens // TILE,),
        in_specs=[pl.BlockSpec(memory_space=pltpu.SMEM), pl.BlockSpec((TILE, depth), lambda i: (i, 0))]
        + [pl.BlockSpec((p.shape[0], LANES), lambda i: (0, last)) for p in pieces],
        out_specs=[
            pl.BlockSpec((LANES, TILE), lambda i: (0, i)),
            pl.BlockSpec((share, TILE), lambda i: (0, i)),
            pl.BlockSpec((depth, LANES), whole),
            pl.BlockSpec((share, depth), whole),
        ],
        out_shape=[
            jax.ShapeDtypeStruct((LANES, tokens), f32),
            jax.ShapeDtypeStruct((share, tokens), bf16),
            jax.ShapeDtypeStruct((depth, LANES), bf16),
            jax.ShapeDtypeStruct((share, depth), bf16),
        ],
        compiler_params=params(),
        cost_estimate=cost(20),
        name="project_small",
    )(idx, lhs, *pieces)


def project_kernel(idx_ref, lhs_ref, *refs, count):
    pieces, (x_ref, w_ref) = refs[:count], refs[count:]

    @pl.when(pl.program_id(0) == 0)
    def _():
        fill(w_ref, pieces, idx_ref)

    x_ref[...] = dot_nn(lhs_ref[...], w_ref[...])


def project(lhs, pieces, idx, channels):
    tokens, depth = lhs.shape
    whole = lambda i: (0, 0)
    return pl.pallas_call(
        functools.partial(project_kernel, count=len(pieces)),
        grid=(tokens // TILE,),
        in_specs=[pl.BlockSpec(memory_space=pltpu.SMEM), pl.BlockSpec((TILE, depth), lambda i: (i, 0))]
        + [pl.BlockSpec((p.shape[0], channels), whole) for p in pieces],
        out_specs=[pl.BlockSpec((TILE, channels), lambda i: (i, 0)), pl.BlockSpec((depth, channels), whole)],
        out_shape=[
            hbm((tokens, channels), f32),
            hbm((depth, channels), bf16),
        ],
        compiler_params=params(),
        cost_estimate=cost(0.1),
        name="project",
    )(idx, lhs, *pieces)


def column_to_row(col):
    return jnp.broadcast_to(col, (col.shape[0], LANES)).T[0:8, :]


def row_to_column(row):
    return jnp.broadcast_to(row, (LANES, row.shape[1])).T[:, 0:1]


def gate_kernel(idx_ref, lhs_ref, mixed_ref, *refs, count):
    pieces, (gate_ref, sums_ref, w_ref) = refs[:count], refs[count:]

    @pl.when(pl.program_id(0) == 0)
    def _():
        fill(w_ref, pieces, idx_ref)

    gate = dot_nn(lhs_ref[...], w_ref[...])
    gate_ref[...] = gate
    gated = mixed_ref[...] * (gate * sigmoid(gate))
    sums_ref[...] = column_to_row(jnp.sum(gated * gated, axis=1, keepdims=True))


def gate_forward(lhs, mixed, pieces, idx):
    tokens, depth = lhs.shape
    channels = mixed.shape[1]
    whole = lambda i: (0, 0)
    now = lambda i: (i, 0)
    return pl.pallas_call(
        functools.partial(gate_kernel, count=len(pieces)),
        grid=(tokens // TILE,),
        in_specs=[
            pl.BlockSpec(memory_space=pltpu.SMEM),
            pl.BlockSpec((TILE, depth), now),
            pl.BlockSpec((TILE, channels), now),
        ]
        + [pl.BlockSpec(p.shape, whole) for p in pieces],
        out_specs=[
            pl.BlockSpec((TILE, channels), now),
            pl.BlockSpec((8, TILE), lambda i: (0, i)),
            pl.BlockSpec((depth, channels), whole),
        ],
        out_shape=[
            jax.ShapeDtypeStruct((tokens, channels), f32),
            jax.ShapeDtypeStruct((8, tokens), f32),
            hbm((depth, channels), bf16),
        ],
        compiler_params=params(),
        cost_estimate=cost(0.1),
        name="gate_forward",
    )(idx, lhs, from_hbm(mixed), *pieces)


def gated_kernel(gate_ref, mixed_ref, square_ref, conv_ref, out_ref, *, inner_total):
    gate = gate_ref[...]
    scale = lax.rsqrt(row_to_column(square_ref[0:1, :]) / inner_total + EPSILON)
    gated = mixed_ref[...] * (gate * sigmoid(gate))
    out_ref[...] = (gated * scale * conv_ref[5:6, :]).astype(bf16)


def gated_norm(gate, mixed, square, conv_rows, inner_total):
    tokens, channels = gate.shape
    block = pl.BlockSpec((TILE, channels), lambda i: (i, 0))
    return pl.pallas_call(
        functools.partial(gated_kernel, inner_total=inner_total),
        grid=(tokens // TILE,),
        in_specs=[block, block, pl.BlockSpec((8, TILE), lambda i: (0, i)), pl.BlockSpec((8, channels), lambda i: (0, 0))],
        out_specs=block,
        out_shape=jax.ShapeDtypeStruct((tokens, channels), bf16),
        compiler_params=params(),
        cost_estimate=cost(0.1),
        name="gated_norm",
    )(gate, mixed, square, conv_rows)


def gout_kernel(idx_ref, cot_ref, gate_ref, mixed_ref, conv_ref, *refs, count):
    pieces, (gout_ref, sums_ref, w_ref) = refs[:count], refs[count:]

    @pl.when(pl.program_id(0) == 0)
    def _():
        fill(w_ref, pieces, idx_ref)

    gout = dot_nn(cot_ref[...], w_ref[...])
    gout_ref[...] = gout
    gate = gate_ref[...]
    gated = mixed_ref[...] * (gate * sigmoid(gate))
    sums_ref[...] = column_to_row(jnp.sum(gout * conv_ref[5:6, :] * gated, axis=1, keepdims=True))


def grad_gout(cot, gate, mixed, conv_rows, pieces, idx):
    tokens, depth = cot.shape
    channels = mixed.shape[1]
    whole = lambda i: (0, 0)
    now = lambda i: (i, 0)
    return pl.pallas_call(
        functools.partial(gout_kernel, count=len(pieces)),
        grid=(tokens // TILE,),
        in_specs=[
            pl.BlockSpec(memory_space=pltpu.SMEM),
            pl.BlockSpec((TILE, depth), now),
            pl.BlockSpec((TILE, channels), now),
            pl.BlockSpec((TILE, channels), now),
            pl.BlockSpec((8, channels), whole),
        ]
        + [pl.BlockSpec(p.shape, whole) for p in pieces],
        out_specs=[
            pl.BlockSpec((TILE, channels), now),
            pl.BlockSpec((8, TILE), lambda i: (0, i)),
            pl.BlockSpec((depth, channels), whole),
        ],
        out_shape=[
            jax.ShapeDtypeStruct((tokens, channels), f32),
            jax.ShapeDtypeStruct((8, tokens), f32),
            jax.ShapeDtypeStruct((depth, channels), bf16),
        ],
        compiler_params=params(),
        cost_estimate=cost(20),
        name="grad_gout",
    )(idx, cot, gate, mixed, conv_rows, *pieces)


def gate_back_kernel(gate_ref, gout_ref, mixed_ref, square_ref, inner_ref, conv_ref, dmixed_ref, dgate_ref, dgain_ref, *, inner_total):
    gate, gout, mixed = gate_ref[...], gout_ref[...], mixed_ref[...]
    gain = conv_ref[5:6, :]
    square, inner = row_to_column(square_ref[0:1, :]), row_to_column(inner_ref[0:1, :])
    scale = lax.rsqrt(square / inner_total + EPSILON)
    sg = sigmoid(gate)
    act = gate * sg
    gated = mixed * act
    dgated = scale * (gain * gout) - gated * (scale * scale * scale * inner / inner_total)
    dmixed_ref[...] = (dgated * act).astype(bf16)
    dgate_ref[...] = (dgated * mixed * sg * (1.0 + gate * (1.0 - sg))).astype(bf16)

    @pl.when(pl.program_id(0) == 0)
    def _():
        dgain_ref[...] = jnp.zeros_like(dgain_ref)

    dgain_ref[5:6, :] += jnp.sum(gout * gated * scale, axis=0, keepdims=True)


def gate_backward(gate, gout, mixed, square, inner, conv_rows, inner_total):
    tokens, channels = gate.shape
    whole = lambda i: (0, 0)
    block = pl.BlockSpec((TILE, channels), lambda i: (i, 0))
    row = pl.BlockSpec((8, TILE), lambda i: (0, i))
    return pl.pallas_call(
        functools.partial(gate_back_kernel, inner_total=inner_total),
        grid=(tokens // TILE,),
        in_specs=[block, block, block, row, row, pl.BlockSpec((8, channels), whole)],
        out_specs=[block, block, pl.BlockSpec((8, channels), whole)],
        out_shape=[
            jax.ShapeDtypeStruct((tokens, channels), bf16),
            jax.ShapeDtypeStruct((tokens, channels), bf16),
            jax.ShapeDtypeStruct((8, channels), f32),
        ],
        compiler_params=params(),
        cost_estimate=cost(0.1),
        name="gate_backward",
    )(from_hbm(gate), from_hbm(gout), from_hbm(mixed), square, inner, conv_rows)


def weight_grad_kernel(idx_ref, lhs_ref, rhs_ref, *refs, rows, turned):
    outs, scratch = refs[:-1], refs[-1]
    at = pl.program_id(0)
    scratch[pl.ds(pl.multiple_of(at * TILE_D, TILE_D), TILE_D), :] = (dot_nt if turned else dot_nn)(
        lhs_ref[...], rhs_ref[...]
    ).astype(bf16)

    @pl.when(at == pl.num_programs(0) - 1)
    def _():
        s = 0
        for out in outs:
            for b in range(out.shape[0] // rows):
                start = pl.multiple_of(idx_ref[s] * rows, rows)
                out[b * rows:(b + 1) * rows, :] = scratch[pl.ds(start, rows), :]
                s += 1


def weight_grad(lhs_t, rhs, idx, sizes, us=0.1, turned=False):
    depth, tokens = lhs_t.shape
    width = rhs.shape[0 if turned else 1]
    rows = depth // idx.shape[0]
    whole = lambda i: (0, 0)
    return pl.pallas_call(
        functools.partial(weight_grad_kernel, rows=rows, turned=turned),
        grid=(depth // TILE_D,),
        in_specs=[
            pl.BlockSpec(memory_space=pltpu.SMEM),
            pl.BlockSpec((TILE_D, tokens), lambda i: (i, 0)),
            pl.BlockSpec(rhs.shape, whole),
        ],
        out_specs=[pl.BlockSpec((size * rows, width), whole) for size in sizes],
        out_shape=[hbm((size * rows, width), bf16) for size in sizes],
        scratch_shapes=[pltpu.VMEM((depth, width), bf16)],
        compiler_params=params(),
        cost_estimate=cost(us),
        name="weight_grad",
    )(idx, lhs_t, rhs)


def out_kernel(rank_ref, lhs_ref, w_ref, *outs):
    product = dot_nt(lhs_ref[...], w_ref[...]).astype(bf16)
    for r, out in enumerate(outs):
        @pl.when(pl.program_id(0) == r)
        def _():
            out[...] = product


def out_partial(gated_out, w_out, rank, ranks):
    tokens, channels = gated_out.shape
    depth = w_out.shape[0]
    width = depth // ranks
    whole = lambda i, rank_ref: (0, 0)
    return pl.pallas_call(
        out_kernel,
        grid_spec=pltpu.PrefetchScalarGridSpec(
            num_scalar_prefetch=1,
            grid=(ranks,),
            in_specs=[
                pl.BlockSpec((tokens, channels), whole),
                pl.BlockSpec((width, channels), lambda i, rank_ref: (i ^ rank_ref[0], 0)),
            ],
            out_specs=[pl.BlockSpec((tokens, width), whole)] * ranks,
        ),
        out_shape=[hbm((tokens, width), bf16)] * ranks,
        compiler_params=params(),
        cost_estimate=cost(0.1),
        name="out_partial",
    )(rank, gated_out, w_out)


def term_kernel(rank_ref, gx_ref, wx_ref, gg_ref, wg_ref, gs_ref, ws_ref, gb_ref, wbt_ref, hidden_ref, inv_ref, *refs, apart):
    dgain_ref, outs = refs[-1], refs[:-1]
    gain = None
    for r, out in zip(apart, outs):
        rows = out.shape[0]
        span = pl.ds(pl.multiple_of((rank_ref[0] ^ r) * rows, rows), rows)
        total = dot_nt(gx_ref[span, :], wx_ref[...]) + dot_nt(gg_ref[span, :], wg_ref[...])
        total = total + dot_nt(gs_ref[span, :], ws_ref[...]) + dot_nn(gb_ref[span, :], wbt_ref[...])
        out[...] = total.astype(bf16)
        normed = hidden_ref[span, :].astype(f32) * row_to_column(inv_ref[0:1, span])
        own = jnp.sum(total * normed, axis=0, keepdims=True)
        gain = own if gain is None else gain + own
    dgain_ref[...] = jnp.broadcast_to(gain, dgain_ref.shape)


def normed_term(dx, dgate, dstep, dbc, w_a, w_b, w_s, w_bct, hidden, inv_rms, rank, ranks, apart):
    tokens, channels = dx.shape
    depth = w_a.shape[0]
    rows = tokens // ranks
    whole = lambda i: (0, 0)
    return pl.pallas_call(
        functools.partial(term_kernel, apart=apart),
        grid=(depth // TILE_D,),
        in_specs=[
            pl.BlockSpec(memory_space=pltpu.SMEM),
            pl.BlockSpec(dx.shape, whole),
            pl.BlockSpec((TILE_D, channels), lambda i: (i, 0)),
            pl.BlockSpec(dgate.shape, whole),
            pl.BlockSpec((TILE_D, channels), lambda i: (i, 0)),
            pl.BlockSpec(dstep.shape, whole),
            pl.BlockSpec((TILE_D, LANES), lambda i: (i, 0)),
            pl.BlockSpec(dbc.shape, whole),
            pl.BlockSpec((w_bct.shape[0], TILE_D), lambda i: (0, i)),
            pl.BlockSpec((tokens, TILE_D), lambda i: (0, i)),
            pl.BlockSpec(inv_rms.shape, whole),
        ],
        out_specs=[pl.BlockSpec((rows, TILE_D), lambda i: (0, i))] * len(apart) + [pl.BlockSpec((8, TILE_D), lambda i: (0, i))],
        out_shape=[jax.ShapeDtypeStruct((rows, depth), bf16)] * len(apart) + [jax.ShapeDtypeStruct((8, depth), f32)],
        compiler_params=params(32),
        cost_estimate=cost(20),
        name="normed_term",
    )(
        rank, dx, from_hbm(w_a), dgate, from_hbm(w_b), dstep, from_hbm(w_s), dbc,
        from_hbm(w_bct), from_hbm(hidden), inv_rms,
    )


def norm_back_kernel(rank_ref, a_ref, b_ref, hidden_ref, cot_ref, gain_ref, out_ref):
    grad = a_ref[...].astype(f32) + b_ref[...].astype(f32)
    inputs = hidden_ref[...].astype(f32)
    inv_rms = lax.rsqrt(jnp.mean(inputs * inputs, axis=1, keepdims=True) + EPSILON)
    normed = inputs * inv_rms
    scaled = grad * gain_ref[0:1, :]
    mean = jnp.mean(scaled * normed, axis=1, keepdims=True)
    out_ref[...] = (inv_rms * (scaled - normed * mean) + cot_ref[...].astype(f32)).astype(out_ref.dtype)


def norm_backward(a, b, hidden, cot, gain_rows, rank):
    rows, depth = a.shape
    mine = lambda i, rank_ref: (rank_ref[0], 0)
    whole = lambda i, rank_ref: (0, 0)
    return pl.pallas_call(
        norm_back_kernel,
        grid_spec=pltpu.PrefetchScalarGridSpec(
            num_scalar_prefetch=1,
            grid=(1,),
            in_specs=[
                pl.BlockSpec((rows, depth), whole),
                pl.BlockSpec((rows, depth), whole),
                pl.BlockSpec((rows, depth), mine),
                pl.BlockSpec((rows, depth), mine),
                pl.BlockSpec((8, depth), whole),
            ],
            out_specs=pl.BlockSpec((rows, depth), whole),
        ),
        out_shape=jax.ShapeDtypeStruct((rows, depth), bf16),
        compiler_params=params(),
        cost_estimate=cost(0.1),
        name="norm_backward",
    )(rank, a, b, from_hbm(hidden), from_hbm(cot), gain_rows)


def moved(weight, moment, grad):
    fresh = 0.5 * moment + 0.5 * grad
    return fresh, weight - LEARN_RATE * fresh - LEARN_RATE * DECAY_RATE * weight


def add_up(refs):
    total = refs[0][...].astype(f32)
    for ref in refs[1:]:
        total = total + ref[...].astype(f32)
    return total


def update_in_kernel(w_ref, m_ref, *refs, count):
    gate_refs, x_refs, (m_out, w_out) = refs[:count], refs[count:2 * count], refs[2 * count:]
    for at, parts in ((0, gate_refs), (1, x_refs)):
        fresh, weight = moved(w_ref[:, at, :], m_ref[:, at, :], add_up(parts))
        m_out[:, at, :] = fresh
        w_out[:, at, :] = weight


def update_in(weight, moment, gate_parts, x_parts):
    rows, _, channels = weight.shape
    size = min(rows, 48)
    full = pl.BlockSpec((size, 2, channels), lambda i: (i, 0, 0))
    parts = [*gate_parts, *x_parts]
    return pl.pallas_call(
        functools.partial(update_in_kernel, count=len(gate_parts)),
        grid=(rows // size,),
        in_specs=[full, full] + [pl.BlockSpec((size, channels), functools.partial(lambda at, i: (i, at), at)) for _, at in parts],
        out_specs=[full, full],
        out_shape=[jax.ShapeDtypeStruct(weight.shape, f32)] * 2,
        compiler_params=params(),
        cost_estimate=cost(0.1),
        name="update_in",
    )(from_hbm(weight), from_hbm(moment), *[part for part, _ in parts])


def update_small_kernel(w_ref, m_ref, *refs, share):
    parts, (m_out, w_out, share_out, scratch) = refs[:-4], refs[-4:]
    heads, rows = w_ref.shape
    total = add_up(parts)
    share_out[...] = total
    scratch[0:rows, :] = total
    grad = scratch[...].T[share:share + heads, 0:rows]
    fresh, weight = moved(w_ref[...], m_ref[...], grad)
    m_out[...] = fresh
    w_out[...] = weight


def update_small(weight_t, moment_t, parts, share):
    rows = weight_t.shape[1]
    whole = lambda i: (0, 0)
    spec = pl.BlockSpec(weight_t.shape, whole)
    return pl.pallas_call(
        functools.partial(update_small_kernel, share=share),
        grid=(1,),
        in_specs=[spec, spec] + [pl.BlockSpec((rows, LANES), functools.partial(lambda at, i: (0, at), at)) for _, at in parts],
        out_specs=[spec, spec, pl.BlockSpec((rows, LANES), whole)],
        out_shape=[jax.ShapeDtypeStruct(weight_t.shape, f32)] * 2 + [jax.ShapeDtypeStruct((rows, LANES), f32)],
        scratch_shapes=[pltpu.VMEM((2 * LANES, LANES), f32)],
        compiler_params=params(),
        cost_estimate=cost(0.1),
        name="update_small",
    )(weight_t, moment_t, *[part for part, _ in parts])


def update_bc_kernel(rank_ref, w_ref, m_ref, *refs):
    pieces, (m_out, w_out) = refs[:-2], refs[-2:]
    rows, width = w_ref.shape
    share = width // len(pieces)
    lane = lax.broadcasted_iota(jnp.int32, (rows, LANES), 1)
    for pair in range(width // LANES):
        halves = []
        for member in (2 * pair, 2 * pair + 1):
            own = pieces[0][...]
            for r in range(1, len(pieces)):
                own = jnp.where((rank_ref[0] ^ r) == member, pieces[r][...], own)
            halves.append(own)
        grad = jnp.where(lane < share, halves[0], pltpu.roll(halves[1], share, 1))
        span = slice(pair * LANES, (pair + 1) * LANES)
        fresh, weight = moved(w_ref[:, span], m_ref[:, span], grad)
        m_out[:, span] = fresh
        w_out[:, span] = weight


def update_bc(weight, moment, pieces, rank):
    vmem = pl.BlockSpec(memory_space=pltpu.VMEM)
    return pl.pallas_call(
        update_bc_kernel,
        in_specs=[pl.BlockSpec(memory_space=pltpu.SMEM)] + [vmem] * (2 + len(pieces)),
        out_specs=[vmem, vmem],
        out_shape=[jax.ShapeDtypeStruct(weight.shape, f32)] * 2,
        compiler_params=params(),
        cost_estimate=cost(0.1),
        name="update_bc",
    )(rank, weight, moment, *pieces)


def fence(*values):
    leaves, tree = jax.tree.flatten(values)
    return jax.tree.unflatten(tree, lax.optimization_barrier(leaves))


def outer_from(v, k):
    n = lax.axis_size("dp") // 2
    return lax.ppermute(v, "dp", [(((o + k) % n) * 2 + x, o * 2 + x) for o in range(n) for x in range(2)])


def outer_flip(v, bit):
    n = lax.axis_size("dp") // 2
    return lax.ppermute(v, "dp", [((o ^ bit) * 2 + x, o * 2 + x) for o in range(n) for x in range(2)])


def inner_flip(v):
    return lax.ppermute(v, "dp", [(d ^ 1, d) for d in range(lax.axis_size("dp"))])


def rank_flip(v, bit):
    return lax.ppermute(v, "mp", [(m ^ bit, m) for m in range(lax.axis_size("mp"))])


def hops(n):
    order = []
    for k in range(1, n // 2 + 1):
        order.append(k)
        if n - k != k:
            order.append(n - k)
    return order


def pair_sum(a, b):
    return (a.astype(f32) + b.astype(f32)).astype(bf16)


def outer_blocks(own, here, back, ks):
    rows = own.shape[0]
    back = [part[i:i + rows] for part in back for i in range(0, part.shape[0], rows)]
    return [
        (here[i * rows:(i + 1) * rows].astype(f32) + back[i].astype(f32)).astype(bf16) for i in range(len(ks))
    ]


def outer_send(blocks, ks):
    n = lax.axis_size("dp") // 2
    return [outer_from(block, n - k) for block, k in zip(blocks, ks)]


def outer_sum(v):
    bit = 1
    while bit < lax.axis_size("dp") // 2:
        v = v + outer_flip(v, bit)
        bit *= 2
    return v


def mp_sum(v):
    v = v + rank_flip(v, 1)
    return v + rank_flip(v, 2)


def mp_sum_direct(v):
    return (v + rank_flip(v, 1)) + (rank_flip(v, 2) + rank_flip(v, 3))


def mp_reduce(blocks):
    far = blocks[2].astype(f32) + rank_flip(blocks[3], 1).astype(f32)
    near = blocks[0].astype(f32) + rank_flip(blocks[1], 1).astype(f32)
    return near, rank_flip(far.astype(bf16), 2)


def mp_pieces(v):
    far = rank_flip(v, 2)
    return [v, rank_flip(v, 1), far, rank_flip(far, 1)]


def in_rank_order(pieces, rank, axis):
    odd, high = (rank & 1) == 1, (rank & 2) == 2
    join = lambda a, b: jnp.concatenate([a, b], axis=axis)
    low = jnp.where(odd, join(pieces[1], pieces[0]), join(pieces[0], pieces[1]))
    far = jnp.where(odd, join(pieces[3], pieces[2]), join(pieces[2], pieces[3]))
    return jnp.where(high, join(far, low), join(low, far))


def momentum(moment, grad):
    return 0.5 * moment + 0.5 * grad


def advance(weight, moment, grad):
    fresh = momentum(moment, grad)
    return (fresh, weight - LEARN_RATE * fresh - LEARN_RATE * DECAY_RATE * weight)


def body(
    hidden, segments, cotangent, in_weight, in_moment, bc_weight, bc_moment, step_weight, step_moment,
    out_weight, out_moment, conv_table, conv_moment, bc_table, bc_table_moment, head_table, head_moment,
    norm_gain, gain_moment,
):
    size = lax.axis_size("dp")
    ranks = lax.axis_size("mp")
    n = size // 2
    place, rank = lax.axis_index("dp"), lax.axis_index("mp")
    outer, inner = place // 2, place % 2
    rank1 = rank.reshape(1).astype(jnp.int32)
    rows, _, channels = in_weight.shape
    heads = head_table.shape[1]
    tokens, depth = hidden.shape
    share = bc_weight.shape[1] // ranks

    ks = hops(n)
    near_ks, far_k = ks[:-1], ks[-1]

    def members(order):
        return jnp.stack([((outer + k) % n) * 2 + (inner ^ j) for k, j in order]).astype(jnp.int32)

    first = [(0, 0), (0, 1)]
    idx = members(first + [(k, 0) for k in ks] + [(k, 1) for k in ks])
    idx_s = members([(0, 0)] + [(k, 0) for k in ks] + [(0, 1)] + [(k, 1) for k in ks])
    sizes = (1, 1, n - 1, n - 1)
    split_sizes = (1, 1, n - 1, n - 2, 1)
    width = depth // ranks

    set_a, set_b = pack(in_weight, bc_weight, step_weight.T, rank1)
    set_c = out_weight.T.astype(bf16)

    def blocks(own, z, x):
        return [own, x[0]] + [z[k] for k in ks] + [x[k] for k in ks]

    def block(v, i):
        return v[i * rows:(i + 1) * rows]

    def blocks(own, z, x):
        return [own, x[0]] + [z[k] for k in ks] + [x[k] for k in ks]

    def block(v, i):
        return v[i * rows:(i + 1) * rows]

    def total(own, own_got, got):
        value = own.astype(f32) + own_got.astype(f32)
        for part in got:
            value = value + part.astype(f32)
        return value

    def outer_all(v, some):
        return {k: outer_from(v, k) for k in some}

    def flip_all(z, some):
        return {k: inner_flip(z[k]) for k in some}

    a_z = outer_all(set_a, near_ks)
    a_x = {0: inner_flip(set_a)}
    far_a, a_x[0] = fence(set_a, a_x[0])
    a_z[far_k] = outer_from(far_a, far_k)
    cot_far = rank_flip(cotangent, 2)
    gain_rows = pad_rows(norm_gain[None])
    normed_low, normed_t, inv_rms = prepare(hidden, gain_rows)
    a_x.update(flip_all(a_z, near_ks))
    aux, seg_row = segment_facts(segments)
    head_rows = pad_lanes(pad_rows(head_table))
    facts = (aux, seg_row, pad_rows(conv_table), pad_rows(bc_table), head_rows, head_expand(channels))
    set_a, set_b, set_c, a_z, a_x, cot_far, normed_low, normed_t, inv_rms, facts = fence(
        set_a, set_b, set_c, a_z, a_x, cot_far, normed_low, normed_t, inv_rms, facts
    )

    a_x[far_k] = inner_flip(a_z[far_k])
    b_x = {0: inner_flip(set_b)}
    b_z = outer_all(set_b, near_ks)
    cot, cot_t = join_columns([cotangent, rank_flip(cotangent, 1), cot_far, rank_flip(cot_far, 1)], rank1)
    set_b, set_c, b_z, b_x, a_z, a_x, cot, cot_t, normed_low = fence(
        set_b, set_c, b_z, b_x, a_z, a_x, cot, cot_t, normed_low
    )

    b_z[far_k] = outer_from(set_b, far_k)
    b_x.update(flip_all(b_z, near_ks[:1]))
    c_x = {0: inner_flip(set_c)}
    a_blocks = blocks(set_a, a_z, a_x)
    small, bc_share, w_s, w_bct_share = project_small(normed_low, a_blocks, idx, share)
    bc_pieces = mp_pieces(bc_share)
    x_pre, w_a = project(normed_low, a_blocks, idx, channels)
    bc_pieces, x_pre, small, set_c, w_bct_share, w_s = fence(bc_pieces, x_pre, small, set_c, w_bct_share, w_s)
    bc_pre, step_pre = join_small(bc_pieces, small, rank1)
    set_c, b_z, b_x, c_x, x_pre, bc_pre, step_pre, w_bct_share = fence(
        set_c, b_z, b_x, c_x, x_pre, bc_pre, step_pre, w_bct_share
    )

    c_z = outer_all(set_c, near_ks)
    b_x.update(flip_all(b_z, ks[1:]))
    mixed, states = ssd_forward(x_pre, bc_pre, step_pre, *facts)
    mixed, states, b_x, b_z, c_z, c_x, w_bct_share, set_c = fence(mixed, states, b_x, b_z, c_z, c_x, w_bct_share, set_c)

    c_z[far_k] = outer_from(set_c, far_k)
    c_x.update(flip_all(c_z, near_ks))
    gate_pre, square, w_b = gate_forward(normed_low, mixed, blocks(set_b, b_z, b_x), idx)
    square = mp_sum_direct(square)
    mixed, gate_pre, square, w_b, w_bct_share, c_z, c_x = fence(mixed, gate_pre, square, w_b, w_bct_share, c_z, c_x)

    c_x[far_k] = inner_flip(c_z[far_k])
    conv_rows = facts[2]
    gated_out = gated_norm(gate_pre, mixed, square, conv_rows, channels * ranks)
    gc_own, gc_own1, gc_here, gc_near, gc_far = weight_grad(cot_t, gated_out, idx, split_sizes)
    c_x, square, gated_out, gc_own, gc_own1, gc_here, gc_near, gc_far, w_bct_share = fence(
        c_x, square, gated_out, gc_own, gc_own1, gc_here, gc_near, gc_far, w_bct_share
    )

    gc_far_back, gc_near_back = inner_flip(gc_far), inner_flip(gc_near)
    gout, inner_dot, w_c = grad_gout(cot, gate_pre, mixed, conv_rows, blocks(set_c, c_z, c_x), idx)
    gout, inner_dot, w_c = fence(gout, inner_dot, w_c)
    inner_dot = mp_sum_direct(inner_dot)
    partial = out_partial(gated_out, w_c, rank1, ranks)
    inner_dot, gout, partial, w_bct_share, gc_far_back = fence(inner_dot, gout, partial, w_bct_share, gc_far_back)
    out_back = rank_flip(partial[3], 1)
    w_bct = [w_bct_share] + [rank_flip(w_bct_share, r) for r in (1, 2, 3)]
    dmixed, dgate, dgain = gate_backward(gate_pre, gout, mixed, square, inner_dot, conv_rows, channels * ranks)
    gb_own, gb_own1, gb_here, gb_send = weight_grad(normed_t, dgate, idx, sizes)
    gc_near_back, gc_far_back, w_bct, out_back, gb_own, gb_own1, gb_here, gb_send, partial, dmixed, dgain = fence(
        gc_near_back, gc_far_back, w_bct, out_back, gb_own, gb_own1, gb_here, gb_send, partial, dmixed, dgain
    )
    c_blocks = [pair_sum(block(gc_here, i), block(gc_near_back, i)) for i in range(n - 2)]
    c_blocks.append(pair_sum(block(gc_here, n - 2), gc_far_back))
    out_far = pair_sum(partial[2], out_back)
    w_bct = join_rows(w_bct, rank1)
    c_blocks, out_far, w_bct, dmixed, gb_send = fence(c_blocks, out_far, w_bct, dmixed, gb_send)

    c_got = outer_send(c_blocks, ks)
    gb_back = inner_flip(gb_send)
    out_got = rank_flip(out_far, 2)
    dx, dbc, dbc_keep, dbc_send, dstep, dstep_t, dconv, dbct_part, dheads = ssd_backward(
        rank1, x_pre, bc_pre, step_pre, *facts, mixed, dmixed, states
    )
    c_got, gb_back, out_got, dx, dbc, dbc_keep, dbc_send, dstep, dstep_t, dconv, dbct_part, dheads = fence(
        c_got, gb_back, out_got, dx, dbc, dbc_keep, dbc_send, dstep, dstep_t, dconv, dbct_part, dheads
    )

    b_got = {far_k: outer_from(pair_sum(block(gb_here, n - 2), block(gb_back, n - 2)), n - far_k)}
    dbc_back = rank_flip(dbc_send, 1)
    out_near_back = rank_flip(partial[1], 1)
    ga_own, ga_own1, ga_here, ga_near, ga_far = weight_grad(normed_t, dx, idx, split_sizes, us=20)
    ga_own, ga_own1, ga_here, ga_near, ga_far, dx, dbc_back, gb_back, gb_here, out_near_back = fence(
        ga_own, ga_own1, ga_here, ga_near, ga_far, dx, dbc_back, gb_back, gb_here, out_near_back
    )

    b_near = [pair_sum(block(gb_here, i), block(gb_back, i)) for i in range(n - 2)]
    b_got.update(zip(near_ks, outer_send(b_near, near_ks)))
    ga_far_back = inner_flip(ga_far)
    dbc_pair = pair_sum(dbc_keep, dbc_back)
    dbc_got = rank_flip(dbc_pair[share:], 2)
    operands = (dx, dgate, dstep, dbc, w_a, w_b, w_s, w_bct, hidden, inv_rms, rank1, ranks)
    far_own, far_send, gain_far = normed_term(*operands, (2, 3))
    far_own, far_send, gain_far, dx, dbc_got, dbc_pair, dstep_t, b_got[far_k], ga_near, ga_own1 = fence(
        far_own, far_send, gain_far, dx, dbc_got, dbc_pair, dstep_t, b_got[far_k], ga_near, ga_own1
    )
    far_back = rank_flip(far_send, 1)
    operands = (dx, *operands[1:])
    near_own, near_send, gain_near = normed_term(*operands, (0, 1))
    far_back, near_own, near_send, gain_near, ga_far_back, ga_near, b_got = fence(
        far_back, near_own, near_send, gain_near, ga_far_back, ga_near, b_got
    )
    shared = mp_sum_direct(jnp.concatenate([dbct_part, gain_far + gain_near], axis=1))
    near_back = rank_flip(near_send, 1)
    far = pair_sum(far_own, far_back)
    a_far = pair_sum(block(ga_here, n - 2), ga_far_back)
    dbc_share = pair_sum(dbc_pair[:share], dbc_got)
    dsmall_t = jnp.concatenate([dbc_share, dstep_t, jnp.zeros((LANES - share - 16, tokens), bf16)], axis=0)
    gs_own, gs_here, gs_send = weight_grad(normed_t, dsmall_t, idx_s, (1, n - 1, n), turned=True)
    far, a_far, shared, near_back, gs_send, ga_near = fence(far, a_far, shared, near_back, gs_send, ga_near)

    got = rank_flip(far, 2)
    a_got = {far_k: outer_from(a_far, n - far_k)}
    gs_back = inner_flip(gs_send)
    ga_near_back = inner_flip(ga_near)
    packed = jnp.concatenate([dconv + dgain, dheads, shared], axis=1)
    packed_got = inner_flip(packed)
    near = near_own.astype(f32) + near_back.astype(f32)
    got, near, a_got, ga_near_back, packed, packed_got, gs_back, ga_own1, gb_own1, gc_own1 = fence(
        got, near, a_got, ga_near_back, packed, packed_got, gs_back, ga_own1, gb_own1, gc_own1
    )

    mine = norm_backward(near, got, hidden, cot, gain_rows, rank1)
    mine, ga_near_back, gs_back, packed, packed_got, gc_own1, gb_own1, ga_own1 = fence(
        mine, ga_near_back, gs_back, packed, packed_got, gc_own1, gb_own1, ga_own1
    )
    mine_far = rank_flip(mine, 2)
    own_got = inner_flip(jnp.concatenate([gc_own1, gb_own1, ga_own1], axis=1))
    s_blocks = outer_blocks(gs_own, gs_here, [gs_back[rows:]], ks)
    sums = packed + packed_got
    sums = jnp.concatenate([sums[:, i:i + LANES] for i in range(0, sums.shape[1], LANES)], axis=0)
    depth_s = -(-sums.shape[0] // 112) * 112
    sums = pad_rows(sums, depth_s).astype(bf16)
    wide = (channels + LANES) // LANES
    sums_wide = jnp.concatenate([sums[i * depth_s // wide:(i + 1) * depth_s // wide] for i in range(wide)], axis=1)
    a_blocks = [
        jnp.concatenate(
            [jnp.concatenate([pair_sum(block(ga_here, i), block(ga_near_back, i)), s_blocks[i]], axis=1), sums_wide], axis=0
        )
        for i in range(n - 2)
    ]
    as_got = outer_send(a_blocks, near_ks)
    s_far_got = outer_from(jnp.concatenate([s_blocks[-1], sums], axis=0), n - far_k)
    mine_far, as_got, s_far_got, own_got, mine, sums = fence(mine_far, as_got, s_far_got, own_got, mine, sums)

    mine_near, mine_far_near = rank_flip(mine, 1), rank_flip(mine_far, 1)
    last = channels // LANES
    step_m, step_w, shard_s = update_small(
        step_weight.T, step_moment.T,
        [(gs_own, 0), (gs_back, 0), (s_far_got, 0)] + [(got, last) for got in as_got], share,
    )
    bc_pieces = [shard_s] + [rank_flip(shard_s, r) for r in (1, 2, 3)]
    in_m, in_w = update_in(
        in_weight, in_moment,
        [(gb_own, 0), (own_got, 1)] + [(b_got[k], 0) for k in ks],
        [(ga_own, 0), (own_got, 2), (a_got[far_k], 0)] + [(got, 0) for got in as_got],
    )
    input_grad = join_rows([mine, mine_near, mine_far, mine_far_near], rank1)
    bc_m, bc_w = update_bc(bc_weight, bc_moment, bc_pieces, rank1)

    def unpack(v):
        return v.astype(f32)

    found = {0: unpack(sums), far_k: unpack(s_far_got[rows:])}
    for k, got in zip(near_ks, as_got):
        tail = got[rows:]
        found[n - k] = unpack(jnp.concatenate([tail[:, i:i + LANES] for i in range(0, tail.shape[1], LANES)], axis=0))
    packed = found
    step = n // 2
    while step >= 1:
        packed = {i: packed[i] + packed[i + step] for i in range(step)}
        step //= 2
    packed = packed[0]
    packed = jnp.concatenate([packed[i:i + 8] for i in range(0, packed.shape[0] // 8 * 8, 8)], axis=1)

    resid = lax.dynamic_slice_in_dim(hidden, rank * width, width, 1).astype(f32)
    output = (resid + partial[0].astype(f32) + out_near_back.astype(f32) + out_got.astype(f32)).astype(bf16)
    shard_c = total(gc_own, own_got[:, :channels], c_got)

    cut = channels + LANES
    total_conv = packed[:6, :channels]
    total_head = packed[:3, channels:channels + heads]
    total_bct = packed[:5, cut:cut + 2 * LANES]
    total_gain = packed[0, cut + 2 * LANES:cut + 2 * LANES + depth]

    out_m, out_w = advance(out_weight, out_moment, shard_c.T)
    return (
        output, input_grad, in_m, in_w, bc_m, bc_w, step_m.T, step_w.T, out_m, out_w,
        momentum(conv_moment, total_conv),
        momentum(bc_table_moment, total_bct),
        momentum(head_moment, total_head),
        momentum(gain_moment, total_gain),
    )


def solution(mesh):
    placed = (
        P("dp", None),
        P("dp", None),
        P("dp", "mp"),
        P("dp", None, "mp"),
        P("dp", None, "mp"),
        P("dp", None),
        P("dp", None),
        P("dp", "mp"),
        P("dp", "mp"),
        P("mp", "dp"),
        P("mp", "dp"),
        P(None, "mp"),
        P(None, "mp"),
        P(),
        P(),
        P(None, "mp"),
        P(None, "mp"),
        P(),
        P(),
    )
    return jax.shard_map(
        body,
        mesh=mesh,
        in_specs=placed,
        out_specs=(
            P("dp", "mp"),
            P("dp", None),
            P("dp", None, "mp"),
            P("dp", None, "mp"),
            P("dp", None),
            P("dp", None),
            P("dp", "mp"),
            P("dp", "mp"),
            P("mp", "dp"),
            P("mp", "dp"),
            P(None, "mp"),
            P(),
            P(None, "mp"),
            P(),
        ),
        check_vma=False,
    )
```

```python
import functools

import jax
import jax.numpy as jnp
from jax import lax
from jax.experimental import pallas as pl
from jax.experimental.pallas import tpu as pltpu
from jax.sharding import PartitionSpec as P

CHUNK = 128
EPSILON = 1e-05
LEARN_RATE = 0.0001
DECAY_RATE = 0.1
WIDTH = 64
LANES = 128
HALO = 8
bf16 = jnp.bfloat16
f32 = jnp.float32
MIB = 1024 * 1024


def hbm(shape, dtype):
    return pltpu.HBM(shape, dtype)


def from_hbm(v):
    return pltpu.with_memory_space_constraint(v, pltpu.HBM)


def dot_nn(a, b):
    return lax.dot_general(a, b, (((1,), (0,)), ((), ())), preferred_element_type=f32)


def dot_nt(a, b):
    return lax.dot_general(a, b, (((1,), (1,)), ((), ())), preferred_element_type=f32)


def dot_tn(a, b):
    return lax.dot_general(a, b, (((0,), (0,)), ((), ())), preferred_element_type=f32)


def split3(v):
    high = v.astype(bf16)
    rest = v - high.astype(f32)
    mid = rest.astype(bf16)
    low = (rest - mid.astype(f32)).astype(bf16)
    return high, mid, low


def exact_left(ones, v):
    high, mid, low = split3(v)
    return dot_nn(ones, high) + dot_nn(ones, mid) + dot_nn(ones, low)


def spread(v, expand):
    high, mid, low = split3(v)
    return dot_nn(high, expand) + dot_nn(mid, expand) + dot_nn(low, expand)


def gather_heads(v, expand_t):
    high = v.astype(bf16)
    mid = (v - high.astype(f32)).astype(bf16)
    return dot_nn(high, expand_t) + dot_nn(mid, expand_t)


def sigmoid(v):
    return 0.5 * jnp.tanh(0.5 * v) + 0.5


def conv_block(before, now, taps, keep):
    longer = jnp.concatenate([before, now], axis=0)
    total = taps[4:5, :] + taps[0:1, :] * now
    for lag in (1, 2, 3):
        moved = pltpu.roll(longer, lag, 0)[HALO:, :]
        total = total + taps[lag:lag + 1, :] * (moved * keep[:, lag - 1:lag])
    return total


def step_parts(step_pre, heads):
    raw = step_pre + heads[0:1, :]
    steps = jnp.maximum(raw, 0.0) + jnp.log1p(jnp.exp(-jnp.abs(raw)))
    rates = -jnp.exp(heads[1:2, :])
    return raw, steps, rates


def triangle(lower):
    row = lax.broadcasted_iota(jnp.int32, (CHUNK, CHUNK), 0)
    col = lax.broadcasted_iota(jnp.int32, (CHUNK, CHUNK), 1)
    return row >= col if lower else row <= col


def ssd_forward_kernel(
    x_ref, xb_ref, bc_ref, bcb_ref, st_ref, aux_ref, seg_ref, conv_ref, bct_ref, heads_ref, expand_ref,
    mixed_ref, state_ref, act_ref, slope_ref, xs_ref, xe_ref, step_ref, entry_ref, end_ref, bcact_ref, bcslope_ref,
    state,
):
    chunk = pl.program_id(0)

    @pl.when(chunk == 0)
    def _():
        state[...] = jnp.zeros_like(state)

    channels = x_ref.shape[1]
    aux = aux_ref[...]
    expand = expand_ref[...]
    u = conv_block(xb_ref[...], x_ref[...], conv_ref, aux)
    sg = sigmoid(u)
    x_act = u * sg
    act_ref[...] = x_act
    slope_ref[...] = (sg * (1.0 + u * (1.0 - sg))).astype(bf16)
    ubc = conv_block(bcb_ref[...], bc_ref[...], bct_ref, aux)
    sgbc = sigmoid(ubc)
    bc_act = (ubc * sgbc).astype(bf16)
    bcact_ref[...] = bc_act
    bcslope_ref[...] = sgbc * (1.0 + ubc * (1.0 - sgbc))
    b_mat, c_mat = bc_act[:, :LANES], bc_act[:, LANES:]
    _, steps, rates = step_parts(st_ref[...], heads_ref)
    lower = triangle(True)
    cum = exact_left(lower.astype(bf16), steps * rates)
    cum_t = cum.T
    tail = cum[CHUNK - 1:CHUNK, :]
    entry = jnp.exp(cum) * aux[:, 6:7]
    to_end = jnp.exp(tail - cum) * aux[:, 7:8]
    wide = spread(jnp.concatenate([steps, entry, to_end], axis=0), expand)
    step_e, entry_e, to_end_e = wide[:CHUNK], wide[CHUNK:2 * CHUNK], wide[2 * CHUNK:]
    skip_e = spread(jnp.broadcast_to(heads_ref[2:3, :], (8, LANES)), expand)[0:1, :]
    mask = lower & (aux[:, 8:9] == seg_ref[...])
    scores = jnp.where(mask, dot_nt(c_mat, b_mat), 0.0)
    xs = x_act * step_e
    xs_low = xs.astype(bf16)
    xe_low = (xs * to_end_e).astype(bf16)
    xs_ref[...] = xs_low
    xe_ref[...] = xe_low
    step_ref[...] = step_e.astype(bf16)
    entry_ref[...] = entry_e.astype(bf16)
    end_ref[...] = to_end_e.astype(bf16)
    held = state[...]
    held_low = held.astype(bf16)
    state_ref[...] = held_low
    out = dot_nn(c_mat, held_low) * entry_e + skip_e * x_act
    state[...] = held * entry_e[CHUNK - 1:CHUNK, :] + dot_tn(b_mat, xe_low)
    first = lax.broadcasted_iota(jnp.int32, (CHUNK, LANES), 1) < WIDTH
    zero = jnp.zeros((CHUNK, LANES), bf16)
    for pair in range(channels // LANES):
        span = slice(pair * LANES, (pair + 1) * LANES)
        parts = []
        for head in (2 * pair, 2 * pair + 1):
            diff = cum[:, head:head + 1] - cum_t[head:head + 1, :]
            parts.append((scores * jnp.exp(jnp.minimum(diff, 0.0))).astype(bf16))
        own = xs_low[:, span]
        both = jnp.concatenate([jnp.where(first, own, zero), jnp.where(first, zero, own)], axis=0)
        mixed_ref[:, span] = out[:, span] + dot_nn(jnp.concatenate(parts, axis=1), both)


def ssd_backward_kernel(
    rank_ref, x_ref, bc_ref, st_ref, aux_ref, seg_ref, conv_ref, bct_ref, heads_ref, expand_ref,
    expand_t_ref, mixed_ref, dy_ref, state_ref, act_ref, slope_ref, xs_ref, xe_ref, step_ref, entry_ref, end_ref, bcact_ref,
    bcslope_ref, dx_ref, dbc_ref, keep_ref, send_ref, dst_ref, dst_t_ref, dconv_ref, dbct_ref, dheads_ref,
    dstate, du_scr, dubc_scr, share_scr,
):
    @pl.when(pl.program_id(0) == 0)
    def _():
        for ref in (dstate, du_scr, dubc_scr, dconv_ref, dbct_ref, dheads_ref):
            ref[...] = jnp.zeros_like(ref)

    channels = x_ref.shape[1]
    aux = aux_ref[...]
    expand = expand_ref[...]
    x_act = act_ref[...]
    b_mat, c_mat = bcact_ref[:, :LANES], bcact_ref[:, LANES:]
    raw, steps, rates = step_parts(st_ref[...], heads_ref)
    lower = triangle(True)
    cum = exact_left(lower.astype(bf16), steps * rates)
    cum_t = cum.T
    skip_e = spread(jnp.broadcast_to(heads_ref[2:3, :], (8, LANES)), expand)[0:1, :]
    upper = triangle(False)
    mask = upper & (aux[:, 8:9] == seg_ref[...])
    scores = jnp.where(mask, dot_nt(b_mat, c_mat), 0.0)
    xs_low = xs_ref[...]
    dy_low = dy_ref[...]
    dy = dy_low.astype(f32)
    held_low = state_ref[...]
    grad = dstate[...]
    grad_low = grad.astype(bf16)
    entry_e = entry_ref[...].astype(f32)
    entry_dy = (entry_e * dy).astype(bf16)
    kept_e = entry_e[CHUNK - 1:CHUNK, :]
    dstate[...] = grad * kept_e + dot_tn(c_mat, entry_dy)
    dc = dot_nt(entry_dy, held_low)
    db = dot_nt(xe_ref[...], grad_low)
    q_state = dot_nn(b_mat, grad_low) * end_ref[...].astype(f32)
    first = lax.broadcasted_iota(jnp.int32, (CHUNK, LANES), 1) < WIDTH
    zero = jnp.zeros((CHUNK, LANES), bf16)
    dscores = jnp.zeros((CHUNK, CHUNK), f32)
    q_parts = []
    for pair in range(channels // LANES):
        span = slice(pair * LANES, (pair + 1) * LANES)
        own = dy_low[:, span]
        both = jnp.concatenate([jnp.where(first, own, zero), jnp.where(first, zero, own)], axis=0)
        dweights = dot_nt(xs_low[:, span], both)
        parts = []
        for i, head in enumerate((2 * pair, 2 * pair + 1)):
            diff = cum_t[head:head + 1, :] - cum[:, head:head + 1]
            decay = jnp.exp(jnp.minimum(diff, 0.0))
            parts.append((scores * decay).astype(bf16))
            dscores = dscores + dweights[:, i * LANES:(i + 1) * LANES] * decay
        q_parts.append(dot_nn(jnp.concatenate(parts, axis=1), both))
    q = jnp.concatenate(q_parts, axis=1) + q_state
    dscores_low = jnp.where(mask, dscores, 0.0).astype(bf16)
    db = db + dot_nn(dscores_low, c_mat)
    dc = dc + dot_tn(dscores_low, b_mat)
    xs_round = xs_low.astype(f32)
    expand_t = expand_t_ref[...]
    flow = gather_heads(dy * (mixed_ref[...] - skip_e * x_act) - xs_round * q, expand_t)
    dstep = dot_nn((x_act * q).astype(bf16), expand_t)
    sums = jnp.concatenate(
        [
            jnp.sum(xs_round * q_state + kept_e * (held_low.astype(f32) * grad), axis=0, keepdims=True),
            jnp.sum(dy * x_act, axis=0, keepdims=True),
            jnp.zeros((6, channels), f32),
        ],
        axis=0,
    )
    sums = gather_heads(sums, expand_t)
    dlog = exact_left(upper.astype(bf16), flow) + sums[0:1, :]
    dstep = dstep + rates * dlog
    draw = dstep * sigmoid(raw)
    dst_ref[...] = pltpu.roll(draw, WIDTH, 1).astype(bf16)
    dst_t_ref[...] = draw.T[0:16, :].astype(bf16)
    dheads_ref[0:1, :] += jnp.sum(draw, axis=0, keepdims=True)
    dheads_ref[1:2, :] += rates * jnp.sum(dlog * steps, axis=0, keepdims=True)
    dheads_ref[2:3, :] += sums[1:2, :]
    x_now, bc_now = x_ref[...], bc_ref[...]

    def conv_back(scratch, du, now, taps, dtaps):
        longer = jnp.concatenate([du, scratch[...]], axis=0)
        total = taps[0:1, :] * du
        sums = [jnp.sum(now * du, axis=0, keepdims=True)]
        for lag in (1, 2, 3):
            moved = pltpu.roll(longer, CHUNK + HALO - lag, 0)[0:CHUNK, :] * aux[:, 2 + lag:3 + lag]
            total = total + taps[lag:lag + 1, :] * moved
            sums.append(jnp.sum(now * moved, axis=0, keepdims=True))
        sums.append(jnp.sum(du, axis=0, keepdims=True))
        dtaps[0:5, :] += jnp.concatenate(sums, axis=0)
        scratch[...] = du[0:HALO, :]
        return total

    du = (skip_e * dy + step_ref[...].astype(f32) * q) * slope_ref[...].astype(f32)
    dx_ref[...] = conv_back(du_scr, du, x_now, conv_ref, dconv_ref).astype(dx_ref.dtype)
    dubc = jnp.concatenate([db, dc], axis=1) * bcslope_ref[...]
    dbc = conv_back(dubc_scr, dubc, bc_now, bct_ref, dbct_ref).astype(bf16)
    dbc_ref[...] = dbc
    share = 2 * LANES // 4
    turned = dbc.T
    for member in range(4):
        apart = member ^ rank_ref[0]
        start = pl.multiple_of((apart & 1) * 2 * share + (apart >> 1) * share, share)
        share_scr[pl.ds(start, share), :] = turned[member * share:(member + 1) * share, :]
    keep_ref[...] = share_scr[0:2 * share, :]
    send_ref[...] = share_scr[2 * share:4 * share, :]


def common_specs(place, channels):
    before = lambda i: (jnp.maximum(place(i) * (CHUNK // HALO) - 1, 0), 0)
    now = lambda i: (place(i), 0)
    whole = lambda i: (0, 0)
    return [
        pl.BlockSpec((CHUNK, channels), now),
        pl.BlockSpec((HALO, channels), before),
        pl.BlockSpec((CHUNK, 2 * LANES), now),
        pl.BlockSpec((HALO, 2 * LANES), before),
        pl.BlockSpec((CHUNK, LANES), now),
        pl.BlockSpec((CHUNK, 16), now),
        pl.BlockSpec((1, CHUNK), lambda i: (0, place(i))),
        pl.BlockSpec((8, channels), whole),
        pl.BlockSpec((8, 2 * LANES), whole),
        pl.BlockSpec((8, LANES), whole),
        pl.BlockSpec((LANES, channels), whole),
    ]


def ssd_forward(x_pre, bc_pre, step_pre, aux, seg_row, conv_rows, bc_rows, head_rows, expand):
    tokens, channels = x_pre.shape
    count = tokens // CHUNK
    now = lambda i: (i, 0)
    return pl.pallas_call(
        ssd_forward_kernel,
        grid=(count,),
        in_specs=common_specs(lambda i: i, channels),
        out_specs=[
            pl.BlockSpec((CHUNK, channels), now),
            pl.BlockSpec((None, LANES, channels), lambda i: (i, 0, 0)),
        ]
        + [pl.BlockSpec((CHUNK, channels), now)] * 7
        + [pl.BlockSpec((CHUNK, 2 * LANES), now)] * 2,
        out_shape=[
            hbm((tokens, channels), f32),
            hbm((count, LANES, channels), bf16),
            hbm((tokens, channels), f32),
            *[hbm((tokens, channels), bf16) for _ in range(6)],
            hbm((tokens, 2 * LANES), bf16),
            hbm((tokens, 2 * LANES), f32),
        ],
        scratch_shapes=[
            pltpu.VMEM((LANES, channels), f32),
        ],
        compiler_params=pltpu.CompilerParams(vmem_limit_bytes=18 * MIB),
        cost_estimate=pl.CostEstimate(flops=14 * 10**9, bytes_accessed=40 * 10**6, transcendentals=0),
        name="ssd_forward",
    )(
        from_hbm(x_pre), from_hbm(x_pre), bc_pre, bc_pre, step_pre, aux, seg_row, conv_rows, bc_rows, head_rows, expand
    )


def ssd_backward(rank, x_pre, bc_pre, step_pre, aux, seg_row, conv_rows, bc_rows, head_rows, expand, expand_t, dy, kept):
    tokens, channels = x_pre.shape
    count = tokens // CHUNK
    place = lambda i: count - 1 - i
    now = lambda i: (place(i), 0)
    whole = lambda i: (0, 0)
    wide = pl.BlockSpec((CHUNK, channels), now)
    narrow = pl.BlockSpec((CHUNK, 2 * LANES), now)
    specs = common_specs(place, channels)
    mixed, states, *more = kept
    return pl.pallas_call(
        ssd_backward_kernel,
        grid=(count,),
        in_specs=[pl.BlockSpec(memory_space=pltpu.SMEM), specs[0], specs[2], *specs[4:]]
        + [pl.BlockSpec((channels, LANES), whole), wide, wide, pl.BlockSpec((None, LANES, channels), lambda i: (place(i), 0, 0))]
        + [wide] * 7 + [narrow] * 2,
        out_specs=[
            wide,
            narrow,
            pl.BlockSpec((LANES, CHUNK), lambda i: (0, place(i))),
            pl.BlockSpec((LANES, CHUNK), lambda i: (0, place(i))),
            pl.BlockSpec((CHUNK, LANES), now),
            pl.BlockSpec((16, CHUNK), lambda i: (0, place(i))),
            pl.BlockSpec((8, channels), whole),
            pl.BlockSpec((8, 2 * LANES), whole),
            pl.BlockSpec((8, LANES), whole),
        ],
        out_shape=[
            hbm((tokens, channels), bf16),
            hbm((tokens, 2 * LANES), bf16),
            hbm((LANES, tokens), bf16),
            hbm((LANES, tokens), bf16),
            hbm((tokens, LANES), bf16),
            hbm((16, tokens), bf16),
            jax.ShapeDtypeStruct((8, channels), f32),
            jax.ShapeDtypeStruct((8, 2 * LANES), f32),
            jax.ShapeDtypeStruct((8, LANES), f32),
        ],
        scratch_shapes=[
            pltpu.VMEM((LANES, channels), f32),
            pltpu.VMEM((HALO, channels), f32),
            pltpu.VMEM((HALO, 2 * LANES), f32),
            pltpu.VMEM((2 * LANES, CHUNK), bf16),
        ],
        compiler_params=pltpu.CompilerParams(vmem_limit_bytes=20 * MIB),
        cost_estimate=pl.CostEstimate(flops=28 * 10**9, bytes_accessed=40 * 10**6, transcendentals=0),
        name="ssd_backward",
    )(
        rank, from_hbm(x_pre), bc_pre, step_pre, aux, seg_row, conv_rows, bc_rows, head_rows,
        expand, expand_t, from_hbm(mixed), dy, from_hbm(states), *[from_hbm(v) for v in more],
    )


def segment_facts(seg):
    row = seg[0]
    tokens = row.shape[0]
    cols = []
    for lag in (1, 2, 3):
        cols.append(jnp.pad(row[:-lag], (lag, 0), constant_values=-1) == row)
    for lag in (1, 2, 3):
        cols.append(jnp.pad(row[lag:], (0, lag), constant_values=-1) == row)
    blocks = row.reshape(tokens // CHUNK, CHUNK)
    ends = blocks[:, -1:]
    before = jnp.concatenate([jnp.full((1, 1), -1, row.dtype), ends[:-1]], axis=0)
    cols.append((blocks == before).reshape(-1))
    cols.append((blocks == ends).reshape(-1))
    cols.append(row)
    facts = jnp.stack([c.astype(f32) for c in cols], axis=1)
    return jnp.pad(facts, ((0, 0), (0, 16 - facts.shape[1]))), seg.astype(f32)


def pad_rows(table, rows=8):
    return jnp.pad(table, ((0, rows - table.shape[0]), (0, 0)))


def pad_lanes(table, lanes=LANES):
    return jnp.pad(table, ((0, 0), (0, lanes - table.shape[1])))


def head_expand(channels):
    head, channel = jnp.arange(LANES), jnp.arange(channels) // WIDTH
    return (head[:, None] == channel[None, :]).astype(bf16), (channel[:, None] == head[None, :]).astype(bf16)


TILE = 256
TILE_D = 384


def fill(dest, pieces, idx_ref):
    rows = pieces[0].shape[0]
    s = 0
    for piece in pieces:
        for b in range(piece.shape[0] // rows):
            start = pl.multiple_of(idx_ref[s] * rows, rows)
            dest[pl.ds(start, rows), :] = piece[b * rows:(b + 1) * rows, :]
            s += 1


def params(mib=18):
    return pltpu.CompilerParams(vmem_limit_bytes=mib * MIB)


def cost(us):
    return pl.CostEstimate(flops=int(us * 10**9), bytes_accessed=int(us * 2 * 10**6), transcendentals=0)


def prepare_kernel(hidden_ref, gain_ref, low_ref, low_t_ref, inv_ref):
    inputs = hidden_ref[...].astype(f32)
    inv_rms = lax.rsqrt(jnp.mean(inputs * inputs, axis=1, keepdims=True) + EPSILON)
    low = (inputs * inv_rms * gain_ref[0:1, :]).astype(bf16)
    low_ref[...] = low
    low_t_ref[...] = low.T
    inv_ref[...] = column_to_row(inv_rms)


def prepare(hidden, gain_rows):
    tokens, depth = hidden.shape
    block = pl.BlockSpec((TILE, depth), lambda i: (i, 0))
    return pl.pallas_call(
        prepare_kernel,
        grid=(tokens // TILE,),
        in_specs=[block, pl.BlockSpec((8, depth), lambda i: (0, 0))],
        out_specs=[block, pl.BlockSpec((depth, TILE), lambda i: (0, i)), pl.BlockSpec((8, TILE), lambda i: (0, i))],
        out_shape=[
            hbm((tokens, depth), bf16),
            hbm((depth, tokens), bf16),
            jax.ShapeDtypeStruct((8, tokens), f32),
        ],
        compiler_params=params(),
        cost_estimate=cost(12),
        name="prepare",
    )(hidden, gain_rows)


def pack_kernel(rank_ref, in_ref, bc_ref, step_ref, a_ref, b_ref, scratch):
    channels = b_ref.shape[1]
    rows, width = bc_ref.shape
    share = width // 4
    heads = step_ref.shape[0]
    b_ref[...] = in_ref[:, 0, :].astype(bf16)
    a_ref[:, :channels] = in_ref[:, 1, :].astype(bf16)
    scratch[...] = jnp.zeros_like(scratch)
    scratch[share:share + heads, 0:rows] = step_ref[...]
    step = scratch[...].T[0:rows, :]
    own = bc_ref[:, 0:LANES]
    for member in range(1, 4):
        moved = pltpu.roll(bc_ref[...], width - member * share, 1)[:, 0:LANES]
        own = jnp.where(rank_ref[0] == member, moved, own)
    lane = lax.broadcasted_iota(jnp.int32, (rows, LANES), 1)
    a_ref[:, channels:] = jnp.where(lane < share, own, step).astype(bf16)


def pack(in_weight, bc_weight, step_t, rank):
    rows, _, channels = in_weight.shape
    vmem = pl.BlockSpec(memory_space=pltpu.VMEM)
    return pl.pallas_call(
        pack_kernel,
        in_specs=[pl.BlockSpec(memory_space=pltpu.SMEM), vmem, vmem, vmem],
        out_specs=[vmem, vmem],
        out_shape=[
            jax.ShapeDtypeStruct((rows, channels + LANES), bf16),
            hbm((rows, channels), bf16),
        ],
        scratch_shapes=[pltpu.VMEM((LANES, 2 * LANES), f32)],
        compiler_params=params(),
        cost_estimate=cost(2),
        name="pack",
    )(rank, from_hbm(in_weight), from_hbm(bc_weight), step_t)


def columns_kernel(rank_ref, *refs, count):
    pieces, (full_ref, full_t_ref) = refs[:count], refs[count:]
    for r, piece in enumerate(pieces):
        width = piece.shape[1]
        start = pl.multiple_of((rank_ref[0] ^ r) * width, LANES)
        value = piece[...]
        full_ref[:, pl.ds(start, width)] = value
        full_t_ref[pl.ds(start, width), :] = value.T


def join_columns(pieces, rank):
    tokens, width = pieces[0].shape
    depth = width * len(pieces)
    return pl.pallas_call(
        functools.partial(columns_kernel, count=len(pieces)),
        grid=(tokens // TILE,),
        in_specs=[pl.BlockSpec(memory_space=pltpu.SMEM)] + [pl.BlockSpec((TILE, width), lambda i: (i, 0))] * len(pieces),
        out_specs=[pl.BlockSpec((TILE, depth), lambda i: (i, 0)), pl.BlockSpec((depth, TILE), lambda i: (0, i))],
        out_shape=[jax.ShapeDtypeStruct((tokens, depth), bf16), jax.ShapeDtypeStruct((depth, tokens), bf16)],
        compiler_params=params(),
        cost_estimate=cost(12),
        name="join_columns",
    )(rank, *pieces)


def rows_kernel(rank_ref, *refs, count):
    pieces, full_ref = refs[:count], refs[count]
    for r, piece in enumerate(pieces):
        rows = piece.shape[0]
        full_ref[pl.ds(pl.multiple_of((rank_ref[0] ^ r) * rows, rows), rows), :] = piece[...]


def join_rows(pieces, rank):
    rows, width = pieces[0].shape
    shape = (rows * len(pieces), width)
    return pl.pallas_call(
        functools.partial(rows_kernel, count=len(pieces)),
        in_specs=[pl.BlockSpec(memory_space=pltpu.SMEM)] + [pl.BlockSpec(memory_space=pltpu.VMEM)] * len(pieces),
        out_specs=pl.BlockSpec(memory_space=pltpu.VMEM),
        out_shape=jax.ShapeDtypeStruct(shape, pieces[0].dtype),
        compiler_params=params(),
        cost_estimate=cost(0.1),
        name="join_rows",
    )(rank, *pieces)


def small_kernel(rank_ref, *refs, count):
    pieces, (small_ref, bc_ref, step_ref, scratch) = refs[:count], refs[count:]
    share = pieces[0].shape[0]
    for r, piece in enumerate(pieces):
        scratch[pl.ds(pl.multiple_of((rank_ref[0] ^ r) * share, share), share), :] = piece[...].astype(f32)
    bc_ref[...] = scratch[...].T
    turned = small_ref[...].T
    lane = lax.broadcasted_iota(jnp.int32, turned.shape, 1)
    step_ref[...] = jnp.where(lane < LANES - share, pltpu.roll(turned, LANES - share, 1), 0.0)


def join_small(pieces, small, rank):
    share, tokens = pieces[0].shape
    width = share * len(pieces)
    return pl.pallas_call(
        functools.partial(small_kernel, count=len(pieces)),
        grid=(tokens // TILE,),
        in_specs=[pl.BlockSpec(memory_space=pltpu.SMEM)]
        + [pl.BlockSpec((share, TILE), lambda i: (0, i))] * len(pieces)
        + [pl.BlockSpec((LANES, TILE), lambda i: (0, i))],
        out_specs=[pl.BlockSpec((TILE, width), lambda i: (i, 0)), pl.BlockSpec((TILE, LANES), lambda i: (i, 0))],
        out_shape=[jax.ShapeDtypeStruct((tokens, width), f32), jax.ShapeDtypeStruct((tokens, LANES), f32)],
        scratch_shapes=[pltpu.VMEM((width, TILE), f32)],
        compiler_params=params(),
        cost_estimate=cost(0.1),
        name="join_small",
    )(rank, *pieces, small)


def project_small_kernel(idx_ref, lhs_ref, *refs, count):
    pieces, (small_ref, share_ref, w_ref, wt_ref) = refs[:count], refs[count:]

    @pl.when(pl.program_id(0) == 0)
    def _():
        fill(w_ref, pieces, idx_ref)
        wt_ref[...] = w_ref[...].T[0:wt_ref.shape[0], :]

    small = dot_nn(lhs_ref[...], w_ref[...]).T
    small_ref[...] = small
    share_ref[...] = small[0:share_ref.shape[0], :].astype(bf16)


def project_small(lhs, pieces, idx, share):
    tokens, depth = lhs.shape
    count, last = len(pieces), pieces[0].shape[1] // LANES - 1
    whole = lambda i: (0, 0)
    return pl.pallas_call(
        functools.partial(project_small_kernel, count=count),
        grid=(tokens // TILE,),
        in_specs=[pl.BlockSpec(memory_space=pltpu.SMEM), pl.BlockSpec((TILE, depth), lambda i: (i, 0))]
        + [pl.BlockSpec((p.shape[0], LANES), lambda i: (0, last)) for p in pieces],
        out_specs=[
            pl.BlockSpec((LANES, TILE), lambda i: (0, i)),
            pl.BlockSpec((share, TILE), lambda i: (0, i)),
            pl.BlockSpec((depth, LANES), whole),
            pl.BlockSpec((share, depth), whole),
        ],
        out_shape=[
            jax.ShapeDtypeStruct((LANES, tokens), f32),
            jax.ShapeDtypeStruct((share, tokens), bf16),
            hbm((depth, LANES), bf16),
            jax.ShapeDtypeStruct((share, depth), bf16),
        ],
        compiler_params=params(),
        cost_estimate=cost(20),
        name="project_small",
    )(idx, lhs, *pieces)


def project_kernel(idx_ref, lhs_ref, *refs, count):
    pieces, (x_ref, w_ref) = refs[:count], refs[count:]

    @pl.when(pl.program_id(0) == 0)
    def _():
        fill(w_ref, pieces, idx_ref)

    x_ref[...] = dot_nn(lhs_ref[...], w_ref[...])


def project(lhs, pieces, idx, channels):
    tokens, depth = lhs.shape
    whole = lambda i: (0, 0)
    return pl.pallas_call(
        functools.partial(project_kernel, count=len(pieces)),
        grid=(tokens // TILE,),
        in_specs=[pl.BlockSpec(memory_space=pltpu.SMEM), pl.BlockSpec((TILE, depth), lambda i: (i, 0))]
        + [pl.BlockSpec((p.shape[0], channels), whole) for p in pieces],
        out_specs=[pl.BlockSpec((TILE, channels), lambda i: (i, 0)), pl.BlockSpec((depth, channels), whole)],
        out_shape=[
            hbm((tokens, channels), f32),
            hbm((depth, channels), bf16),
        ],
        compiler_params=params(),
        cost_estimate=cost(0.1),
        name="project",
    )(idx, lhs, *pieces)


def column_to_row(col):
    return jnp.broadcast_to(col, (col.shape[0], LANES)).T[0:8, :]


def row_to_column(row):
    return jnp.broadcast_to(row, (LANES, row.shape[1])).T[:, 0:1]


def gate_kernel(idx_ref, lhs_ref, mixed_ref, *refs, count):
    pieces, (gate_ref, sums_ref, w_ref) = refs[:count], refs[count:]

    @pl.when(pl.program_id(0) == 0)
    def _():
        fill(w_ref, pieces, idx_ref)

    gate = dot_nn(lhs_ref[...], w_ref[...])
    gate_ref[...] = gate
    gated = mixed_ref[...] * (gate * sigmoid(gate))
    sums_ref[...] = column_to_row(jnp.sum(gated * gated, axis=1, keepdims=True))


def gate_forward(lhs, mixed, pieces, idx):
    tokens, depth = lhs.shape
    channels = mixed.shape[1]
    whole = lambda i: (0, 0)
    now = lambda i: (i, 0)
    return pl.pallas_call(
        functools.partial(gate_kernel, count=len(pieces)),
        grid=(tokens // TILE,),
        in_specs=[
            pl.BlockSpec(memory_space=pltpu.SMEM),
            pl.BlockSpec((TILE, depth), now),
            pl.BlockSpec((TILE, channels), now),
        ]
        + [pl.BlockSpec(p.shape, whole) for p in pieces],
        out_specs=[
            pl.BlockSpec((TILE, channels), now),
            pl.BlockSpec((8, TILE), lambda i: (0, i)),
            pl.BlockSpec((depth, channels), whole),
        ],
        out_shape=[
            jax.ShapeDtypeStruct((tokens, channels), f32),
            jax.ShapeDtypeStruct((8, tokens), f32),
            hbm((depth, channels), bf16),
        ],
        compiler_params=params(),
        cost_estimate=cost(0.1),
        name="gate_forward",
    )(idx, lhs, from_hbm(mixed), *pieces)


def gated_kernel(gate_ref, mixed_ref, square_ref, conv_ref, out_ref, *, inner_total):
    gate = gate_ref[...]
    scale = lax.rsqrt(row_to_column(square_ref[0:1, :]) / inner_total + EPSILON)
    gated = mixed_ref[...] * (gate * sigmoid(gate))
    out_ref[...] = (gated * scale * conv_ref[5:6, :]).astype(bf16)


def gated_norm(gate, mixed, square, conv_rows, inner_total):
    tokens, channels = gate.shape
    block = pl.BlockSpec((TILE, channels), lambda i: (i, 0))
    return pl.pallas_call(
        functools.partial(gated_kernel, inner_total=inner_total),
        grid=(tokens // TILE,),
        in_specs=[block, block, pl.BlockSpec((8, TILE), lambda i: (0, i)), pl.BlockSpec((8, channels), lambda i: (0, 0))],
        out_specs=block,
        out_shape=jax.ShapeDtypeStruct((tokens, channels), bf16),
        compiler_params=params(),
        cost_estimate=cost(0.1),
        name="gated_norm",
    )(gate, mixed, square, conv_rows)


def gout_kernel(idx_ref, cot_ref, gate_ref, mixed_ref, conv_ref, *refs, count):
    pieces, (gout_ref, sums_ref, w_ref) = refs[:count], refs[count:]

    @pl.when(pl.program_id(0) == 0)
    def _():
        fill(w_ref, pieces, idx_ref)

    gout = dot_nn(cot_ref[...], w_ref[...])
    gout_ref[...] = gout
    gate = gate_ref[...]
    gated = mixed_ref[...] * (gate * sigmoid(gate))
    sums_ref[...] = column_to_row(jnp.sum(gout * conv_ref[5:6, :] * gated, axis=1, keepdims=True))


def grad_gout(cot, gate, mixed, conv_rows, pieces, idx):
    tokens, depth = cot.shape
    channels = mixed.shape[1]
    whole = lambda i: (0, 0)
    now = lambda i: (i, 0)
    return pl.pallas_call(
        functools.partial(gout_kernel, count=len(pieces)),
        grid=(tokens // TILE,),
        in_specs=[
            pl.BlockSpec(memory_space=pltpu.SMEM),
            pl.BlockSpec((TILE, depth), now),
            pl.BlockSpec((TILE, channels), now),
            pl.BlockSpec((TILE, channels), now),
            pl.BlockSpec((8, channels), whole),
        ]
        + [pl.BlockSpec(p.shape, whole) for p in pieces],
        out_specs=[
            pl.BlockSpec((TILE, channels), now),
            pl.BlockSpec((8, TILE), lambda i: (0, i)),
            pl.BlockSpec((depth, channels), whole),
        ],
        out_shape=[
            jax.ShapeDtypeStruct((tokens, channels), f32),
            jax.ShapeDtypeStruct((8, tokens), f32),
            jax.ShapeDtypeStruct((depth, channels), bf16),
        ],
        compiler_params=params(),
        cost_estimate=cost(20),
        name="grad_gout",
    )(idx, cot, gate, mixed, conv_rows, *pieces)


def gate_back_kernel(gate_ref, gout_ref, mixed_ref, square_ref, inner_ref, conv_ref, dmixed_ref, dgate_ref, dgain_ref, *, inner_total):
    gate, gout, mixed = gate_ref[...], gout_ref[...], mixed_ref[...]
    gain = conv_ref[5:6, :]
    square, inner = row_to_column(square_ref[0:1, :]), row_to_column(inner_ref[0:1, :])
    scale = lax.rsqrt(square / inner_total + EPSILON)
    sg = sigmoid(gate)
    act = gate * sg
    gated = mixed * act
    dgated = scale * (gain * gout) - gated * (scale * scale * scale * inner / inner_total)
    dmixed_ref[...] = (dgated * act).astype(bf16)
    dgate_ref[...] = (dgated * mixed * sg * (1.0 + gate * (1.0 - sg))).astype(bf16)

    @pl.when(pl.program_id(0) == 0)
    def _():
        dgain_ref[...] = jnp.zeros_like(dgain_ref)

    dgain_ref[5:6, :] += jnp.sum(gout * gated * scale, axis=0, keepdims=True)


def gate_backward(gate, gout, mixed, square, inner, conv_rows, inner_total):
    tokens, channels = gate.shape
    whole = lambda i: (0, 0)
    block = pl.BlockSpec((TILE, channels), lambda i: (i, 0))
    row = pl.BlockSpec((8, TILE), lambda i: (0, i))
    return pl.pallas_call(
        functools.partial(gate_back_kernel, inner_total=inner_total),
        grid=(tokens // TILE,),
        in_specs=[block, block, block, row, row, pl.BlockSpec((8, channels), whole)],
        out_specs=[block, block, pl.BlockSpec((8, channels), whole)],
        out_shape=[
            jax.ShapeDtypeStruct((tokens, channels), bf16),
            jax.ShapeDtypeStruct((tokens, channels), bf16),
            jax.ShapeDtypeStruct((8, channels), f32),
        ],
        compiler_params=params(),
        cost_estimate=cost(0.1),
        name="gate_backward",
    )(from_hbm(gate), from_hbm(gout), from_hbm(mixed), square, inner, conv_rows)


def weight_grad_kernel(idx_ref, lhs_ref, rhs_ref, *refs, rows, turned):
    outs, scratch = refs[:-1], refs[-1]
    at = pl.program_id(0)
    scratch[pl.ds(pl.multiple_of(at * TILE_D, TILE_D), TILE_D), :] = (dot_nt if turned else dot_nn)(
        lhs_ref[...], rhs_ref[...]
    ).astype(bf16)

    @pl.when(at == pl.num_programs(0) - 1)
    def _():
        s = 0
        for out in outs:
            for b in range(out.shape[0] // rows):
                start = pl.multiple_of(idx_ref[s] * rows, rows)
                out[b * rows:(b + 1) * rows, :] = scratch[pl.ds(start, rows), :]
                s += 1


def weight_grad(lhs_t, rhs, idx, sizes, us=0.1, turned=False):
    depth, tokens = lhs_t.shape
    width = rhs.shape[0 if turned else 1]
    rows = depth // idx.shape[0]
    whole = lambda i: (0, 0)
    return pl.pallas_call(
        functools.partial(weight_grad_kernel, rows=rows, turned=turned),
        grid=(depth // TILE_D,),
        in_specs=[
            pl.BlockSpec(memory_space=pltpu.SMEM),
            pl.BlockSpec((TILE_D, tokens), lambda i: (i, 0)),
            pl.BlockSpec(rhs.shape, whole),
        ],
        out_specs=[pl.BlockSpec((size * rows, width), whole) for size in sizes],
        out_shape=[hbm((size * rows, width), bf16) for size in sizes],
        scratch_shapes=[pltpu.VMEM((depth, width), bf16)],
        compiler_params=params(),
        cost_estimate=cost(us),
        name="weight_grad",
    )(idx, lhs_t, rhs)


def out_kernel(rank_ref, lhs_ref, w_ref, *outs):
    product = dot_nt(lhs_ref[...], w_ref[...]).astype(bf16)
    for r, out in enumerate(outs):
        @pl.when(pl.program_id(0) == r)
        def _():
            out[...] = product


def out_partial(gated_out, w_out, rank, ranks):
    tokens, channels = gated_out.shape
    depth = w_out.shape[0]
    width = depth // ranks
    whole = lambda i, rank_ref: (0, 0)
    return pl.pallas_call(
        out_kernel,
        grid_spec=pltpu.PrefetchScalarGridSpec(
            num_scalar_prefetch=1,
            grid=(ranks,),
            in_specs=[
                pl.BlockSpec((tokens, channels), whole),
                pl.BlockSpec((width, channels), lambda i, rank_ref: (i ^ rank_ref[0], 0)),
            ],
            out_specs=[pl.BlockSpec((tokens, width), whole)] * ranks,
        ),
        out_shape=[hbm((tokens, width), bf16)] * ranks,
        compiler_params=params(),
        cost_estimate=cost(0.1),
        name="out_partial",
    )(rank, gated_out, w_out)


def term_kernel(rank_ref, gx_ref, wx_ref, gg_ref, wg_ref, gs_ref, ws_ref, gb_ref, wbt_ref, hidden_ref, inv_ref, *refs, apart):
    dgain_ref, outs = refs[-1], refs[:-1]
    gain = None
    for r, out in zip(apart, outs):
        rows = out.shape[0]
        span = pl.ds(pl.multiple_of((rank_ref[0] ^ r) * rows, rows), rows)
        total = dot_nt(gx_ref[span, :], wx_ref[...]) + dot_nt(gg_ref[span, :], wg_ref[...])
        total = total + dot_nt(gs_ref[span, :], ws_ref[...]) + dot_nn(gb_ref[span, :], wbt_ref[...])
        out[...] = total.astype(bf16)
        normed = hidden_ref[span, :].astype(f32) * row_to_column(inv_ref[0:1, span])
        own = jnp.sum(total * normed, axis=0, keepdims=True)
        gain = own if gain is None else gain + own
    cut = [gain[:, i:i + LANES] for i in range(0, gain.shape[1], LANES)]
    dgain_ref[...] = jnp.concatenate(cut + [jnp.zeros((8 - len(cut), LANES), f32)], axis=0)


def normed_term(dx, dgate, dstep, dbc, w_a, w_b, w_s, w_bct, hidden, inv_rms, rank, ranks, apart):
    tokens, channels = dx.shape
    depth = w_a.shape[0]
    rows = tokens // ranks
    whole = lambda i: (0, 0)
    return pl.pallas_call(
        functools.partial(term_kernel, apart=apart),
        grid=(depth // TILE_D,),
        in_specs=[
            pl.BlockSpec(memory_space=pltpu.SMEM),
            pl.BlockSpec(dx.shape, whole),
            pl.BlockSpec((TILE_D, channels), lambda i: (i, 0)),
            pl.BlockSpec(dgate.shape, whole),
            pl.BlockSpec((TILE_D, channels), lambda i: (i, 0)),
            pl.BlockSpec(dstep.shape, whole),
            pl.BlockSpec((TILE_D, LANES), lambda i: (i, 0)),
            pl.BlockSpec(dbc.shape, whole),
            pl.BlockSpec((w_bct.shape[0], TILE_D), lambda i: (0, i)),
            pl.BlockSpec((tokens, TILE_D), lambda i: (0, i)),
            pl.BlockSpec(inv_rms.shape, whole),
        ],
        out_specs=[pl.BlockSpec((rows, TILE_D), lambda i: (0, i))] * len(apart) + [pl.BlockSpec((8, LANES), lambda i: (i, 0))],
        out_shape=[jax.ShapeDtypeStruct((rows, depth), bf16)] * len(apart)
        + [jax.ShapeDtypeStruct((8 * (depth // TILE_D), LANES), f32)],
        compiler_params=params(32),
        cost_estimate=cost(20 if 2 in apart else 0.1),
        name="normed_term",
    )(
        rank, dx, from_hbm(w_a), dgate, from_hbm(w_b), dstep, from_hbm(w_s), dbc,
        from_hbm(w_bct), from_hbm(hidden), inv_rms,
    )


def norm_back_kernel(rank_ref, a_ref, b_ref, hidden_ref, cot_ref, gain_ref, out_ref):
    grad = a_ref[...].astype(f32) + b_ref[...].astype(f32)
    inputs = hidden_ref[...].astype(f32)
    inv_rms = lax.rsqrt(jnp.mean(inputs * inputs, axis=1, keepdims=True) + EPSILON)
    normed = inputs * inv_rms
    scaled = grad * gain_ref[0:1, :]
    mean = jnp.mean(scaled * normed, axis=1, keepdims=True)
    out_ref[...] = (inv_rms * (scaled - normed * mean) + cot_ref[...].astype(f32)).astype(out_ref.dtype)


def norm_backward(a, b, hidden, cot, gain_rows, rank):
    rows, depth = a.shape
    mine = lambda i, rank_ref: (rank_ref[0], 0)
    whole = lambda i, rank_ref: (0, 0)
    return pl.pallas_call(
        norm_back_kernel,
        grid_spec=pltpu.PrefetchScalarGridSpec(
            num_scalar_prefetch=1,
            grid=(1,),
            in_specs=[
                pl.BlockSpec((rows, depth), whole),
                pl.BlockSpec((rows, depth), whole),
                pl.BlockSpec((rows, depth), mine),
                pl.BlockSpec((rows, depth), mine),
                pl.BlockSpec((8, depth), whole),
            ],
            out_specs=pl.BlockSpec((rows, depth), whole),
        ),
        out_shape=jax.ShapeDtypeStruct((rows, depth), bf16),
        compiler_params=params(),
        cost_estimate=cost(0.1),
        name="norm_backward",
    )(rank, a, b, from_hbm(hidden), from_hbm(cot), gain_rows)


def moved(weight, moment, grad):
    fresh = 0.5 * moment + 0.5 * grad
    return fresh, weight - LEARN_RATE * fresh - LEARN_RATE * DECAY_RATE * weight


def add_up(refs):
    total = refs[0][...].astype(f32)
    for ref in refs[1:]:
        total = total + ref[...].astype(f32)
    return total


def update_in_kernel(w_ref, m_ref, *refs, count):
    gate_refs, x_refs, (m_out, w_out) = refs[:count], refs[count:2 * count], refs[2 * count:]
    for at, parts in ((0, gate_refs), (1, x_refs)):
        fresh, weight = moved(w_ref[:, at, :], m_ref[:, at, :], add_up(parts))
        m_out[:, at, :] = fresh
        w_out[:, at, :] = weight


def update_in(weight, moment, gate_parts, x_parts):
    rows, _, channels = weight.shape
    size = min(rows, 48)
    full = pl.BlockSpec((size, 2, channels), lambda i: (i, 0, 0))
    parts = [*gate_parts, *x_parts]
    return pl.pallas_call(
        functools.partial(update_in_kernel, count=len(gate_parts)),
        grid=(rows // size,),
        in_specs=[full, full] + [pl.BlockSpec((size, channels), functools.partial(lambda at, i: (i, at), at)) for _, at in parts],
        out_specs=[full, full],
        out_shape=[jax.ShapeDtypeStruct(weight.shape, f32)] * 2,
        compiler_params=params(),
        cost_estimate=cost(0.1),
        name="update_in",
    )(from_hbm(weight), from_hbm(moment), *[part for part, _ in parts])


def update_small_kernel(w_ref, m_ref, sums_ref, own_ref, back_ref, *refs, share, order, shared):
    alone, late, (m_out, w_out, exchange, totals, scratch) = refs[:order[0]], refs[order[0]:-5], refs[-5:]
    heads, rows = w_ref.shape
    count = sums_ref.shape[0]
    last = late[0].shape[1] - LANES
    grad = own_ref[...].astype(f32) + back_ref[...].astype(f32)
    found = {0: sums_ref[...].astype(f32)}
    for at, ref in zip(order[1], alone):
        grad = grad + ref[0:rows, :].astype(f32)
        found[at] = ref[rows:, :].astype(f32)
    for at, ref in zip(order[2], late):
        grad = grad + ref[0:rows, last:].astype(f32)
        tail = ref[rows:, :].astype(f32)
        found[at] = jnp.concatenate([tail[:, i:i + LANES] for i in range(0, tail.shape[1], LANES)], axis=0)
    step = len(found) // 2
    while step >= 1:
        found = {i: found[i] + found[i + step] for i in range(step)}
        step //= 2
    totals[...] = found[0]
    exchange[0:rows, :] = grad
    exchange[rows:, :] = found[0][shared[0]:shared[1], :]
    scratch[0:rows, :] = grad
    turned = scratch[...].T[share:share + heads, 0:rows]
    fresh, weight = moved(w_ref[...], m_ref[...], turned)
    m_out[...] = fresh
    w_out[...] = weight


def update_small(weight_t, moment_t, sums, own, back, alone, late, order, shared, share):
    rows = weight_t.shape[1]
    count = sums.shape[0]
    whole = lambda i: (0, 0)
    spec = pl.BlockSpec(weight_t.shape, whole)
    return pl.pallas_call(
        functools.partial(update_small_kernel, share=share, order=order, shared=shared),
        grid=(1,),
        in_specs=[spec, spec, pl.BlockSpec(sums.shape, whole)] + [pl.BlockSpec((rows, LANES), whole)] * 2
        + [pl.BlockSpec(v.shape, whole) for v in (*alone, *late)],
        out_specs=[
            spec, spec,
            pl.BlockSpec((rows + shared[1] - shared[0], LANES), whole),
            pl.BlockSpec((count, LANES), whole),
        ],
        out_shape=[jax.ShapeDtypeStruct(weight_t.shape, f32)] * 2
        + [jax.ShapeDtypeStruct((rows + shared[1] - shared[0], LANES), f32), jax.ShapeDtypeStruct((count, LANES), f32)],
        scratch_shapes=[pltpu.VMEM((2 * LANES, LANES), f32)],
        compiler_params=params(),
        cost_estimate=cost(0.1),
        name="update_small",
    )(weight_t, moment_t, sums, own, back, *alone, *late)


def update_bc_kernel(rank_ref, w_ref, m_ref, *refs):
    pieces, (m_out, w_out, shared_out) = refs[:-3], refs[-3:]
    rows, width = w_ref.shape
    share = width // len(pieces)
    shared_out[...] = (pieces[0][rows:, :] + pieces[1][rows:, :]) + (pieces[2][rows:, :] + pieces[3][rows:, :])
    lane = lax.broadcasted_iota(jnp.int32, (rows, LANES), 1)
    for pair in range(width // LANES):
        halves = []
        for member in (2 * pair, 2 * pair + 1):
            own = pieces[0][0:rows, :]
            for r in range(1, len(pieces)):
                own = jnp.where((rank_ref[0] ^ r) == member, pieces[r][0:rows, :], own)
            halves.append(own)
        grad = jnp.where(lane < share, halves[0], pltpu.roll(halves[1], share, 1))
        span = slice(pair * LANES, (pair + 1) * LANES)
        fresh, weight = moved(w_ref[:, span], m_ref[:, span], grad)
        m_out[:, span] = fresh
        w_out[:, span] = weight


def update_bc(weight, moment, pieces, rank):
    vmem = pl.BlockSpec(memory_space=pltpu.VMEM)
    return pl.pallas_call(
        update_bc_kernel,
        in_specs=[pl.BlockSpec(memory_space=pltpu.SMEM)] + [vmem] * (2 + len(pieces)),
        out_specs=[vmem] * 3,
        out_shape=[jax.ShapeDtypeStruct(weight.shape, f32)] * 2
        + [jax.ShapeDtypeStruct((pieces[0].shape[0] - weight.shape[0], LANES), f32)],
        compiler_params=params(),
        cost_estimate=cost(0.1),
        name="update_bc",
    )(rank, weight, moment, *pieces)


def fence(*values):
    leaves, tree = jax.tree.flatten(values)
    return jax.tree.unflatten(tree, lax.optimization_barrier(leaves))


def outer_from(v, k):
    n = lax.axis_size("dp") // 2
    return lax.ppermute(v, "dp", [(((o + k) % n) * 2 + x, o * 2 + x) for o in range(n) for x in range(2)])


def outer_flip(v, bit):
    n = lax.axis_size("dp") // 2
    return lax.ppermute(v, "dp", [((o ^ bit) * 2 + x, o * 2 + x) for o in range(n) for x in range(2)])


def inner_flip(v):
    return lax.ppermute(v, "dp", [(d ^ 1, d) for d in range(lax.axis_size("dp"))])


def rank_flip(v, bit):
    return lax.ppermute(v, "mp", [(m ^ bit, m) for m in range(lax.axis_size("mp"))])


def hops(n):
    order = []
    for k in range(1, n // 2 + 1):
        order.append(k)
        if n - k != k:
            order.append(n - k)
    return order


def pair_sum(a, b):
    return (a.astype(f32) + b.astype(f32)).astype(bf16)


def outer_blocks(own, here, back, ks):
    rows = own.shape[0]
    back = [part[i:i + rows] for part in back for i in range(0, part.shape[0], rows)]
    return [
        (here[i * rows:(i + 1) * rows].astype(f32) + back[i].astype(f32)).astype(bf16) for i in range(len(ks))
    ]


def outer_send(blocks, ks):
    n = lax.axis_size("dp") // 2
    return [outer_from(block, n - k) for block, k in zip(blocks, ks)]


def outer_sum(v):
    bit = 1
    while bit < lax.axis_size("dp") // 2:
        v = v + outer_flip(v, bit)
        bit *= 2
    return v


def mp_sum(v):
    v = v + rank_flip(v, 1)
    return v + rank_flip(v, 2)


def mp_sum_direct(v):
    return (v + rank_flip(v, 1)) + (rank_flip(v, 2) + rank_flip(v, 3))


def mp_reduce(blocks):
    far = blocks[2].astype(f32) + rank_flip(blocks[3], 1).astype(f32)
    near = blocks[0].astype(f32) + rank_flip(blocks[1], 1).astype(f32)
    return near, rank_flip(far.astype(bf16), 2)


def mp_pieces(v):
    far = rank_flip(v, 2)
    return [v, rank_flip(v, 1), far, rank_flip(far, 1)]


def in_rank_order(pieces, rank, axis):
    odd, high = (rank & 1) == 1, (rank & 2) == 2
    join = lambda a, b: jnp.concatenate([a, b], axis=axis)
    low = jnp.where(odd, join(pieces[1], pieces[0]), join(pieces[0], pieces[1]))
    far = jnp.where(odd, join(pieces[3], pieces[2]), join(pieces[2], pieces[3]))
    return jnp.where(high, join(far, low), join(low, far))


def momentum(moment, grad):
    return 0.5 * moment + 0.5 * grad


def advance(weight, moment, grad):
    fresh = momentum(moment, grad)
    return (fresh, weight - LEARN_RATE * fresh - LEARN_RATE * DECAY_RATE * weight)


def body(
    hidden, segments, cotangent, in_weight, in_moment, bc_weight, bc_moment, step_weight, step_moment,
    out_weight, out_moment, conv_table, conv_moment, bc_table, bc_table_moment, head_table, head_moment,
    norm_gain, gain_moment,
):
    size = lax.axis_size("dp")
    ranks = lax.axis_size("mp")
    n = size // 2
    place, rank = lax.axis_index("dp"), lax.axis_index("mp")
    outer, inner = place // 2, place % 2
    rank1 = rank.reshape(1).astype(jnp.int32)
    rows, _, channels = in_weight.shape
    heads = head_table.shape[1]
    tokens, depth = hidden.shape
    share = bc_weight.shape[1] // ranks

    ks = hops(n)
    near_ks, far_k = ks[:-1], ks[-1]

    def members(order):
        return jnp.stack([((outer + k) % n) * 2 + (inner ^ j) for k, j in order]).astype(jnp.int32)

    first = [(0, 0), (0, 1)]
    idx = members(first + [(k, 0) for k in ks] + [(k, 1) for k in ks])
    idx_s = members([(0, 0)] + [(k, 0) for k in ks] + [(0, 1)] + [(k, 1) for k in ks])
    sizes = (1, 1, n - 1, n - 1)
    split_sizes = (1, 1, n - 1, n - 2, 1)
    width = depth // ranks

    set_a, set_b = pack(in_weight, bc_weight, step_weight.T, rank1)
    set_c = out_weight.T.astype(bf16)

    def blocks(own, z, x):
        return [own, x[0]] + [z[k] for k in ks] + [x[k] for k in ks]

    def block(v, i):
        return v[i * rows:(i + 1) * rows]

    def blocks(own, z, x):
        return [own, x[0]] + [z[k] for k in ks] + [x[k] for k in ks]

    def block(v, i):
        return v[i * rows:(i + 1) * rows]

    def total(own, own_got, got):
        value = own.astype(f32) + own_got.astype(f32)
        for part in got:
            value = value + part.astype(f32)
        return value

    def outer_all(v, some):
        return {k: outer_from(v, k) for k in some}

    def flip_all(z, some):
        return {k: inner_flip(z[k]) for k in some}

    a_z = outer_all(set_a, near_ks)
    a_x = {0: inner_flip(set_a)}
    far_a, a_x[0] = fence(set_a, a_x[0])
    a_z[far_k] = outer_from(far_a, far_k)
    cot_far = rank_flip(cotangent, 2)
    gain_rows = pad_rows(norm_gain[None])
    normed_low, normed_t, inv_rms = prepare(hidden, gain_rows)
    a_x.update(flip_all(a_z, near_ks))
    aux, seg_row = segment_facts(segments)
    head_rows = pad_lanes(pad_rows(head_table))
    facts = (aux, seg_row, pad_rows(conv_table), pad_rows(bc_table), head_rows, *head_expand(channels))
    set_a, set_b, set_c, a_z, a_x, cot_far, normed_low, normed_t, inv_rms, facts = fence(
        set_a, set_b, set_c, a_z, a_x, cot_far, normed_low, normed_t, inv_rms, facts
    )

    a_x[far_k] = inner_flip(a_z[far_k])
    b_x = {0: inner_flip(set_b)}
    b_z = outer_all(set_b, near_ks)
    cot, cot_t = join_columns([cotangent, rank_flip(cotangent, 1), cot_far, rank_flip(cot_far, 1)], rank1)
    set_b, set_c, b_z, b_x, a_z, a_x, cot, cot_t, normed_low = fence(
        set_b, set_c, b_z, b_x, a_z, a_x, cot, cot_t, normed_low
    )

    b_z[far_k] = outer_from(set_b, far_k)
    b_x.update(flip_all(b_z, near_ks[:1]))
    c_x = {0: inner_flip(set_c)}
    a_blocks = blocks(set_a, a_z, a_x)
    small, bc_share, w_s, w_bct_share = project_small(normed_low, a_blocks, idx, share)
    bc_pieces = mp_pieces(bc_share)
    x_pre, w_a = project(normed_low, a_blocks, idx, channels)
    bc_pieces, x_pre, small, set_c, w_bct_share, w_s = fence(bc_pieces, x_pre, small, set_c, w_bct_share, w_s)
    bc_pre, step_pre = join_small(bc_pieces, small, rank1)
    set_c, b_z, b_x, c_x, x_pre, bc_pre, step_pre, w_bct_share = fence(
        set_c, b_z, b_x, c_x, x_pre, bc_pre, step_pre, w_bct_share
    )

    c_z = outer_all(set_c, near_ks)
    b_x.update(flip_all(b_z, ks[1:]))
    kept = ssd_forward(x_pre, bc_pre, step_pre, *facts[:-1])
    mixed = kept[0]
    mixed, b_x, b_z, c_z, c_x, w_bct_share, set_c = fence(mixed, b_x, b_z, c_z, c_x, w_bct_share, set_c)

    c_z[far_k] = outer_from(set_c, far_k)
    c_x.update(flip_all(c_z, near_ks))
    gate_pre, square, w_b = gate_forward(normed_low, mixed, blocks(set_b, b_z, b_x), idx)
    square = mp_sum_direct(square)
    mixed, gate_pre, square, w_b, w_bct_share, c_z, c_x = fence(mixed, gate_pre, square, w_b, w_bct_share, c_z, c_x)

    c_x[far_k] = inner_flip(c_z[far_k])
    w_bct = [w_bct_share, rank_flip(w_bct_share, 2)]
    conv_rows = facts[2]
    gated_out = gated_norm(gate_pre, mixed, square, conv_rows, channels * ranks)
    gc_own, gc_own1, gc_here, gc_near, gc_far = weight_grad(cot_t, gated_out, idx, split_sizes)
    c_x, square, gated_out, gc_own, gc_own1, gc_here, gc_near, gc_far, w_bct = fence(
        c_x, square, gated_out, gc_own, gc_own1, gc_here, gc_near, gc_far, w_bct
    )

    gc_far_back, gc_near_back = inner_flip(gc_far), inner_flip(gc_near)
    gout, inner_dot, w_c = grad_gout(cot, gate_pre, mixed, conv_rows, blocks(set_c, c_z, c_x), idx)
    gout, inner_dot, w_c = fence(gout, inner_dot, w_c)
    inner_dot = mp_sum_direct(inner_dot)
    partial = out_partial(gated_out, w_c, rank1, ranks)
    inner_dot, gout, partial, w_bct, gc_far_back = fence(inner_dot, gout, partial, w_bct, gc_far_back)
    c_far_got = outer_from(pair_sum(block(gc_here, n - 2), gc_far_back), n - far_k)
    out_back = rank_flip(partial[3], 1)
    w_bct = [w_bct[0], rank_flip(w_bct[0], 1), w_bct[1], rank_flip(w_bct[1], 1)]
    dmixed, dgate, dgain = gate_backward(gate_pre, gout, mixed, square, inner_dot, conv_rows, channels * ranks)
    gb_own, gb_own1, gb_here, gb_send = weight_grad(normed_t, dgate, idx, sizes)
    gc_near_back, c_far_got, w_bct, out_back, gb_own, gb_own1, gb_here, gb_send, partial, dmixed, dgain = fence(
        gc_near_back, c_far_got, w_bct, out_back, gb_own, gb_own1, gb_here, gb_send, partial, dmixed, dgain
    )
    c_blocks = [pair_sum(block(gc_here, i), block(gc_near_back, i)) for i in range(n - 2)]
    out_far = pair_sum(partial[2], out_back)
    w_bct = join_rows(w_bct, rank1)
    c_blocks, out_far, w_bct, dmixed, gb_send = fence(c_blocks, out_far, w_bct, dmixed, gb_send)

    c_got = outer_send(c_blocks, near_ks) + [c_far_got]
    gb_back = inner_flip(gb_send)
    out_got = rank_flip(out_far, 2)
    dx, dbc, dbc_keep, dbc_send, dstep, dstep_t, dconv, dbct_part, dheads = ssd_backward(
        rank1, x_pre, bc_pre, step_pre, *facts, dmixed, kept
    )
    c_got, gb_back, out_got, dx, dbc, dbc_keep, dbc_send, dstep, dstep_t, dconv, dbct_part, dheads = fence(
        c_got, gb_back, out_got, dx, dbc, dbc_keep, dbc_send, dstep, dstep_t, dconv, dbct_part, dheads
    )

    b_got = {far_k: outer_from(pair_sum(block(gb_here, n - 2), block(gb_back, n - 2)), n - far_k)}
    dbc_back = rank_flip(dbc_send, 1)
    out_near_back = rank_flip(partial[1], 1)
    ga_own, ga_own1, ga_here, ga_send = weight_grad(normed_t, dx, idx, sizes, us=20)
    ga_own, ga_own1, ga_here, ga_send, dx, dbc_back, gb_back, gb_here, out_near_back = fence(
        ga_own, ga_own1, ga_here, ga_send, dx, dbc_back, gb_back, gb_here, out_near_back
    )

    b_near = [pair_sum(block(gb_here, i), block(gb_back, i)) for i in range(n - 2)]
    b_got.update(zip(near_ks, outer_send(b_near, near_ks)))
    ga_back = inner_flip(ga_send)
    dbc_pair = pair_sum(dbc_keep, dbc_back)
    dbc_got = rank_flip(dbc_pair[share:], 2)
    operands = (dx, dgate, dstep, dbc, w_a, w_b, w_s, w_bct, hidden, inv_rms, rank1, ranks)
    far_own, far_send, gain_far = normed_term(*operands, (2, 3))
    far_own, far_send, gain_far, dx, dbc_got, dbc_pair, dstep_t, b_got[far_k] = fence(
        far_own, far_send, gain_far, dx, dbc_got, dbc_pair, dstep_t, b_got[far_k]
    )
    far_back = rank_flip(far_send, 1)
    operands = (dx, *operands[1:])
    near_own, near_send, gain_near = normed_term(*operands, (0, 1))
    far_back, near_own, near_send, gain_near, ga_back, b_got = fence(
        far_back, near_own, near_send, gain_near, ga_back, b_got
    )
    near_back = rank_flip(near_send, 1)
    far = pair_sum(far_own, far_back)
    a_blocks = [pair_sum(block(ga_here, i), block(ga_back, i)) for i in range(n - 1)]
    dbc_share = pair_sum(dbc_pair[:share], dbc_got)
    dsmall_t = jnp.concatenate([dbc_share, dstep_t, jnp.zeros((LANES - share - 16, tokens), bf16)], axis=0)
    gs_own, gs_here, gs_send = weight_grad(normed_t, dsmall_t, idx_s, (1, n - 1, n), turned=True)
    far, a_blocks, near_back, gs_send, gc_own1, gb_own1 = fence(far, a_blocks, near_back, gs_send, gc_own1, gb_own1)

    early, late = near_ks[:(n - 2) // 2], near_ks[(n - 2) // 2:]
    got = rank_flip(far, 2)
    a_got = dict(zip([far_k, *early], outer_send([a_blocks[-1], *a_blocks[:len(early)]], [far_k, *early])))
    cut = lambda v: [v[:, i:i + LANES] for i in range(0, v.shape[1], LANES)]
    alone = channels // LANES * 8 + 8
    sums = jnp.concatenate([*cut(dconv + dgain), dheads, *cut(dbct_part), gain_far + gain_near], axis=0)
    shared = (alone, sums.shape[0])
    wide = (channels + LANES) // LANES
    sums = pad_rows(sums, -(-sums.shape[0] // (16 * wide)) * 16 * wide).astype(bf16)
    small_back = inner_flip(jnp.concatenate([gs_send, sums], axis=0))
    own_got = inner_flip(jnp.concatenate([gc_own1, gb_own1], axis=1))
    near = near_own.astype(f32) + near_back.astype(f32)
    got, near, a_got, small_back, sums, own_got, ga_own1, a_late = fence(
        got, near, a_got, small_back, sums, own_got, ga_own1, a_blocks[len(early):-1]
    )

    mine = norm_backward(near, got, hidden, cot, gain_rows, rank1)
    mine, small_back, sums, ga_own1, a_late, gs_here, out_got, out_near_back = fence(
        mine, small_back, sums, ga_own1, a_late, gs_here, out_got, out_near_back
    )
    a_own_got = inner_flip(ga_own1)
    gs_back, sums_back = small_back[:n * rows], small_back[n * rows:]
    s_blocks = dict(zip(ks, outer_blocks(gs_own, gs_here, [gs_back[rows:]], ks)))
    sums = pair_sum(sums, sums_back)
    size = sums.shape[0] // wide
    sums_wide = jnp.concatenate([sums[i * size:(i + 1) * size] for i in range(wide)], axis=1)
    late_got = outer_send(
        [
            jnp.concatenate([jnp.concatenate([a_block, s_blocks[k]], axis=1), sums_wide], axis=0)
            for k, a_block in zip(late, a_late)
        ],
        late,
    )
    s_got = outer_send([jnp.concatenate([s_blocks[k], sums], axis=0) for k in (far_k, *early)], (far_k, *early))
    mine_far = rank_flip(mine, 2)
    mine_far, mine = fence(mine_far, mine)
    late_got, s_got, a_own_got, sums = fence(late_got, s_got, a_own_got, sums)

    mine_near, mine_far_near = rank_flip(mine, 1), rank_flip(mine_far, 1)
    step_m, step_w, exchange, totals = update_small(
        step_weight.T, step_moment.T, sums, gs_own, gs_back, s_got, late_got,
        (len(s_got), [n - k for k in (far_k, *early)], [n - k for k in late]), shared, share,
    )
    exchanged = [exchange] + [rank_flip(exchange, r) for r in (1, 2, 3)]
    in_m, in_w = update_in(
        in_weight, in_moment,
        [(gb_own, 0), (own_got, 1)] + [(b_got[k], 0) for k in ks],
        [(ga_own, 0), (a_own_got, 0)] + [(a_got[k], 0) for k in (far_k, *early)] + [(v, 0) for v in late_got],
    )
    input_grad = join_rows([mine, mine_near, mine_far, mine_far_near], rank1)
    bc_m, bc_w, totals_shared = update_bc(bc_weight, bc_moment, exchanged, rank1)

    resid = lax.dynamic_slice_in_dim(hidden, rank * width, width, 1).astype(f32)
    output = (resid + partial[0].astype(f32) + out_near_back.astype(f32) + out_got.astype(f32)).astype(bf16)
    shard_c = total(gc_own, own_got[:, :channels], c_got)

    side_by_side = lambda v: jnp.concatenate([v[i:i + 8] for i in range(0, v.shape[0], 8)], axis=1)
    total_conv = side_by_side(totals[:alone - 8])[:6]
    total_head = totals[alone - 8:alone - 5, :heads]
    total_bct = side_by_side(totals_shared[:16])[:5]
    per = TILE_D // LANES
    total_gain = jnp.concatenate([totals_shared[i:i + per] for i in range(16, totals_shared.shape[0], 8)], axis=0).reshape(-1)

    out_m, out_w = advance(out_weight, out_moment, shard_c.T)
    return (
        output, input_grad, in_m, in_w, bc_m, bc_w, step_m.T, step_w.T, out_m, out_w,
        momentum(conv_moment, total_conv),
        momentum(bc_table_moment, total_bct),
        momentum(head_moment, total_head),
        momentum(gain_moment, total_gain),
    )


def solution(mesh):
    placed = (
        P("dp", None),
        P("dp", None),
        P("dp", "mp"),
        P("dp", None, "mp"),
        P("dp", None, "mp"),
        P("dp", None),
        P("dp", None),
        P("dp", "mp"),
        P("dp", "mp"),
        P("mp", "dp"),
        P("mp", "dp"),
        P(None, "mp"),
        P(None, "mp"),
        P(),
        P(),
        P(None, "mp"),
        P(None, "mp"),
        P(),
        P(),
    )
    return jax.shard_map(
        body,
        mesh=mesh,
        in_specs=placed,
        out_specs=(
            P("dp", "mp"),
            P("dp", None),
            P("dp", None, "mp"),
            P("dp", None, "mp"),
            P("dp", None),
            P("dp", None),
            P("dp", "mp"),
            P("dp", "mp"),
            P("mp", "dp"),
            P("mp", "dp"),
            P(None, "mp"),
            P(),
            P(None, "mp"),
            P(),
        ),
        check_vma=False,
    )
```

```python
import functools

import jax
import jax.numpy as jnp
from jax import lax
from jax.experimental import pallas as pl
from jax.experimental.pallas import tpu as pltpu
from jax.sharding import PartitionSpec as P

CHUNK = 128
EPSILON = 1e-05
LEARN_RATE = 0.0001
DECAY_RATE = 0.1
WIDTH = 64
LANES = 128
HALO = 8
bf16 = jnp.bfloat16
f32 = jnp.float32
MIB = 1024 * 1024


def hbm(shape, dtype):
    return pltpu.HBM(shape, dtype)


def from_hbm(v):
    return pltpu.with_memory_space_constraint(v, pltpu.HBM)


def dot_nn(a, b):
    return lax.dot_general(a, b, (((1,), (0,)), ((), ())), preferred_element_type=f32)


def dot_nt(a, b):
    return lax.dot_general(a, b, (((1,), (1,)), ((), ())), preferred_element_type=f32)


def dot_tn(a, b):
    return lax.dot_general(a, b, (((0,), (0,)), ((), ())), preferred_element_type=f32)


def split3(v):
    high = v.astype(bf16)
    rest = v - high.astype(f32)
    mid = rest.astype(bf16)
    low = (rest - mid.astype(f32)).astype(bf16)
    return high, mid, low


def exact_left(ones, v):
    high, mid, low = split3(v)
    return dot_nn(ones, high) + dot_nn(ones, mid) + dot_nn(ones, low)


def spread(v, expand):
    high, mid, low = split3(v)
    return dot_nn(high, expand) + dot_nn(mid, expand) + dot_nn(low, expand)


def gather_heads(v, expand_t):
    high = v.astype(bf16)
    mid = (v - high.astype(f32)).astype(bf16)
    return dot_nn(high, expand_t) + dot_nn(mid, expand_t)


def sigmoid(v):
    return 0.5 * jnp.tanh(0.5 * v) + 0.5


def conv_block(before, now, taps, keep):
    longer = jnp.concatenate([before, now], axis=0)
    total = taps[4:5, :] + taps[0:1, :] * now
    for lag in (1, 2, 3):
        moved = pltpu.roll(longer, lag, 0)[HALO:, :]
        total = total + taps[lag:lag + 1, :] * (moved * keep[:, lag - 1:lag])
    return total


def step_parts(step_pre, heads):
    raw = step_pre + heads[0:1, :]
    small = jnp.exp(-jnp.abs(raw))
    steps = jnp.maximum(raw, 0.0) + jnp.log1p(small)
    slope = jnp.where(raw >= 0.0, 1.0, small) / (1.0 + small)
    rates = -jnp.exp(heads[1:2, :])
    return slope, steps, rates


def triangle(lower):
    row = lax.broadcasted_iota(jnp.int32, (CHUNK, CHUNK), 0)
    col = lax.broadcasted_iota(jnp.int32, (CHUNK, CHUNK), 1)
    return row >= col if lower else row <= col


def ssd_forward_kernel(
    x_ref, xb_ref, bc_ref, bcb_ref, st_ref, aux_ref, seg_ref, conv_ref, bct_ref, heads_ref, expand_ref,
    mixed_ref, state_ref, act_ref, slope_ref, xs_ref, xe_ref, step_ref, entry_ref, end_ref, bcact_ref, bcslope_ref,
    state,
):
    chunk = pl.program_id(0)

    @pl.when(chunk == 0)
    def _():
        state[...] = jnp.zeros_like(state)

    channels = x_ref.shape[1]
    aux = aux_ref[...]
    expand = expand_ref[...]
    u = conv_block(xb_ref[...], x_ref[...], conv_ref, aux)
    sg = sigmoid(u)
    x_act = u * sg
    act_ref[...] = x_act
    slope_ref[...] = (sg * (1.0 + u * (1.0 - sg))).astype(bf16)
    ubc = conv_block(bcb_ref[...], bc_ref[...], bct_ref, aux)
    sgbc = sigmoid(ubc)
    bc_act = (ubc * sgbc).astype(bf16)
    bcact_ref[...] = bc_act
    bcslope_ref[...] = sgbc * (1.0 + ubc * (1.0 - sgbc))
    b_mat, c_mat = bc_act[:, :LANES], bc_act[:, LANES:]
    _, steps, rates = step_parts(st_ref[...], heads_ref)
    lower = triangle(True)
    cum = exact_left(lower.astype(bf16), steps * rates)
    cum_t = cum.T
    tail = cum[CHUNK - 1:CHUNK, :]
    entry = jnp.exp(cum) * aux[:, 6:7]
    to_end = jnp.exp(tail - cum) * aux[:, 7:8]
    wide = spread(jnp.concatenate([steps, entry, to_end], axis=0), expand)
    step_e, entry_e, to_end_e = wide[:CHUNK], wide[CHUNK:2 * CHUNK], wide[2 * CHUNK:]
    skip_e = spread(jnp.broadcast_to(heads_ref[2:3, :], (8, LANES)), expand)[0:1, :]
    mask = lower & (aux[:, 8:9] == seg_ref[...])
    scores = jnp.where(mask, dot_nt(c_mat, b_mat), 0.0)
    xs = x_act * step_e
    xs_low = xs.astype(bf16)
    xe_low = (xs * to_end_e).astype(bf16)
    xs_ref[...] = xs_low
    xe_ref[...] = xe_low
    step_ref[...] = step_e.astype(bf16)
    entry_ref[...] = entry_e.astype(bf16)
    end_ref[...] = to_end_e.astype(bf16)
    held = state[...]
    held_low = held.astype(bf16)
    state_ref[...] = held_low
    out = dot_nn(c_mat, held_low) * entry_e + skip_e * x_act
    state[...] = held * entry_e[CHUNK - 1:CHUNK, :] + dot_tn(b_mat, xe_low)
    first = lax.broadcasted_iota(jnp.int32, (CHUNK, LANES), 1) < WIDTH
    zero = jnp.zeros((CHUNK, LANES), bf16)
    for pair in range(channels // LANES):
        span = slice(pair * LANES, (pair + 1) * LANES)
        parts = []
        for head in (2 * pair, 2 * pair + 1):
            diff = cum[:, head:head + 1] - cum_t[head:head + 1, :]
            parts.append((scores * jnp.exp(jnp.minimum(diff, 0.0))).astype(bf16))
        own = xs_low[:, span]
        both = jnp.concatenate([jnp.where(first, own, zero), jnp.where(first, zero, own)], axis=0)
        mixed_ref[:, span] = out[:, span] + dot_nn(jnp.concatenate(parts, axis=1), both)


def ssd_backward_kernel(
    rank_ref, x_ref, bc_ref, st_ref, aux_ref, seg_ref, conv_ref, bct_ref, heads_ref, expand_ref,
    expand_t_ref, mixed_ref, dy_ref, state_ref, act_ref, slope_ref, xs_ref, xe_ref, step_ref, entry_ref, end_ref, bcact_ref,
    bcslope_ref, dx_ref, dbc_ref, keep_ref, send_ref, dst_ref, dst_t_ref, dconv_ref, dbct_ref, dheads_ref,
    dstate, du_scr, dubc_scr, share_scr,
):
    @pl.when(pl.program_id(0) == 0)
    def _():
        for ref in (dstate, du_scr, dubc_scr, dconv_ref, dbct_ref, dheads_ref):
            ref[...] = jnp.zeros_like(ref)

    channels = x_ref.shape[1]
    aux = aux_ref[...]
    expand = expand_ref[...]
    x_act = act_ref[...]
    b_mat, c_mat = bcact_ref[:, :LANES], bcact_ref[:, LANES:]
    slope, steps, rates = step_parts(st_ref[...], heads_ref)
    lower = triangle(True)
    cum = exact_left(lower.astype(bf16), steps * rates)
    cum_t = cum.T
    skip_e = spread(jnp.broadcast_to(heads_ref[2:3, :], (8, LANES)), expand)[0:1, :]
    upper = triangle(False)
    mask = upper & (aux[:, 8:9] == seg_ref[...])
    scores = jnp.where(mask, dot_nt(b_mat, c_mat), 0.0)
    xs_low = xs_ref[...]
    dy_low = dy_ref[...]
    dy = dy_low.astype(f32)
    held_low = state_ref[...]
    grad = dstate[...]
    grad_low = grad.astype(bf16)
    entry_e = entry_ref[...].astype(f32)
    entry_dy = (entry_e * dy).astype(bf16)
    kept_e = entry_e[CHUNK - 1:CHUNK, :]
    dstate[...] = grad * kept_e + dot_tn(c_mat, entry_dy)
    dc = dot_nt(entry_dy, held_low)
    db = dot_nt(xe_ref[...], grad_low)
    q_state = dot_nn(b_mat, grad_low) * end_ref[...].astype(f32)
    first = lax.broadcasted_iota(jnp.int32, (CHUNK, LANES), 1) < WIDTH
    zero = jnp.zeros((CHUNK, LANES), bf16)
    dscores = jnp.zeros((CHUNK, CHUNK), f32)
    q_parts = []
    for pair in range(channels // LANES):
        span = slice(pair * LANES, (pair + 1) * LANES)
        own = dy_low[:, span]
        both = jnp.concatenate([jnp.where(first, own, zero), jnp.where(first, zero, own)], axis=0)
        dweights = dot_nt(xs_low[:, span], both)
        parts = []
        for i, head in enumerate((2 * pair, 2 * pair + 1)):
            diff = cum_t[head:head + 1, :] - cum[:, head:head + 1]
            decay = jnp.exp(jnp.minimum(diff, 0.0))
            parts.append((scores * decay).astype(bf16))
            dscores = dscores + dweights[:, i * LANES:(i + 1) * LANES] * decay
        q_parts.append(dot_nn(jnp.concatenate(parts, axis=1), both))
    q = jnp.concatenate(q_parts, axis=1) + q_state
    dscores_low = jnp.where(mask, dscores, 0.0).astype(bf16)
    db = db + dot_nn(dscores_low, c_mat)
    dc = dc + dot_tn(dscores_low, b_mat)
    xs_round = xs_low.astype(f32)
    expand_t = expand_t_ref[...]
    flow = gather_heads(dy * (mixed_ref[...] - skip_e * x_act) - xs_round * q, expand_t)
    dstep = dot_nn((x_act * q).astype(bf16), expand_t)
    sums = jnp.concatenate(
        [
            jnp.sum(xs_round * q_state + kept_e * (held_low.astype(f32) * grad), axis=0, keepdims=True),
            jnp.sum(dy * x_act, axis=0, keepdims=True),
            jnp.zeros((6, channels), f32),
        ],
        axis=0,
    )
    sums = gather_heads(sums, expand_t)
    dlog = exact_left(upper.astype(bf16), flow) + sums[0:1, :]
    dstep = dstep + rates * dlog
    draw = dstep * slope
    dst_ref[...] = pltpu.roll(draw, WIDTH, 1).astype(bf16)
    dst_t_ref[...] = draw.T[0:16, :].astype(bf16)
    dheads_ref[0:1, :] += jnp.sum(draw, axis=0, keepdims=True)
    dheads_ref[1:2, :] += rates * jnp.sum(dlog * steps, axis=0, keepdims=True)
    dheads_ref[2:3, :] += sums[1:2, :]
    x_now, bc_now = x_ref[...], bc_ref[...]

    def conv_back(scratch, du, now, taps, dtaps):
        longer = jnp.concatenate([du, scratch[...]], axis=0)
        total = taps[0:1, :] * du
        sums = [jnp.sum(now * du, axis=0, keepdims=True)]
        for lag in (1, 2, 3):
            moved = pltpu.roll(longer, CHUNK + HALO - lag, 0)[0:CHUNK, :] * aux[:, 2 + lag:3 + lag]
            total = total + taps[lag:lag + 1, :] * moved
            sums.append(jnp.sum(now * moved, axis=0, keepdims=True))
        sums.append(jnp.sum(du, axis=0, keepdims=True))
        dtaps[0:5, :] += jnp.concatenate(sums, axis=0)
        scratch[...] = du[0:HALO, :]
        return total

    du = (skip_e * dy + step_ref[...].astype(f32) * q) * slope_ref[...].astype(f32)
    dx_ref[...] = conv_back(du_scr, du, x_now, conv_ref, dconv_ref).astype(dx_ref.dtype)
    dubc = jnp.concatenate([db, dc], axis=1) * bcslope_ref[...]
    dbc = conv_back(dubc_scr, dubc, bc_now, bct_ref, dbct_ref).astype(bf16)
    swapped = jnp.concatenate([dbc[:, LANES:], dbc[:, :LANES]], axis=1)
    ordered = jnp.where((rank_ref[0] & 2) == 2, swapped, dbc)
    swapped = jnp.concatenate(
        [pltpu.roll(ordered[:, :LANES].astype(f32), WIDTH, 1), pltpu.roll(ordered[:, LANES:].astype(f32), WIDTH, 1)], axis=1
    ).astype(bf16)
    dbc_ref[...] = jnp.where((rank_ref[0] & 1) == 1, swapped, ordered)
    share = 2 * LANES // 4
    turned = dbc.T
    for member in range(4):
        apart = member ^ rank_ref[0]
        start = pl.multiple_of((apart & 1) * 2 * share + (apart >> 1) * share, share)
        share_scr[pl.ds(start, share), :] = turned[member * share:(member + 1) * share, :]
    keep_ref[...] = share_scr[0:2 * share, :]
    send_ref[...] = share_scr[2 * share:4 * share, :]


def common_specs(place, channels):
    before = lambda i: (jnp.maximum(place(i) * (CHUNK // HALO) - 1, 0), 0)
    now = lambda i: (place(i), 0)
    whole = lambda i: (0, 0)
    return [
        pl.BlockSpec((CHUNK, channels), now),
        pl.BlockSpec((HALO, channels), before),
        pl.BlockSpec((CHUNK, 2 * LANES), now),
        pl.BlockSpec((HALO, 2 * LANES), before),
        pl.BlockSpec((CHUNK, LANES), now),
        pl.BlockSpec((CHUNK, 16), now),
        pl.BlockSpec((1, CHUNK), lambda i: (0, place(i))),
        pl.BlockSpec((8, channels), whole),
        pl.BlockSpec((8, 2 * LANES), whole),
        pl.BlockSpec((8, LANES), whole),
        pl.BlockSpec((LANES, channels), whole),
    ]


def ssd_forward(x_pre, bc_pre, step_pre, aux, seg_row, conv_rows, bc_rows, head_rows, expand):
    tokens, channels = x_pre.shape
    count = tokens // CHUNK
    now = lambda i: (i, 0)
    return pl.pallas_call(
        ssd_forward_kernel,
        grid=(count,),
        in_specs=common_specs(lambda i: i, channels),
        out_specs=[
            pl.BlockSpec((CHUNK, channels), now),
            pl.BlockSpec((None, LANES, channels), lambda i: (i, 0, 0)),
        ]
        + [pl.BlockSpec((CHUNK, channels), now)] * 7
        + [pl.BlockSpec((CHUNK, 2 * LANES), now)] * 2,
        out_shape=[
            hbm((tokens, channels), f32),
            hbm((count, LANES, channels), bf16),
            hbm((tokens, channels), f32),
            *[hbm((tokens, channels), bf16) for _ in range(6)],
            hbm((tokens, 2 * LANES), bf16),
            hbm((tokens, 2 * LANES), f32),
        ],
        scratch_shapes=[
            pltpu.VMEM((LANES, channels), f32),
        ],
        compiler_params=pltpu.CompilerParams(vmem_limit_bytes=18 * MIB),
        cost_estimate=pl.CostEstimate(flops=14 * 10**9, bytes_accessed=40 * 10**6, transcendentals=0),
        name="ssd_forward",
    )(
        from_hbm(x_pre), from_hbm(x_pre), bc_pre, bc_pre, step_pre, aux, seg_row, conv_rows, bc_rows, head_rows, expand
    )


def ssd_backward(rank, x_pre, bc_pre, step_pre, aux, seg_row, conv_rows, bc_rows, head_rows, expand, expand_t, dy, kept):
    tokens, channels = x_pre.shape
    count = tokens // CHUNK
    place = lambda i: count - 1 - i
    now = lambda i: (place(i), 0)
    whole = lambda i: (0, 0)
    wide = pl.BlockSpec((CHUNK, channels), now)
    narrow = pl.BlockSpec((CHUNK, 2 * LANES), now)
    specs = common_specs(place, channels)
    mixed, states, *more = kept
    return pl.pallas_call(
        ssd_backward_kernel,
        grid=(count,),
        in_specs=[pl.BlockSpec(memory_space=pltpu.SMEM), specs[0], specs[2], *specs[4:]]
        + [pl.BlockSpec((channels, LANES), whole), wide, wide, pl.BlockSpec((None, LANES, channels), lambda i: (place(i), 0, 0))]
        + [wide] * 7 + [narrow] * 2,
        out_specs=[
            wide,
            narrow,
            pl.BlockSpec((LANES, CHUNK), lambda i: (0, place(i))),
            pl.BlockSpec((LANES, CHUNK), lambda i: (0, place(i))),
            pl.BlockSpec((CHUNK, LANES), now),
            pl.BlockSpec((16, CHUNK), lambda i: (0, place(i))),
            pl.BlockSpec((8, channels), whole),
            pl.BlockSpec((8, 2 * LANES), whole),
            pl.BlockSpec((8, LANES), whole),
        ],
        out_shape=[
            jax.ShapeDtypeStruct((tokens, channels), bf16),
            jax.ShapeDtypeStruct((tokens, 2 * LANES), bf16),
            hbm((LANES, tokens), bf16),
            hbm((LANES, tokens), bf16),
            jax.ShapeDtypeStruct((tokens, LANES), bf16),
            hbm((16, tokens), bf16),
            jax.ShapeDtypeStruct((8, channels), f32),
            jax.ShapeDtypeStruct((8, 2 * LANES), f32),
            jax.ShapeDtypeStruct((8, LANES), f32),
        ],
        scratch_shapes=[
            pltpu.VMEM((LANES, channels), f32),
            pltpu.VMEM((HALO, channels), f32),
            pltpu.VMEM((HALO, 2 * LANES), f32),
            pltpu.VMEM((2 * LANES, CHUNK), bf16),
        ],
        compiler_params=pltpu.CompilerParams(vmem_limit_bytes=20 * MIB),
        cost_estimate=pl.CostEstimate(flops=28 * 10**9, bytes_accessed=40 * 10**6, transcendentals=0),
        name="ssd_backward",
    )(
        rank, from_hbm(x_pre), bc_pre, step_pre, aux, seg_row, conv_rows, bc_rows, head_rows,
        expand, expand_t, from_hbm(mixed), dy, from_hbm(states), *[from_hbm(v) for v in more],
    )


def segment_facts(seg):
    row = seg[0]
    tokens = row.shape[0]
    cols = []
    for lag in (1, 2, 3):
        cols.append(jnp.pad(row[:-lag], (lag, 0), constant_values=-1) == row)
    for lag in (1, 2, 3):
        cols.append(jnp.pad(row[lag:], (0, lag), constant_values=-1) == row)
    blocks = row.reshape(tokens // CHUNK, CHUNK)
    ends = blocks[:, -1:]
    before = jnp.concatenate([jnp.full((1, 1), -1, row.dtype), ends[:-1]], axis=0)
    cols.append((blocks == before).reshape(-1))
    cols.append((blocks == ends).reshape(-1))
    cols.append(row)
    facts = jnp.stack([c.astype(f32) for c in cols], axis=1)
    return jnp.pad(facts, ((0, 0), (0, 16 - facts.shape[1]))), seg.astype(f32)


def pad_rows(table, rows=8):
    return jnp.pad(table, ((0, rows - table.shape[0]), (0, 0)))


def pad_lanes(table, lanes=LANES):
    return jnp.pad(table, ((0, 0), (0, lanes - table.shape[1])))


def head_expand(channels):
    head, channel = jnp.arange(LANES), jnp.arange(channels) // WIDTH
    return (head[:, None] == channel[None, :]).astype(bf16), (channel[:, None] == head[None, :]).astype(bf16)


TILE = 256
TILE_D = 384


def fill(dest, pieces, idx_ref):
    rows = pieces[0].shape[0]
    s = 0
    for piece in pieces:
        for b in range(piece.shape[0] // rows):
            start = pl.multiple_of(idx_ref[s] * rows, rows)
            dest[pl.ds(start, rows), :] = piece[b * rows:(b + 1) * rows, :]
            s += 1


def params(mib=18):
    return pltpu.CompilerParams(vmem_limit_bytes=mib * MIB)


def cost(us):
    return pl.CostEstimate(flops=int(us * 10**9), bytes_accessed=int(us * 2 * 10**6), transcendentals=0)


def prepare_kernel(hidden_ref, gain_ref, low_ref, low_t_ref, inv_ref):
    inputs = hidden_ref[...].astype(f32)
    inv_rms = lax.rsqrt(jnp.mean(inputs * inputs, axis=1, keepdims=True) + EPSILON)
    low = (inputs * inv_rms * gain_ref[0:1, :]).astype(bf16)
    low_ref[...] = low
    low_t_ref[...] = low.T
    inv_ref[...] = column_to_row(inv_rms)


def prepare(hidden, gain_rows):
    tokens, depth = hidden.shape
    block = pl.BlockSpec((TILE, depth), lambda i: (i, 0))
    return pl.pallas_call(
        prepare_kernel,
        grid=(tokens // TILE,),
        in_specs=[block, pl.BlockSpec((8, depth), lambda i: (0, 0))],
        out_specs=[block, pl.BlockSpec((depth, TILE), lambda i: (0, i)), pl.BlockSpec((8, TILE), lambda i: (0, i))],
        out_shape=[
            hbm((tokens, depth), bf16),
            hbm((depth, tokens), bf16),
            jax.ShapeDtypeStruct((8, tokens), f32),
        ],
        compiler_params=params(),
        cost_estimate=cost(12),
        name="prepare",
    )(hidden, gain_rows)


def pack_kernel(rank_ref, in_ref, bc_ref, step_ref, a_ref, scratch):
    rows, width = bc_ref.shape
    channels = in_ref.shape[2]
    share = width // 4
    heads = step_ref.shape[0]
    a_ref[:, :channels] = in_ref[:, 1, :].astype(bf16)
    scratch[...] = jnp.zeros_like(scratch)
    scratch[share:share + heads, 0:rows] = step_ref[...]
    step = scratch[...].T[0:rows, :]
    own = bc_ref[:, 0:LANES]
    for member in range(1, 4):
        turned = pltpu.roll(bc_ref[...], width - member * share, 1)[:, 0:LANES]
        own = jnp.where(rank_ref[0] == member, turned, own)
    lane = lax.broadcasted_iota(jnp.int32, (rows, LANES), 1)
    a_ref[:, channels:] = jnp.where(lane < share, own, step).astype(bf16)


def pack(in_weight, bc_weight, step_t, rank):
    rows, _, channels = in_weight.shape
    vmem = pl.BlockSpec(memory_space=pltpu.VMEM)
    return pl.pallas_call(
        pack_kernel,
        in_specs=[pl.BlockSpec(memory_space=pltpu.SMEM), vmem, vmem, vmem],
        out_specs=vmem,
        out_shape=jax.ShapeDtypeStruct((rows, channels + LANES), bf16),
        scratch_shapes=[pltpu.VMEM((LANES, 2 * LANES), f32)],
        compiler_params=params(),
        cost_estimate=cost(2),
        name="pack",
    )(rank, from_hbm(in_weight), from_hbm(bc_weight), from_hbm(step_t))


def pack_gate_kernel(in_ref, b_ref):
    b_ref[...] = in_ref[:, 0, :].astype(bf16)


def pack_gate(in_weight):
    rows, _, channels = in_weight.shape
    vmem = pl.BlockSpec(memory_space=pltpu.VMEM)
    return pl.pallas_call(
        pack_gate_kernel,
        in_specs=[vmem],
        out_specs=vmem,
        out_shape=hbm((rows, channels), bf16),
        compiler_params=params(),
        cost_estimate=cost(2),
        name="pack_gate",
    )(from_hbm(in_weight))


def columns_kernel(rank_ref, *refs, count):
    pieces, (full_ref, full_t_ref) = refs[:count], refs[count:]
    for r, piece in enumerate(pieces):
        width = piece.shape[1]
        start = pl.multiple_of((rank_ref[0] ^ r) * width, LANES)
        value = piece[...]
        full_ref[:, pl.ds(start, width)] = value
        full_t_ref[pl.ds(start, width), :] = value.T


def join_columns(pieces, rank):
    tokens, width = pieces[0].shape
    depth = width * len(pieces)
    return pl.pallas_call(
        functools.partial(columns_kernel, count=len(pieces)),
        grid=(tokens // TILE,),
        in_specs=[pl.BlockSpec(memory_space=pltpu.SMEM)] + [pl.BlockSpec((TILE, width), lambda i: (i, 0))] * len(pieces),
        out_specs=[pl.BlockSpec((TILE, depth), lambda i: (i, 0)), pl.BlockSpec((depth, TILE), lambda i: (0, i))],
        out_shape=[jax.ShapeDtypeStruct((tokens, depth), bf16), jax.ShapeDtypeStruct((depth, tokens), bf16)],
        compiler_params=params(),
        cost_estimate=cost(12),
        name="join_columns",
    )(rank, *pieces)


def rows_kernel(rank_ref, *refs, count):
    pieces, full_ref = refs[:count], refs[count]
    for r, piece in enumerate(pieces):
        rows = piece.shape[0]
        full_ref[pl.ds(pl.multiple_of((rank_ref[0] ^ r) * rows, rows), rows), :] = piece[...]


def join_rows(pieces, rank):
    rows, width = pieces[0].shape
    shape = (rows * len(pieces), width)
    return pl.pallas_call(
        functools.partial(rows_kernel, count=len(pieces)),
        in_specs=[pl.BlockSpec(memory_space=pltpu.SMEM)] + [pl.BlockSpec(memory_space=pltpu.VMEM)] * len(pieces),
        out_specs=pl.BlockSpec(memory_space=pltpu.VMEM),
        out_shape=jax.ShapeDtypeStruct(shape, pieces[0].dtype),
        compiler_params=params(),
        cost_estimate=cost(0.1),
        name="join_rows",
    )(rank, *pieces)


def small_kernel(rank_ref, *refs, count):
    pieces, (small_ref, bc_ref, step_ref, scratch) = refs[:count], refs[count:]
    share = pieces[0].shape[0]
    for r, piece in enumerate(pieces):
        scratch[pl.ds(pl.multiple_of((rank_ref[0] ^ r) * share, share), share), :] = piece[...].astype(f32)
    bc_ref[...] = scratch[...].T
    turned = small_ref[...].T
    lane = lax.broadcasted_iota(jnp.int32, turned.shape, 1)
    step_ref[...] = jnp.where(lane < LANES - share, pltpu.roll(turned, LANES - share, 1), 0.0)


def join_small(pieces, small, rank):
    share, tokens = pieces[0].shape
    width = share * len(pieces)
    return pl.pallas_call(
        functools.partial(small_kernel, count=len(pieces)),
        grid=(tokens // TILE,),
        in_specs=[pl.BlockSpec(memory_space=pltpu.SMEM)]
        + [pl.BlockSpec((share, TILE), lambda i: (0, i))] * len(pieces)
        + [pl.BlockSpec((LANES, TILE), lambda i: (0, i))],
        out_specs=[pl.BlockSpec((TILE, width), lambda i: (i, 0)), pl.BlockSpec((TILE, LANES), lambda i: (i, 0))],
        out_shape=[jax.ShapeDtypeStruct((tokens, width), f32), jax.ShapeDtypeStruct((tokens, LANES), f32)],
        scratch_shapes=[pltpu.VMEM((width, TILE), f32)],
        compiler_params=params(),
        cost_estimate=cost(0.1),
        name="join_small",
    )(rank, *pieces, small)


def project_small_kernel(idx_ref, lhs_ref, *refs, count):
    pieces, (small_ref, share_ref, w_ref, wt_ref) = refs[:count], refs[count:]

    @pl.when(pl.program_id(0) == 0)
    def _():
        fill(w_ref, pieces, idx_ref)
        wt_ref[...] = w_ref[...].T[0:wt_ref.shape[0], :]

    small = dot_nn(lhs_ref[...], w_ref[...]).T
    small_ref[...] = small
    share_ref[...] = small[0:share_ref.shape[0], :].astype(bf16)


def project_small(lhs, pieces, idx, share):
    tokens, depth = lhs.shape
    count, last = len(pieces), pieces[0].shape[1] // LANES - 1
    whole = lambda i: (0, 0)
    return pl.pallas_call(
        functools.partial(project_small_kernel, count=count),
        grid=(tokens // TILE,),
        in_specs=[pl.BlockSpec(memory_space=pltpu.SMEM), pl.BlockSpec((TILE, depth), lambda i: (i, 0))]
        + [pl.BlockSpec((p.shape[0], LANES), lambda i: (0, last)) for p in pieces],
        out_specs=[
            pl.BlockSpec((LANES, TILE), lambda i: (0, i)),
            pl.BlockSpec((share, TILE), lambda i: (0, i)),
            pl.BlockSpec((depth, LANES), whole),
            pl.BlockSpec((share, depth), whole),
        ],
        out_shape=[
            jax.ShapeDtypeStruct((LANES, tokens), f32),
            jax.ShapeDtypeStruct((share, tokens), bf16),
            hbm((depth, LANES), bf16),
            jax.ShapeDtypeStruct((share, depth), bf16),
        ],
        compiler_params=params(),
        cost_estimate=cost(20),
        name="project_small",
    )(idx, lhs, *pieces)


def project_kernel(idx_ref, lhs_ref, *refs, count):
    pieces, (x_ref, w_ref) = refs[:count], refs[count:]

    @pl.when(pl.program_id(0) == 0)
    def _():
        fill(w_ref, pieces, idx_ref)

    x_ref[...] = dot_nn(lhs_ref[...], w_ref[...])


def project(lhs, pieces, idx, channels):
    tokens, depth = lhs.shape
    whole = lambda i: (0, 0)
    return pl.pallas_call(
        functools.partial(project_kernel, count=len(pieces)),
        grid=(tokens // TILE,),
        in_specs=[pl.BlockSpec(memory_space=pltpu.SMEM), pl.BlockSpec((TILE, depth), lambda i: (i, 0))]
        + [pl.BlockSpec((p.shape[0], channels), whole) for p in pieces],
        out_specs=[pl.BlockSpec((TILE, channels), lambda i: (i, 0)), pl.BlockSpec((depth, channels), whole)],
        out_shape=[
            hbm((tokens, channels), f32),
            hbm((depth, channels), bf16),
        ],
        compiler_params=params(),
        cost_estimate=cost(0.1),
        name="project",
    )(idx, lhs, *pieces)


def column_to_row(col):
    return jnp.broadcast_to(col, (col.shape[0], LANES)).T[0:8, :]


def row_to_column(row):
    return jnp.broadcast_to(row, (LANES, row.shape[1])).T[:, 0:1]


def gate_kernel(idx_ref, lhs_ref, mixed_ref, *refs, count):
    pieces, (gate_ref, sums_ref, w_ref) = refs[:count], refs[count:]

    @pl.when(pl.program_id(0) == 0)
    def _():
        fill(w_ref, pieces, idx_ref)

    gate = dot_nn(lhs_ref[...], w_ref[...])
    gate_ref[...] = gate
    gated = mixed_ref[...] * (gate * sigmoid(gate))
    sums_ref[...] = column_to_row(jnp.sum(gated * gated, axis=1, keepdims=True))


def gate_forward(lhs, mixed, pieces, idx):
    tokens, depth = lhs.shape
    channels = mixed.shape[1]
    whole = lambda i: (0, 0)
    now = lambda i: (i, 0)
    return pl.pallas_call(
        functools.partial(gate_kernel, count=len(pieces)),
        grid=(tokens // TILE,),
        in_specs=[
            pl.BlockSpec(memory_space=pltpu.SMEM),
            pl.BlockSpec((TILE, depth), now),
            pl.BlockSpec((TILE, channels), now),
        ]
        + [pl.BlockSpec(p.shape, whole) for p in pieces],
        out_specs=[
            pl.BlockSpec((TILE, channels), now),
            pl.BlockSpec((8, TILE), lambda i: (0, i)),
            pl.BlockSpec((depth, channels), whole),
        ],
        out_shape=[
            jax.ShapeDtypeStruct((tokens, channels), f32),
            jax.ShapeDtypeStruct((8, tokens), f32),
            hbm((depth, channels), bf16),
        ],
        compiler_params=params(),
        cost_estimate=cost(0.1),
        name="gate_forward",
    )(idx, lhs, from_hbm(mixed), *pieces)


def gated_kernel(gate_ref, mixed_ref, square_ref, conv_ref, out_ref, *, inner_total):
    gate = gate_ref[...]
    scale = lax.rsqrt(row_to_column(square_ref[0:1, :]) / inner_total + EPSILON)
    gated = mixed_ref[...] * (gate * sigmoid(gate))
    out_ref[...] = (gated * scale * conv_ref[5:6, :]).astype(bf16)


def gated_norm(gate, mixed, square, conv_rows, inner_total):
    tokens, channels = gate.shape
    block = pl.BlockSpec((TILE, channels), lambda i: (i, 0))
    return pl.pallas_call(
        functools.partial(gated_kernel, inner_total=inner_total),
        grid=(tokens // TILE,),
        in_specs=[block, block, pl.BlockSpec((8, TILE), lambda i: (0, i)), pl.BlockSpec((8, channels), lambda i: (0, 0))],
        out_specs=block,
        out_shape=jax.ShapeDtypeStruct((tokens, channels), bf16),
        compiler_params=params(),
        cost_estimate=cost(0.1),
        name="gated_norm",
    )(gate, mixed, square, conv_rows)


def gout_kernel(idx_ref, cot_ref, gate_ref, mixed_ref, conv_ref, *refs, count):
    pieces, (gout_ref, sums_ref, w_ref) = refs[:count], refs[count:]

    @pl.when(pl.program_id(0) == 0)
    def _():
        fill(w_ref, pieces, idx_ref)

    gout = dot_nn(cot_ref[...], w_ref[...])
    gout_ref[...] = gout
    gate = gate_ref[...]
    gated = mixed_ref[...] * (gate * sigmoid(gate))
    sums_ref[...] = column_to_row(jnp.sum(gout * conv_ref[5:6, :] * gated, axis=1, keepdims=True))


def grad_gout(cot, gate, mixed, conv_rows, pieces, idx):
    tokens, depth = cot.shape
    channels = mixed.shape[1]
    whole = lambda i: (0, 0)
    now = lambda i: (i, 0)
    return pl.pallas_call(
        functools.partial(gout_kernel, count=len(pieces)),
        grid=(tokens // TILE,),
        in_specs=[
            pl.BlockSpec(memory_space=pltpu.SMEM),
            pl.BlockSpec((TILE, depth), now),
            pl.BlockSpec((TILE, channels), now),
            pl.BlockSpec((TILE, channels), now),
            pl.BlockSpec((8, channels), whole),
        ]
        + [pl.BlockSpec(p.shape, whole) for p in pieces],
        out_specs=[
            pl.BlockSpec((TILE, channels), now),
            pl.BlockSpec((8, TILE), lambda i: (0, i)),
            pl.BlockSpec((depth, channels), whole),
        ],
        out_shape=[
            jax.ShapeDtypeStruct((tokens, channels), f32),
            jax.ShapeDtypeStruct((8, tokens), f32),
            jax.ShapeDtypeStruct((depth, channels), bf16),
        ],
        compiler_params=params(),
        cost_estimate=cost(20),
        name="grad_gout",
    )(idx, cot, gate, mixed, conv_rows, *pieces)


def gate_back_kernel(gate_ref, gout_ref, mixed_ref, square_ref, inner_ref, conv_ref, dmixed_ref, dgate_ref, dgain_ref, *, inner_total):
    gate, gout, mixed = gate_ref[...], gout_ref[...], mixed_ref[...]
    gain = conv_ref[5:6, :]
    square, inner = row_to_column(square_ref[0:1, :]), row_to_column(inner_ref[0:1, :])
    scale = lax.rsqrt(square / inner_total + EPSILON)
    sg = sigmoid(gate)
    act = gate * sg
    gated = mixed * act
    dgated = scale * (gain * gout) - gated * (scale * scale * scale * inner / inner_total)
    dmixed_ref[...] = (dgated * act).astype(bf16)
    dgate_ref[...] = (dgated * mixed * sg * (1.0 + gate * (1.0 - sg))).astype(bf16)

    @pl.when(pl.program_id(0) == 0)
    def _():
        dgain_ref[...] = jnp.zeros_like(dgain_ref)

    dgain_ref[5:6, :] += jnp.sum(gout * gated * scale, axis=0, keepdims=True)


def gate_backward(gate, gout, mixed, square, inner, conv_rows, inner_total):
    tokens, channels = gate.shape
    whole = lambda i: (0, 0)
    block = pl.BlockSpec((TILE, channels), lambda i: (i, 0))
    row = pl.BlockSpec((8, TILE), lambda i: (0, i))
    return pl.pallas_call(
        functools.partial(gate_back_kernel, inner_total=inner_total),
        grid=(tokens // TILE,),
        in_specs=[block, block, block, row, row, pl.BlockSpec((8, channels), whole)],
        out_specs=[block, block, pl.BlockSpec((8, channels), whole)],
        out_shape=[
            jax.ShapeDtypeStruct((tokens, channels), bf16),
            jax.ShapeDtypeStruct((tokens, channels), bf16),
            jax.ShapeDtypeStruct((8, channels), f32),
        ],
        compiler_params=params(),
        cost_estimate=cost(0.1),
        name="gate_backward",
    )(from_hbm(gate), from_hbm(gout), from_hbm(mixed), square, inner, conv_rows)


def weight_grad_kernel(idx_ref, lhs_ref, rhs_ref, *refs, rows, turned):
    outs, scratch = refs[:-1], refs[-1]
    at = pl.program_id(0)
    scratch[pl.ds(pl.multiple_of(at * TILE_D, TILE_D), TILE_D), :] = (dot_nt if turned else dot_nn)(
        lhs_ref[...], rhs_ref[...]
    ).astype(bf16)

    @pl.when(at == pl.num_programs(0) - 1)
    def _():
        s = 0
        for out in outs:
            for b in range(out.shape[0] // rows):
                start = pl.multiple_of(idx_ref[s] * rows, rows)
                out[b * rows:(b + 1) * rows, :] = scratch[pl.ds(start, rows), :]
                s += 1


def weight_grad(lhs_t, rhs, idx, sizes, us=0.1, turned=False):
    depth, tokens = lhs_t.shape
    width = rhs.shape[0 if turned else 1]
    rows = depth // idx.shape[0]
    whole = lambda i: (0, 0)
    return pl.pallas_call(
        functools.partial(weight_grad_kernel, rows=rows, turned=turned),
        grid=(depth // TILE_D,),
        in_specs=[
            pl.BlockSpec(memory_space=pltpu.SMEM),
            pl.BlockSpec((TILE_D, tokens), lambda i: (i, 0)),
            pl.BlockSpec(rhs.shape, whole),
        ],
        out_specs=[pl.BlockSpec((size * rows, width), whole) for size in sizes],
        out_shape=[hbm((size * rows, width), bf16) for size in sizes],
        scratch_shapes=[pltpu.VMEM((depth, width), bf16)],
        compiler_params=params(),
        cost_estimate=cost(us),
        name="weight_grad",
    )(idx, lhs_t, rhs)


def out_kernel(rank_ref, lhs_ref, w_ref, *outs):
    product = dot_nt(lhs_ref[...], w_ref[...]).astype(bf16)
    for r, out in enumerate(outs):
        @pl.when(pl.program_id(0) == r)
        def _():
            out[...] = product


def out_partial(gated_out, w_out, rank, ranks):
    tokens, channels = gated_out.shape
    depth = w_out.shape[0]
    width = depth // ranks
    whole = lambda i, rank_ref: (0, 0)
    return pl.pallas_call(
        out_kernel,
        grid_spec=pltpu.PrefetchScalarGridSpec(
            num_scalar_prefetch=1,
            grid=(ranks,),
            in_specs=[
                pl.BlockSpec((tokens, channels), whole),
                pl.BlockSpec((width, channels), lambda i, rank_ref: (i ^ rank_ref[0], 0)),
            ],
            out_specs=[pl.BlockSpec((tokens, width), whole)] * ranks,
        ),
        out_shape=[hbm((tokens, width), bf16)] * ranks,
        compiler_params=params(),
        cost_estimate=cost(0.1),
        name="out_partial",
    )(rank, gated_out, w_out)


def term_kernel(rank_ref, gx_ref, wx_ref, gg_ref, wg_ref, gs_ref, ws_ref, gb_ref, hidden_ref, inv_ref, *refs, apart):
    wbt_refs, outs, dgain_ref = refs[:4], refs[4:-1], refs[-1]
    w_bct = jnp.concatenate([ref[...] for ref in wbt_refs], axis=0)
    gain = None
    for r, out in zip(apart, outs):
        rows = out.shape[0]
        span = pl.ds(pl.multiple_of((rank_ref[0] ^ r) * rows, rows), rows)
        total = dot_nt(gx_ref[span, :], wx_ref[...]) + dot_nt(gg_ref[span, :], wg_ref[...])
        total = total + dot_nt(gs_ref[span, :], ws_ref[...]) + dot_nn(gb_ref[span, :], w_bct)
        out[...] = total.astype(bf16)
        normed = hidden_ref[span, :].astype(f32) * row_to_column(inv_ref[0:1, span])
        own = jnp.sum(total * normed, axis=0, keepdims=True)
        gain = own if gain is None else gain + own
    cut = [gain[:, i:i + LANES] for i in range(0, gain.shape[1], LANES)]
    dgain_ref[...] = jnp.concatenate(cut + [jnp.zeros((8 - len(cut), LANES), f32)], axis=0)


def normed_term(dx, dgate, dstep, dbc, w_a, w_b, w_s, w_bct, hidden, inv_rms, rank, ranks, apart):
    tokens, channels = dx.shape
    depth = w_a.shape[0]
    rows = tokens // ranks
    whole = lambda i: (0, 0)
    return pl.pallas_call(
        functools.partial(term_kernel, apart=apart),
        grid=(depth // TILE_D,),
        in_specs=[
            pl.BlockSpec(memory_space=pltpu.SMEM),
            pl.BlockSpec(dx.shape, whole),
            pl.BlockSpec((TILE_D, channels), lambda i: (i, 0)),
            pl.BlockSpec(dgate.shape, whole),
            pl.BlockSpec((TILE_D, channels), lambda i: (i, 0)),
            pl.BlockSpec(dstep.shape, whole),
            pl.BlockSpec((TILE_D, LANES), lambda i: (i, 0)),
            pl.BlockSpec(dbc.shape, whole),
            pl.BlockSpec((tokens, TILE_D), lambda i: (0, i)),
            pl.BlockSpec(inv_rms.shape, whole),
        ]
        + [pl.BlockSpec((w.shape[0], TILE_D), lambda i: (0, i)) for w in w_bct],
        out_specs=[pl.BlockSpec((rows, TILE_D), lambda i: (0, i))] * len(apart) + [pl.BlockSpec((8, LANES), lambda i: (i, 0))],
        out_shape=[jax.ShapeDtypeStruct((rows, depth), bf16)] * len(apart)
        + [jax.ShapeDtypeStruct((8 * (depth // TILE_D), LANES), f32)],
        compiler_params=params(32),
        cost_estimate=cost(20 if 2 in apart else 0.1),
        name="normed_term",
    )(
        rank, dx, from_hbm(w_a), dgate, from_hbm(w_b), dstep, from_hbm(w_s), dbc, from_hbm(hidden), inv_rms, *w_bct
    )


def norm_back_kernel(rank_ref, a_ref, b_ref, hidden_ref, cot_ref, gain_ref, out_ref):
    grad = a_ref[...].astype(f32) + b_ref[...].astype(f32)
    inputs = hidden_ref[...].astype(f32)
    inv_rms = lax.rsqrt(jnp.mean(inputs * inputs, axis=1, keepdims=True) + EPSILON)
    normed = inputs * inv_rms
    scaled = grad * gain_ref[0:1, :]
    mean = jnp.mean(scaled * normed, axis=1, keepdims=True)
    out_ref[...] = (inv_rms * (scaled - normed * mean) + cot_ref[...].astype(f32)).astype(out_ref.dtype)


def norm_backward(a, b, hidden, cot, gain_rows, rank):
    rows, depth = a.shape
    mine = lambda i, rank_ref: (rank_ref[0], 0)
    whole = lambda i, rank_ref: (0, 0)
    return pl.pallas_call(
        norm_back_kernel,
        grid_spec=pltpu.PrefetchScalarGridSpec(
            num_scalar_prefetch=1,
            grid=(1,),
            in_specs=[
                pl.BlockSpec((rows, depth), whole),
                pl.BlockSpec((rows, depth), whole),
                pl.BlockSpec((rows, depth), mine),
                pl.BlockSpec((rows, depth), mine),
                pl.BlockSpec((8, depth), whole),
            ],
            out_specs=pl.BlockSpec((rows, depth), whole),
        ),
        out_shape=jax.ShapeDtypeStruct((rows, depth), bf16),
        compiler_params=params(),
        cost_estimate=cost(0.1),
        name="norm_backward",
    )(rank, a, b, from_hbm(hidden), from_hbm(cot), gain_rows)


def moved(weight, moment, grad):
    fresh = 0.5 * moment + 0.5 * grad
    return fresh, weight - LEARN_RATE * fresh - LEARN_RATE * DECAY_RATE * weight


def add_up(refs):
    total = refs[0][...].astype(f32)
    for ref in refs[1:]:
        total = total + ref[...].astype(f32)
    return total


def update_in_kernel(w_ref, m_ref, *refs, count):
    gate_refs, x_refs, (m_out, w_out) = refs[:count], refs[count:2 * count], refs[2 * count:]
    for at, parts in ((0, gate_refs), (1, x_refs)):
        fresh, weight = moved(w_ref[:, at, :], m_ref[:, at, :], add_up(parts))
        m_out[:, at, :] = fresh
        w_out[:, at, :] = weight


def update_in(weight, moment, gate_parts, x_parts):
    rows, _, channels = weight.shape
    size = min(rows, 96)
    full = pl.BlockSpec((size, 2, channels), lambda i: (i, 0, 0))
    parts = [*gate_parts, *x_parts]
    return pl.pallas_call(
        functools.partial(update_in_kernel, count=len(gate_parts)),
        grid=(rows // size,),
        in_specs=[full, full] + [pl.BlockSpec((size, channels), functools.partial(lambda at, i: (i, at), at)) for _, at in parts],
        out_specs=[full, full],
        out_shape=[jax.ShapeDtypeStruct(weight.shape, f32)] * 2,
        compiler_params=params(),
        cost_estimate=cost(0.1),
        name="update_in",
    )(from_hbm(weight), from_hbm(moment), *[part for part, _ in parts])


def update_small_kernel(w_ref, m_ref, sums_ref, own_ref, back_ref, *refs, share, order, shared):
    alone, late, (m_out, w_out, exchange, totals, scratch) = refs[:order[0]], refs[order[0]:-5], refs[-5:]
    heads, rows = w_ref.shape
    count = sums_ref.shape[0]
    last = late[0].shape[1] - LANES
    grad = own_ref[...].astype(f32) + back_ref[...].astype(f32)
    found = {0: sums_ref[...].astype(f32)}
    for at, ref in zip(order[1], alone):
        grad = grad + ref[0:rows, :].astype(f32)
        found[at] = ref[rows:, :].astype(f32)
    for at, ref in zip(order[2], late):
        grad = grad + ref[0:rows, last:].astype(f32)
        tail = ref[rows:, :].astype(f32)
        found[at] = jnp.concatenate([tail[:, i:i + LANES] for i in range(0, tail.shape[1], LANES)], axis=0)
    step = len(found) // 2
    while step >= 1:
        found = {i: found[i] + found[i + step] for i in range(step)}
        step //= 2
    totals[...] = found[0]
    exchange[0:rows, :] = grad
    exchange[rows:, :] = found[0][shared[0]:shared[1], :]
    scratch[0:rows, :] = grad
    turned = scratch[...].T[share:share + heads, 0:rows]
    fresh, weight = moved(w_ref[...], m_ref[...], turned)
    m_out[...] = fresh
    w_out[...] = weight


def update_small(weight_t, moment_t, sums, own, back, alone, late, order, shared, share):
    rows = weight_t.shape[1]
    count = sums.shape[0]
    whole = lambda i: (0, 0)
    spec = pl.BlockSpec(weight_t.shape, whole)
    return pl.pallas_call(
        functools.partial(update_small_kernel, share=share, order=order, shared=shared),
        grid=(1,),
        in_specs=[spec, spec, pl.BlockSpec(sums.shape, whole)] + [pl.BlockSpec((rows, LANES), whole)] * 2
        + [pl.BlockSpec(v.shape, whole) for v in (*alone, *late)],
        out_specs=[
            spec, spec,
            pl.BlockSpec((rows + shared[1] - shared[0], LANES), whole),
            pl.BlockSpec((count, LANES), whole),
        ],
        out_shape=[jax.ShapeDtypeStruct(weight_t.shape, f32)] * 2
        + [jax.ShapeDtypeStruct((rows + shared[1] - shared[0], LANES), f32), jax.ShapeDtypeStruct((count, LANES), f32)],
        scratch_shapes=[pltpu.VMEM((2 * LANES, LANES), f32)],
        compiler_params=params(),
        cost_estimate=cost(0.1),
        name="update_small",
    )(weight_t, moment_t, sums, own, back, *alone, *late)


def update_bc_kernel(rank_ref, w_ref, m_ref, *refs):
    pieces, (m_out, w_out, shared_out) = refs[:-3], refs[-3:]
    rows, width = w_ref.shape
    share = width // len(pieces)
    shared_out[...] = (pieces[0][rows:, :] + pieces[1][rows:, :]) + (pieces[2][rows:, :] + pieces[3][rows:, :])
    lane = lax.broadcasted_iota(jnp.int32, (rows, LANES), 1)
    for pair in range(width // LANES):
        halves = []
        for member in (2 * pair, 2 * pair + 1):
            own = pieces[0][0:rows, :]
            for r in range(1, len(pieces)):
                own = jnp.where((rank_ref[0] ^ r) == member, pieces[r][0:rows, :], own)
            halves.append(own)
        grad = jnp.where(lane < share, halves[0], pltpu.roll(halves[1], share, 1))
        span = slice(pair * LANES, (pair + 1) * LANES)
        fresh, weight = moved(w_ref[:, span], m_ref[:, span], grad)
        m_out[:, span] = fresh
        w_out[:, span] = weight


def update_bc(weight, moment, pieces, rank):
    vmem = pl.BlockSpec(memory_space=pltpu.VMEM)
    return pl.pallas_call(
        update_bc_kernel,
        in_specs=[pl.BlockSpec(memory_space=pltpu.SMEM)] + [vmem] * (2 + len(pieces)),
        out_specs=[vmem] * 3,
        out_shape=[jax.ShapeDtypeStruct(weight.shape, f32)] * 2
        + [jax.ShapeDtypeStruct((pieces[0].shape[0] - weight.shape[0], LANES), f32)],
        compiler_params=params(),
        cost_estimate=cost(0.1),
        name="update_bc",
    )(rank, weight, moment, *pieces)


def fence(*values):
    leaves, tree = jax.tree.flatten(values)
    return jax.tree.unflatten(tree, lax.optimization_barrier(leaves))


def outer_from(v, k):
    n = lax.axis_size("dp") // 2
    return lax.ppermute(v, "dp", [(((o + k) % n) * 2 + x, o * 2 + x) for o in range(n) for x in range(2)])


def outer_flip(v, bit):
    n = lax.axis_size("dp") // 2
    return lax.ppermute(v, "dp", [((o ^ bit) * 2 + x, o * 2 + x) for o in range(n) for x in range(2)])


def inner_flip(v):
    return lax.ppermute(v, "dp", [(d ^ 1, d) for d in range(lax.axis_size("dp"))])


def rank_flip(v, bit):
    return lax.ppermute(v, "mp", [(m ^ bit, m) for m in range(lax.axis_size("mp"))])


def hops(n):
    order = []
    for k in range(1, n // 2 + 1):
        order.append(k)
        if n - k != k:
            order.append(n - k)
    return order


def pair_sum(a, b):
    return (a.astype(f32) + b.astype(f32)).astype(bf16)


def outer_blocks(own, here, back, ks):
    rows = own.shape[0]
    back = [part[i:i + rows] for part in back for i in range(0, part.shape[0], rows)]
    return [
        (here[i * rows:(i + 1) * rows].astype(f32) + back[i].astype(f32)).astype(bf16) for i in range(len(ks))
    ]


def outer_send(blocks, ks):
    n = lax.axis_size("dp") // 2
    return [outer_from(block, n - k) for block, k in zip(blocks, ks)]


def outer_sum(v):
    bit = 1
    while bit < lax.axis_size("dp") // 2:
        v = v + outer_flip(v, bit)
        bit *= 2
    return v


def mp_sum(v):
    v = v + rank_flip(v, 1)
    return v + rank_flip(v, 2)


def mp_sum_direct(v):
    return (v + rank_flip(v, 1)) + (rank_flip(v, 2) + rank_flip(v, 3))


def mp_reduce(blocks):
    far = blocks[2].astype(f32) + rank_flip(blocks[3], 1).astype(f32)
    near = blocks[0].astype(f32) + rank_flip(blocks[1], 1).astype(f32)
    return near, rank_flip(far.astype(bf16), 2)


def mp_pieces(v):
    far = rank_flip(v, 2)
    return [v, rank_flip(v, 1), far, rank_flip(far, 1)]


def in_rank_order(pieces, rank, axis):
    odd, high = (rank & 1) == 1, (rank & 2) == 2
    join = lambda a, b: jnp.concatenate([a, b], axis=axis)
    low = jnp.where(odd, join(pieces[1], pieces[0]), join(pieces[0], pieces[1]))
    far = jnp.where(odd, join(pieces[3], pieces[2]), join(pieces[2], pieces[3]))
    return jnp.where(high, join(far, low), join(low, far))


def momentum(moment, grad):
    return 0.5 * moment + 0.5 * grad


def advance(weight, moment, grad):
    fresh = momentum(moment, grad)
    return (fresh, weight - LEARN_RATE * fresh - LEARN_RATE * DECAY_RATE * weight)


def body(
    hidden, segments, cotangent, in_weight, in_moment, bc_weight, bc_moment, step_weight, step_moment,
    out_weight, out_moment, conv_table, conv_moment, bc_table, bc_table_moment, head_table, head_moment,
    norm_gain, gain_moment,
):
    size = lax.axis_size("dp")
    ranks = lax.axis_size("mp")
    n = size // 2
    place, rank = lax.axis_index("dp"), lax.axis_index("mp")
    outer, inner = place // 2, place % 2
    rank1 = rank.reshape(1).astype(jnp.int32)
    rows, _, channels = in_weight.shape
    heads = head_table.shape[1]
    tokens, depth = hidden.shape
    share = bc_weight.shape[1] // ranks

    ks = hops(n)
    near_ks, far_k = ks[:-1], ks[-1]

    def members(order):
        return jnp.stack([((outer + k) % n) * 2 + (inner ^ j) for k, j in order]).astype(jnp.int32)

    first = [(0, 0), (0, 1)]
    idx = members(first + [(k, 0) for k in ks] + [(k, 1) for k in ks])
    idx_s = members([(0, 0)] + [(k, 0) for k in ks] + [(0, 1)] + [(k, 1) for k in ks])
    sizes = (1, 1, n - 1, n - 1)
    split_sizes = (1, 1, n - 1, n - 2, 1)
    width = depth // ranks

    set_a, set_b = pack(in_weight, bc_weight, step_weight.T, rank1), pack_gate(in_weight)
    set_c = out_weight.T.astype(bf16)

    def blocks(own, z, x):
        return [own, x[0]] + [z[k] for k in ks] + [x[k] for k in ks]

    def block(v, i):
        return v[i * rows:(i + 1) * rows]

    def blocks(own, z, x):
        return [own, x[0]] + [z[k] for k in ks] + [x[k] for k in ks]

    def block(v, i):
        return v[i * rows:(i + 1) * rows]

    def total(own, own_got, got):
        value = own.astype(f32) + own_got.astype(f32)
        for part in got:
            value = value + part.astype(f32)
        return value

    def outer_all(v, some):
        return {k: outer_from(v, k) for k in some}

    def flip_all(z, some):
        return {k: inner_flip(z[k]) for k in some}

    a_z = outer_all(set_a, near_ks)
    a_x = {0: inner_flip(set_a)}
    far_a, a_x[0] = fence(set_a, a_x[0])
    a_z[far_k] = outer_from(far_a, far_k)
    cot_far = rank_flip(cotangent, 2)
    gain_rows = pad_rows(norm_gain[None])
    normed_low, normed_t, inv_rms = prepare(hidden, gain_rows)
    a_x.update(flip_all(a_z, near_ks))
    aux, seg_row = segment_facts(segments)
    head_rows = pad_lanes(pad_rows(head_table))
    facts = (aux, seg_row, pad_rows(conv_table), pad_rows(bc_table), head_rows, *head_expand(channels))
    set_a, set_b, set_c, a_z, a_x, cot_far, normed_low, normed_t, inv_rms, facts = fence(
        set_a, set_b, set_c, a_z, a_x, cot_far, normed_low, normed_t, inv_rms, facts
    )

    a_x[far_k] = inner_flip(a_z[far_k])
    b_x = {0: inner_flip(set_b)}
    b_z = outer_all(set_b, near_ks)
    cot, cot_t = join_columns([cotangent, rank_flip(cotangent, 1), cot_far, rank_flip(cot_far, 1)], rank1)
    set_b, set_c, b_z, b_x, a_z, a_x, cot, cot_t, normed_low = fence(
        set_b, set_c, b_z, b_x, a_z, a_x, cot, cot_t, normed_low
    )

    b_z[far_k] = outer_from(set_b, far_k)
    b_x.update(flip_all(b_z, near_ks[:1]))
    c_x = {0: inner_flip(set_c)}
    a_blocks = blocks(set_a, a_z, a_x)
    small, bc_share, w_s, w_bct_share = project_small(normed_low, a_blocks, idx, share)
    bc_far, bc_near = rank_flip(bc_share, 2), rank_flip(bc_share, 1)
    x_pre, w_a = project(normed_low, a_blocks, idx, channels)
    bc_far, x_pre, small, set_c, w_bct_share, w_s = fence(bc_far, x_pre, small, set_c, w_bct_share, w_s)
    bc_pieces = [bc_share, bc_near, bc_far, rank_flip(bc_far, 1)]
    bc_pre, step_pre = join_small(bc_pieces, small, rank1)
    set_c, b_z, b_x, c_x, x_pre, bc_pre, step_pre, w_bct_share = fence(
        set_c, b_z, b_x, c_x, x_pre, bc_pre, step_pre, w_bct_share
    )

    c_z = outer_all(set_c, near_ks)
    b_x.update(flip_all(b_z, ks[1:]))
    kept = ssd_forward(x_pre, bc_pre, step_pre, *facts[:-1])
    mixed = kept[0]
    mixed, b_x, b_z, c_z, c_x, w_bct_share, set_c = fence(mixed, b_x, b_z, c_z, c_x, w_bct_share, set_c)

    c_z[far_k] = outer_from(set_c, far_k)
    c_x.update(flip_all(c_z, near_ks))
    gate_pre, square, w_b = gate_forward(normed_low, mixed, blocks(set_b, b_z, b_x), idx)
    square = mp_sum_direct(square)
    mixed, gate_pre, square, w_b, w_bct_share, c_z, c_x = fence(mixed, gate_pre, square, w_b, w_bct_share, c_z, c_x)

    c_x[far_k] = inner_flip(c_z[far_k])
    w_bct = [w_bct_share, rank_flip(w_bct_share, 2)]
    conv_rows = facts[2]
    gated_out = gated_norm(gate_pre, mixed, square, conv_rows, channels * ranks)
    gc_own, gc_own1, gc_here, gc_near, gc_far = weight_grad(cot_t, gated_out, idx, split_sizes)
    c_x, square, gated_out, gc_own, gc_own1, gc_here, gc_near, gc_far, w_bct = fence(
        c_x, square, gated_out, gc_own, gc_own1, gc_here, gc_near, gc_far, w_bct
    )

    gc_far_back, gc_near_back = inner_flip(gc_far), inner_flip(gc_near)
    gout, inner_dot, w_c = grad_gout(cot, gate_pre, mixed, conv_rows, blocks(set_c, c_z, c_x), idx)
    gout, inner_dot, w_c = fence(gout, inner_dot, w_c)
    inner_dot = mp_sum_direct(inner_dot)
    partial = out_partial(gated_out, w_c, rank1, ranks)
    inner_dot, gout, partial, w_bct, gc_far_back = fence(inner_dot, gout, partial, w_bct, gc_far_back)
    c_far_got = outer_from(pair_sum(block(gc_here, n - 2), gc_far_back), n - far_k)
    out_back = rank_flip(partial[3], 1)
    w_bct = [w_bct[0], rank_flip(w_bct[0], 1), w_bct[1], rank_flip(w_bct[1], 1)]
    dmixed, dgate, dgain = gate_backward(gate_pre, gout, mixed, square, inner_dot, conv_rows, channels * ranks)
    gb_own, gb_own1, gb_here, gb_send = weight_grad(normed_t, dgate, idx, sizes)
    gc_near_back, c_far_got, w_bct, out_back, gb_own, gb_own1, gb_here, gb_send, partial, dmixed, dgain = fence(
        gc_near_back, c_far_got, w_bct, out_back, gb_own, gb_own1, gb_here, gb_send, partial, dmixed, dgain
    )
    c_blocks = [pair_sum(block(gc_here, i), block(gc_near_back, i)) for i in range(n - 2)]
    out_far = pair_sum(partial[2], out_back)
    c_blocks, out_far, w_bct, dmixed, gb_send = fence(c_blocks, out_far, w_bct, dmixed, gb_send)

    c_got = outer_send(c_blocks, near_ks) + [c_far_got]
    gb_back = inner_flip(gb_send)
    out_got = rank_flip(out_far, 2)
    dx, dbc, dbc_keep, dbc_send, dstep, dstep_t, dconv, dbct_part, dheads = ssd_backward(
        rank1, x_pre, bc_pre, step_pre, *facts, dmixed, kept
    )
    c_got, gb_back, out_got, dx, dbc, dbc_keep, dbc_send, dstep, dstep_t, dconv, dbct_part, dheads = fence(
        c_got, gb_back, out_got, dx, dbc, dbc_keep, dbc_send, dstep, dstep_t, dconv, dbct_part, dheads
    )

    b_got = {far_k: outer_from(pair_sum(block(gb_here, n - 2), block(gb_back, n - 2)), n - far_k)}
    dbc_back = rank_flip(dbc_send, 1)
    out_near_back = rank_flip(partial[1], 1)
    ga_own, ga_own1, ga_here, ga_send = weight_grad(normed_t, dx, idx, sizes, us=20)
    ga_own, ga_own1, ga_here, ga_send, dx, dbc_back, gb_back, gb_here, out_near_back = fence(
        ga_own, ga_own1, ga_here, ga_send, dx, dbc_back, gb_back, gb_here, out_near_back
    )

    b_near = [pair_sum(block(gb_here, i), block(gb_back, i)) for i in range(n - 2)]
    b_got.update(zip(near_ks, outer_send(b_near, near_ks)))
    ga_back = inner_flip(ga_send)
    dbc_pair = pair_sum(dbc_keep, dbc_back)
    dbc_got = rank_flip(dbc_pair[share:], 2)
    operands = (dx, dgate, dstep, dbc, w_a, w_b, w_s, w_bct, hidden, inv_rms, rank1, ranks)
    far_own, far_send, gain_far = normed_term(*operands, (2, 3))
    far_own, far_send, gain_far, dx, dbc_got, dbc_pair, dstep_t, b_got[far_k] = fence(
        far_own, far_send, gain_far, dx, dbc_got, dbc_pair, dstep_t, b_got[far_k]
    )
    far_back = rank_flip(far_send, 1)
    operands = (dx, *operands[1:])
    near_own, near_send, gain_near = normed_term(*operands, (0, 1))
    far_back, near_own, near_send, gain_near, ga_back = fence(far_back, near_own, near_send, gain_near, ga_back)
    near_back = rank_flip(near_send, 1)
    far = pair_sum(far_own, far_back)
    a_blocks = [pair_sum(block(ga_here, i), block(ga_back, i)) for i in range(n - 1)]
    dbc_share = pair_sum(dbc_pair[:share], dbc_got)
    dsmall_t = jnp.concatenate([dbc_share, dstep_t, jnp.zeros((LANES - share - 16, tokens), bf16)], axis=0)
    gs_own, gs_here, gs_send = weight_grad(normed_t, dsmall_t, idx_s, (1, n - 1, n), turned=True)
    far, a_blocks, near_back, gs_send, gc_own1, gb_own1, b_got = fence(
        far, a_blocks, near_back, gs_send, gc_own1, gb_own1, b_got
    )

    early, late = [], near_ks
    got = rank_flip(far, 2)
    a_got = dict(zip([far_k, *early], outer_send([a_blocks[-1], *a_blocks[:len(early)]], [far_k, *early])))
    cut = lambda v: [v[:, i:i + LANES] for i in range(0, v.shape[1], LANES)]
    alone = channels // LANES * 8 + 8
    sums = jnp.concatenate([*cut(dconv + dgain), dheads, *cut(dbct_part), gain_far + gain_near], axis=0)
    shared = (alone, sums.shape[0])
    wide = (channels + LANES) // LANES
    sums = pad_rows(sums, -(-sums.shape[0] // (16 * wide)) * 16 * wide).astype(bf16)
    small_back = inner_flip(jnp.concatenate([gs_send, sums], axis=0))
    own_got = inner_flip(jnp.concatenate([gc_own1, gb_own1], axis=1))
    near = near_own.astype(f32) + near_back.astype(f32)
    got, near, a_got, small_back, sums, own_got, ga_own1, a_late = fence(
        got, near, a_got, small_back, sums, own_got, ga_own1, a_blocks[len(early):-1]
    )

    mine = norm_backward(near, got, hidden, cot, gain_rows, rank1)
    mine, small_back, sums, ga_own1, a_late, gs_here, out_got, out_near_back = fence(
        mine, small_back, sums, ga_own1, a_late, gs_here, out_got, out_near_back
    )
    a_own_got = inner_flip(ga_own1)
    gs_back, sums_back = small_back[:n * rows], small_back[n * rows:]
    s_blocks = dict(zip(ks, outer_blocks(gs_own, gs_here, [gs_back[rows:]], ks)))
    sums = pair_sum(sums, sums_back)
    size = sums.shape[0] // wide
    sums_wide = jnp.concatenate([sums[i * size:(i + 1) * size] for i in range(wide)], axis=1)
    late_got = outer_send(
        [
            jnp.concatenate([jnp.concatenate([a_block, s_blocks[k]], axis=1), sums_wide], axis=0)
            for k, a_block in zip(late, a_late)
        ],
        late,
    )
    s_got = outer_send([jnp.concatenate([s_blocks[k], sums], axis=0) for k in (far_k, *early)], (far_k, *early))
    mine_far = rank_flip(mine, 2)
    mine_far, mine = fence(mine_far, mine)
    late_got, s_got, a_own_got, sums = fence(late_got, s_got, a_own_got, sums)

    mine_near, mine_far_near = rank_flip(mine, 1), rank_flip(mine_far, 1)
    step_m, step_w, exchange, totals = update_small(
        step_weight.T, step_moment.T, sums, gs_own, gs_back, s_got, late_got,
        (len(s_got), [n - k for k in (far_k, *early)], [n - k for k in late]), shared, share,
    )
    exchanged = [exchange] + [rank_flip(exchange, r) for r in (1, 2, 3)]
    in_m, in_w = update_in(
        in_weight, in_moment,
        [(gb_own, 0), (own_got, 1)] + [(b_got[k], 0) for k in ks],
        [(ga_own, 0), (a_own_got, 0)] + [(a_got[k], 0) for k in (far_k, *early)] + [(v, 0) for v in late_got],
    )
    input_grad = join_rows([mine, mine_near, mine_far, mine_far_near], rank1)
    exchanged, mine_far_near = fence(exchanged, mine_far_near)
    bc_m, bc_w, totals_shared = update_bc(bc_weight, bc_moment, exchanged, rank1)

    resid = lax.dynamic_slice_in_dim(hidden, rank * width, width, 1).astype(f32)
    output = (resid + partial[0].astype(f32) + out_near_back.astype(f32) + out_got.astype(f32)).astype(bf16)
    shard_c = total(gc_own, own_got[:, :channels], c_got)

    side_by_side = lambda v: jnp.concatenate([v[i:i + 8] for i in range(0, v.shape[0], 8)], axis=1)
    total_conv = side_by_side(totals[:alone - 8])[:6]
    total_head = totals[alone - 8:alone - 5, :heads]
    total_bct = side_by_side(totals_shared[:16])[:5]
    per = TILE_D // LANES
    total_gain = jnp.concatenate([totals_shared[i:i + per] for i in range(16, totals_shared.shape[0], 8)], axis=0).reshape(-1)

    out_m, out_w = advance(out_weight, out_moment, shard_c.T)
    return (
        output, input_grad, in_m, in_w, bc_m, bc_w, step_m.T, step_w.T, out_m, out_w,
        momentum(conv_moment, total_conv),
        momentum(bc_table_moment, total_bct),
        momentum(head_moment, total_head),
        momentum(gain_moment, total_gain),
    )


def solution(mesh):
    placed = (
        P("dp", None),
        P("dp", None),
        P("dp", "mp"),
        P("dp", None, "mp"),
        P("dp", None, "mp"),
        P("dp", None),
        P("dp", None),
        P("dp", "mp"),
        P("dp", "mp"),
        P("mp", "dp"),
        P("mp", "dp"),
        P(None, "mp"),
        P(None, "mp"),
        P(),
        P(),
        P(None, "mp"),
        P(None, "mp"),
        P(),
        P(),
    )
    return jax.shard_map(
        body,
        mesh=mesh,
        in_specs=placed,
        out_specs=(
            P("dp", "mp"),
            P("dp", None),
            P("dp", None, "mp"),
            P("dp", None, "mp"),
            P("dp", None),
            P("dp", None),
            P("dp", "mp"),
            P("dp", "mp"),
            P("mp", "dp"),
            P("mp", "dp"),
            P(None, "mp"),
            P(),
            P(None, "mp"),
            P(),
        ),
        check_vma=False,
    )
```

```python
import functools

import jax
import jax.numpy as jnp
from jax import lax
from jax.experimental import pallas as pl
from jax.experimental.pallas import tpu as pltpu
from jax.sharding import PartitionSpec as P

CHUNK = 128
EPSILON = 1e-05
LEARN_RATE = 0.0001
DECAY_RATE = 0.1
WIDTH = 64
LANES = 128
HALO = 8
bf16 = jnp.bfloat16
f32 = jnp.float32
MIB = 1024 * 1024


def hbm(shape, dtype):
    return pltpu.HBM(shape, dtype)


def from_hbm(v):
    return pltpu.with_memory_space_constraint(v, pltpu.HBM)


def dot_nn(a, b):
    return lax.dot_general(a, b, (((1,), (0,)), ((), ())), preferred_element_type=f32)


def dot_nt(a, b):
    return lax.dot_general(a, b, (((1,), (1,)), ((), ())), preferred_element_type=f32)


def dot_tn(a, b):
    return lax.dot_general(a, b, (((0,), (0,)), ((), ())), preferred_element_type=f32)


def split3(v):
    high = v.astype(bf16)
    rest = v - high.astype(f32)
    mid = rest.astype(bf16)
    low = (rest - mid.astype(f32)).astype(bf16)
    return high, mid, low


def exact_left(ones, v):
    high, mid, low = split3(v)
    return dot_nn(ones, high) + dot_nn(ones, mid) + dot_nn(ones, low)


def spread(v, expand):
    high, mid, low = split3(v)
    return dot_nn(high, expand) + dot_nn(mid, expand) + dot_nn(low, expand)


def gather_heads(v, expand_t):
    high = v.astype(bf16)
    mid = (v - high.astype(f32)).astype(bf16)
    return dot_nn(high, expand_t) + dot_nn(mid, expand_t)


def sigmoid(v):
    return 0.5 * jnp.tanh(0.5 * v) + 0.5


def conv_block(before, now, taps, keep):
    longer = jnp.concatenate([before, now], axis=0)
    total = taps[4:5, :] + taps[0:1, :] * now
    for lag in (1, 2, 3):
        moved = pltpu.roll(longer, lag, 0)[HALO:, :]
        total = total + taps[lag:lag + 1, :] * (moved * keep[:, lag - 1:lag])
    return total


def step_parts(step_pre, heads):
    raw = step_pre + heads[0:1, :]
    small = jnp.exp(-jnp.abs(raw))
    steps = jnp.maximum(raw, 0.0) + jnp.log1p(small)
    slope = jnp.where(raw >= 0.0, 1.0, small) / (1.0 + small)
    rates = -jnp.exp(heads[1:2, :])
    return slope, steps, rates


def triangle(lower):
    row = lax.broadcasted_iota(jnp.int32, (CHUNK, CHUNK), 0)
    col = lax.broadcasted_iota(jnp.int32, (CHUNK, CHUNK), 1)
    return row >= col if lower else row <= col


def ssd_forward_kernel(
    x_ref, xb_ref, bc_ref, bcb_ref, st_ref, aux_ref, seg_ref, conv_ref, bct_ref, heads_ref, expand_ref,
    mixed_ref, state_ref, act_ref, slope_ref, xs_ref, xe_ref, step_ref, entry_ref, end_ref, bcact_ref, bcslope_ref,
    state,
):
    chunk = pl.program_id(0)

    @pl.when(chunk == 0)
    def _():
        state[...] = jnp.zeros_like(state)

    channels = x_ref.shape[1]
    aux = aux_ref[...]
    expand = expand_ref[...]
    u = conv_block(xb_ref[...], x_ref[...], conv_ref, aux)
    sg = sigmoid(u)
    x_act = u * sg
    act_ref[...] = x_act
    slope_ref[...] = (sg * (1.0 + u * (1.0 - sg))).astype(bf16)
    ubc = conv_block(bcb_ref[...], bc_ref[...], bct_ref, aux)
    sgbc = sigmoid(ubc)
    bc_act = (ubc * sgbc).astype(bf16)
    bcact_ref[...] = bc_act
    bcslope_ref[...] = sgbc * (1.0 + ubc * (1.0 - sgbc))
    b_mat, c_mat = bc_act[:, :LANES], bc_act[:, LANES:]
    _, steps, rates = step_parts(st_ref[...], heads_ref)
    lower = triangle(True)
    cum = exact_left(lower.astype(bf16), steps * rates)
    cum_t = cum.T
    tail = cum[CHUNK - 1:CHUNK, :]
    entry = jnp.exp(cum) * aux[:, 6:7]
    to_end = jnp.exp(tail - cum) * aux[:, 7:8]
    wide = spread(jnp.concatenate([steps, entry, to_end], axis=0), expand)
    step_e, entry_e, to_end_e = wide[:CHUNK], wide[CHUNK:2 * CHUNK], wide[2 * CHUNK:]
    skip_e = spread(jnp.broadcast_to(heads_ref[2:3, :], (8, LANES)), expand)[0:1, :]
    mask = lower & (aux[:, 8:9] == seg_ref[...])
    scores = jnp.where(mask, dot_nt(c_mat, b_mat), 0.0)
    xs = x_act * step_e
    xs_low = xs.astype(bf16)
    xe_low = (xs * to_end_e).astype(bf16)
    xs_ref[...] = xs_low
    xe_ref[...] = xe_low
    step_ref[...] = step_e.astype(bf16)
    entry_ref[...] = entry_e.astype(bf16)
    end_ref[...] = to_end_e.astype(bf16)
    held = state[...]
    held_low = held.astype(bf16)
    state_ref[...] = held_low
    out = dot_nn(c_mat, held_low) * entry_e + skip_e * x_act
    state[...] = held * entry_e[CHUNK - 1:CHUNK, :] + dot_tn(b_mat, xe_low)
    first = lax.broadcasted_iota(jnp.int32, (CHUNK, LANES), 1) < WIDTH
    zero = jnp.zeros((CHUNK, LANES), bf16)
    for pair in range(channels // LANES):
        span = slice(pair * LANES, (pair + 1) * LANES)
        parts = []
        for head in (2 * pair, 2 * pair + 1):
            diff = cum[:, head:head + 1] - cum_t[head:head + 1, :]
            parts.append((scores * jnp.exp(jnp.minimum(diff, 0.0))).astype(bf16))
        own = xs_low[:, span]
        both = jnp.concatenate([jnp.where(first, own, zero), jnp.where(first, zero, own)], axis=0)
        mixed_ref[:, span] = out[:, span] + dot_nn(jnp.concatenate(parts, axis=1), both)


def ssd_backward_kernel(
    rank_ref, x_ref, bc_ref, st_ref, aux_ref, seg_ref, conv_ref, bct_ref, heads_ref, expand_ref,
    expand_t_ref, mixed_ref, dy_ref, state_ref, act_ref, slope_ref, xs_ref, xe_ref, step_ref, entry_ref, end_ref, bcact_ref,
    bcslope_ref, dx_ref, dbc_ref, keep_ref, send_ref, dst_ref, dst_t_ref, dconv_ref, dbct_ref, dheads_ref,
    dstate, du_scr, dubc_scr, share_scr,
):
    @pl.when(pl.program_id(0) == 0)
    def _():
        for ref in (dstate, du_scr, dubc_scr, dconv_ref, dbct_ref, dheads_ref):
            ref[...] = jnp.zeros_like(ref)

    channels = x_ref.shape[1]
    aux = aux_ref[...]
    expand = expand_ref[...]
    x_act = act_ref[...]
    b_mat, c_mat = bcact_ref[:, :LANES], bcact_ref[:, LANES:]
    slope, steps, rates = step_parts(st_ref[...], heads_ref)
    lower = triangle(True)
    cum = exact_left(lower.astype(bf16), steps * rates)
    cum_t = cum.T
    skip_e = spread(jnp.broadcast_to(heads_ref[2:3, :], (8, LANES)), expand)[0:1, :]
    upper = triangle(False)
    mask = upper & (aux[:, 8:9] == seg_ref[...])
    scores = jnp.where(mask, dot_nt(b_mat, c_mat), 0.0)
    xs_low = xs_ref[...]
    dy_low = dy_ref[...]
    dy = dy_low.astype(f32)
    held_low = state_ref[...]
    grad = dstate[...]
    grad_low = grad.astype(bf16)
    entry_e = entry_ref[...].astype(f32)
    entry_dy = (entry_e * dy).astype(bf16)
    kept_e = entry_e[CHUNK - 1:CHUNK, :]
    dstate[...] = grad * kept_e + dot_tn(c_mat, entry_dy)
    dc = dot_nt(entry_dy, held_low)
    db = dot_nt(xe_ref[...], grad_low)
    q_state = dot_nn(b_mat, grad_low) * end_ref[...].astype(f32)
    first = lax.broadcasted_iota(jnp.int32, (CHUNK, LANES), 1) < WIDTH
    zero = jnp.zeros((CHUNK, LANES), bf16)
    dscores = jnp.zeros((CHUNK, CHUNK), f32)
    q_parts = []
    for pair in range(channels // LANES):
        span = slice(pair * LANES, (pair + 1) * LANES)
        own = dy_low[:, span]
        both = jnp.concatenate([jnp.where(first, own, zero), jnp.where(first, zero, own)], axis=0)
        dweights = dot_nt(xs_low[:, span], both)
        parts = []
        for i, head in enumerate((2 * pair, 2 * pair + 1)):
            diff = cum_t[head:head + 1, :] - cum[:, head:head + 1]
            decay = jnp.exp(jnp.minimum(diff, 0.0))
            parts.append((scores * decay).astype(bf16))
            dscores = dscores + dweights[:, i * LANES:(i + 1) * LANES] * decay
        q_parts.append(dot_nn(jnp.concatenate(parts, axis=1), both))
    q = jnp.concatenate(q_parts, axis=1) + q_state
    dscores_low = jnp.where(mask, dscores, 0.0).astype(bf16)
    db = db + dot_nn(dscores_low, c_mat)
    dc = dc + dot_tn(dscores_low, b_mat)
    xs_round = xs_low.astype(f32)
    expand_t = expand_t_ref[...]
    flow = gather_heads(dy * (mixed_ref[...] - skip_e * x_act) - xs_round * q, expand_t)
    dstep = dot_nn((x_act * q).astype(bf16), expand_t)
    sums = jnp.concatenate(
        [
            jnp.sum(xs_round * q_state + kept_e * (held_low.astype(f32) * grad), axis=0, keepdims=True),
            jnp.sum(dy * x_act, axis=0, keepdims=True),
            jnp.zeros((6, channels), f32),
        ],
        axis=0,
    )
    sums = gather_heads(sums, expand_t)
    dlog = exact_left(upper.astype(bf16), flow) + sums[0:1, :]
    dstep = dstep + rates * dlog
    draw = dstep * slope
    dst_ref[...] = pltpu.roll(draw, WIDTH, 1).astype(bf16)
    dst_t_ref[...] = draw.T[0:16, :].astype(bf16)
    dheads_ref[0:1, :] += jnp.sum(draw, axis=0, keepdims=True)
    dheads_ref[1:2, :] += rates * jnp.sum(dlog * steps, axis=0, keepdims=True)
    dheads_ref[2:3, :] += sums[1:2, :]
    x_now, bc_now = x_ref[...], bc_ref[...]

    def conv_back(scratch, du, now, taps, dtaps):
        longer = jnp.concatenate([du, scratch[...]], axis=0)
        total = taps[0:1, :] * du
        sums = [jnp.sum(now * du, axis=0, keepdims=True)]
        for lag in (1, 2, 3):
            moved = pltpu.roll(longer, CHUNK + HALO - lag, 0)[0:CHUNK, :] * aux[:, 2 + lag:3 + lag]
            total = total + taps[lag:lag + 1, :] * moved
            sums.append(jnp.sum(now * moved, axis=0, keepdims=True))
        sums.append(jnp.sum(du, axis=0, keepdims=True))
        dtaps[0:5, :] += jnp.concatenate(sums, axis=0)
        scratch[...] = du[0:HALO, :]
        return total

    du = (skip_e * dy + step_ref[...].astype(f32) * q) * slope_ref[...].astype(f32)
    dx_ref[...] = conv_back(du_scr, du, x_now, conv_ref, dconv_ref).astype(dx_ref.dtype)
    dubc = jnp.concatenate([db, dc], axis=1) * bcslope_ref[...]
    dbc = conv_back(dubc_scr, dubc, bc_now, bct_ref, dbct_ref).astype(bf16)
    swapped = jnp.concatenate([dbc[:, LANES:], dbc[:, :LANES]], axis=1)
    ordered = jnp.where((rank_ref[0] & 2) == 2, swapped, dbc)
    swapped = jnp.concatenate(
        [pltpu.roll(ordered[:, :LANES].astype(f32), WIDTH, 1), pltpu.roll(ordered[:, LANES:].astype(f32), WIDTH, 1)], axis=1
    ).astype(bf16)
    dbc_ref[...] = jnp.where((rank_ref[0] & 1) == 1, swapped, ordered)
    share = 2 * LANES // 4
    turned = dbc.T
    for member in range(4):
        apart = member ^ rank_ref[0]
        start = pl.multiple_of((apart & 1) * 2 * share + (apart >> 1) * share, share)
        share_scr[pl.ds(start, share), :] = turned[member * share:(member + 1) * share, :]
    keep_ref[...] = share_scr[0:2 * share, :]
    send_ref[...] = share_scr[2 * share:4 * share, :]


def common_specs(place, channels):
    before = lambda i: (jnp.maximum(place(i) * (CHUNK // HALO) - 1, 0), 0)
    now = lambda i: (place(i), 0)
    whole = lambda i: (0, 0)
    return [
        pl.BlockSpec((CHUNK, channels), now),
        pl.BlockSpec((HALO, channels), before),
        pl.BlockSpec((CHUNK, 2 * LANES), now),
        pl.BlockSpec((HALO, 2 * LANES), before),
        pl.BlockSpec((CHUNK, LANES), now),
        pl.BlockSpec((CHUNK, 16), now),
        pl.BlockSpec((1, CHUNK), lambda i: (0, place(i))),
        pl.BlockSpec((8, channels), whole),
        pl.BlockSpec((8, 2 * LANES), whole),
        pl.BlockSpec((8, LANES), whole),
        pl.BlockSpec((LANES, channels), whole),
    ]


def ssd_forward(x_pre, bc_pre, step_pre, aux, seg_row, conv_rows, bc_rows, head_rows, expand):
    tokens, channels = x_pre.shape
    count = tokens // CHUNK
    now = lambda i: (i, 0)
    return pl.pallas_call(
        ssd_forward_kernel,
        grid=(count,),
        in_specs=common_specs(lambda i: i, channels),
        out_specs=[
            pl.BlockSpec((CHUNK, channels), now),
            pl.BlockSpec((None, LANES, channels), lambda i: (i, 0, 0)),
        ]
        + [pl.BlockSpec((CHUNK, channels), now)] * 7
        + [pl.BlockSpec((CHUNK, 2 * LANES), now)] * 2,
        out_shape=[
            hbm((tokens, channels), f32),
            hbm((count, LANES, channels), bf16),
            hbm((tokens, channels), f32),
            *[hbm((tokens, channels), bf16) for _ in range(6)],
            hbm((tokens, 2 * LANES), bf16),
            hbm((tokens, 2 * LANES), f32),
        ],
        scratch_shapes=[
            pltpu.VMEM((LANES, channels), f32),
        ],
        compiler_params=pltpu.CompilerParams(vmem_limit_bytes=18 * MIB),
        cost_estimate=pl.CostEstimate(flops=14 * 10**9, bytes_accessed=40 * 10**6, transcendentals=0),
        name="ssd_forward",
    )(
        from_hbm(x_pre), from_hbm(x_pre), bc_pre, bc_pre, step_pre, aux, seg_row, conv_rows, bc_rows, head_rows, expand
    )


def ssd_backward(rank, x_pre, bc_pre, step_pre, aux, seg_row, conv_rows, bc_rows, head_rows, expand, expand_t, dy, kept):
    tokens, channels = x_pre.shape
    count = tokens // CHUNK
    place = lambda i: count - 1 - i
    now = lambda i: (place(i), 0)
    whole = lambda i: (0, 0)
    wide = pl.BlockSpec((CHUNK, channels), now)
    narrow = pl.BlockSpec((CHUNK, 2 * LANES), now)
    specs = common_specs(place, channels)
    mixed, states, *more = kept
    return pl.pallas_call(
        ssd_backward_kernel,
        grid=(count,),
        in_specs=[pl.BlockSpec(memory_space=pltpu.SMEM), specs[0], specs[2], *specs[4:]]
        + [pl.BlockSpec((channels, LANES), whole), wide, wide, pl.BlockSpec((None, LANES, channels), lambda i: (place(i), 0, 0))]
        + [wide] * 7 + [narrow] * 2,
        out_specs=[
            wide,
            narrow,
            pl.BlockSpec((LANES, CHUNK), lambda i: (0, place(i))),
            pl.BlockSpec((LANES, CHUNK), lambda i: (0, place(i))),
            pl.BlockSpec((CHUNK, LANES), now),
            pl.BlockSpec((16, CHUNK), lambda i: (0, place(i))),
            pl.BlockSpec((8, channels), whole),
            pl.BlockSpec((8, 2 * LANES), whole),
            pl.BlockSpec((8, LANES), whole),
        ],
        out_shape=[
            jax.ShapeDtypeStruct((tokens, channels), bf16),
            jax.ShapeDtypeStruct((tokens, 2 * LANES), bf16),
            hbm((LANES, tokens), bf16),
            hbm((LANES, tokens), bf16),
            jax.ShapeDtypeStruct((tokens, LANES), bf16),
            hbm((16, tokens), bf16),
            jax.ShapeDtypeStruct((8, channels), f32),
            jax.ShapeDtypeStruct((8, 2 * LANES), f32),
            jax.ShapeDtypeStruct((8, LANES), f32),
        ],
        scratch_shapes=[
            pltpu.VMEM((LANES, channels), f32),
            pltpu.VMEM((HALO, channels), f32),
            pltpu.VMEM((HALO, 2 * LANES), f32),
            pltpu.VMEM((2 * LANES, CHUNK), bf16),
        ],
        compiler_params=pltpu.CompilerParams(vmem_limit_bytes=20 * MIB),
        cost_estimate=pl.CostEstimate(flops=28 * 10**9, bytes_accessed=40 * 10**6, transcendentals=0),
        name="ssd_backward",
    )(
        rank, from_hbm(x_pre), bc_pre, step_pre, aux, seg_row, conv_rows, bc_rows, head_rows,
        expand, expand_t, from_hbm(mixed), dy, from_hbm(states), *[from_hbm(v) for v in more],
    )


def segment_facts(seg):
    row = seg[0]
    tokens = row.shape[0]
    cols = []
    for lag in (1, 2, 3):
        cols.append(jnp.pad(row[:-lag], (lag, 0), constant_values=-1) == row)
    for lag in (1, 2, 3):
        cols.append(jnp.pad(row[lag:], (0, lag), constant_values=-1) == row)
    blocks = row.reshape(tokens // CHUNK, CHUNK)
    ends = blocks[:, -1:]
    before = jnp.concatenate([jnp.full((1, 1), -1, row.dtype), ends[:-1]], axis=0)
    cols.append((blocks == before).reshape(-1))
    cols.append((blocks == ends).reshape(-1))
    cols.append(row)
    facts = jnp.stack([c.astype(f32) for c in cols], axis=1)
    return jnp.pad(facts, ((0, 0), (0, 16 - facts.shape[1]))), seg.astype(f32)


def pad_rows(table, rows=8):
    return jnp.pad(table, ((0, rows - table.shape[0]), (0, 0)))


def pad_lanes(table, lanes=LANES):
    return jnp.pad(table, ((0, 0), (0, lanes - table.shape[1])))


def head_expand(channels):
    head, channel = jnp.arange(LANES), jnp.arange(channels) // WIDTH
    return (head[:, None] == channel[None, :]).astype(bf16), (channel[:, None] == head[None, :]).astype(bf16)


TILE = 256
TILE_D = 512


def fill(dest, pieces, idx_ref):
    rows = pieces[0].shape[0]
    s = 0
    for piece in pieces:
        for b in range(piece.shape[0] // rows):
            start = pl.multiple_of(idx_ref[s] * rows, rows)
            dest[pl.ds(start, rows), :] = piece[b * rows:(b + 1) * rows, :]
            s += 1


def params(mib=18):
    return pltpu.CompilerParams(vmem_limit_bytes=mib * MIB)


def cost(us):
    return pl.CostEstimate(flops=int(us * 10**9), bytes_accessed=int(us * 2 * 10**6), transcendentals=0)


def prepare_kernel(hidden_ref, gain_ref, low_ref, low_t_ref, inv_ref):
    inputs = hidden_ref[...].astype(f32)
    inv_rms = lax.rsqrt(jnp.mean(inputs * inputs, axis=1, keepdims=True) + EPSILON)
    low = (inputs * inv_rms * gain_ref[0:1, :]).astype(bf16)
    low_ref[...] = low
    low_t_ref[...] = low.T
    inv_ref[...] = column_to_row(inv_rms)


def prepare(hidden, gain_rows):
    tokens, depth = hidden.shape
    block = pl.BlockSpec((TILE, depth), lambda i: (i, 0))
    return pl.pallas_call(
        prepare_kernel,
        grid=(tokens // TILE,),
        in_specs=[block, pl.BlockSpec((8, depth), lambda i: (0, 0))],
        out_specs=[block, pl.BlockSpec((depth, TILE), lambda i: (0, i)), pl.BlockSpec((8, TILE), lambda i: (0, i))],
        out_shape=[
            hbm((tokens, depth), bf16),
            hbm((depth, tokens), bf16),
            jax.ShapeDtypeStruct((8, tokens), f32),
        ],
        compiler_params=params(),
        cost_estimate=cost(12),
        name="prepare",
    )(hidden, gain_rows)


def pack_kernel(rank_ref, in_ref, bc_ref, step_ref, a_ref, scratch):
    rows, width = bc_ref.shape
    channels = in_ref.shape[2]
    share = width // 4
    heads = step_ref.shape[0]
    a_ref[:, :channels] = in_ref[:, 1, :].astype(bf16)
    scratch[...] = jnp.zeros_like(scratch)
    scratch[share:share + heads, 0:rows] = step_ref[...]
    step = scratch[...].T[0:rows, :]
    own = bc_ref[:, 0:LANES]
    for member in range(1, 4):
        turned = pltpu.roll(bc_ref[...], width - member * share, 1)[:, 0:LANES]
        own = jnp.where(rank_ref[0] == member, turned, own)
    lane = lax.broadcasted_iota(jnp.int32, (rows, LANES), 1)
    a_ref[:, channels:] = jnp.where(lane < share, own, step).astype(bf16)


def pack(in_weight, bc_weight, step_t, rank):
    rows, _, channels = in_weight.shape
    vmem = pl.BlockSpec(memory_space=pltpu.VMEM)
    return pl.pallas_call(
        pack_kernel,
        in_specs=[pl.BlockSpec(memory_space=pltpu.SMEM), vmem, vmem, vmem],
        out_specs=vmem,
        out_shape=jax.ShapeDtypeStruct((rows, channels + LANES), bf16),
        scratch_shapes=[pltpu.VMEM((LANES, 2 * LANES), f32)],
        compiler_params=params(),
        cost_estimate=cost(2),
        name="pack",
    )(rank, from_hbm(in_weight), from_hbm(bc_weight), from_hbm(step_t))


def pack_gate_kernel(in_ref, b_ref):
    b_ref[...] = in_ref[:, 0, :].astype(bf16)


def pack_gate(in_weight):
    rows, _, channels = in_weight.shape
    vmem = pl.BlockSpec(memory_space=pltpu.VMEM)
    return pl.pallas_call(
        pack_gate_kernel,
        in_specs=[vmem],
        out_specs=vmem,
        out_shape=hbm((rows, channels), bf16),
        compiler_params=params(),
        cost_estimate=cost(2),
        name="pack_gate",
    )(from_hbm(in_weight))


def columns_kernel(rank_ref, *refs, count):
    pieces, (full_ref, full_t_ref) = refs[:count], refs[count:]
    for r, piece in enumerate(pieces):
        width = piece.shape[1]
        start = pl.multiple_of((rank_ref[0] ^ r) * width, LANES)
        value = piece[...]
        full_ref[:, pl.ds(start, width)] = value
        full_t_ref[pl.ds(start, width), :] = value.T


def join_columns(pieces, rank):
    tokens, width = pieces[0].shape
    depth = width * len(pieces)
    return pl.pallas_call(
        functools.partial(columns_kernel, count=len(pieces)),
        grid=(tokens // TILE,),
        in_specs=[pl.BlockSpec(memory_space=pltpu.SMEM)] + [pl.BlockSpec((TILE, width), lambda i: (i, 0))] * len(pieces),
        out_specs=[pl.BlockSpec((TILE, depth), lambda i: (i, 0)), pl.BlockSpec((depth, TILE), lambda i: (0, i))],
        out_shape=[jax.ShapeDtypeStruct((tokens, depth), bf16), jax.ShapeDtypeStruct((depth, tokens), bf16)],
        compiler_params=params(),
        cost_estimate=cost(12),
        name="join_columns",
    )(rank, *pieces)


def rows_kernel(rank_ref, *refs, count):
    pieces, full_ref = refs[:count], refs[count]
    for r, piece in enumerate(pieces):
        rows = piece.shape[0]
        full_ref[pl.ds(pl.multiple_of((rank_ref[0] ^ r) * rows, rows), rows), :] = piece[...]


def join_rows(pieces, rank):
    rows, width = pieces[0].shape
    shape = (rows * len(pieces), width)
    return pl.pallas_call(
        functools.partial(rows_kernel, count=len(pieces)),
        in_specs=[pl.BlockSpec(memory_space=pltpu.SMEM)] + [pl.BlockSpec(memory_space=pltpu.VMEM)] * len(pieces),
        out_specs=pl.BlockSpec(memory_space=pltpu.VMEM),
        out_shape=jax.ShapeDtypeStruct(shape, pieces[0].dtype),
        compiler_params=params(),
        cost_estimate=cost(0.1),
        name="join_rows",
    )(rank, *pieces)


def small_kernel(rank_ref, *refs, count):
    pieces, (small_ref, bc_ref, step_ref, scratch) = refs[:count], refs[count:]
    share = pieces[0].shape[0]
    for r, piece in enumerate(pieces):
        scratch[pl.ds(pl.multiple_of((rank_ref[0] ^ r) * share, share), share), :] = piece[...].astype(f32)
    bc_ref[...] = scratch[...].T
    turned = small_ref[...].T
    lane = lax.broadcasted_iota(jnp.int32, turned.shape, 1)
    step_ref[...] = jnp.where(lane < LANES - share, pltpu.roll(turned, LANES - share, 1), 0.0)


def join_small(pieces, small, rank):
    share, tokens = pieces[0].shape
    width = share * len(pieces)
    return pl.pallas_call(
        functools.partial(small_kernel, count=len(pieces)),
        grid=(tokens // TILE,),
        in_specs=[pl.BlockSpec(memory_space=pltpu.SMEM)]
        + [pl.BlockSpec((share, TILE), lambda i: (0, i))] * len(pieces)
        + [pl.BlockSpec((LANES, TILE), lambda i: (0, i))],
        out_specs=[pl.BlockSpec((TILE, width), lambda i: (i, 0)), pl.BlockSpec((TILE, LANES), lambda i: (i, 0))],
        out_shape=[jax.ShapeDtypeStruct((tokens, width), f32), jax.ShapeDtypeStruct((tokens, LANES), f32)],
        scratch_shapes=[pltpu.VMEM((width, TILE), f32)],
        compiler_params=params(),
        cost_estimate=cost(0.1),
        name="join_small",
    )(rank, *pieces, small)


def project_small_kernel(idx_ref, lhs_ref, *refs, count):
    pieces, (small_ref, share_ref, w_ref, wt_ref) = refs[:count], refs[count:]

    @pl.when(pl.program_id(0) == 0)
    def _():
        fill(w_ref, pieces, idx_ref)
        wt_ref[...] = w_ref[...].T[0:wt_ref.shape[0], :]

    small = dot_nn(lhs_ref[...], w_ref[...]).T
    small_ref[...] = small
    share_ref[...] = small[0:share_ref.shape[0], :].astype(bf16)


def project_small(lhs, pieces, idx, share):
    tokens, depth = lhs.shape
    count, last = len(pieces), pieces[0].shape[1] // LANES - 1
    whole = lambda i: (0, 0)
    return pl.pallas_call(
        functools.partial(project_small_kernel, count=count),
        grid=(tokens // TILE,),
        in_specs=[pl.BlockSpec(memory_space=pltpu.SMEM), pl.BlockSpec((TILE, depth), lambda i: (i, 0))]
        + [pl.BlockSpec((p.shape[0], LANES), lambda i: (0, last)) for p in pieces],
        out_specs=[
            pl.BlockSpec((LANES, TILE), lambda i: (0, i)),
            pl.BlockSpec((share, TILE), lambda i: (0, i)),
            pl.BlockSpec((depth, LANES), whole),
            pl.BlockSpec((share, depth), whole),
        ],
        out_shape=[
            jax.ShapeDtypeStruct((LANES, tokens), f32),
            jax.ShapeDtypeStruct((share, tokens), bf16),
            hbm((depth, LANES), bf16),
            jax.ShapeDtypeStruct((share, depth), bf16),
        ],
        compiler_params=params(),
        cost_estimate=cost(20),
        name="project_small",
    )(idx, lhs, *pieces)


def project_kernel(idx_ref, lhs_ref, *refs, count):
    pieces, (x_ref, w_ref) = refs[:count], refs[count:]

    @pl.when(pl.program_id(0) == 0)
    def _():
        fill(w_ref, pieces, idx_ref)

    x_ref[...] = dot_nn(lhs_ref[...], w_ref[...])


def project(lhs, pieces, idx, channels):
    tokens, depth = lhs.shape
    whole = lambda i: (0, 0)
    return pl.pallas_call(
        functools.partial(project_kernel, count=len(pieces)),
        grid=(tokens // TILE,),
        in_specs=[pl.BlockSpec(memory_space=pltpu.SMEM), pl.BlockSpec((TILE, depth), lambda i: (i, 0))]
        + [pl.BlockSpec((p.shape[0], channels), whole) for p in pieces],
        out_specs=[pl.BlockSpec((TILE, channels), lambda i: (i, 0)), pl.BlockSpec((depth, channels), whole)],
        out_shape=[
            hbm((tokens, channels), f32),
            hbm((depth, channels), bf16),
        ],
        compiler_params=params(),
        cost_estimate=cost(0.1),
        name="project",
    )(idx, lhs, *pieces)


def column_to_row(col):
    return jnp.broadcast_to(col, (col.shape[0], LANES)).T[0:8, :]


def row_to_column(row):
    return jnp.broadcast_to(row, (LANES, row.shape[1])).T[:, 0:1]


def gate_kernel(idx_ref, lhs_ref, mixed_ref, *refs, count):
    pieces, (gate_ref, sums_ref, w_ref) = refs[:count], refs[count:]

    @pl.when(pl.program_id(0) == 0)
    def _():
        fill(w_ref, pieces, idx_ref)

    gate = dot_nn(lhs_ref[...], w_ref[...])
    gate_ref[...] = gate
    gated = mixed_ref[...] * (gate * sigmoid(gate))
    sums_ref[...] = column_to_row(jnp.sum(gated * gated, axis=1, keepdims=True))


def gate_forward(lhs, mixed, pieces, idx):
    tokens, depth = lhs.shape
    channels = mixed.shape[1]
    whole = lambda i: (0, 0)
    now = lambda i: (i, 0)
    return pl.pallas_call(
        functools.partial(gate_kernel, count=len(pieces)),
        grid=(tokens // TILE,),
        in_specs=[
            pl.BlockSpec(memory_space=pltpu.SMEM),
            pl.BlockSpec((TILE, depth), now),
            pl.BlockSpec((TILE, channels), now),
        ]
        + [pl.BlockSpec(p.shape, whole) for p in pieces],
        out_specs=[
            pl.BlockSpec((TILE, channels), now),
            pl.BlockSpec((8, TILE), lambda i: (0, i)),
            pl.BlockSpec((depth, channels), whole),
        ],
        out_shape=[
            jax.ShapeDtypeStruct((tokens, channels), f32),
            jax.ShapeDtypeStruct((8, tokens), f32),
            hbm((depth, channels), bf16),
        ],
        compiler_params=params(),
        cost_estimate=cost(0.1),
        name="gate_forward",
    )(idx, lhs, from_hbm(mixed), *pieces)


def gated_kernel(gate_ref, mixed_ref, square_ref, conv_ref, out_ref, *, inner_total):
    gate = gate_ref[...]
    scale = lax.rsqrt(row_to_column(square_ref[0:1, :]) / inner_total + EPSILON)
    gated = mixed_ref[...] * (gate * sigmoid(gate))
    out_ref[...] = (gated * scale * conv_ref[5:6, :]).astype(bf16)


def gated_norm(gate, mixed, square, conv_rows, inner_total):
    tokens, channels = gate.shape
    block = pl.BlockSpec((TILE, channels), lambda i: (i, 0))
    return pl.pallas_call(
        functools.partial(gated_kernel, inner_total=inner_total),
        grid=(tokens // TILE,),
        in_specs=[block, block, pl.BlockSpec((8, TILE), lambda i: (0, i)), pl.BlockSpec((8, channels), lambda i: (0, 0))],
        out_specs=block,
        out_shape=jax.ShapeDtypeStruct((tokens, channels), bf16),
        compiler_params=params(),
        cost_estimate=cost(0.1),
        name="gated_norm",
    )(gate, mixed, square, conv_rows)


def gout_kernel(idx_ref, cot_ref, gate_ref, mixed_ref, conv_ref, *refs, count):
    pieces, (gout_ref, sums_ref, w_ref) = refs[:count], refs[count:]

    @pl.when(pl.program_id(0) == 0)
    def _():
        fill(w_ref, pieces, idx_ref)

    gout = dot_nn(cot_ref[...], w_ref[...])
    gout_ref[...] = gout
    gate = gate_ref[...]
    gated = mixed_ref[...] * (gate * sigmoid(gate))
    sums_ref[...] = column_to_row(jnp.sum(gout * conv_ref[5:6, :] * gated, axis=1, keepdims=True))


def grad_gout(cot, gate, mixed, conv_rows, pieces, idx):
    tokens, depth = cot.shape
    channels = mixed.shape[1]
    whole = lambda i: (0, 0)
    now = lambda i: (i, 0)
    return pl.pallas_call(
        functools.partial(gout_kernel, count=len(pieces)),
        grid=(tokens // TILE,),
        in_specs=[
            pl.BlockSpec(memory_space=pltpu.SMEM),
            pl.BlockSpec((TILE, depth), now),
            pl.BlockSpec((TILE, channels), now),
            pl.BlockSpec((TILE, channels), now),
            pl.BlockSpec((8, channels), whole),
        ]
        + [pl.BlockSpec(p.shape, whole) for p in pieces],
        out_specs=[
            pl.BlockSpec((TILE, channels), now),
            pl.BlockSpec((8, TILE), lambda i: (0, i)),
            pl.BlockSpec((depth, channels), whole),
        ],
        out_shape=[
            jax.ShapeDtypeStruct((tokens, channels), f32),
            jax.ShapeDtypeStruct((8, tokens), f32),
            jax.ShapeDtypeStruct((depth, channels), bf16),
        ],
        compiler_params=params(),
        cost_estimate=cost(20),
        name="grad_gout",
    )(idx, cot, gate, mixed, conv_rows, *pieces)


def gate_back_kernel(gate_ref, gout_ref, mixed_ref, square_ref, inner_ref, conv_ref, dmixed_ref, dgate_ref, dgain_ref, *, inner_total):
    gate, gout, mixed = gate_ref[...], gout_ref[...], mixed_ref[...]
    gain = conv_ref[5:6, :]
    square, inner = row_to_column(square_ref[0:1, :]), row_to_column(inner_ref[0:1, :])
    scale = lax.rsqrt(square / inner_total + EPSILON)
    sg = sigmoid(gate)
    act = gate * sg
    gated = mixed * act
    dgated = scale * (gain * gout) - gated * (scale * scale * scale * inner / inner_total)
    dmixed_ref[...] = (dgated * act).astype(bf16)
    dgate_ref[...] = (dgated * mixed * sg * (1.0 + gate * (1.0 - sg))).astype(bf16)

    @pl.when(pl.program_id(0) == 0)
    def _():
        dgain_ref[...] = jnp.zeros_like(dgain_ref)

    dgain_ref[5:6, :] += jnp.sum(gout * gated * scale, axis=0, keepdims=True)


def gate_backward(gate, gout, mixed, square, inner, conv_rows, inner_total):
    tokens, channels = gate.shape
    whole = lambda i: (0, 0)
    block = pl.BlockSpec((TILE, channels), lambda i: (i, 0))
    row = pl.BlockSpec((8, TILE), lambda i: (0, i))
    return pl.pallas_call(
        functools.partial(gate_back_kernel, inner_total=inner_total),
        grid=(tokens // TILE,),
        in_specs=[block, block, block, row, row, pl.BlockSpec((8, channels), whole)],
        out_specs=[block, block, pl.BlockSpec((8, channels), whole)],
        out_shape=[
            jax.ShapeDtypeStruct((tokens, channels), bf16),
            jax.ShapeDtypeStruct((tokens, channels), bf16),
            jax.ShapeDtypeStruct((8, channels), f32),
        ],
        compiler_params=params(),
        cost_estimate=cost(0.1),
        name="gate_backward",
    )(from_hbm(gate), from_hbm(gout), from_hbm(mixed), square, inner, conv_rows)


def weight_grad_kernel(idx_ref, lhs_ref, rhs_ref, *refs, rows, turned):
    outs, scratch = refs[:-1], refs[-1]
    at = pl.program_id(0)
    scratch[pl.ds(pl.multiple_of(at * TILE_D, TILE_D), TILE_D), :] = (dot_nt if turned else dot_nn)(
        lhs_ref[...], rhs_ref[...]
    ).astype(bf16)

    @pl.when(at == pl.num_programs(0) - 1)
    def _():
        s = 0
        for out in outs:
            for b in range(out.shape[0] // rows):
                start = pl.multiple_of(idx_ref[s] * rows, rows)
                out[b * rows:(b + 1) * rows, :] = scratch[pl.ds(start, rows), :]
                s += 1


def weight_grad(lhs_t, rhs, idx, sizes, us=0.1, turned=False):
    depth, tokens = lhs_t.shape
    width = rhs.shape[0 if turned else 1]
    rows = depth // idx.shape[0]
    whole = lambda i: (0, 0)
    return pl.pallas_call(
        functools.partial(weight_grad_kernel, rows=rows, turned=turned),
        grid=(depth // TILE_D,),
        in_specs=[
            pl.BlockSpec(memory_space=pltpu.SMEM),
            pl.BlockSpec((TILE_D, tokens), lambda i: (i, 0)),
            pl.BlockSpec(rhs.shape, whole),
        ],
        out_specs=[pl.BlockSpec((size * rows, width), whole) for size in sizes],
        out_shape=[hbm((size * rows, width), bf16) for size in sizes],
        scratch_shapes=[pltpu.VMEM((depth, width), bf16)],
        compiler_params=params(),
        cost_estimate=cost(us),
        name="weight_grad",
    )(idx, lhs_t, rhs)


def out_kernel(rank_ref, lhs_ref, w_ref, *outs):
    product = dot_nt(lhs_ref[...], w_ref[...]).astype(bf16)
    for r, out in enumerate(outs):
        @pl.when(pl.program_id(0) == r)
        def _():
            out[...] = product


def out_partial(gated_out, w_out, rank, ranks):
    tokens, channels = gated_out.shape
    depth = w_out.shape[0]
    width = depth // ranks
    whole = lambda i, rank_ref: (0, 0)
    return pl.pallas_call(
        out_kernel,
        grid_spec=pltpu.PrefetchScalarGridSpec(
            num_scalar_prefetch=1,
            grid=(ranks,),
            in_specs=[
                pl.BlockSpec((tokens, channels), whole),
                pl.BlockSpec((width, channels), lambda i, rank_ref: (i ^ rank_ref[0], 0)),
            ],
            out_specs=[pl.BlockSpec((tokens, width), whole)] * ranks,
        ),
        out_shape=[hbm((tokens, width), bf16)] * ranks,
        compiler_params=params(),
        cost_estimate=cost(0.1),
        name="out_partial",
    )(rank, gated_out, w_out)


def term_kernel(rank_ref, gx_ref, wx_ref, gg_ref, wg_ref, gs_ref, ws_ref, gb_ref, hidden_ref, inv_ref, *refs, apart):
    wbt_refs, outs, dgain_ref = refs[:4], refs[4:-1], refs[-1]
    w_bct = jnp.concatenate([ref[...] for ref in wbt_refs], axis=0)
    gain = None
    for r, out in zip(apart, outs):
        rows = out.shape[0]
        span = pl.ds(pl.multiple_of((rank_ref[0] ^ r) * rows, rows), rows)
        total = dot_nt(gx_ref[span, :], wx_ref[...]) + dot_nt(gg_ref[span, :], wg_ref[...])
        total = total + dot_nt(gs_ref[span, :], ws_ref[...]) + dot_nn(gb_ref[span, :], w_bct)
        out[...] = total.astype(bf16)
        normed = hidden_ref[span, :].astype(f32) * row_to_column(inv_ref[0:1, span])
        own = jnp.sum(total * normed, axis=0, keepdims=True)
        gain = own if gain is None else gain + own
    cut = [gain[:, i:i + LANES] for i in range(0, gain.shape[1], LANES)]
    dgain_ref[...] = jnp.concatenate(cut + [jnp.zeros((8 - len(cut), LANES), f32)], axis=0)


def normed_term(dx, dgate, dstep, dbc, w_a, w_b, w_s, w_bct, hidden, inv_rms, rank, ranks, apart):
    tokens, channels = dx.shape
    depth = w_a.shape[0]
    rows = tokens // ranks
    whole = lambda i: (0, 0)
    return pl.pallas_call(
        functools.partial(term_kernel, apart=apart),
        grid=(depth // TILE_D,),
        in_specs=[
            pl.BlockSpec(memory_space=pltpu.SMEM),
            pl.BlockSpec(dx.shape, whole),
            pl.BlockSpec((TILE_D, channels), lambda i: (i, 0)),
            pl.BlockSpec(dgate.shape, whole),
            pl.BlockSpec((TILE_D, channels), lambda i: (i, 0)),
            pl.BlockSpec(dstep.shape, whole),
            pl.BlockSpec((TILE_D, LANES), lambda i: (i, 0)),
            pl.BlockSpec(dbc.shape, whole),
            pl.BlockSpec((tokens, TILE_D), lambda i: (0, i)),
            pl.BlockSpec(inv_rms.shape, whole),
        ]
        + [pl.BlockSpec((w.shape[0], TILE_D), lambda i: (0, i)) for w in w_bct],
        out_specs=[pl.BlockSpec((rows, TILE_D), lambda i: (0, i))] * len(apart) + [pl.BlockSpec((8, LANES), lambda i: (i, 0))],
        out_shape=[jax.ShapeDtypeStruct((rows, depth), bf16)] * len(apart)
        + [jax.ShapeDtypeStruct((8 * (depth // TILE_D), LANES), f32)],
        compiler_params=params(32),
        cost_estimate=cost(20 if 2 in apart else 0.1),
        name="normed_term",
    )(
        rank, dx, from_hbm(w_a), dgate, from_hbm(w_b), dstep, from_hbm(w_s), dbc, from_hbm(hidden), inv_rms, *w_bct
    )


def norm_back_kernel(rank_ref, a_ref, b_ref, hidden_ref, cot_ref, gain_ref, out_ref):
    grad = a_ref[...].astype(f32) + b_ref[...].astype(f32)
    inputs = hidden_ref[...].astype(f32)
    inv_rms = lax.rsqrt(jnp.mean(inputs * inputs, axis=1, keepdims=True) + EPSILON)
    normed = inputs * inv_rms
    scaled = grad * gain_ref[0:1, :]
    mean = jnp.mean(scaled * normed, axis=1, keepdims=True)
    out_ref[...] = (inv_rms * (scaled - normed * mean) + cot_ref[...].astype(f32)).astype(out_ref.dtype)


def norm_backward(a, b, hidden, cot, gain_rows, rank):
    rows, depth = a.shape
    mine = lambda i, rank_ref: (rank_ref[0], 0)
    whole = lambda i, rank_ref: (0, 0)
    return pl.pallas_call(
        norm_back_kernel,
        grid_spec=pltpu.PrefetchScalarGridSpec(
            num_scalar_prefetch=1,
            grid=(1,),
            in_specs=[
                pl.BlockSpec((rows, depth), whole),
                pl.BlockSpec((rows, depth), whole),
                pl.BlockSpec((rows, depth), mine),
                pl.BlockSpec((rows, depth), mine),
                pl.BlockSpec((8, depth), whole),
            ],
            out_specs=pl.BlockSpec((rows, depth), whole),
        ),
        out_shape=jax.ShapeDtypeStruct((rows, depth), bf16),
        compiler_params=params(),
        cost_estimate=cost(0.1),
        name="norm_backward",
    )(rank, a, b, from_hbm(hidden), from_hbm(cot), gain_rows)


def moved(weight, moment, grad):
    fresh = 0.5 * moment + 0.5 * grad
    return fresh, weight - LEARN_RATE * fresh - LEARN_RATE * DECAY_RATE * weight


def add_up(refs):
    total = refs[0][...].astype(f32)
    for ref in refs[1:]:
        total = total + ref[...].astype(f32)
    return total


def update_in_kernel(w_ref, m_ref, *refs, count):
    gate_refs, x_refs, (m_out, w_out) = refs[:count], refs[count:2 * count], refs[2 * count:]
    for at, parts in ((0, gate_refs), (1, x_refs)):
        fresh, weight = moved(w_ref[:, at, :], m_ref[:, at, :], add_up(parts))
        m_out[:, at, :] = fresh
        w_out[:, at, :] = weight


def update_in(weight, moment, gate_parts, x_parts):
    rows, _, channels = weight.shape
    size = min(rows, 96)
    full = pl.BlockSpec((size, 2, channels), lambda i: (i, 0, 0))
    parts = [*gate_parts, *x_parts]
    return pl.pallas_call(
        functools.partial(update_in_kernel, count=len(gate_parts)),
        grid=(rows // size,),
        in_specs=[full, full] + [pl.BlockSpec((size, channels), functools.partial(lambda at, i: (i, at), at)) for _, at in parts],
        out_specs=[full, full],
        out_shape=[jax.ShapeDtypeStruct(weight.shape, f32)] * 2,
        compiler_params=params(),
        cost_estimate=cost(0.1),
        name="update_in",
    )(from_hbm(weight), from_hbm(moment), *[part for part, _ in parts])


def update_small_kernel(w_ref, m_ref, sums_ref, own_ref, back_ref, *refs, share, order, shared):
    alone, late, (m_out, w_out, exchange, totals, scratch) = refs[:order[0]], refs[order[0]:-5], refs[-5:]
    heads, rows = w_ref.shape
    count = sums_ref.shape[0]
    last = late[0].shape[1] - LANES
    grad = own_ref[...].astype(f32) + back_ref[...].astype(f32)
    found = {0: sums_ref[...].astype(f32)}
    for at, ref in zip(order[1], alone):
        grad = grad + ref[0:rows, :].astype(f32)
        found[at] = ref[rows:, :].astype(f32)
    for at, ref in zip(order[2], late):
        grad = grad + ref[0:rows, last:].astype(f32)
        tail = ref[rows:, :].astype(f32)
        found[at] = jnp.concatenate([tail[:, i:i + LANES] for i in range(0, tail.shape[1], LANES)], axis=0)
    step = len(found) // 2
    while step >= 1:
        found = {i: found[i] + found[i + step] for i in range(step)}
        step //= 2
    totals[...] = found[0]
    exchange[0:rows, :] = grad
    exchange[rows:, :] = found[0][shared[0]:shared[1], :]
    scratch[0:rows, :] = grad
    turned = scratch[...].T[share:share + heads, 0:rows]
    fresh, weight = moved(w_ref[...], m_ref[...], turned)
    m_out[...] = fresh
    w_out[...] = weight


def update_small(weight_t, moment_t, sums, own, back, alone, late, order, shared, share):
    rows = weight_t.shape[1]
    count = sums.shape[0]
    whole = lambda i: (0, 0)
    spec = pl.BlockSpec(weight_t.shape, whole)
    return pl.pallas_call(
        functools.partial(update_small_kernel, share=share, order=order, shared=shared),
        grid=(1,),
        in_specs=[spec, spec, pl.BlockSpec(sums.shape, whole)] + [pl.BlockSpec((rows, LANES), whole)] * 2
        + [pl.BlockSpec(v.shape, whole) for v in (*alone, *late)],
        out_specs=[
            spec, spec,
            pl.BlockSpec((rows + shared[1] - shared[0], LANES), whole),
            pl.BlockSpec((count, LANES), whole),
        ],
        out_shape=[jax.ShapeDtypeStruct(weight_t.shape, f32)] * 2
        + [jax.ShapeDtypeStruct((rows + shared[1] - shared[0], LANES), f32), jax.ShapeDtypeStruct((count, LANES), f32)],
        scratch_shapes=[pltpu.VMEM((2 * LANES, LANES), f32)],
        compiler_params=params(),
        cost_estimate=cost(0.1),
        name="update_small",
    )(weight_t, moment_t, sums, own, back, *alone, *late)


def update_bc_kernel(rank_ref, w_ref, m_ref, *refs):
    pieces, (m_out, w_out, shared_out) = refs[:-3], refs[-3:]
    rows, width = w_ref.shape
    share = width // len(pieces)
    shared_out[...] = (pieces[0][rows:, :] + pieces[1][rows:, :]) + (pieces[2][rows:, :] + pieces[3][rows:, :])
    lane = lax.broadcasted_iota(jnp.int32, (rows, LANES), 1)
    for pair in range(width // LANES):
        halves = []
        for member in (2 * pair, 2 * pair + 1):
            own = pieces[0][0:rows, :]
            for r in range(1, len(pieces)):
                own = jnp.where((rank_ref[0] ^ r) == member, pieces[r][0:rows, :], own)
            halves.append(own)
        grad = jnp.where(lane < share, halves[0], pltpu.roll(halves[1], share, 1))
        span = slice(pair * LANES, (pair + 1) * LANES)
        fresh, weight = moved(w_ref[:, span], m_ref[:, span], grad)
        m_out[:, span] = fresh
        w_out[:, span] = weight


def update_bc(weight, moment, pieces, rank):
    vmem = pl.BlockSpec(memory_space=pltpu.VMEM)
    return pl.pallas_call(
        update_bc_kernel,
        in_specs=[pl.BlockSpec(memory_space=pltpu.SMEM)] + [vmem] * (2 + len(pieces)),
        out_specs=[vmem] * 3,
        out_shape=[jax.ShapeDtypeStruct(weight.shape, f32)] * 2
        + [jax.ShapeDtypeStruct((pieces[0].shape[0] - weight.shape[0], LANES), f32)],
        compiler_params=params(),
        cost_estimate=cost(0.1),
        name="update_bc",
    )(rank, weight, moment, *pieces)


def fence(*values):
    leaves, tree = jax.tree.flatten(values)
    return jax.tree.unflatten(tree, lax.optimization_barrier(leaves))


def outer_from(v, k):
    n = lax.axis_size("dp") // 2
    return lax.ppermute(v, "dp", [(((o + k) % n) * 2 + x, o * 2 + x) for o in range(n) for x in range(2)])


def outer_flip(v, bit):
    n = lax.axis_size("dp") // 2
    return lax.ppermute(v, "dp", [((o ^ bit) * 2 + x, o * 2 + x) for o in range(n) for x in range(2)])


def inner_flip(v):
    return lax.ppermute(v, "dp", [(d ^ 1, d) for d in range(lax.axis_size("dp"))])


def rank_flip(v, bit):
    return lax.ppermute(v, "mp", [(m ^ bit, m) for m in range(lax.axis_size("mp"))])


def hops(n):
    order = []
    for k in range(1, n // 2 + 1):
        order.append(k)
        if n - k != k:
            order.append(n - k)
    return order


def pair_sum(a, b):
    return (a.astype(f32) + b.astype(f32)).astype(bf16)


def outer_blocks(own, here, back, ks):
    rows = own.shape[0]
    back = [part[i:i + rows] for part in back for i in range(0, part.shape[0], rows)]
    return [
        (here[i * rows:(i + 1) * rows].astype(f32) + back[i].astype(f32)).astype(bf16) for i in range(len(ks))
    ]


def outer_send(blocks, ks):
    n = lax.axis_size("dp") // 2
    return [outer_from(block, n - k) for block, k in zip(blocks, ks)]


def outer_sum(v):
    bit = 1
    while bit < lax.axis_size("dp") // 2:
        v = v + outer_flip(v, bit)
        bit *= 2
    return v


def mp_sum(v):
    v = v + rank_flip(v, 1)
    return v + rank_flip(v, 2)


def mp_sum_direct(v):
    return (v + rank_flip(v, 1)) + (rank_flip(v, 2) + rank_flip(v, 3))


def mp_reduce(blocks):
    far = blocks[2].astype(f32) + rank_flip(blocks[3], 1).astype(f32)
    near = blocks[0].astype(f32) + rank_flip(blocks[1], 1).astype(f32)
    return near, rank_flip(far.astype(bf16), 2)


def mp_pieces(v):
    far = rank_flip(v, 2)
    return [v, rank_flip(v, 1), far, rank_flip(far, 1)]


def in_rank_order(pieces, rank, axis):
    odd, high = (rank & 1) == 1, (rank & 2) == 2
    join = lambda a, b: jnp.concatenate([a, b], axis=axis)
    low = jnp.where(odd, join(pieces[1], pieces[0]), join(pieces[0], pieces[1]))
    far = jnp.where(odd, join(pieces[3], pieces[2]), join(pieces[2], pieces[3]))
    return jnp.where(high, join(far, low), join(low, far))


def momentum(moment, grad):
    return 0.5 * moment + 0.5 * grad


def advance(weight, moment, grad):
    fresh = momentum(moment, grad)
    return (fresh, weight - LEARN_RATE * fresh - LEARN_RATE * DECAY_RATE * weight)


def body(
    hidden, segments, cotangent, in_weight, in_moment, bc_weight, bc_moment, step_weight, step_moment,
    out_weight, out_moment, conv_table, conv_moment, bc_table, bc_table_moment, head_table, head_moment,
    norm_gain, gain_moment,
):
    size = lax.axis_size("dp")
    ranks = lax.axis_size("mp")
    n = size // 2
    place, rank = lax.axis_index("dp"), lax.axis_index("mp")
    outer, inner = place // 2, place % 2
    rank1 = rank.reshape(1).astype(jnp.int32)
    rows, _, channels = in_weight.shape
    heads = head_table.shape[1]
    tokens, depth = hidden.shape
    share = bc_weight.shape[1] // ranks

    ks = hops(n)
    near_ks, far_k = ks[:-1], ks[-1]

    def members(order):
        return jnp.stack([((outer + k) % n) * 2 + (inner ^ j) for k, j in order]).astype(jnp.int32)

    first = [(0, 0), (0, 1)]
    idx = members(first + [(k, 0) for k in ks] + [(k, 1) for k in ks])
    idx_s = members([(0, 0)] + [(k, 0) for k in ks] + [(0, 1)] + [(k, 1) for k in ks])
    sizes = (1, 1, n - 1, n - 1)
    split_sizes = (1, 1, n - 1, n - 2, 1)
    width = depth // ranks

    set_a = pack(in_weight, bc_weight, step_weight.T, rank1)
    set_c = out_weight.T.astype(bf16)

    def blocks(own, z, x):
        return [own, x[0]] + [z[k] for k in ks] + [x[k] for k in ks]

    def block(v, i):
        return v[i * rows:(i + 1) * rows]

    def blocks(own, z, x):
        return [own, x[0]] + [z[k] for k in ks] + [x[k] for k in ks]

    def block(v, i):
        return v[i * rows:(i + 1) * rows]

    def total(own, own_got, got):
        value = own.astype(f32) + own_got.astype(f32)
        for part in got:
            value = value + part.astype(f32)
        return value

    def outer_all(v, some):
        return {k: outer_from(v, k) for k in some}

    def flip_all(z, some):
        return {k: inner_flip(z[k]) for k in some}

    a_z = outer_all(set_a, near_ks)
    a_x = {0: inner_flip(set_a)}
    far_a, a_x[0], hidden, segments, in_gate = fence(set_a, a_x[0], hidden, segments, in_weight)
    set_b = pack_gate(in_gate)
    a_z[far_k] = outer_from(far_a, far_k)
    cot_far = rank_flip(cotangent, 2)
    gain_rows = pad_rows(norm_gain[None])
    normed_low, normed_t, inv_rms = prepare(hidden, gain_rows)
    a_x.update(flip_all(a_z, near_ks))
    aux, seg_row = segment_facts(segments)
    head_rows = pad_lanes(pad_rows(head_table))
    facts = (aux, seg_row, pad_rows(conv_table), pad_rows(bc_table), head_rows, *head_expand(channels))
    set_a, set_b, set_c, a_z, a_x, cot_far, normed_low, normed_t, inv_rms, facts = fence(
        set_a, set_b, set_c, a_z, a_x, cot_far, normed_low, normed_t, inv_rms, facts
    )

    a_x[far_k] = inner_flip(a_z[far_k])
    b_x = {0: inner_flip(set_b)}
    b_z = outer_all(set_b, near_ks)
    cot, cot_t = join_columns([cotangent, rank_flip(cotangent, 1), cot_far, rank_flip(cot_far, 1)], rank1)
    set_b, set_c, b_z, b_x, a_z, a_x, cot, cot_t, normed_low = fence(
        set_b, set_c, b_z, b_x, a_z, a_x, cot, cot_t, normed_low
    )

    b_z[far_k] = outer_from(set_b, far_k)
    b_x.update(flip_all(b_z, near_ks[:1]))
    c_x = {0: inner_flip(set_c)}
    a_blocks = blocks(set_a, a_z, a_x)
    small, bc_share, w_s, w_bct_share = project_small(normed_low, a_blocks, idx, share)
    bc_far, bc_near = rank_flip(bc_share, 2), rank_flip(bc_share, 1)
    x_pre, w_a = project(normed_low, a_blocks, idx, channels)
    bc_far, x_pre, small, set_c, w_bct_share, w_s = fence(bc_far, x_pre, small, set_c, w_bct_share, w_s)
    bc_pieces = [bc_share, bc_near, bc_far, rank_flip(bc_far, 1)]
    bc_pre, step_pre = join_small(bc_pieces, small, rank1)
    set_c, b_z, b_x, c_x, x_pre, bc_pre, step_pre, w_bct_share = fence(
        set_c, b_z, b_x, c_x, x_pre, bc_pre, step_pre, w_bct_share
    )

    c_z = outer_all(set_c, near_ks)
    b_x.update(flip_all(b_z, ks[1:]))
    kept = ssd_forward(x_pre, bc_pre, step_pre, *facts[:-1])
    mixed = kept[0]
    mixed, b_x, b_z, c_z, c_x, w_bct_share, set_c = fence(mixed, b_x, b_z, c_z, c_x, w_bct_share, set_c)

    c_z[far_k] = outer_from(set_c, far_k)
    c_x.update(flip_all(c_z, near_ks))
    gate_pre, square, w_b = gate_forward(normed_low, mixed, blocks(set_b, b_z, b_x), idx)
    square = mp_sum_direct(square)
    mixed, gate_pre, square, w_b, w_bct_share, c_z, c_x = fence(mixed, gate_pre, square, w_b, w_bct_share, c_z, c_x)

    c_x[far_k] = inner_flip(c_z[far_k])
    w_bct = [w_bct_share, rank_flip(w_bct_share, 2)]
    conv_rows = facts[2]
    gated_out = gated_norm(gate_pre, mixed, square, conv_rows, channels * ranks)
    gc_own, gc_own1, gc_here, gc_near, gc_far = weight_grad(cot_t, gated_out, idx, split_sizes)
    c_x, square, gated_out, gc_own, gc_own1, gc_here, gc_near, gc_far, w_bct = fence(
        c_x, square, gated_out, gc_own, gc_own1, gc_here, gc_near, gc_far, w_bct
    )

    gc_far_back, gc_near_back = inner_flip(gc_far), inner_flip(gc_near)
    gout, inner_dot, w_c = grad_gout(cot, gate_pre, mixed, conv_rows, blocks(set_c, c_z, c_x), idx)
    gout, inner_dot, w_c = fence(gout, inner_dot, w_c)
    inner_dot = mp_sum_direct(inner_dot)
    partial = out_partial(gated_out, w_c, rank1, ranks)
    inner_dot, gout, partial, w_bct, gc_far_back = fence(inner_dot, gout, partial, w_bct, gc_far_back)
    c_far_got = outer_from(pair_sum(block(gc_here, n - 2), gc_far_back), n - far_k)
    out_back = rank_flip(partial[3], 1)
    w_bct = [w_bct[0], rank_flip(w_bct[0], 1), w_bct[1], rank_flip(w_bct[1], 1)]
    dmixed, dgate, dgain = gate_backward(gate_pre, gout, mixed, square, inner_dot, conv_rows, channels * ranks)
    gb_own, gb_own1, gb_here, gb_send = weight_grad(normed_t, dgate, idx, sizes)
    gc_near_back, c_far_got, w_bct, out_back, gb_own, gb_own1, gb_here, gb_send, partial, dmixed, dgain = fence(
        gc_near_back, c_far_got, w_bct, out_back, gb_own, gb_own1, gb_here, gb_send, partial, dmixed, dgain
    )
    c_blocks = [pair_sum(block(gc_here, i), block(gc_near_back, i)) for i in range(n - 2)]
    out_far = pair_sum(partial[2], out_back)
    c_blocks, out_far, w_bct, dmixed, gb_send = fence(c_blocks, out_far, w_bct, dmixed, gb_send)

    c_got = outer_send(c_blocks, near_ks) + [c_far_got]
    gb_back = inner_flip(gb_send)
    out_got = rank_flip(out_far, 2)
    dx, dbc, dbc_keep, dbc_send, dstep, dstep_t, dconv, dbct_part, dheads = ssd_backward(
        rank1, x_pre, bc_pre, step_pre, *facts, dmixed, kept
    )
    c_got, gb_back, out_got, dx, dbc, dbc_keep, dbc_send, dstep, dstep_t, dconv, dbct_part, dheads = fence(
        c_got, gb_back, out_got, dx, dbc, dbc_keep, dbc_send, dstep, dstep_t, dconv, dbct_part, dheads
    )

    b_got = {far_k: outer_from(pair_sum(block(gb_here, n - 2), block(gb_back, n - 2)), n - far_k)}
    dbc_back = rank_flip(dbc_send, 1)
    out_near_back = rank_flip(partial[1], 1)
    ga_own, ga_own1, ga_here, ga_send = weight_grad(normed_t, dx, idx, sizes, us=20)
    ga_own, ga_own1, ga_here, ga_send, dx, dbc_back, gb_back, gb_here, out_near_back = fence(
        ga_own, ga_own1, ga_here, ga_send, dx, dbc_back, gb_back, gb_here, out_near_back
    )

    b_near = [pair_sum(block(gb_here, i), block(gb_back, i)) for i in range(n - 2)]
    b_got.update(zip(near_ks, outer_send(b_near, near_ks)))
    ga_back = inner_flip(ga_send)
    dbc_pair = pair_sum(dbc_keep, dbc_back)
    dbc_got = rank_flip(dbc_pair[share:], 2)
    operands = (dx, dgate, dstep, dbc, w_a, w_b, w_s, w_bct, hidden, inv_rms, rank1, ranks)
    far_own, far_send, gain_far = normed_term(*operands, (2, 3))
    far_own, far_send, gain_far, dx, dbc_got, dbc_pair, dstep_t, b_got[far_k] = fence(
        far_own, far_send, gain_far, dx, dbc_got, dbc_pair, dstep_t, b_got[far_k]
    )
    far_back = rank_flip(far_send, 1)
    operands = (dx, *operands[1:])
    near_own, near_send, gain_near = normed_term(*operands, (0, 1))
    far_back, near_own, near_send, gain_near, ga_back = fence(far_back, near_own, near_send, gain_near, ga_back)
    near_back = rank_flip(near_send, 1)
    far = pair_sum(far_own, far_back)
    a_blocks = [pair_sum(block(ga_here, i), block(ga_back, i)) for i in range(n - 1)]
    dbc_share = pair_sum(dbc_pair[:share], dbc_got)
    dsmall_t = jnp.concatenate([dbc_share, dstep_t, jnp.zeros((LANES - share - 16, tokens), bf16)], axis=0)
    gs_own, gs_here, gs_send = weight_grad(normed_t, dsmall_t, idx_s, (1, n - 1, n), turned=True)
    far, a_blocks, near_back, gs_send, gc_own1, gb_own1, b_got = fence(
        far, a_blocks, near_back, gs_send, gc_own1, gb_own1, b_got
    )

    early, late = [], near_ks
    got = rank_flip(far, 2)
    a_got = dict(zip([far_k, *early], outer_send([a_blocks[-1], *a_blocks[:len(early)]], [far_k, *early])))
    cut = lambda v: [v[:, i:i + LANES] for i in range(0, v.shape[1], LANES)]
    alone = channels // LANES * 8 + 8
    sums = jnp.concatenate([*cut(dconv + dgain), dheads, *cut(dbct_part), gain_far + gain_near], axis=0)
    shared = (alone, sums.shape[0])
    wide = (channels + LANES) // LANES
    sums = pad_rows(sums, -(-sums.shape[0] // (16 * wide)) * 16 * wide).astype(bf16)
    small_back = inner_flip(jnp.concatenate([gs_send, sums], axis=0))
    own_got = inner_flip(jnp.concatenate([gc_own1, gb_own1], axis=1))
    near = near_own.astype(f32) + near_back.astype(f32)
    got, near, a_got, small_back, sums, own_got, ga_own1, a_late = fence(
        got, near, a_got, small_back, sums, own_got, ga_own1, a_blocks[len(early):-1]
    )

    mine = norm_backward(near, got, hidden, cot, gain_rows, rank1)
    mine, small_back, sums, ga_own1, a_late, gs_here, out_got, out_near_back = fence(
        mine, small_back, sums, ga_own1, a_late, gs_here, out_got, out_near_back
    )
    a_own_got = inner_flip(ga_own1)
    gs_back, sums_back = small_back[:n * rows], small_back[n * rows:]
    s_blocks = dict(zip(ks, outer_blocks(gs_own, gs_here, [gs_back[rows:]], ks)))
    sums = pair_sum(sums, sums_back)
    size = sums.shape[0] // wide
    sums_wide = jnp.concatenate([sums[i * size:(i + 1) * size] for i in range(wide)], axis=1)
    late_got = outer_send(
        [
            jnp.concatenate([jnp.concatenate([a_block, s_blocks[k]], axis=1), sums_wide], axis=0)
            for k, a_block in zip(late, a_late)
        ],
        late,
    )
    s_got = outer_send([jnp.concatenate([s_blocks[k], sums], axis=0) for k in (far_k, *early)], (far_k, *early))
    mine_far = rank_flip(mine, 2)
    mine_far, mine = fence(mine_far, mine)
    late_got, s_got, a_own_got, sums = fence(late_got, s_got, a_own_got, sums)

    mine_near, mine_far_near = rank_flip(mine, 1), rank_flip(mine_far, 1)
    step_m, step_w, exchange, totals = update_small(
        step_weight.T, step_moment.T, sums, gs_own, gs_back, s_got, late_got,
        (len(s_got), [n - k for k in (far_k, *early)], [n - k for k in late]), shared, share,
    )
    exchanged = [exchange] + [rank_flip(exchange, r) for r in (1, 2, 3)]
    in_m, in_w = update_in(
        in_weight, in_moment,
        [(gb_own, 0), (own_got, 1)] + [(b_got[k], 0) for k in ks],
        [(ga_own, 0), (a_own_got, 0)] + [(a_got[k], 0) for k in (far_k, *early)] + [(v, 0) for v in late_got],
    )
    input_grad = join_rows([mine, mine_near, mine_far, mine_far_near], rank1)
    exchanged, mine_far_near = fence(exchanged, mine_far_near)
    bc_m, bc_w, totals_shared = update_bc(bc_weight, bc_moment, exchanged, rank1)

    resid = lax.dynamic_slice_in_dim(hidden, rank * width, width, 1).astype(f32)
    output = (resid + partial[0].astype(f32) + out_near_back.astype(f32) + out_got.astype(f32)).astype(bf16)
    shard_c = total(gc_own, own_got[:, :channels], c_got)

    side_by_side = lambda v: jnp.concatenate([v[i:i + 8] for i in range(0, v.shape[0], 8)], axis=1)
    total_conv = side_by_side(totals[:alone - 8])[:6]
    total_head = totals[alone - 8:alone - 5, :heads]
    total_bct = side_by_side(totals_shared[:16])[:5]
    per = TILE_D // LANES
    total_gain = jnp.concatenate([totals_shared[i:i + per] for i in range(16, totals_shared.shape[0], 8)], axis=0).reshape(-1)

    out_m, out_w = advance(out_weight, out_moment, shard_c.T)
    return (
        output, input_grad, in_m, in_w, bc_m, bc_w, step_m.T, step_w.T, out_m, out_w,
        momentum(conv_moment, total_conv),
        momentum(bc_table_moment, total_bct),
        momentum(head_moment, total_head),
        momentum(gain_moment, total_gain),
    )


def solution(mesh):
    placed = (
        P("dp", None),
        P("dp", None),
        P("dp", "mp"),
        P("dp", None, "mp"),
        P("dp", None, "mp"),
        P("dp", None),
        P("dp", None),
        P("dp", "mp"),
        P("dp", "mp"),
        P("mp", "dp"),
        P("mp", "dp"),
        P(None, "mp"),
        P(None, "mp"),
        P(),
        P(),
        P(None, "mp"),
        P(None, "mp"),
        P(),
        P(),
    )
    return jax.shard_map(
        body,
        mesh=mesh,
        in_specs=placed,
        out_specs=(
            P("dp", "mp"),
            P("dp", None),
            P("dp", None, "mp"),
            P("dp", None, "mp"),
            P("dp", None),
            P("dp", None),
            P("dp", "mp"),
            P("dp", "mp"),
            P("mp", "dp"),
            P("mp", "dp"),
            P(None, "mp"),
            P(),
            P(None, "mp"),
            P(),
        ),
        check_vma=False,
    )
```

```python
import functools

import jax
import jax.numpy as jnp
from jax import lax
from jax.experimental import pallas as pl
from jax.experimental.pallas import tpu as pltpu
from jax.sharding import PartitionSpec as P

CHUNK = 128
EPSILON = 1e-05
LEARN_RATE = 0.0001
DECAY_RATE = 0.1
WIDTH = 64
LANES = 128
HALO = 8
bf16 = jnp.bfloat16
f32 = jnp.float32
MIB = 1024 * 1024


def hbm(shape, dtype):
    return pltpu.HBM(shape, dtype)


def from_hbm(v):
    return pltpu.with_memory_space_constraint(v, pltpu.HBM)


def dot_nn(a, b):
    return lax.dot_general(a, b, (((1,), (0,)), ((), ())), preferred_element_type=f32)


def dot_nt(a, b):
    return lax.dot_general(a, b, (((1,), (1,)), ((), ())), preferred_element_type=f32)


def dot_tn(a, b):
    return lax.dot_general(a, b, (((0,), (0,)), ((), ())), preferred_element_type=f32)


def split3(v):
    high = v.astype(bf16)
    rest = v - high.astype(f32)
    mid = rest.astype(bf16)
    low = (rest - mid.astype(f32)).astype(bf16)
    return high, mid, low


def exact_left(ones, v):
    high, mid, low = split3(v)
    return dot_nn(ones, high) + dot_nn(ones, mid) + dot_nn(ones, low)


def spread(v, expand):
    high, mid, low = split3(v)
    return dot_nn(high, expand) + dot_nn(mid, expand) + dot_nn(low, expand)


def gather_heads(v, expand_t):
    high = v.astype(bf16)
    mid = (v - high.astype(f32)).astype(bf16)
    return dot_nn(high, expand_t) + dot_nn(mid, expand_t)


def sigmoid(v):
    return 0.5 * jnp.tanh(0.5 * v) + 0.5


def conv_block(before, now, taps, keep):
    longer = jnp.concatenate([before, now], axis=0)
    total = taps[4:5, :] + taps[0:1, :] * now
    for lag in (1, 2, 3):
        moved = pltpu.roll(longer, lag, 0)[HALO:, :]
        total = total + taps[lag:lag + 1, :] * (moved * keep[:, lag - 1:lag])
    return total


def step_parts(step_pre, heads):
    raw = step_pre + heads[0:1, :]
    small = jnp.exp(-jnp.abs(raw))
    steps = jnp.maximum(raw, 0.0) + jnp.log1p(small)
    slope = jnp.where(raw >= 0.0, 1.0, small) / (1.0 + small)
    rates = -jnp.exp(heads[1:2, :])
    return slope, steps, rates


def triangle(lower):
    row = lax.broadcasted_iota(jnp.int32, (CHUNK, CHUNK), 0)
    col = lax.broadcasted_iota(jnp.int32, (CHUNK, CHUNK), 1)
    return row >= col if lower else row <= col


def ssd_forward_kernel(
    x_ref, xb_ref, bc_ref, bcb_ref, st_ref, aux_ref, seg_ref, conv_ref, bct_ref, heads_ref, expand_ref,
    mixed_ref, state_ref, act_ref, slope_ref, xs_ref, xe_ref, step_ref, entry_ref, end_ref, bcact_ref, bcslope_ref,
    state,
):
    chunk = pl.program_id(0)

    @pl.when(chunk == 0)
    def _():
        state[...] = jnp.zeros_like(state)

    channels = x_ref.shape[1]
    aux = aux_ref[...]
    expand = expand_ref[...]
    u = conv_block(xb_ref[...], x_ref[...], conv_ref, aux)
    sg = sigmoid(u)
    x_act = u * sg
    act_ref[...] = x_act
    slope_ref[...] = (sg * (1.0 + u * (1.0 - sg))).astype(bf16)
    ubc = conv_block(bcb_ref[...], bc_ref[...], bct_ref, aux)
    sgbc = sigmoid(ubc)
    bc_act = (ubc * sgbc).astype(bf16)
    bcact_ref[...] = bc_act
    bcslope_ref[...] = sgbc * (1.0 + ubc * (1.0 - sgbc))
    b_mat, c_mat = bc_act[:, :LANES], bc_act[:, LANES:]
    _, steps, rates = step_parts(st_ref[...], heads_ref)
    lower = triangle(True)
    cum = exact_left(lower.astype(bf16), steps * rates)
    cum_t = cum.T
    tail = cum[CHUNK - 1:CHUNK, :]
    entry = jnp.exp(cum) * aux[:, 6:7]
    to_end = jnp.exp(tail - cum) * aux[:, 7:8]
    wide = spread(jnp.concatenate([steps, entry, to_end], axis=0), expand)
    step_e, entry_e, to_end_e = wide[:CHUNK], wide[CHUNK:2 * CHUNK], wide[2 * CHUNK:]
    skip_e = spread(jnp.broadcast_to(heads_ref[2:3, :], (8, LANES)), expand)[0:1, :]
    mask = lower & (aux[:, 8:9] == seg_ref[...])
    scores = jnp.where(mask, dot_nt(c_mat, b_mat), 0.0)
    xs = x_act * step_e
    xs_low = xs.astype(bf16)
    xe_low = (xs * to_end_e).astype(bf16)
    xs_ref[...] = xs_low
    xe_ref[...] = xe_low
    step_ref[...] = step_e.astype(bf16)
    entry_ref[...] = entry_e.astype(bf16)
    end_ref[...] = to_end_e.astype(bf16)
    held = state[...]
    held_low = held.astype(bf16)
    state_ref[...] = held_low
    out = dot_nn(c_mat, held_low) * entry_e + skip_e * x_act
    state[...] = held * entry_e[CHUNK - 1:CHUNK, :] + dot_tn(b_mat, xe_low)
    first = lax.broadcasted_iota(jnp.int32, (CHUNK, LANES), 1) < WIDTH
    zero = jnp.zeros((CHUNK, LANES), bf16)
    for pair in range(channels // LANES):
        span = slice(pair * LANES, (pair + 1) * LANES)
        parts = []
        for head in (2 * pair, 2 * pair + 1):
            diff = cum[:, head:head + 1] - cum_t[head:head + 1, :]
            parts.append((scores * jnp.exp(jnp.minimum(diff, 0.0))).astype(bf16))
        own = xs_low[:, span]
        both = jnp.concatenate([jnp.where(first, own, zero), jnp.where(first, zero, own)], axis=0)
        mixed_ref[:, span] = out[:, span] + dot_nn(jnp.concatenate(parts, axis=1), both)


def ssd_backward_kernel(
    rank_ref, x_ref, bc_ref, st_ref, aux_ref, seg_ref, conv_ref, bct_ref, heads_ref, expand_ref,
    expand_t_ref, mixed_ref, dy_ref, state_ref, act_ref, slope_ref, xs_ref, xe_ref, step_ref, entry_ref, end_ref, bcact_ref,
    bcslope_ref, dx_ref, dbc_ref, keep_ref, send_ref, dst_ref, dst_t_ref, dconv_ref, dbct_ref, dheads_ref,
    dstate, du_scr, dubc_scr, share_scr,
):
    @pl.when(pl.program_id(0) == 0)
    def _():
        for ref in (dstate, du_scr, dubc_scr, dconv_ref, dbct_ref, dheads_ref):
            ref[...] = jnp.zeros_like(ref)

    channels = x_ref.shape[1]
    aux = aux_ref[...]
    expand = expand_ref[...]
    x_act = act_ref[...]
    b_mat, c_mat = bcact_ref[:, :LANES], bcact_ref[:, LANES:]
    slope, steps, rates = step_parts(st_ref[...], heads_ref)
    lower = triangle(True)
    cum = exact_left(lower.astype(bf16), steps * rates)
    cum_t = cum.T
    skip_e = spread(jnp.broadcast_to(heads_ref[2:3, :], (8, LANES)), expand)[0:1, :]
    upper = triangle(False)
    mask = upper & (aux[:, 8:9] == seg_ref[...])
    scores = jnp.where(mask, dot_nt(b_mat, c_mat), 0.0)
    xs_low = xs_ref[...]
    dy_low = dy_ref[...]
    dy = dy_low.astype(f32)
    held_low = state_ref[...]
    grad = dstate[...]
    grad_low = grad.astype(bf16)
    entry_e = entry_ref[...].astype(f32)
    entry_dy = (entry_e * dy).astype(bf16)
    kept_e = entry_e[CHUNK - 1:CHUNK, :]
    dstate[...] = grad * kept_e + dot_tn(c_mat, entry_dy)
    dc = dot_nt(entry_dy, held_low)
    db = dot_nt(xe_ref[...], grad_low)
    q_state = dot_nn(b_mat, grad_low) * end_ref[...].astype(f32)
    first = lax.broadcasted_iota(jnp.int32, (CHUNK, LANES), 1) < WIDTH
    zero = jnp.zeros((CHUNK, LANES), bf16)
    dscores = jnp.zeros((CHUNK, CHUNK), f32)
    q_parts = []
    for pair in range(channels // LANES):
        span = slice(pair * LANES, (pair + 1) * LANES)
        own = dy_low[:, span]
        both = jnp.concatenate([jnp.where(first, own, zero), jnp.where(first, zero, own)], axis=0)
        dweights = dot_nt(xs_low[:, span], both)
        parts = []
        for i, head in enumerate((2 * pair, 2 * pair + 1)):
            diff = cum_t[head:head + 1, :] - cum[:, head:head + 1]
            decay = jnp.exp(jnp.minimum(diff, 0.0))
            parts.append((scores * decay).astype(bf16))
            dscores = dscores + dweights[:, i * LANES:(i + 1) * LANES] * decay
        q_parts.append(dot_nn(jnp.concatenate(parts, axis=1), both))
    q = jnp.concatenate(q_parts, axis=1) + q_state
    dscores_low = jnp.where(mask, dscores, 0.0).astype(bf16)
    db = db + dot_nn(dscores_low, c_mat)
    dc = dc + dot_tn(dscores_low, b_mat)
    xs_round = xs_low.astype(f32)
    expand_t = expand_t_ref[...]
    flow = gather_heads(dy * (mixed_ref[...] - skip_e * x_act) - xs_round * q, expand_t)
    dstep = dot_nn((x_act * q).astype(bf16), expand_t)
    sums = jnp.concatenate(
        [
            jnp.sum(xs_round * q_state + kept_e * (held_low.astype(f32) * grad), axis=0, keepdims=True),
            jnp.sum(dy * x_act, axis=0, keepdims=True),
            jnp.zeros((6, channels), f32),
        ],
        axis=0,
    )
    sums = gather_heads(sums, expand_t)
    dlog = exact_left(upper.astype(bf16), flow) + sums[0:1, :]
    dstep = dstep + rates * dlog
    draw = dstep * slope
    dst_ref[...] = pltpu.roll(draw, WIDTH, 1).astype(bf16)
    dst_t_ref[...] = draw.T[0:16, :].astype(bf16)
    dheads_ref[0:1, :] += jnp.sum(draw, axis=0, keepdims=True)
    dheads_ref[1:2, :] += rates * jnp.sum(dlog * steps, axis=0, keepdims=True)
    dheads_ref[2:3, :] += sums[1:2, :]
    x_now, bc_now = x_ref[...], bc_ref[...]

    def conv_back(scratch, du, now, taps, dtaps):
        longer = jnp.concatenate([du, scratch[...]], axis=0)
        total = taps[0:1, :] * du
        sums = [jnp.sum(now * du, axis=0, keepdims=True)]
        for lag in (1, 2, 3):
            moved = pltpu.roll(longer, CHUNK + HALO - lag, 0)[0:CHUNK, :] * aux[:, 2 + lag:3 + lag]
            total = total + taps[lag:lag + 1, :] * moved
            sums.append(jnp.sum(now * moved, axis=0, keepdims=True))
        sums.append(jnp.sum(du, axis=0, keepdims=True))
        dtaps[0:5, :] += jnp.concatenate(sums, axis=0)
        scratch[...] = du[0:HALO, :]
        return total

    du = (skip_e * dy + step_ref[...].astype(f32) * q) * slope_ref[...].astype(f32)
    dx_ref[...] = conv_back(du_scr, du, x_now, conv_ref, dconv_ref).astype(dx_ref.dtype)
    dubc = jnp.concatenate([db, dc], axis=1) * bcslope_ref[...]
    dbc = conv_back(dubc_scr, dubc, bc_now, bct_ref, dbct_ref).astype(bf16)
    swapped = jnp.concatenate([dbc[:, LANES:], dbc[:, :LANES]], axis=1)
    ordered = jnp.where((rank_ref[0] & 2) == 2, swapped, dbc)
    swapped = jnp.concatenate(
        [pltpu.roll(ordered[:, :LANES].astype(f32), WIDTH, 1), pltpu.roll(ordered[:, LANES:].astype(f32), WIDTH, 1)], axis=1
    ).astype(bf16)
    dbc_ref[...] = jnp.where((rank_ref[0] & 1) == 1, swapped, ordered)
    share = 2 * LANES // 4
    turned = dbc.T
    for member in range(4):
        apart = member ^ rank_ref[0]
        start = pl.multiple_of((apart & 1) * 2 * share + (apart >> 1) * share, share)
        share_scr[pl.ds(start, share), :] = turned[member * share:(member + 1) * share, :]
    keep_ref[...] = share_scr[0:2 * share, :]
    send_ref[...] = share_scr[2 * share:4 * share, :]


def common_specs(place, channels):
    before = lambda i: (jnp.maximum(place(i) * (CHUNK // HALO) - 1, 0), 0)
    now = lambda i: (place(i), 0)
    whole = lambda i: (0, 0)
    return [
        pl.BlockSpec((CHUNK, channels), now),
        pl.BlockSpec((HALO, channels), before),
        pl.BlockSpec((CHUNK, 2 * LANES), now),
        pl.BlockSpec((HALO, 2 * LANES), before),
        pl.BlockSpec((CHUNK, LANES), now),
        pl.BlockSpec((CHUNK, 16), now),
        pl.BlockSpec((1, CHUNK), lambda i: (0, place(i))),
        pl.BlockSpec((8, channels), whole),
        pl.BlockSpec((8, 2 * LANES), whole),
        pl.BlockSpec((8, LANES), whole),
        pl.BlockSpec((LANES, channels), whole),
    ]


def ssd_forward(x_pre, bc_pre, step_pre, aux, seg_row, conv_rows, bc_rows, head_rows, expand):
    tokens, channels = x_pre.shape
    count = tokens // CHUNK
    now = lambda i: (i, 0)
    return pl.pallas_call(
        ssd_forward_kernel,
        grid=(count,),
        in_specs=common_specs(lambda i: i, channels),
        out_specs=[
            pl.BlockSpec((CHUNK, channels), now),
            pl.BlockSpec((None, LANES, channels), lambda i: (i, 0, 0)),
        ]
        + [pl.BlockSpec((CHUNK, channels), now)] * 7
        + [pl.BlockSpec((CHUNK, 2 * LANES), now)] * 2,
        out_shape=[
            hbm((tokens, channels), f32),
            hbm((count, LANES, channels), bf16),
            hbm((tokens, channels), f32),
            *[hbm((tokens, channels), bf16) for _ in range(6)],
            hbm((tokens, 2 * LANES), bf16),
            hbm((tokens, 2 * LANES), f32),
        ],
        scratch_shapes=[
            pltpu.VMEM((LANES, channels), f32),
        ],
        compiler_params=pltpu.CompilerParams(vmem_limit_bytes=18 * MIB),
        cost_estimate=pl.CostEstimate(flops=14 * 10**9, bytes_accessed=40 * 10**6, transcendentals=0),
        name="ssd_forward",
    )(
        from_hbm(x_pre), from_hbm(x_pre), bc_pre, bc_pre, step_pre, aux, seg_row, conv_rows, bc_rows, head_rows, expand
    )


def ssd_backward(rank, x_pre, bc_pre, step_pre, aux, seg_row, conv_rows, bc_rows, head_rows, expand, expand_t, dy, kept):
    tokens, channels = x_pre.shape
    count = tokens // CHUNK
    place = lambda i: count - 1 - i
    now = lambda i: (place(i), 0)
    whole = lambda i: (0, 0)
    wide = pl.BlockSpec((CHUNK, channels), now)
    narrow = pl.BlockSpec((CHUNK, 2 * LANES), now)
    specs = common_specs(place, channels)
    mixed, states, *more = kept
    return pl.pallas_call(
        ssd_backward_kernel,
        grid=(count,),
        in_specs=[pl.BlockSpec(memory_space=pltpu.SMEM), specs[0], specs[2], *specs[4:]]
        + [pl.BlockSpec((channels, LANES), whole), wide, wide, pl.BlockSpec((None, LANES, channels), lambda i: (place(i), 0, 0))]
        + [wide] * 7 + [narrow] * 2,
        out_specs=[
            wide,
            narrow,
            pl.BlockSpec((LANES, CHUNK), lambda i: (0, place(i))),
            pl.BlockSpec((LANES, CHUNK), lambda i: (0, place(i))),
            pl.BlockSpec((CHUNK, LANES), now),
            pl.BlockSpec((16, CHUNK), lambda i: (0, place(i))),
            pl.BlockSpec((8, channels), whole),
            pl.BlockSpec((8, 2 * LANES), whole),
            pl.BlockSpec((8, LANES), whole),
        ],
        out_shape=[
            jax.ShapeDtypeStruct((tokens, channels), bf16),
            jax.ShapeDtypeStruct((tokens, 2 * LANES), bf16),
            hbm((LANES, tokens), bf16),
            hbm((LANES, tokens), bf16),
            jax.ShapeDtypeStruct((tokens, LANES), bf16),
            hbm((16, tokens), bf16),
            jax.ShapeDtypeStruct((8, channels), f32),
            jax.ShapeDtypeStruct((8, 2 * LANES), f32),
            jax.ShapeDtypeStruct((8, LANES), f32),
        ],
        scratch_shapes=[
            pltpu.VMEM((LANES, channels), f32),
            pltpu.VMEM((HALO, channels), f32),
            pltpu.VMEM((HALO, 2 * LANES), f32),
            pltpu.VMEM((2 * LANES, CHUNK), bf16),
        ],
        compiler_params=pltpu.CompilerParams(vmem_limit_bytes=20 * MIB),
        cost_estimate=pl.CostEstimate(flops=28 * 10**9, bytes_accessed=40 * 10**6, transcendentals=0),
        name="ssd_backward",
    )(
        rank, from_hbm(x_pre), bc_pre, step_pre, aux, seg_row, conv_rows, bc_rows, head_rows,
        expand, expand_t, from_hbm(mixed), dy, from_hbm(states), *[from_hbm(v) for v in more],
    )


def segment_facts(seg):
    row = seg[0]
    tokens = row.shape[0]
    cols = []
    for lag in (1, 2, 3):
        cols.append(jnp.pad(row[:-lag], (lag, 0), constant_values=-1) == row)
    for lag in (1, 2, 3):
        cols.append(jnp.pad(row[lag:], (0, lag), constant_values=-1) == row)
    blocks = row.reshape(tokens // CHUNK, CHUNK)
    ends = blocks[:, -1:]
    before = jnp.concatenate([jnp.full((1, 1), -1, row.dtype), ends[:-1]], axis=0)
    cols.append((blocks == before).reshape(-1))
    cols.append((blocks == ends).reshape(-1))
    cols.append(row)
    facts = jnp.stack([c.astype(f32) for c in cols], axis=1)
    return jnp.pad(facts, ((0, 0), (0, 16 - facts.shape[1]))), seg.astype(f32)


def pad_rows(table, rows=8):
    return jnp.pad(table, ((0, rows - table.shape[0]), (0, 0)))


def pad_lanes(table, lanes=LANES):
    return jnp.pad(table, ((0, 0), (0, lanes - table.shape[1])))


def head_expand(channels):
    head, channel = jnp.arange(LANES), jnp.arange(channels) // WIDTH
    return (head[:, None] == channel[None, :]).astype(bf16), (channel[:, None] == head[None, :]).astype(bf16)


TILE = 512
TILE_D = 512


def fill(dest, pieces, idx_ref):
    rows = pieces[0].shape[0]
    s = 0
    for piece in pieces:
        for b in range(piece.shape[0] // rows):
            start = pl.multiple_of(idx_ref[s] * rows, rows)
            dest[pl.ds(start, rows), :] = piece[b * rows:(b + 1) * rows, :]
            s += 1


def params(mib=24):
    return pltpu.CompilerParams(vmem_limit_bytes=mib * MIB)


def cost(us):
    return pl.CostEstimate(flops=int(us * 10**9), bytes_accessed=int(us * 2 * 10**6), transcendentals=0)


def prepare_kernel(hidden_ref, gain_ref, low_ref, low_t_ref, inv_ref):
    inputs = hidden_ref[...].astype(f32)
    inv_rms = lax.rsqrt(jnp.mean(inputs * inputs, axis=1, keepdims=True) + EPSILON)
    low = (inputs * inv_rms * gain_ref[0:1, :]).astype(bf16)
    low_ref[...] = low
    low_t_ref[...] = low.T
    inv_ref[...] = column_to_row(inv_rms)


def prepare(hidden, gain_rows):
    tokens, depth = hidden.shape
    block = pl.BlockSpec((TILE, depth), lambda i: (i, 0))
    return pl.pallas_call(
        prepare_kernel,
        grid=(tokens // TILE,),
        in_specs=[block, pl.BlockSpec((8, depth), lambda i: (0, 0))],
        out_specs=[block, pl.BlockSpec((depth, TILE), lambda i: (0, i)), pl.BlockSpec((8, TILE), lambda i: (0, i))],
        out_shape=[
            hbm((tokens, depth), bf16),
            hbm((depth, tokens), bf16),
            jax.ShapeDtypeStruct((8, tokens), f32),
        ],
        compiler_params=params(),
        cost_estimate=cost(12),
        name="prepare",
    )(hidden, gain_rows)


def pack_kernel(rank_ref, in_ref, bc_ref, step_ref, a_ref, scratch):
    rows, width = bc_ref.shape
    channels = in_ref.shape[2]
    share = width // 4
    heads = step_ref.shape[0]
    a_ref[:, :channels] = in_ref[:, 1, :].astype(bf16)
    scratch[...] = jnp.zeros_like(scratch)
    scratch[share:share + heads, 0:rows] = step_ref[...]
    step = scratch[...].T[0:rows, :]
    own = bc_ref[:, 0:LANES]
    for member in range(1, 4):
        turned = pltpu.roll(bc_ref[...], width - member * share, 1)[:, 0:LANES]
        own = jnp.where(rank_ref[0] == member, turned, own)
    lane = lax.broadcasted_iota(jnp.int32, (rows, LANES), 1)
    a_ref[:, channels:] = jnp.where(lane < share, own, step).astype(bf16)


def pack(in_weight, bc_weight, step_t, rank):
    rows, _, channels = in_weight.shape
    vmem = pl.BlockSpec(memory_space=pltpu.VMEM)
    return pl.pallas_call(
        pack_kernel,
        in_specs=[pl.BlockSpec(memory_space=pltpu.SMEM), vmem, vmem, vmem],
        out_specs=vmem,
        out_shape=jax.ShapeDtypeStruct((rows, channels + LANES), bf16),
        scratch_shapes=[pltpu.VMEM((LANES, 2 * LANES), f32)],
        compiler_params=params(),
        cost_estimate=cost(2),
        name="pack",
    )(rank, from_hbm(in_weight), from_hbm(bc_weight), from_hbm(step_t))


def pack_gate_kernel(in_ref, b_ref):
    b_ref[...] = in_ref[:, 0, :].astype(bf16)


def pack_gate(in_weight):
    rows, _, channels = in_weight.shape
    vmem = pl.BlockSpec(memory_space=pltpu.VMEM)
    return pl.pallas_call(
        pack_gate_kernel,
        in_specs=[vmem],
        out_specs=vmem,
        out_shape=hbm((rows, channels), bf16),
        compiler_params=params(),
        cost_estimate=cost(2),
        name="pack_gate",
    )(from_hbm(in_weight))


def columns_kernel(rank_ref, *refs, count):
    pieces, (full_ref, full_t_ref) = refs[:count], refs[count:]
    for r, piece in enumerate(pieces):
        width = piece.shape[1]
        start = pl.multiple_of((rank_ref[0] ^ r) * width, LANES)
        value = piece[...]
        full_ref[:, pl.ds(start, width)] = value
        full_t_ref[pl.ds(start, width), :] = value.T


def join_columns(pieces, rank):
    tokens, width = pieces[0].shape
    depth = width * len(pieces)
    return pl.pallas_call(
        functools.partial(columns_kernel, count=len(pieces)),
        grid=(tokens // TILE,),
        in_specs=[pl.BlockSpec(memory_space=pltpu.SMEM)] + [pl.BlockSpec((TILE, width), lambda i: (i, 0))] * len(pieces),
        out_specs=[pl.BlockSpec((TILE, depth), lambda i: (i, 0)), pl.BlockSpec((depth, TILE), lambda i: (0, i))],
        out_shape=[jax.ShapeDtypeStruct((tokens, depth), bf16), jax.ShapeDtypeStruct((depth, tokens), bf16)],
        compiler_params=params(),
        cost_estimate=cost(12),
        name="join_columns",
    )(rank, *pieces)


def rows_kernel(rank_ref, *refs, count):
    pieces, full_ref = refs[:count], refs[count]
    for r, piece in enumerate(pieces):
        rows = piece.shape[0]
        full_ref[pl.ds(pl.multiple_of((rank_ref[0] ^ r) * rows, rows), rows), :] = piece[...]


def join_rows(pieces, rank):
    rows, width = pieces[0].shape
    shape = (rows * len(pieces), width)
    return pl.pallas_call(
        functools.partial(rows_kernel, count=len(pieces)),
        in_specs=[pl.BlockSpec(memory_space=pltpu.SMEM)] + [pl.BlockSpec(memory_space=pltpu.VMEM)] * len(pieces),
        out_specs=pl.BlockSpec(memory_space=pltpu.VMEM),
        out_shape=jax.ShapeDtypeStruct(shape, pieces[0].dtype),
        compiler_params=params(),
        cost_estimate=cost(0.1),
        name="join_rows",
    )(rank, *pieces)


def small_kernel(rank_ref, *refs, count):
    pieces, (small_ref, bc_ref, step_ref, scratch) = refs[:count], refs[count:]
    share = pieces[0].shape[0]
    for r, piece in enumerate(pieces):
        scratch[pl.ds(pl.multiple_of((rank_ref[0] ^ r) * share, share), share), :] = piece[...].astype(f32)
    bc_ref[...] = scratch[...].T
    turned = small_ref[...].T
    lane = lax.broadcasted_iota(jnp.int32, turned.shape, 1)
    step_ref[...] = jnp.where(lane < LANES - share, pltpu.roll(turned, LANES - share, 1), 0.0)


def join_small(pieces, small, rank):
    share, tokens = pieces[0].shape
    width = share * len(pieces)
    return pl.pallas_call(
        functools.partial(small_kernel, count=len(pieces)),
        grid=(tokens // TILE,),
        in_specs=[pl.BlockSpec(memory_space=pltpu.SMEM)]
        + [pl.BlockSpec((share, TILE), lambda i: (0, i))] * len(pieces)
        + [pl.BlockSpec((LANES, TILE), lambda i: (0, i))],
        out_specs=[pl.BlockSpec((TILE, width), lambda i: (i, 0)), pl.BlockSpec((TILE, LANES), lambda i: (i, 0))],
        out_shape=[jax.ShapeDtypeStruct((tokens, width), f32), jax.ShapeDtypeStruct((tokens, LANES), f32)],
        scratch_shapes=[pltpu.VMEM((width, TILE), f32)],
        compiler_params=params(),
        cost_estimate=cost(0.1),
        name="join_small",
    )(rank, *pieces, small)


def project_small_kernel(idx_ref, lhs_ref, *refs, count):
    pieces, (small_ref, share_ref, w_ref, wt_ref) = refs[:count], refs[count:]

    @pl.when(pl.program_id(0) == 0)
    def _():
        fill(w_ref, pieces, idx_ref)
        wt_ref[...] = w_ref[...].T[0:wt_ref.shape[0], :]

    small = dot_nn(lhs_ref[...], w_ref[...]).T
    small_ref[...] = small
    share_ref[...] = small[0:share_ref.shape[0], :].astype(bf16)


def project_small(lhs, pieces, idx, share):
    tokens, depth = lhs.shape
    count, last = len(pieces), pieces[0].shape[1] // LANES - 1
    whole = lambda i: (0, 0)
    return pl.pallas_call(
        functools.partial(project_small_kernel, count=count),
        grid=(tokens // TILE,),
        in_specs=[pl.BlockSpec(memory_space=pltpu.SMEM), pl.BlockSpec((TILE, depth), lambda i: (i, 0))]
        + [pl.BlockSpec((p.shape[0], LANES), lambda i: (0, last)) for p in pieces],
        out_specs=[
            pl.BlockSpec((LANES, TILE), lambda i: (0, i)),
            pl.BlockSpec((share, TILE), lambda i: (0, i)),
            pl.BlockSpec((depth, LANES), whole),
            pl.BlockSpec((share, depth), whole),
        ],
        out_shape=[
            jax.ShapeDtypeStruct((LANES, tokens), f32),
            jax.ShapeDtypeStruct((share, tokens), bf16),
            hbm((depth, LANES), bf16),
            jax.ShapeDtypeStruct((share, depth), bf16),
        ],
        compiler_params=params(),
        cost_estimate=cost(20),
        name="project_small",
    )(idx, lhs, *pieces)


def project_kernel(idx_ref, lhs_ref, *refs, count):
    pieces, (x_ref, w_ref) = refs[:count], refs[count:]

    @pl.when(pl.program_id(0) == 0)
    def _():
        fill(w_ref, pieces, idx_ref)

    x_ref[...] = dot_nn(lhs_ref[...], w_ref[...])


def project(lhs, pieces, idx, channels):
    tokens, depth = lhs.shape
    whole = lambda i: (0, 0)
    return pl.pallas_call(
        functools.partial(project_kernel, count=len(pieces)),
        grid=(tokens // TILE,),
        in_specs=[pl.BlockSpec(memory_space=pltpu.SMEM), pl.BlockSpec((TILE, depth), lambda i: (i, 0))]
        + [pl.BlockSpec((p.shape[0], channels), whole) for p in pieces],
        out_specs=[pl.BlockSpec((TILE, channels), lambda i: (i, 0)), pl.BlockSpec((depth, channels), whole)],
        out_shape=[
            hbm((tokens, channels), f32),
            hbm((depth, channels), bf16),
        ],
        compiler_params=params(),
        cost_estimate=cost(0.1),
        name="project",
    )(idx, lhs, *pieces)


def column_to_row(col):
    return jnp.broadcast_to(col, (col.shape[0], LANES)).T[0:8, :]


def row_to_column(row):
    return jnp.broadcast_to(row, (LANES, row.shape[1])).T[:, 0:1]


def gate_kernel(idx_ref, lhs_ref, mixed_ref, *refs, count):
    pieces, (gate_ref, sums_ref, w_ref) = refs[:count], refs[count:]

    @pl.when(pl.program_id(0) == 0)
    def _():
        fill(w_ref, pieces, idx_ref)

    gate = dot_nn(lhs_ref[...], w_ref[...])
    gate_ref[...] = gate
    gated = mixed_ref[...] * (gate * sigmoid(gate))
    sums_ref[...] = column_to_row(jnp.sum(gated * gated, axis=1, keepdims=True))


def gate_forward(lhs, mixed, pieces, idx):
    tokens, depth = lhs.shape
    channels = mixed.shape[1]
    whole = lambda i: (0, 0)
    now = lambda i: (i, 0)
    return pl.pallas_call(
        functools.partial(gate_kernel, count=len(pieces)),
        grid=(tokens // TILE,),
        in_specs=[
            pl.BlockSpec(memory_space=pltpu.SMEM),
            pl.BlockSpec((TILE, depth), now),
            pl.BlockSpec((TILE, channels), now),
        ]
        + [pl.BlockSpec(p.shape, whole) for p in pieces],
        out_specs=[
            pl.BlockSpec((TILE, channels), now),
            pl.BlockSpec((8, TILE), lambda i: (0, i)),
            pl.BlockSpec((depth, channels), whole),
        ],
        out_shape=[
            jax.ShapeDtypeStruct((tokens, channels), f32),
            jax.ShapeDtypeStruct((8, tokens), f32),
            hbm((depth, channels), bf16),
        ],
        compiler_params=params(),
        cost_estimate=cost(0.1),
        name="gate_forward",
    )(idx, lhs, from_hbm(mixed), *pieces)


def gated_kernel(gate_ref, mixed_ref, square_ref, conv_ref, out_ref, *, inner_total):
    gate = gate_ref[...]
    scale = lax.rsqrt(row_to_column(square_ref[0:1, :]) / inner_total + EPSILON)
    gated = mixed_ref[...] * (gate * sigmoid(gate))
    out_ref[...] = (gated * scale * conv_ref[5:6, :]).astype(bf16)


def gated_norm(gate, mixed, square, conv_rows, inner_total):
    tokens, channels = gate.shape
    block = pl.BlockSpec((TILE, channels), lambda i: (i, 0))
    return pl.pallas_call(
        functools.partial(gated_kernel, inner_total=inner_total),
        grid=(tokens // TILE,),
        in_specs=[block, block, pl.BlockSpec((8, TILE), lambda i: (0, i)), pl.BlockSpec((8, channels), lambda i: (0, 0))],
        out_specs=block,
        out_shape=jax.ShapeDtypeStruct((tokens, channels), bf16),
        compiler_params=params(),
        cost_estimate=cost(0.1),
        name="gated_norm",
    )(gate, mixed, square, conv_rows)


def gout_kernel(idx_ref, cot_ref, gate_ref, mixed_ref, conv_ref, *refs, count):
    pieces, (gout_ref, sums_ref, w_ref) = refs[:count], refs[count:]

    @pl.when(pl.program_id(0) == 0)
    def _():
        fill(w_ref, pieces, idx_ref)

    gout = dot_nn(cot_ref[...], w_ref[...])
    gout_ref[...] = gout
    gate = gate_ref[...]
    gated = mixed_ref[...] * (gate * sigmoid(gate))
    sums_ref[...] = column_to_row(jnp.sum(gout * conv_ref[5:6, :] * gated, axis=1, keepdims=True))


def grad_gout(cot, gate, mixed, conv_rows, pieces, idx):
    tokens, depth = cot.shape
    channels = mixed.shape[1]
    whole = lambda i: (0, 0)
    now = lambda i: (i, 0)
    return pl.pallas_call(
        functools.partial(gout_kernel, count=len(pieces)),
        grid=(tokens // TILE,),
        in_specs=[
            pl.BlockSpec(memory_space=pltpu.SMEM),
            pl.BlockSpec((TILE, depth), now),
            pl.BlockSpec((TILE, channels), now),
            pl.BlockSpec((TILE, channels), now),
            pl.BlockSpec((8, channels), whole),
        ]
        + [pl.BlockSpec(p.shape, whole) for p in pieces],
        out_specs=[
            pl.BlockSpec((TILE, channels), now),
            pl.BlockSpec((8, TILE), lambda i: (0, i)),
            pl.BlockSpec((depth, channels), whole),
        ],
        out_shape=[
            jax.ShapeDtypeStruct((tokens, channels), f32),
            jax.ShapeDtypeStruct((8, tokens), f32),
            jax.ShapeDtypeStruct((depth, channels), bf16),
        ],
        compiler_params=params(),
        cost_estimate=cost(20),
        name="grad_gout",
    )(idx, cot, gate, mixed, conv_rows, *pieces)


def gate_back_kernel(gate_ref, gout_ref, mixed_ref, square_ref, inner_ref, conv_ref, dmixed_ref, dgate_ref, dgain_ref, *, inner_total):
    gate, gout, mixed = gate_ref[...], gout_ref[...], mixed_ref[...]
    gain = conv_ref[5:6, :]
    square, inner = row_to_column(square_ref[0:1, :]), row_to_column(inner_ref[0:1, :])
    scale = lax.rsqrt(square / inner_total + EPSILON)
    sg = sigmoid(gate)
    act = gate * sg
    gated = mixed * act
    dgated = scale * (gain * gout) - gated * (scale * scale * scale * inner / inner_total)
    dmixed_ref[...] = (dgated * act).astype(bf16)
    dgate_ref[...] = (dgated * mixed * sg * (1.0 + gate * (1.0 - sg))).astype(bf16)

    @pl.when(pl.program_id(0) == 0)
    def _():
        dgain_ref[...] = jnp.zeros_like(dgain_ref)

    dgain_ref[5:6, :] += jnp.sum(gout * gated * scale, axis=0, keepdims=True)


def gate_backward(gate, gout, mixed, square, inner, conv_rows, inner_total):
    tokens, channels = gate.shape
    whole = lambda i: (0, 0)
    block = pl.BlockSpec((TILE, channels), lambda i: (i, 0))
    row = pl.BlockSpec((8, TILE), lambda i: (0, i))
    return pl.pallas_call(
        functools.partial(gate_back_kernel, inner_total=inner_total),
        grid=(tokens // TILE,),
        in_specs=[block, block, block, row, row, pl.BlockSpec((8, channels), whole)],
        out_specs=[block, block, pl.BlockSpec((8, channels), whole)],
        out_shape=[
            jax.ShapeDtypeStruct((tokens, channels), bf16),
            jax.ShapeDtypeStruct((tokens, channels), bf16),
            jax.ShapeDtypeStruct((8, channels), f32),
        ],
        compiler_params=params(),
        cost_estimate=cost(0.1),
        name="gate_backward",
    )(from_hbm(gate), from_hbm(gout), from_hbm(mixed), square, inner, conv_rows)


def weight_grad_kernel(idx_ref, lhs_ref, rhs_ref, *refs, rows, turned):
    outs, scratch = refs[:-1], refs[-1]
    at = pl.program_id(0)
    scratch[pl.ds(pl.multiple_of(at * TILE_D, TILE_D), TILE_D), :] = (dot_nt if turned else dot_nn)(
        lhs_ref[...], rhs_ref[...]
    ).astype(bf16)

    @pl.when(at == pl.num_programs(0) - 1)
    def _():
        s = 0
        for out in outs:
            for b in range(out.shape[0] // rows):
                start = pl.multiple_of(idx_ref[s] * rows, rows)
                out[b * rows:(b + 1) * rows, :] = scratch[pl.ds(start, rows), :]
                s += 1


def weight_grad(lhs_t, rhs, idx, sizes, us=0.1, turned=False):
    depth, tokens = lhs_t.shape
    width = rhs.shape[0 if turned else 1]
    rows = depth // idx.shape[0]
    whole = lambda i: (0, 0)
    return pl.pallas_call(
        functools.partial(weight_grad_kernel, rows=rows, turned=turned),
        grid=(depth // TILE_D,),
        in_specs=[
            pl.BlockSpec(memory_space=pltpu.SMEM),
            pl.BlockSpec((TILE_D, tokens), lambda i: (i, 0)),
            pl.BlockSpec(rhs.shape, whole),
        ],
        out_specs=[pl.BlockSpec((size * rows, width), whole) for size in sizes],
        out_shape=[hbm((size * rows, width), bf16) for size in sizes],
        scratch_shapes=[pltpu.VMEM((depth, width), bf16)],
        compiler_params=params(),
        cost_estimate=cost(us),
        name="weight_grad",
    )(idx, lhs_t, rhs)


def out_kernel(rank_ref, lhs_ref, w_ref, *outs):
    product = dot_nt(lhs_ref[...], w_ref[...]).astype(bf16)
    for r, out in enumerate(outs):
        @pl.when(pl.program_id(0) == r)
        def _():
            out[...] = product


def out_partial(gated_out, w_out, rank, ranks):
    tokens, channels = gated_out.shape
    depth = w_out.shape[0]
    width = depth // ranks
    whole = lambda i, rank_ref: (0, 0)
    return pl.pallas_call(
        out_kernel,
        grid_spec=pltpu.PrefetchScalarGridSpec(
            num_scalar_prefetch=1,
            grid=(ranks,),
            in_specs=[
                pl.BlockSpec((tokens, channels), whole),
                pl.BlockSpec((width, channels), lambda i, rank_ref: (i ^ rank_ref[0], 0)),
            ],
            out_specs=[pl.BlockSpec((tokens, width), whole)] * ranks,
        ),
        out_shape=[hbm((tokens, width), bf16)] * ranks,
        compiler_params=params(),
        cost_estimate=cost(0.1),
        name="out_partial",
    )(rank, gated_out, w_out)


def term_kernel(rank_ref, gx_ref, wx_ref, gg_ref, wg_ref, gs_ref, ws_ref, gb_ref, hidden_ref, inv_ref, *refs, apart):
    wbt_refs, outs, dgain_ref = refs[:4], refs[4:-1], refs[-1]
    w_bct = jnp.concatenate([ref[...] for ref in wbt_refs], axis=0)
    gain = None
    for r, out in zip(apart, outs):
        rows = out.shape[0]
        span = pl.ds(pl.multiple_of((rank_ref[0] ^ r) * rows, rows), rows)
        total = dot_nt(gx_ref[span, :], wx_ref[...]) + dot_nt(gg_ref[span, :], wg_ref[...])
        total = total + dot_nt(gs_ref[span, :], ws_ref[...]) + dot_nn(gb_ref[span, :], w_bct)
        out[...] = total.astype(bf16)
        normed = hidden_ref[span, :].astype(f32) * row_to_column(inv_ref[0:1, span])
        own = jnp.sum(total * normed, axis=0, keepdims=True)
        gain = own if gain is None else gain + own
    cut = [gain[:, i:i + LANES] for i in range(0, gain.shape[1], LANES)]
    dgain_ref[...] = jnp.concatenate(cut + [jnp.zeros((8 - len(cut), LANES), f32)], axis=0)


def normed_term(dx, dgate, dstep, dbc, w_a, w_b, w_s, w_bct, hidden, inv_rms, rank, ranks, apart):
    tokens, channels = dx.shape
    depth = w_a.shape[0]
    rows = tokens // ranks
    whole = lambda i: (0, 0)
    return pl.pallas_call(
        functools.partial(term_kernel, apart=apart),
        grid=(depth // TILE_D,),
        in_specs=[
            pl.BlockSpec(memory_space=pltpu.SMEM),
            pl.BlockSpec(dx.shape, whole),
            pl.BlockSpec((TILE_D, channels), lambda i: (i, 0)),
            pl.BlockSpec(dgate.shape, whole),
            pl.BlockSpec((TILE_D, channels), lambda i: (i, 0)),
            pl.BlockSpec(dstep.shape, whole),
            pl.BlockSpec((TILE_D, LANES), lambda i: (i, 0)),
            pl.BlockSpec(dbc.shape, whole),
            pl.BlockSpec((tokens, TILE_D), lambda i: (0, i)),
            pl.BlockSpec(inv_rms.shape, whole),
        ]
        + [pl.BlockSpec((w.shape[0], TILE_D), lambda i: (0, i)) for w in w_bct],
        out_specs=[pl.BlockSpec((rows, TILE_D), lambda i: (0, i))] * len(apart) + [pl.BlockSpec((8, LANES), lambda i: (i, 0))],
        out_shape=[jax.ShapeDtypeStruct((rows, depth), bf16)] * len(apart)
        + [jax.ShapeDtypeStruct((8 * (depth // TILE_D), LANES), f32)],
        compiler_params=params(32),
        cost_estimate=cost(5 if 2 in apart else 5),
        name="normed_term",
    )(
        rank, dx, from_hbm(w_a), dgate, from_hbm(w_b), dstep, from_hbm(w_s), dbc, from_hbm(hidden), inv_rms, *w_bct
    )


def norm_back_kernel(rank_ref, a_ref, b_ref, hidden_ref, cot_ref, gain_ref, out_ref):
    grad = a_ref[...].astype(f32) + b_ref[...].astype(f32)
    inputs = hidden_ref[...].astype(f32)
    inv_rms = lax.rsqrt(jnp.mean(inputs * inputs, axis=1, keepdims=True) + EPSILON)
    normed = inputs * inv_rms
    scaled = grad * gain_ref[0:1, :]
    mean = jnp.mean(scaled * normed, axis=1, keepdims=True)
    out_ref[...] = (inv_rms * (scaled - normed * mean) + cot_ref[...].astype(f32)).astype(out_ref.dtype)


def norm_backward(a, b, hidden, cot, gain_rows, rank):
    rows, depth = a.shape
    mine = lambda i, rank_ref: (rank_ref[0], 0)
    whole = lambda i, rank_ref: (0, 0)
    return pl.pallas_call(
        norm_back_kernel,
        grid_spec=pltpu.PrefetchScalarGridSpec(
            num_scalar_prefetch=1,
            grid=(1,),
            in_specs=[
                pl.BlockSpec((rows, depth), whole),
                pl.BlockSpec((rows, depth), whole),
                pl.BlockSpec((rows, depth), mine),
                pl.BlockSpec((rows, depth), mine),
                pl.BlockSpec((8, depth), whole),
            ],
            out_specs=pl.BlockSpec((rows, depth), whole),
        ),
        out_shape=jax.ShapeDtypeStruct((rows, depth), bf16),
        compiler_params=params(),
        cost_estimate=cost(0.1),
        name="norm_backward",
    )(rank, a, b, from_hbm(hidden), from_hbm(cot), gain_rows)


def moved(weight, moment, grad):
    fresh = 0.5 * moment + 0.5 * grad
    return fresh, weight - LEARN_RATE * fresh - LEARN_RATE * DECAY_RATE * weight


def add_up(refs):
    total = refs[0][...].astype(f32)
    for ref in refs[1:]:
        total = total + ref[...].astype(f32)
    return total


def update_in_kernel(w_ref, m_ref, *refs, count):
    gate_refs, x_refs, (m_out, w_out) = refs[:count], refs[count:2 * count], refs[2 * count:]
    for at, parts in ((0, gate_refs), (1, x_refs)):
        fresh, weight = moved(w_ref[:, at, :], m_ref[:, at, :], add_up(parts))
        m_out[:, at, :] = fresh
        w_out[:, at, :] = weight


def update_in(weight, moment, gate_parts, x_parts):
    rows, _, channels = weight.shape
    size = min(rows, 96)
    full = pl.BlockSpec((size, 2, channels), lambda i: (i, 0, 0))
    parts = [*gate_parts, *x_parts]
    return pl.pallas_call(
        functools.partial(update_in_kernel, count=len(gate_parts)),
        grid=(rows // size,),
        in_specs=[full, full] + [pl.BlockSpec((size, channels), functools.partial(lambda at, i: (i, at), at)) for _, at in parts],
        out_specs=[full, full],
        out_shape=[jax.ShapeDtypeStruct(weight.shape, f32)] * 2,
        compiler_params=params(),
        cost_estimate=cost(0.1),
        name="update_in",
    )(from_hbm(weight), from_hbm(moment), *[part for part, _ in parts])


def update_small_kernel(w_ref, m_ref, sums_ref, own_ref, back_ref, *refs, share, order, shared):
    alone, late, (m_out, w_out, exchange, totals, scratch) = refs[:order[0]], refs[order[0]:-5], refs[-5:]
    heads, rows = w_ref.shape
    count = sums_ref.shape[0]
    last = late[0].shape[1] - LANES
    grad = own_ref[...].astype(f32) + back_ref[...].astype(f32)
    found = {0: sums_ref[...].astype(f32)}
    for at, ref in zip(order[1], alone):
        grad = grad + ref[0:rows, :].astype(f32)
        found[at] = ref[rows:, :].astype(f32)
    for at, ref in zip(order[2], late):
        grad = grad + ref[0:rows, last:].astype(f32)
        tail = ref[rows:, :].astype(f32)
        found[at] = jnp.concatenate([tail[:, i:i + LANES] for i in range(0, tail.shape[1], LANES)], axis=0)
    step = len(found) // 2
    while step >= 1:
        found = {i: found[i] + found[i + step] for i in range(step)}
        step //= 2
    totals[...] = found[0]
    exchange[0:rows, :] = grad
    exchange[rows:, :] = found[0][shared[0]:shared[1], :]
    scratch[0:rows, :] = grad
    turned = scratch[...].T[share:share + heads, 0:rows]
    fresh, weight = moved(w_ref[...], m_ref[...], turned)
    m_out[...] = fresh
    w_out[...] = weight


def update_small(weight_t, moment_t, sums, own, back, alone, late, order, shared, share):
    rows = weight_t.shape[1]
    count = sums.shape[0]
    whole = lambda i: (0, 0)
    spec = pl.BlockSpec(weight_t.shape, whole)
    return pl.pallas_call(
        functools.partial(update_small_kernel, share=share, order=order, shared=shared),
        grid=(1,),
        in_specs=[spec, spec, pl.BlockSpec(sums.shape, whole)] + [pl.BlockSpec((rows, LANES), whole)] * 2
        + [pl.BlockSpec(v.shape, whole) for v in (*alone, *late)],
        out_specs=[
            spec, spec,
            pl.BlockSpec((rows + shared[1] - shared[0], LANES), whole),
            pl.BlockSpec((count, LANES), whole),
        ],
        out_shape=[jax.ShapeDtypeStruct(weight_t.shape, f32)] * 2
        + [jax.ShapeDtypeStruct((rows + shared[1] - shared[0], LANES), f32), jax.ShapeDtypeStruct((count, LANES), f32)],
        scratch_shapes=[pltpu.VMEM((2 * LANES, LANES), f32)],
        compiler_params=params(),
        cost_estimate=cost(0.1),
        name="update_small",
    )(weight_t, moment_t, sums, own, back, *alone, *late)


def update_bc_kernel(rank_ref, w_ref, m_ref, *refs):
    pieces, (m_out, w_out, shared_out) = refs[:-3], refs[-3:]
    rows, width = w_ref.shape
    share = width // len(pieces)
    shared_out[...] = (pieces[0][rows:, :] + pieces[1][rows:, :]) + (pieces[2][rows:, :] + pieces[3][rows:, :])
    lane = lax.broadcasted_iota(jnp.int32, (rows, LANES), 1)
    for pair in range(width // LANES):
        halves = []
        for member in (2 * pair, 2 * pair + 1):
            own = pieces[0][0:rows, :]
            for r in range(1, len(pieces)):
                own = jnp.where((rank_ref[0] ^ r) == member, pieces[r][0:rows, :], own)
            halves.append(own)
        grad = jnp.where(lane < share, halves[0], pltpu.roll(halves[1], share, 1))
        span = slice(pair * LANES, (pair + 1) * LANES)
        fresh, weight = moved(w_ref[:, span], m_ref[:, span], grad)
        m_out[:, span] = fresh
        w_out[:, span] = weight


def update_bc(weight, moment, pieces, rank):
    vmem = pl.BlockSpec(memory_space=pltpu.VMEM)
    return pl.pallas_call(
        update_bc_kernel,
        in_specs=[pl.BlockSpec(memory_space=pltpu.SMEM)] + [vmem] * (2 + len(pieces)),
        out_specs=[vmem] * 3,
        out_shape=[jax.ShapeDtypeStruct(weight.shape, f32)] * 2
        + [jax.ShapeDtypeStruct((pieces[0].shape[0] - weight.shape[0], LANES), f32)],
        compiler_params=params(),
        cost_estimate=cost(0.1),
        name="update_bc",
    )(rank, weight, moment, *pieces)


def fence(*values):
    leaves, tree = jax.tree.flatten(values)
    return jax.tree.unflatten(tree, lax.optimization_barrier(leaves))


def outer_from(v, k):
    n = lax.axis_size("dp") // 2
    return lax.ppermute(v, "dp", [(((o + k) % n) * 2 + x, o * 2 + x) for o in range(n) for x in range(2)])


def outer_flip(v, bit):
    n = lax.axis_size("dp") // 2
    return lax.ppermute(v, "dp", [((o ^ bit) * 2 + x, o * 2 + x) for o in range(n) for x in range(2)])


def inner_flip(v):
    return lax.ppermute(v, "dp", [(d ^ 1, d) for d in range(lax.axis_size("dp"))])


def rank_flip(v, bit):
    return lax.ppermute(v, "mp", [(m ^ bit, m) for m in range(lax.axis_size("mp"))])


def hops(n):
    order = []
    for k in range(1, n // 2 + 1):
        order.append(k)
        if n - k != k:
            order.append(n - k)
    return order


def pair_sum(a, b):
    return (a.astype(f32) + b.astype(f32)).astype(bf16)


def outer_blocks(own, here, back, ks):
    rows = own.shape[0]
    back = [part[i:i + rows] for part in back for i in range(0, part.shape[0], rows)]
    return [
        (here[i * rows:(i + 1) * rows].astype(f32) + back[i].astype(f32)).astype(bf16) for i in range(len(ks))
    ]


def outer_send(blocks, ks):
    n = lax.axis_size("dp") // 2
    return [outer_from(block, n - k) for block, k in zip(blocks, ks)]


def outer_sum(v):
    bit = 1
    while bit < lax.axis_size("dp") // 2:
        v = v + outer_flip(v, bit)
        bit *= 2
    return v


def mp_sum(v):
    v = v + rank_flip(v, 1)
    return v + rank_flip(v, 2)


def mp_sum_direct(v):
    return (v + rank_flip(v, 1)) + (rank_flip(v, 2) + rank_flip(v, 3))


def mp_reduce(blocks):
    far = blocks[2].astype(f32) + rank_flip(blocks[3], 1).astype(f32)
    near = blocks[0].astype(f32) + rank_flip(blocks[1], 1).astype(f32)
    return near, rank_flip(far.astype(bf16), 2)


def mp_pieces(v):
    far = rank_flip(v, 2)
    return [v, rank_flip(v, 1), far, rank_flip(far, 1)]


def in_rank_order(pieces, rank, axis):
    odd, high = (rank & 1) == 1, (rank & 2) == 2
    join = lambda a, b: jnp.concatenate([a, b], axis=axis)
    low = jnp.where(odd, join(pieces[1], pieces[0]), join(pieces[0], pieces[1]))
    far = jnp.where(odd, join(pieces[3], pieces[2]), join(pieces[2], pieces[3]))
    return jnp.where(high, join(far, low), join(low, far))


def momentum(moment, grad):
    return 0.5 * moment + 0.5 * grad


def advance(weight, moment, grad):
    fresh = momentum(moment, grad)
    return (fresh, weight - LEARN_RATE * fresh - LEARN_RATE * DECAY_RATE * weight)


def body(
    hidden, segments, cotangent, in_weight, in_moment, bc_weight, bc_moment, step_weight, step_moment,
    out_weight, out_moment, conv_table, conv_moment, bc_table, bc_table_moment, head_table, head_moment,
    norm_gain, gain_moment,
):
    size = lax.axis_size("dp")
    ranks = lax.axis_size("mp")
    n = size // 2
    place, rank = lax.axis_index("dp"), lax.axis_index("mp")
    outer, inner = place // 2, place % 2
    rank1 = rank.reshape(1).astype(jnp.int32)
    rows, _, channels = in_weight.shape
    heads = head_table.shape[1]
    tokens, depth = hidden.shape
    share = bc_weight.shape[1] // ranks

    ks = hops(n)
    near_ks, far_k = ks[:-1], ks[-1]

    def members(order):
        return jnp.stack([((outer + k) % n) * 2 + (inner ^ j) for k, j in order]).astype(jnp.int32)

    first = [(0, 0), (0, 1)]
    idx = members(first + [(k, 0) for k in ks] + [(k, 1) for k in ks])
    idx_s = members([(0, 0)] + [(k, 0) for k in ks] + [(0, 1)] + [(k, 1) for k in ks])
    sizes = (1, 1, n - 1, n - 1)
    split_sizes = (1, 1, n - 1, n - 2, 1)
    width = depth // ranks

    set_a = pack(in_weight, bc_weight, step_weight.T, rank1)
    set_c = out_weight.T.astype(bf16)

    def blocks(own, z, x):
        return [own, x[0]] + [z[k] for k in ks] + [x[k] for k in ks]

    def block(v, i):
        return v[i * rows:(i + 1) * rows]

    def blocks(own, z, x):
        return [own, x[0]] + [z[k] for k in ks] + [x[k] for k in ks]

    def block(v, i):
        return v[i * rows:(i + 1) * rows]

    def total(own, own_got, got):
        value = own.astype(f32) + own_got.astype(f32)
        for part in got:
            value = value + part.astype(f32)
        return value

    def outer_all(v, some):
        return {k: outer_from(v, k) for k in some}

    def flip_all(z, some):
        return {k: inner_flip(z[k]) for k in some}

    a_z = outer_all(set_a, near_ks)
    a_x = {0: inner_flip(set_a)}
    far_a, a_x[0], hidden, segments, in_gate = fence(set_a, a_x[0], hidden, segments, in_weight)
    set_b = pack_gate(in_gate)
    a_z[far_k] = outer_from(far_a, far_k)
    cot_far = rank_flip(cotangent, 2)
    gain_rows = pad_rows(norm_gain[None])
    normed_low, normed_t, inv_rms = prepare(hidden, gain_rows)
    a_x.update(flip_all(a_z, near_ks))
    aux, seg_row = segment_facts(segments)
    head_rows = pad_lanes(pad_rows(head_table))
    facts = (aux, seg_row, pad_rows(conv_table), pad_rows(bc_table), head_rows, *head_expand(channels))
    set_a, set_b, set_c, a_z, a_x, cot_far, normed_low, normed_t, inv_rms, facts = fence(
        set_a, set_b, set_c, a_z, a_x, cot_far, normed_low, normed_t, inv_rms, facts
    )

    a_x[far_k] = inner_flip(a_z[far_k])
    b_x = {0: inner_flip(set_b)}
    b_z = outer_all(set_b, near_ks)
    cot, cot_t = join_columns([cotangent, rank_flip(cotangent, 1), cot_far, rank_flip(cot_far, 1)], rank1)
    set_b, set_c, b_z, b_x, a_z, a_x, cot, cot_t, normed_low = fence(
        set_b, set_c, b_z, b_x, a_z, a_x, cot, cot_t, normed_low
    )

    b_z[far_k] = outer_from(set_b, far_k)
    b_x.update(flip_all(b_z, near_ks[:1]))
    c_x = {0: inner_flip(set_c)}
    a_blocks = blocks(set_a, a_z, a_x)
    small, bc_share, w_s, w_bct_share = project_small(normed_low, a_blocks, idx, share)
    bc_far, bc_near = rank_flip(bc_share, 2), rank_flip(bc_share, 1)
    x_pre, w_a = project(normed_low, a_blocks, idx, channels)
    bc_far, x_pre, small, set_c, w_bct_share, w_s = fence(bc_far, x_pre, small, set_c, w_bct_share, w_s)
    bc_pieces = [bc_share, bc_near, bc_far, rank_flip(bc_far, 1)]
    bc_pre, step_pre = join_small(bc_pieces, small, rank1)
    set_c, b_z, b_x, c_x, x_pre, bc_pre, step_pre, w_bct_share = fence(
        set_c, b_z, b_x, c_x, x_pre, bc_pre, step_pre, w_bct_share
    )

    c_z = outer_all(set_c, near_ks)
    b_x.update(flip_all(b_z, ks[1:]))
    kept = ssd_forward(x_pre, bc_pre, step_pre, *facts[:-1])
    mixed = kept[0]
    mixed, b_x, b_z, c_z, c_x, w_bct_share, set_c = fence(mixed, b_x, b_z, c_z, c_x, w_bct_share, set_c)

    c_z[far_k] = outer_from(set_c, far_k)
    c_x.update(flip_all(c_z, near_ks))
    gate_pre, square, w_b = gate_forward(normed_low, mixed, blocks(set_b, b_z, b_x), idx)
    square = mp_sum_direct(square)
    mixed, gate_pre, square, w_b, w_bct_share, c_z, c_x = fence(mixed, gate_pre, square, w_b, w_bct_share, c_z, c_x)

    c_x[far_k] = inner_flip(c_z[far_k])
    w_bct = [w_bct_share, rank_flip(w_bct_share, 2)]
    conv_rows = facts[2]
    gated_out = gated_norm(gate_pre, mixed, square, conv_rows, channels * ranks)
    gc_own, gc_own1, gc_here, gc_near, gc_far = weight_grad(cot_t, gated_out, idx, split_sizes)
    c_x, square, gated_out, gc_own, gc_own1, gc_here, gc_near, gc_far, w_bct = fence(
        c_x, square, gated_out, gc_own, gc_own1, gc_here, gc_near, gc_far, w_bct
    )

    gc_far_back, gc_near_back = inner_flip(gc_far), inner_flip(gc_near)
    gout, inner_dot, w_c = grad_gout(cot, gate_pre, mixed, conv_rows, blocks(set_c, c_z, c_x), idx)
    gout, inner_dot, w_c = fence(gout, inner_dot, w_c)
    inner_dot = mp_sum_direct(inner_dot)
    partial = out_partial(gated_out, w_c, rank1, ranks)
    inner_dot, gout, partial, w_bct, gc_far_back = fence(inner_dot, gout, partial, w_bct, gc_far_back)
    c_far_got = outer_from(pair_sum(block(gc_here, n - 2), gc_far_back), n - far_k)
    out_back = rank_flip(partial[3], 1)
    w_bct = [w_bct[0], rank_flip(w_bct[0], 1), w_bct[1], rank_flip(w_bct[1], 1)]
    dmixed, dgate, dgain = gate_backward(gate_pre, gout, mixed, square, inner_dot, conv_rows, channels * ranks)
    gb_own, gb_own1, gb_here, gb_send = weight_grad(normed_t, dgate, idx, sizes)
    gc_near_back, c_far_got, w_bct, out_back, gb_own, gb_own1, gb_here, gb_send, partial, dmixed, dgain = fence(
        gc_near_back, c_far_got, w_bct, out_back, gb_own, gb_own1, gb_here, gb_send, partial, dmixed, dgain
    )
    c_blocks = [pair_sum(block(gc_here, i), block(gc_near_back, i)) for i in range(n - 2)]
    out_far = pair_sum(partial[2], out_back)
    c_blocks, out_far, w_bct, dmixed, gb_send = fence(c_blocks, out_far, w_bct, dmixed, gb_send)

    c_got = outer_send(c_blocks, near_ks) + [c_far_got]
    gb_back = inner_flip(gb_send)
    out_got = rank_flip(out_far, 2)
    dx, dbc, dbc_keep, dbc_send, dstep, dstep_t, dconv, dbct_part, dheads = ssd_backward(
        rank1, x_pre, bc_pre, step_pre, *facts, dmixed, kept
    )
    c_got, gb_back, out_got, dx, dbc, dbc_keep, dbc_send, dstep, dstep_t, dconv, dbct_part, dheads = fence(
        c_got, gb_back, out_got, dx, dbc, dbc_keep, dbc_send, dstep, dstep_t, dconv, dbct_part, dheads
    )

    b_got = {far_k: outer_from(pair_sum(block(gb_here, n - 2), block(gb_back, n - 2)), n - far_k)}
    dbc_back = rank_flip(dbc_send, 1)
    out_near_back = rank_flip(partial[1], 1)
    ga_own, ga_own1, ga_here, ga_send = weight_grad(normed_t, dx, idx, sizes, us=20)
    ga_own, ga_own1, ga_here, ga_send, dx, dbc_back, gb_back, gb_here, out_near_back = fence(
        ga_own, ga_own1, ga_here, ga_send, dx, dbc_back, gb_back, gb_here, out_near_back
    )

    b_near = [pair_sum(block(gb_here, i), block(gb_back, i)) for i in range(n - 2)]
    b_got.update(zip(near_ks, outer_send(b_near, near_ks)))
    ga_back = inner_flip(ga_send)
    dbc_pair = pair_sum(dbc_keep, dbc_back)
    dbc_got = rank_flip(dbc_pair[share:], 2)
    operands = (dx, dgate, dstep, dbc, w_a, w_b, w_s, w_bct, hidden, inv_rms, rank1, ranks)
    far_own, far_send, gain_far = normed_term(*operands, (2, 3))
    far_own, far_send, gain_far, dx, dbc_got, dbc_pair, dstep_t, b_got[far_k] = fence(
        far_own, far_send, gain_far, dx, dbc_got, dbc_pair, dstep_t, b_got[far_k]
    )
    far_back = rank_flip(far_send, 1)
    operands = (dx, *operands[1:])
    near_own, near_send, gain_near = normed_term(*operands, (0, 1))
    far_back, near_own, near_send, gain_near, ga_back = fence(far_back, near_own, near_send, gain_near, ga_back)
    near_back = rank_flip(near_send, 1)
    far = pair_sum(far_own, far_back)
    a_blocks = [pair_sum(block(ga_here, i), block(ga_back, i)) for i in range(n - 1)]
    dbc_share = pair_sum(dbc_pair[:share], dbc_got)
    dsmall_t = jnp.concatenate([dbc_share, dstep_t, jnp.zeros((LANES - share - 16, tokens), bf16)], axis=0)
    gs_own, gs_here, gs_send = weight_grad(normed_t, dsmall_t, idx_s, (1, n - 1, n), turned=True)
    far, a_blocks, near_back, gs_send, gc_own1, gb_own1, b_got = fence(
        far, a_blocks, near_back, gs_send, gc_own1, gb_own1, b_got
    )

    early, late = [], near_ks
    got = rank_flip(far, 2)
    a_got = dict(zip([far_k, *early], outer_send([a_blocks[-1], *a_blocks[:len(early)]], [far_k, *early])))
    cut = lambda v: [v[:, i:i + LANES] for i in range(0, v.shape[1], LANES)]
    alone = channels // LANES * 8 + 8
    sums = jnp.concatenate([*cut(dconv + dgain), dheads, *cut(dbct_part), gain_far + gain_near], axis=0)
    shared = (alone, sums.shape[0])
    wide = (channels + LANES) // LANES
    sums = pad_rows(sums, -(-sums.shape[0] // (16 * wide)) * 16 * wide).astype(bf16)
    small_back = inner_flip(jnp.concatenate([gs_send, sums], axis=0))
    own_got = inner_flip(jnp.concatenate([gc_own1, gb_own1], axis=1))
    near = near_own.astype(f32) + near_back.astype(f32)
    got, near, a_got, small_back, sums, own_got, ga_own1, a_late = fence(
        got, near, a_got, small_back, sums, own_got, ga_own1, a_blocks[len(early):-1]
    )

    mine = norm_backward(near, got, hidden, cot, gain_rows, rank1)
    mine, small_back, sums, ga_own1, a_late, gs_here, out_got, out_near_back = fence(
        mine, small_back, sums, ga_own1, a_late, gs_here, out_got, out_near_back
    )
    a_own_got = inner_flip(ga_own1)
    gs_back, sums_back = small_back[:n * rows], small_back[n * rows:]
    s_blocks = dict(zip(ks, outer_blocks(gs_own, gs_here, [gs_back[rows:]], ks)))
    sums = pair_sum(sums, sums_back)
    size = sums.shape[0] // wide
    sums_wide = jnp.concatenate([sums[i * size:(i + 1) * size] for i in range(wide)], axis=1)
    late_got = outer_send(
        [
            jnp.concatenate([jnp.concatenate([a_block, s_blocks[k]], axis=1), sums_wide], axis=0)
            for k, a_block in zip(late, a_late)
        ],
        late,
    )
    s_got = outer_send([jnp.concatenate([s_blocks[k], sums], axis=0) for k in (far_k, *early)], (far_k, *early))
    mine_far = rank_flip(mine, 2)
    mine_far, mine = fence(mine_far, mine)
    late_got, s_got, a_own_got, sums = fence(late_got, s_got, a_own_got, sums)

    mine_near, mine_far_near = rank_flip(mine, 1), rank_flip(mine_far, 1)
    step_m, step_w, exchange, totals = update_small(
        step_weight.T, step_moment.T, sums, gs_own, gs_back, s_got, late_got,
        (len(s_got), [n - k for k in (far_k, *early)], [n - k for k in late]), shared, share,
    )
    exchanged = [exchange] + [rank_flip(exchange, r) for r in (1, 2, 3)]
    in_m, in_w = update_in(
        in_weight, in_moment,
        [(gb_own, 0), (own_got, 1)] + [(b_got[k], 0) for k in ks],
        [(ga_own, 0), (a_own_got, 0)] + [(a_got[k], 0) for k in (far_k, *early)] + [(v, 0) for v in late_got],
    )
    input_grad = join_rows([mine, mine_near, mine_far, mine_far_near], rank1)
    exchanged, mine_far_near = fence(exchanged, mine_far_near)
    bc_m, bc_w, totals_shared = update_bc(bc_weight, bc_moment, exchanged, rank1)

    resid = lax.dynamic_slice_in_dim(hidden, rank * width, width, 1).astype(f32)
    output = (resid + partial[0].astype(f32) + out_near_back.astype(f32) + out_got.astype(f32)).astype(bf16)
    shard_c = total(gc_own, own_got[:, :channels], c_got)

    side_by_side = lambda v: jnp.concatenate([v[i:i + 8] for i in range(0, v.shape[0], 8)], axis=1)
    total_conv = side_by_side(totals[:alone - 8])[:6]
    total_head = totals[alone - 8:alone - 5, :heads]
    total_bct = side_by_side(totals_shared[:16])[:5]
    per = TILE_D // LANES
    total_gain = jnp.concatenate([totals_shared[i:i + per] for i in range(16, totals_shared.shape[0], 8)], axis=0).reshape(-1)

    out_m, out_w = advance(out_weight, out_moment, shard_c.T)
    return (
        output, input_grad, in_m, in_w, bc_m, bc_w, step_m.T, step_w.T, out_m, out_w,
        momentum(conv_moment, total_conv),
        momentum(bc_table_moment, total_bct),
        momentum(head_moment, total_head),
        momentum(gain_moment, total_gain),
    )


def solution(mesh):
    placed = (
        P("dp", None),
        P("dp", None),
        P("dp", "mp"),
        P("dp", None, "mp"),
        P("dp", None, "mp"),
        P("dp", None),
        P("dp", None),
        P("dp", "mp"),
        P("dp", "mp"),
        P("mp", "dp"),
        P("mp", "dp"),
        P(None, "mp"),
        P(None, "mp"),
        P(),
        P(),
        P(None, "mp"),
        P(None, "mp"),
        P(),
        P(),
    )
    return jax.shard_map(
        body,
        mesh=mesh,
        in_specs=placed,
        out_specs=(
            P("dp", "mp"),
            P("dp", None),
            P("dp", None, "mp"),
            P("dp", None, "mp"),
            P("dp", None),
            P("dp", None),
            P("dp", "mp"),
            P("dp", "mp"),
            P("mp", "dp"),
            P("mp", "dp"),
            P(None, "mp"),
            P(),
            P(None, "mp"),
            P(),
        ),
        check_vma=False,
    )
```

```python
import functools

import jax
import jax.numpy as jnp
from jax import lax
from jax.experimental import pallas as pl
from jax.experimental.pallas import tpu as pltpu
from jax.sharding import PartitionSpec as P

CHUNK = 128
EPSILON = 1e-05
LEARN_RATE = 0.0001
DECAY_RATE = 0.1
WIDTH = 64
LANES = 128
HALO = 8
bf16 = jnp.bfloat16
f32 = jnp.float32
MIB = 1024 * 1024


def hbm(shape, dtype):
    return pltpu.HBM(shape, dtype)


def from_hbm(v):
    return pltpu.with_memory_space_constraint(v, pltpu.HBM)


def dot_nn(a, b):
    return lax.dot_general(a, b, (((1,), (0,)), ((), ())), preferred_element_type=f32)


def dot_nt(a, b):
    return lax.dot_general(a, b, (((1,), (1,)), ((), ())), preferred_element_type=f32)


def dot_tn(a, b):
    return lax.dot_general(a, b, (((0,), (0,)), ((), ())), preferred_element_type=f32)


def split3(v):
    high = v.astype(bf16)
    rest = v - high.astype(f32)
    mid = rest.astype(bf16)
    low = (rest - mid.astype(f32)).astype(bf16)
    return high, mid, low


def exact_left(ones, v):
    high, mid, low = split3(v)
    return dot_nn(ones, high) + dot_nn(ones, mid) + dot_nn(ones, low)


def spread(v, expand):
    high, mid, low = split3(v)
    return dot_nn(high, expand) + dot_nn(mid, expand) + dot_nn(low, expand)


def gather_heads(v, expand_t):
    high = v.astype(bf16)
    mid = (v - high.astype(f32)).astype(bf16)
    return dot_nn(high, expand_t) + dot_nn(mid, expand_t)


def sigmoid(v):
    return 0.5 * jnp.tanh(0.5 * v) + 0.5


def conv_block(before, now, taps, keep):
    longer = jnp.concatenate([before, now], axis=0)
    total = taps[4:5, :] + taps[0:1, :] * now
    for lag in (1, 2, 3):
        moved = pltpu.roll(longer, lag, 0)[HALO:, :]
        total = total + taps[lag:lag + 1, :] * (moved * keep[:, lag - 1:lag])
    return total


def step_parts(step_pre, heads):
    raw = step_pre + heads[0:1, :]
    small = jnp.exp(-jnp.abs(raw))
    steps = jnp.maximum(raw, 0.0) + jnp.log1p(small)
    slope = jnp.where(raw >= 0.0, 1.0, small) / (1.0 + small)
    rates = -jnp.exp(heads[1:2, :])
    return slope, steps, rates


def triangle(lower):
    row = lax.broadcasted_iota(jnp.int32, (CHUNK, CHUNK), 0)
    col = lax.broadcasted_iota(jnp.int32, (CHUNK, CHUNK), 1)
    return row >= col if lower else row <= col


def ssd_forward_kernel(
    x_ref, xb_ref, bc_ref, bcb_ref, st_ref, aux_ref, seg_ref, conv_ref, bct_ref, heads_ref, expand_ref,
    mixed_ref, state_ref, act_ref, slope_ref, xs_ref, xe_ref, step_ref, entry_ref, end_ref, bcact_ref, bcslope_ref,
    state,
):
    chunk = pl.program_id(0)

    @pl.when(chunk == 0)
    def _():
        state[...] = jnp.zeros_like(state)

    channels = x_ref.shape[1]
    aux = aux_ref[...]
    expand = expand_ref[...]
    u = conv_block(xb_ref[...], x_ref[...], conv_ref, aux)
    sg = sigmoid(u)
    x_act = u * sg
    act_ref[...] = x_act
    slope_ref[...] = (sg * (1.0 + u * (1.0 - sg))).astype(bf16)
    ubc = conv_block(bcb_ref[...], bc_ref[...], bct_ref, aux)
    sgbc = sigmoid(ubc)
    bc_act = (ubc * sgbc).astype(bf16)
    bcact_ref[...] = bc_act
    bcslope_ref[...] = sgbc * (1.0 + ubc * (1.0 - sgbc))
    b_mat, c_mat = bc_act[:, :LANES], bc_act[:, LANES:]
    _, steps, rates = step_parts(st_ref[...], heads_ref)
    lower = triangle(True)
    cum = exact_left(lower.astype(bf16), steps * rates)
    cum_t = cum.T
    tail = cum[CHUNK - 1:CHUNK, :]
    entry = jnp.exp(cum) * aux[:, 6:7]
    to_end = jnp.exp(tail - cum) * aux[:, 7:8]
    wide = spread(jnp.concatenate([steps, entry, to_end], axis=0), expand)
    step_e, entry_e, to_end_e = wide[:CHUNK], wide[CHUNK:2 * CHUNK], wide[2 * CHUNK:]
    skip_e = spread(jnp.broadcast_to(heads_ref[2:3, :], (8, LANES)), expand)[0:1, :]
    mask = lower & (aux[:, 8:9] == seg_ref[...])
    scores = jnp.where(mask, dot_nt(c_mat, b_mat), 0.0)
    xs = x_act * step_e
    xs_low = xs.astype(bf16)
    xe_low = (xs * to_end_e).astype(bf16)
    xs_ref[...] = xs_low
    xe_ref[...] = xe_low
    step_ref[...] = step_e.astype(bf16)
    entry_ref[...] = entry_e.astype(bf16)
    end_ref[...] = to_end_e.astype(bf16)
    held = state[...]
    held_low = held.astype(bf16)
    state_ref[...] = held_low
    out = dot_nn(c_mat, held_low) * entry_e + skip_e * x_act
    state[...] = held * entry_e[CHUNK - 1:CHUNK, :] + dot_tn(b_mat, xe_low)
    first = lax.broadcasted_iota(jnp.int32, (CHUNK, LANES), 1) < WIDTH
    zero = jnp.zeros((CHUNK, LANES), bf16)
    for pair in range(channels // LANES):
        span = slice(pair * LANES, (pair + 1) * LANES)
        parts = []
        for head in (2 * pair, 2 * pair + 1):
            diff = cum[:, head:head + 1] - cum_t[head:head + 1, :]
            parts.append((scores * jnp.exp(jnp.minimum(diff, 0.0))).astype(bf16))
        own = xs_low[:, span]
        both = jnp.concatenate([jnp.where(first, own, zero), jnp.where(first, zero, own)], axis=0)
        mixed_ref[:, span] = out[:, span] + dot_nn(jnp.concatenate(parts, axis=1), both)


def ssd_backward_kernel(
    rank_ref, x_ref, bc_ref, st_ref, aux_ref, seg_ref, conv_ref, bct_ref, heads_ref, expand_ref,
    expand_t_ref, mixed_ref, dy_ref, state_ref, act_ref, slope_ref, xs_ref, xe_ref, step_ref, entry_ref, end_ref, bcact_ref,
    bcslope_ref, dx_ref, dbc_ref, keep_ref, send_ref, dst_ref, dst_t_ref, dconv_ref, dbct_ref, dheads_ref,
    dstate, du_scr, dubc_scr, share_scr,
):
    @pl.when(pl.program_id(0) == 0)
    def _():
        for ref in (dstate, du_scr, dubc_scr, dconv_ref, dbct_ref, dheads_ref):
            ref[...] = jnp.zeros_like(ref)

    channels = x_ref.shape[1]
    aux = aux_ref[...]
    expand = expand_ref[...]
    x_act = act_ref[...]
    b_mat, c_mat = bcact_ref[:, :LANES], bcact_ref[:, LANES:]
    slope, steps, rates = step_parts(st_ref[...], heads_ref)
    lower = triangle(True)
    cum = exact_left(lower.astype(bf16), steps * rates)
    cum_t = cum.T
    skip_e = spread(jnp.broadcast_to(heads_ref[2:3, :], (8, LANES)), expand)[0:1, :]
    upper = triangle(False)
    mask = upper & (aux[:, 8:9] == seg_ref[...])
    scores = jnp.where(mask, dot_nt(b_mat, c_mat), 0.0)
    xs_low = xs_ref[...]
    dy_low = dy_ref[...]
    dy = dy_low.astype(f32)
    held_low = state_ref[...]
    grad = dstate[...]
    grad_low = grad.astype(bf16)
    entry_e = entry_ref[...].astype(f32)
    entry_dy = (entry_e * dy).astype(bf16)
    kept_e = entry_e[CHUNK - 1:CHUNK, :]
    dstate[...] = grad * kept_e + dot_tn(c_mat, entry_dy)
    dc = dot_nt(entry_dy, held_low)
    db = dot_nt(xe_ref[...], grad_low)
    q_state = dot_nn(b_mat, grad_low) * end_ref[...].astype(f32)
    first = lax.broadcasted_iota(jnp.int32, (CHUNK, LANES), 1) < WIDTH
    zero = jnp.zeros((CHUNK, LANES), bf16)
    dscores = jnp.zeros((CHUNK, CHUNK), f32)
    q_parts = []
    for pair in range(channels // LANES):
        span = slice(pair * LANES, (pair + 1) * LANES)
        own = dy_low[:, span]
        both = jnp.concatenate([jnp.where(first, own, zero), jnp.where(first, zero, own)], axis=0)
        dweights = dot_nt(xs_low[:, span], both)
        parts = []
        for i, head in enumerate((2 * pair, 2 * pair + 1)):
            diff = cum_t[head:head + 1, :] - cum[:, head:head + 1]
            decay = jnp.exp(jnp.minimum(diff, 0.0))
            parts.append((scores * decay).astype(bf16))
            dscores = dscores + dweights[:, i * LANES:(i + 1) * LANES] * decay
        q_parts.append(dot_nn(jnp.concatenate(parts, axis=1), both))
    q = jnp.concatenate(q_parts, axis=1) + q_state
    dscores_low = jnp.where(mask, dscores, 0.0).astype(bf16)
    db = db + dot_nn(dscores_low, c_mat)
    dc = dc + dot_tn(dscores_low, b_mat)
    xs_round = xs_low.astype(f32)
    expand_t = expand_t_ref[...]
    flow = gather_heads(dy * (mixed_ref[...] - skip_e * x_act) - xs_round * q, expand_t)
    dstep = dot_nn((x_act * q).astype(bf16), expand_t)
    sums = jnp.concatenate(
        [
            jnp.sum(xs_round * q_state + kept_e * (held_low.astype(f32) * grad), axis=0, keepdims=True),
            jnp.sum(dy * x_act, axis=0, keepdims=True),
            jnp.zeros((6, channels), f32),
        ],
        axis=0,
    )
    sums = gather_heads(sums, expand_t)
    dlog = exact_left(upper.astype(bf16), flow) + sums[0:1, :]
    dstep = dstep + rates * dlog
    draw = dstep * slope
    dst_ref[...] = pltpu.roll(draw, WIDTH, 1).astype(bf16)
    dst_t_ref[...] = draw.T[0:16, :].astype(bf16)
    dheads_ref[0:1, :] += jnp.sum(draw, axis=0, keepdims=True)
    dheads_ref[1:2, :] += rates * jnp.sum(dlog * steps, axis=0, keepdims=True)
    dheads_ref[2:3, :] += sums[1:2, :]
    x_now, bc_now = x_ref[...], bc_ref[...]

    def conv_back(scratch, du, now, taps, dtaps):
        longer = jnp.concatenate([du, scratch[...]], axis=0)
        total = taps[0:1, :] * du
        sums = [jnp.sum(now * du, axis=0, keepdims=True)]
        for lag in (1, 2, 3):
            moved = pltpu.roll(longer, CHUNK + HALO - lag, 0)[0:CHUNK, :] * aux[:, 2 + lag:3 + lag]
            total = total + taps[lag:lag + 1, :] * moved
            sums.append(jnp.sum(now * moved, axis=0, keepdims=True))
        sums.append(jnp.sum(du, axis=0, keepdims=True))
        dtaps[0:5, :] += jnp.concatenate(sums, axis=0)
        scratch[...] = du[0:HALO, :]
        return total

    du = (skip_e * dy + step_ref[...].astype(f32) * q) * slope_ref[...].astype(f32)
    dx_ref[...] = conv_back(du_scr, du, x_now, conv_ref, dconv_ref).astype(dx_ref.dtype)
    dubc = jnp.concatenate([db, dc], axis=1) * bcslope_ref[...]
    dbc = conv_back(dubc_scr, dubc, bc_now, bct_ref, dbct_ref).astype(bf16)
    swapped = jnp.concatenate([dbc[:, LANES:], dbc[:, :LANES]], axis=1)
    ordered = jnp.where((rank_ref[0] & 2) == 2, swapped, dbc)
    swapped = jnp.concatenate(
        [pltpu.roll(ordered[:, :LANES].astype(f32), WIDTH, 1), pltpu.roll(ordered[:, LANES:].astype(f32), WIDTH, 1)], axis=1
    ).astype(bf16)
    dbc_ref[...] = jnp.where((rank_ref[0] & 1) == 1, swapped, ordered)
    share = 2 * LANES // 4
    turned = dbc.T
    for member in range(4):
        apart = member ^ rank_ref[0]
        start = pl.multiple_of((apart & 1) * 2 * share + (apart >> 1) * share, share)
        share_scr[pl.ds(start, share), :] = turned[member * share:(member + 1) * share, :]
    keep_ref[...] = share_scr[0:2 * share, :]
    send_ref[...] = share_scr[2 * share:4 * share, :]


def common_specs(place, channels):
    before = lambda i: (jnp.maximum(place(i) * (CHUNK // HALO) - 1, 0), 0)
    now = lambda i: (place(i), 0)
    whole = lambda i: (0, 0)
    return [
        pl.BlockSpec((CHUNK, channels), now),
        pl.BlockSpec((HALO, channels), before),
        pl.BlockSpec((CHUNK, 2 * LANES), now),
        pl.BlockSpec((HALO, 2 * LANES), before),
        pl.BlockSpec((CHUNK, LANES), now),
        pl.BlockSpec((CHUNK, 16), now),
        pl.BlockSpec((1, CHUNK), lambda i: (0, place(i))),
        pl.BlockSpec((8, channels), whole),
        pl.BlockSpec((8, 2 * LANES), whole),
        pl.BlockSpec((8, LANES), whole),
        pl.BlockSpec((LANES, channels), whole),
    ]


def ssd_forward(x_pre, bc_pre, step_pre, aux, seg_row, conv_rows, bc_rows, head_rows, expand):
    tokens, channels = x_pre.shape
    count = tokens // CHUNK
    now = lambda i: (i, 0)
    return pl.pallas_call(
        ssd_forward_kernel,
        grid=(count,),
        in_specs=common_specs(lambda i: i, channels),
        out_specs=[
            pl.BlockSpec((CHUNK, channels), now),
            pl.BlockSpec((None, LANES, channels), lambda i: (i, 0, 0)),
        ]
        + [pl.BlockSpec((CHUNK, channels), now)] * 7
        + [pl.BlockSpec((CHUNK, 2 * LANES), now)] * 2,
        out_shape=[
            hbm((tokens, channels), f32),
            hbm((count, LANES, channels), bf16),
            hbm((tokens, channels), f32),
            *[hbm((tokens, channels), bf16) for _ in range(6)],
            hbm((tokens, 2 * LANES), bf16),
            hbm((tokens, 2 * LANES), f32),
        ],
        scratch_shapes=[
            pltpu.VMEM((LANES, channels), f32),
        ],
        compiler_params=pltpu.CompilerParams(vmem_limit_bytes=18 * MIB),
        cost_estimate=pl.CostEstimate(flops=14 * 10**9, bytes_accessed=40 * 10**6, transcendentals=0),
        name="ssd_forward",
    )(
        from_hbm(x_pre), from_hbm(x_pre), bc_pre, bc_pre, step_pre, aux, seg_row, conv_rows, bc_rows, head_rows, expand
    )


def ssd_backward(rank, x_pre, bc_pre, step_pre, aux, seg_row, conv_rows, bc_rows, head_rows, expand, expand_t, dy, kept):
    tokens, channels = x_pre.shape
    count = tokens // CHUNK
    place = lambda i: count - 1 - i
    now = lambda i: (place(i), 0)
    whole = lambda i: (0, 0)
    wide = pl.BlockSpec((CHUNK, channels), now)
    narrow = pl.BlockSpec((CHUNK, 2 * LANES), now)
    specs = common_specs(place, channels)
    mixed, states, *more = kept
    return pl.pallas_call(
        ssd_backward_kernel,
        grid=(count,),
        in_specs=[pl.BlockSpec(memory_space=pltpu.SMEM), specs[0], specs[2], *specs[4:]]
        + [pl.BlockSpec((channels, LANES), whole), wide, wide, pl.BlockSpec((None, LANES, channels), lambda i: (place(i), 0, 0))]
        + [wide] * 7 + [narrow] * 2,
        out_specs=[
            wide,
            narrow,
            pl.BlockSpec((LANES, CHUNK), lambda i: (0, place(i))),
            pl.BlockSpec((LANES, CHUNK), lambda i: (0, place(i))),
            pl.BlockSpec((CHUNK, LANES), now),
            pl.BlockSpec((16, CHUNK), lambda i: (0, place(i))),
            pl.BlockSpec((8, channels), whole),
            pl.BlockSpec((8, 2 * LANES), whole),
            pl.BlockSpec((8, LANES), whole),
        ],
        out_shape=[
            jax.ShapeDtypeStruct((tokens, channels), bf16),
            jax.ShapeDtypeStruct((tokens, 2 * LANES), bf16),
            hbm((LANES, tokens), bf16),
            hbm((LANES, tokens), bf16),
            jax.ShapeDtypeStruct((tokens, LANES), bf16),
            hbm((16, tokens), bf16),
            jax.ShapeDtypeStruct((8, channels), f32),
            jax.ShapeDtypeStruct((8, 2 * LANES), f32),
            jax.ShapeDtypeStruct((8, LANES), f32),
        ],
        scratch_shapes=[
            pltpu.VMEM((LANES, channels), f32),
            pltpu.VMEM((HALO, channels), f32),
            pltpu.VMEM((HALO, 2 * LANES), f32),
            pltpu.VMEM((2 * LANES, CHUNK), bf16),
        ],
        compiler_params=pltpu.CompilerParams(vmem_limit_bytes=20 * MIB),
        cost_estimate=pl.CostEstimate(flops=28 * 10**9, bytes_accessed=40 * 10**6, transcendentals=0),
        name="ssd_backward",
    )(
        rank, from_hbm(x_pre), bc_pre, step_pre, aux, seg_row, conv_rows, bc_rows, head_rows,
        expand, expand_t, from_hbm(mixed), dy, from_hbm(states), *[from_hbm(v) for v in more],
    )


def segment_facts(seg):
    row = seg[0]
    tokens = row.shape[0]
    cols = []
    for lag in (1, 2, 3):
        cols.append(jnp.pad(row[:-lag], (lag, 0), constant_values=-1) == row)
    for lag in (1, 2, 3):
        cols.append(jnp.pad(row[lag:], (0, lag), constant_values=-1) == row)
    blocks = row.reshape(tokens // CHUNK, CHUNK)
    ends = blocks[:, -1:]
    before = jnp.concatenate([jnp.full((1, 1), -1, row.dtype), ends[:-1]], axis=0)
    cols.append((blocks == before).reshape(-1))
    cols.append((blocks == ends).reshape(-1))
    cols.append(row)
    facts = jnp.stack([c.astype(f32) for c in cols], axis=1)
    return jnp.pad(facts, ((0, 0), (0, 16 - facts.shape[1]))), seg.astype(f32)


def pad_rows(table, rows=8):
    return jnp.pad(table, ((0, rows - table.shape[0]), (0, 0)))


def pad_lanes(table, lanes=LANES):
    return jnp.pad(table, ((0, 0), (0, lanes - table.shape[1])))


def head_expand(channels):
    head, channel = jnp.arange(LANES), jnp.arange(channels) // WIDTH
    return (head[:, None] == channel[None, :]).astype(bf16), (channel[:, None] == head[None, :]).astype(bf16)


TILE = 512
TILE_D = 512


def fill(dest, pieces, idx_ref):
    rows = pieces[0].shape[0]
    s = 0
    for piece in pieces:
        for b in range(piece.shape[0] // rows):
            start = pl.multiple_of(idx_ref[s] * rows, rows)
            dest[pl.ds(start, rows), :] = piece[b * rows:(b + 1) * rows, :]
            s += 1


def params(mib=24):
    return pltpu.CompilerParams(vmem_limit_bytes=mib * MIB)


def cost(us):
    return pl.CostEstimate(flops=int(us * 10**9), bytes_accessed=int(us * 2 * 10**6), transcendentals=0)


def prepare_kernel(hidden_ref, gain_ref, low_ref, low_t_ref, inv_ref):
    inputs = hidden_ref[...].astype(f32)
    inv_rms = lax.rsqrt(jnp.mean(inputs * inputs, axis=1, keepdims=True) + EPSILON)
    low = (inputs * inv_rms * gain_ref[0:1, :]).astype(bf16)
    low_ref[...] = low
    low_t_ref[...] = low.T
    inv_ref[...] = column_to_row(inv_rms)


def prepare(hidden, gain_rows):
    tokens, depth = hidden.shape
    block = pl.BlockSpec((TILE, depth), lambda i: (i, 0))
    return pl.pallas_call(
        prepare_kernel,
        grid=(tokens // TILE,),
        in_specs=[block, pl.BlockSpec((8, depth), lambda i: (0, 0))],
        out_specs=[block, pl.BlockSpec((depth, TILE), lambda i: (0, i)), pl.BlockSpec((8, TILE), lambda i: (0, i))],
        out_shape=[
            hbm((tokens, depth), bf16),
            hbm((depth, tokens), bf16),
            jax.ShapeDtypeStruct((8, tokens), f32),
        ],
        compiler_params=params(),
        cost_estimate=cost(12),
        name="prepare",
    )(hidden, gain_rows)


def pack_kernel(rank_ref, in_ref, bc_ref, step_ref, a_ref, scratch):
    rows, width = bc_ref.shape
    channels = in_ref.shape[2]
    share = width // 4
    heads = step_ref.shape[0]
    a_ref[:, :channels] = in_ref[:, 1, :].astype(bf16)
    scratch[...] = jnp.zeros_like(scratch)
    scratch[share:share + heads, 0:rows] = step_ref[...]
    step = scratch[...].T[0:rows, :]
    own = bc_ref[:, 0:LANES]
    for member in range(1, 4):
        turned = pltpu.roll(bc_ref[...], width - member * share, 1)[:, 0:LANES]
        own = jnp.where(rank_ref[0] == member, turned, own)
    lane = lax.broadcasted_iota(jnp.int32, (rows, LANES), 1)
    a_ref[:, channels:] = jnp.where(lane < share, own, step).astype(bf16)


def pack(in_weight, bc_weight, step_t, rank):
    rows, _, channels = in_weight.shape
    vmem = pl.BlockSpec(memory_space=pltpu.VMEM)
    return pl.pallas_call(
        pack_kernel,
        in_specs=[pl.BlockSpec(memory_space=pltpu.SMEM), vmem, vmem, vmem],
        out_specs=vmem,
        out_shape=jax.ShapeDtypeStruct((rows, channels + LANES), bf16),
        scratch_shapes=[pltpu.VMEM((LANES, 2 * LANES), f32)],
        compiler_params=params(),
        cost_estimate=cost(2),
        name="pack",
    )(rank, from_hbm(in_weight), from_hbm(bc_weight), from_hbm(step_t))


def pack_gate_kernel(in_ref, b_ref):
    b_ref[...] = in_ref[:, 0, :].astype(bf16)


def pack_gate(in_weight):
    rows, _, channels = in_weight.shape
    vmem = pl.BlockSpec(memory_space=pltpu.VMEM)
    return pl.pallas_call(
        pack_gate_kernel,
        in_specs=[vmem],
        out_specs=vmem,
        out_shape=hbm((rows, channels), bf16),
        compiler_params=params(),
        cost_estimate=cost(2),
        name="pack_gate",
    )(from_hbm(in_weight))


def columns_kernel(rank_ref, *refs, count):
    pieces, (full_ref, full_t_ref) = refs[:count], refs[count:]
    for r, piece in enumerate(pieces):
        width = piece.shape[1]
        start = pl.multiple_of((rank_ref[0] ^ r) * width, LANES)
        value = piece[...]
        full_ref[:, pl.ds(start, width)] = value
        full_t_ref[pl.ds(start, width), :] = value.T


def join_columns(pieces, rank):
    tokens, width = pieces[0].shape
    depth = width * len(pieces)
    return pl.pallas_call(
        functools.partial(columns_kernel, count=len(pieces)),
        grid=(tokens // TILE,),
        in_specs=[pl.BlockSpec(memory_space=pltpu.SMEM)] + [pl.BlockSpec((TILE, width), lambda i: (i, 0))] * len(pieces),
        out_specs=[pl.BlockSpec((TILE, depth), lambda i: (i, 0)), pl.BlockSpec((depth, TILE), lambda i: (0, i))],
        out_shape=[jax.ShapeDtypeStruct((tokens, depth), bf16), jax.ShapeDtypeStruct((depth, tokens), bf16)],
        compiler_params=params(),
        cost_estimate=cost(12),
        name="join_columns",
    )(rank, *pieces)


def rows_kernel(rank_ref, *refs, count):
    pieces, full_ref = refs[:count], refs[count]
    for r, piece in enumerate(pieces):
        rows = piece.shape[0]
        full_ref[pl.ds(pl.multiple_of((rank_ref[0] ^ r) * rows, rows), rows), :] = piece[...]


def join_rows(pieces, rank):
    rows, width = pieces[0].shape
    shape = (rows * len(pieces), width)
    return pl.pallas_call(
        functools.partial(rows_kernel, count=len(pieces)),
        in_specs=[pl.BlockSpec(memory_space=pltpu.SMEM)] + [pl.BlockSpec(memory_space=pltpu.VMEM)] * len(pieces),
        out_specs=pl.BlockSpec(memory_space=pltpu.VMEM),
        out_shape=jax.ShapeDtypeStruct(shape, pieces[0].dtype),
        compiler_params=params(),
        cost_estimate=cost(0.1),
        name="join_rows",
    )(rank, *pieces)


def small_kernel(rank_ref, *refs, count):
    pieces, (small_ref, bc_ref, step_ref, scratch) = refs[:count], refs[count:]
    share = pieces[0].shape[0]
    for r, piece in enumerate(pieces):
        scratch[pl.ds(pl.multiple_of((rank_ref[0] ^ r) * share, share), share), :] = piece[...].astype(f32)
    bc_ref[...] = scratch[...].T
    turned = small_ref[...].T
    lane = lax.broadcasted_iota(jnp.int32, turned.shape, 1)
    step_ref[...] = jnp.where(lane < LANES - share, pltpu.roll(turned, LANES - share, 1), 0.0)


def join_small(pieces, small, rank):
    share, tokens = pieces[0].shape
    width = share * len(pieces)
    return pl.pallas_call(
        functools.partial(small_kernel, count=len(pieces)),
        grid=(tokens // TILE,),
        in_specs=[pl.BlockSpec(memory_space=pltpu.SMEM)]
        + [pl.BlockSpec((share, TILE), lambda i: (0, i))] * len(pieces)
        + [pl.BlockSpec((LANES, TILE), lambda i: (0, i))],
        out_specs=[pl.BlockSpec((TILE, width), lambda i: (i, 0)), pl.BlockSpec((TILE, LANES), lambda i: (i, 0))],
        out_shape=[jax.ShapeDtypeStruct((tokens, width), f32), jax.ShapeDtypeStruct((tokens, LANES), f32)],
        scratch_shapes=[pltpu.VMEM((width, TILE), f32)],
        compiler_params=params(),
        cost_estimate=cost(0.1),
        name="join_small",
    )(rank, *pieces, small)


def project_small_kernel(idx_ref, lhs_ref, *refs, count):
    pieces, (small_ref, share_ref, w_ref, wt_ref) = refs[:count], refs[count:]

    @pl.when(pl.program_id(0) == 0)
    def _():
        fill(w_ref, pieces, idx_ref)
        wt_ref[...] = w_ref[...].T[0:wt_ref.shape[0], :]

    small = dot_nn(lhs_ref[...], w_ref[...]).T
    small_ref[...] = small
    share_ref[...] = small[0:share_ref.shape[0], :].astype(bf16)


def project_small(lhs, pieces, idx, share):
    tokens, depth = lhs.shape
    count, last = len(pieces), pieces[0].shape[1] // LANES - 1
    whole = lambda i: (0, 0)
    return pl.pallas_call(
        functools.partial(project_small_kernel, count=count),
        grid=(tokens // TILE,),
        in_specs=[pl.BlockSpec(memory_space=pltpu.SMEM), pl.BlockSpec((TILE, depth), lambda i: (i, 0))]
        + [pl.BlockSpec((p.shape[0], LANES), lambda i: (0, last)) for p in pieces],
        out_specs=[
            pl.BlockSpec((LANES, TILE), lambda i: (0, i)),
            pl.BlockSpec((share, TILE), lambda i: (0, i)),
            pl.BlockSpec((depth, LANES), whole),
            pl.BlockSpec((share, depth), whole),
        ],
        out_shape=[
            jax.ShapeDtypeStruct((LANES, tokens), f32),
            jax.ShapeDtypeStruct((share, tokens), bf16),
            hbm((depth, LANES), bf16),
            jax.ShapeDtypeStruct((share, depth), bf16),
        ],
        compiler_params=params(),
        cost_estimate=cost(20),
        name="project_small",
    )(idx, lhs, *pieces)


def project_kernel(idx_ref, lhs_ref, *refs, count):
    pieces, (x_ref, w_ref) = refs[:count], refs[count:]

    @pl.when(pl.program_id(0) == 0)
    def _():
        fill(w_ref, pieces, idx_ref)

    x_ref[...] = dot_nn(lhs_ref[...], w_ref[...])


def project(lhs, pieces, idx, channels):
    tokens, depth = lhs.shape
    whole = lambda i: (0, 0)
    return pl.pallas_call(
        functools.partial(project_kernel, count=len(pieces)),
        grid=(tokens // TILE,),
        in_specs=[pl.BlockSpec(memory_space=pltpu.SMEM), pl.BlockSpec((TILE, depth), lambda i: (i, 0))]
        + [pl.BlockSpec((p.shape[0], channels), whole) for p in pieces],
        out_specs=[pl.BlockSpec((TILE, channels), lambda i: (i, 0)), pl.BlockSpec((depth, channels), whole)],
        out_shape=[
            hbm((tokens, channels), f32),
            hbm((depth, channels), bf16),
        ],
        compiler_params=params(),
        cost_estimate=cost(0.1),
        name="project",
    )(idx, lhs, *pieces)


def column_to_row(col):
    return jnp.broadcast_to(col, (col.shape[0], LANES)).T[0:8, :]


def row_to_column(row):
    return jnp.broadcast_to(row, (LANES, row.shape[1])).T[:, 0:1]


def gate_kernel(idx_ref, lhs_ref, mixed_ref, *refs, count):
    pieces, (gate_ref, sums_ref, w_ref) = refs[:count], refs[count:]

    @pl.when(pl.program_id(0) == 0)
    def _():
        fill(w_ref, pieces, idx_ref)

    gate = dot_nn(lhs_ref[...], w_ref[...])
    gate_ref[...] = gate
    gated = mixed_ref[...] * (gate * sigmoid(gate))
    sums_ref[...] = column_to_row(jnp.sum(gated * gated, axis=1, keepdims=True))


def gate_forward(lhs, mixed, pieces, idx):
    tokens, depth = lhs.shape
    channels = mixed.shape[1]
    whole = lambda i: (0, 0)
    now = lambda i: (i, 0)
    return pl.pallas_call(
        functools.partial(gate_kernel, count=len(pieces)),
        grid=(tokens // TILE,),
        in_specs=[
            pl.BlockSpec(memory_space=pltpu.SMEM),
            pl.BlockSpec((TILE, depth), now),
            pl.BlockSpec((TILE, channels), now),
        ]
        + [pl.BlockSpec(p.shape, whole) for p in pieces],
        out_specs=[
            pl.BlockSpec((TILE, channels), now),
            pl.BlockSpec((8, TILE), lambda i: (0, i)),
            pl.BlockSpec((depth, channels), whole),
        ],
        out_shape=[
            jax.ShapeDtypeStruct((tokens, channels), f32),
            jax.ShapeDtypeStruct((8, tokens), f32),
            hbm((depth, channels), bf16),
        ],
        compiler_params=params(),
        cost_estimate=cost(0.1),
        name="gate_forward",
    )(idx, lhs, from_hbm(mixed), *pieces)


def gated_kernel(gate_ref, mixed_ref, square_ref, conv_ref, out_ref, *, inner_total):
    gate = gate_ref[...]
    scale = lax.rsqrt(row_to_column(square_ref[0:1, :]) / inner_total + EPSILON)
    gated = mixed_ref[...] * (gate * sigmoid(gate))
    out_ref[...] = (gated * scale * conv_ref[5:6, :]).astype(bf16)


def gated_norm(gate, mixed, square, conv_rows, inner_total):
    tokens, channels = gate.shape
    block = pl.BlockSpec((TILE, channels), lambda i: (i, 0))
    return pl.pallas_call(
        functools.partial(gated_kernel, inner_total=inner_total),
        grid=(tokens // TILE,),
        in_specs=[block, block, pl.BlockSpec((8, TILE), lambda i: (0, i)), pl.BlockSpec((8, channels), lambda i: (0, 0))],
        out_specs=block,
        out_shape=jax.ShapeDtypeStruct((tokens, channels), bf16),
        compiler_params=params(),
        cost_estimate=cost(0.1),
        name="gated_norm",
    )(gate, mixed, square, conv_rows)


def gout_kernel(idx_ref, cot_ref, gate_ref, mixed_ref, conv_ref, *refs, count):
    pieces, (gout_ref, sums_ref, w_ref) = refs[:count], refs[count:]

    @pl.when(pl.program_id(0) == 0)
    def _():
        fill(w_ref, pieces, idx_ref)

    gout = dot_nn(cot_ref[...], w_ref[...])
    gout_ref[...] = gout
    gate = gate_ref[...]
    gated = mixed_ref[...] * (gate * sigmoid(gate))
    sums_ref[...] = column_to_row(jnp.sum(gout * conv_ref[5:6, :] * gated, axis=1, keepdims=True))


def grad_gout(cot, gate, mixed, conv_rows, pieces, idx):
    tokens, depth = cot.shape
    channels = mixed.shape[1]
    whole = lambda i: (0, 0)
    now = lambda i: (i, 0)
    return pl.pallas_call(
        functools.partial(gout_kernel, count=len(pieces)),
        grid=(tokens // TILE,),
        in_specs=[
            pl.BlockSpec(memory_space=pltpu.SMEM),
            pl.BlockSpec((TILE, depth), now),
            pl.BlockSpec((TILE, channels), now),
            pl.BlockSpec((TILE, channels), now),
            pl.BlockSpec((8, channels), whole),
        ]
        + [pl.BlockSpec(p.shape, whole) for p in pieces],
        out_specs=[
            pl.BlockSpec((TILE, channels), now),
            pl.BlockSpec((8, TILE), lambda i: (0, i)),
            pl.BlockSpec((depth, channels), whole),
        ],
        out_shape=[
            jax.ShapeDtypeStruct((tokens, channels), f32),
            jax.ShapeDtypeStruct((8, tokens), f32),
            jax.ShapeDtypeStruct((depth, channels), bf16),
        ],
        compiler_params=params(),
        cost_estimate=cost(20),
        name="grad_gout",
    )(idx, cot, gate, mixed, conv_rows, *pieces)


def gate_back_kernel(gate_ref, gout_ref, mixed_ref, square_ref, inner_ref, conv_ref, dmixed_ref, dgate_ref, dgain_ref, *, inner_total):
    gate, gout, mixed = gate_ref[...], gout_ref[...], mixed_ref[...]
    gain = conv_ref[5:6, :]
    square, inner = row_to_column(square_ref[0:1, :]), row_to_column(inner_ref[0:1, :])
    scale = lax.rsqrt(square / inner_total + EPSILON)
    sg = sigmoid(gate)
    act = gate * sg
    gated = mixed * act
    dgated = scale * (gain * gout) - gated * (scale * scale * scale * inner / inner_total)
    dmixed_ref[...] = (dgated * act).astype(bf16)
    dgate_ref[...] = (dgated * mixed * sg * (1.0 + gate * (1.0 - sg))).astype(bf16)

    @pl.when(pl.program_id(0) == 0)
    def _():
        dgain_ref[...] = jnp.zeros_like(dgain_ref)

    dgain_ref[5:6, :] += jnp.sum(gout * gated * scale, axis=0, keepdims=True)


def gate_backward(gate, gout, mixed, square, inner, conv_rows, inner_total):
    tokens, channels = gate.shape
    whole = lambda i: (0, 0)
    block = pl.BlockSpec((TILE, channels), lambda i: (i, 0))
    row = pl.BlockSpec((8, TILE), lambda i: (0, i))
    return pl.pallas_call(
        functools.partial(gate_back_kernel, inner_total=inner_total),
        grid=(tokens // TILE,),
        in_specs=[block, block, block, row, row, pl.BlockSpec((8, channels), whole)],
        out_specs=[block, block, pl.BlockSpec((8, channels), whole)],
        out_shape=[
            jax.ShapeDtypeStruct((tokens, channels), bf16),
            jax.ShapeDtypeStruct((tokens, channels), bf16),
            jax.ShapeDtypeStruct((8, channels), f32),
        ],
        compiler_params=params(),
        cost_estimate=cost(0.1),
        name="gate_backward",
    )(from_hbm(gate), from_hbm(gout), from_hbm(mixed), square, inner, conv_rows)


def weight_grad_kernel(idx_ref, lhs_ref, rhs_ref, *refs, rows, turned):
    outs, scratch = refs[:-1], refs[-1]
    at = pl.program_id(0)
    scratch[pl.ds(pl.multiple_of(at * TILE_D, TILE_D), TILE_D), :] = (dot_nt if turned else dot_nn)(
        lhs_ref[...], rhs_ref[...]
    ).astype(bf16)

    @pl.when(at == pl.num_programs(0) - 1)
    def _():
        s = 0
        for out in outs:
            for b in range(out.shape[0] // rows):
                start = pl.multiple_of(idx_ref[s] * rows, rows)
                out[b * rows:(b + 1) * rows, :] = scratch[pl.ds(start, rows), :]
                s += 1


def weight_grad(lhs_t, rhs, idx, sizes, us=0.1, turned=False):
    depth, tokens = lhs_t.shape
    width = rhs.shape[0 if turned else 1]
    rows = depth // idx.shape[0]
    whole = lambda i: (0, 0)
    return pl.pallas_call(
        functools.partial(weight_grad_kernel, rows=rows, turned=turned),
        grid=(depth // TILE_D,),
        in_specs=[
            pl.BlockSpec(memory_space=pltpu.SMEM),
            pl.BlockSpec((TILE_D, tokens), lambda i: (i, 0)),
            pl.BlockSpec(rhs.shape, whole),
        ],
        out_specs=[pl.BlockSpec((size * rows, width), whole) for size in sizes],
        out_shape=[hbm((size * rows, width), bf16) for size in sizes],
        scratch_shapes=[pltpu.VMEM((depth, width), bf16)],
        compiler_params=params(),
        cost_estimate=cost(us),
        name="weight_grad",
    )(idx, lhs_t, rhs)


def out_kernel(rank_ref, lhs_ref, w_ref, *outs):
    product = dot_nt(lhs_ref[...], w_ref[...]).astype(bf16)
    for r, out in enumerate(outs):
        @pl.when(pl.program_id(0) == r)
        def _():
            out[...] = product


def out_partial(gated_out, w_out, rank, ranks):
    tokens, channels = gated_out.shape
    depth = w_out.shape[0]
    width = depth // ranks
    whole = lambda i, rank_ref: (0, 0)
    return pl.pallas_call(
        out_kernel,
        grid_spec=pltpu.PrefetchScalarGridSpec(
            num_scalar_prefetch=1,
            grid=(ranks,),
            in_specs=[
                pl.BlockSpec((tokens, channels), whole),
                pl.BlockSpec((width, channels), lambda i, rank_ref: (i ^ rank_ref[0], 0)),
            ],
            out_specs=[pl.BlockSpec((tokens, width), whole)] * ranks,
        ),
        out_shape=[hbm((tokens, width), bf16)] * ranks,
        compiler_params=params(),
        cost_estimate=cost(0.1),
        name="out_partial",
    )(rank, gated_out, w_out)


def term_kernel(rank_ref, gx_ref, wx_ref, gg_ref, wg_ref, gs_ref, ws_ref, gb_ref, inv_ref, *refs, apart):
    hidden_refs, wbt_refs, outs, dgain_ref = refs[:len(apart)], refs[len(apart):len(apart) + 4], refs[len(apart) + 4:-1], refs[-1]
    w_bct = jnp.concatenate([ref[...] for ref in wbt_refs], axis=0)
    gain = None
    for r, out, hidden_ref in zip(apart, outs, hidden_refs):
        rows = out.shape[0]
        span = pl.ds(pl.multiple_of((rank_ref[0] ^ r) * rows, rows), rows)
        total = dot_nt(gx_ref[span, :], wx_ref[...]) + dot_nt(gg_ref[span, :], wg_ref[...])
        total = total + dot_nt(gs_ref[span, :], ws_ref[...]) + dot_nn(gb_ref[span, :], w_bct)
        out[...] = total.astype(bf16)
        normed = hidden_ref[...].astype(f32) * row_to_column(inv_ref[0:1, span])
        own = jnp.sum(total * normed, axis=0, keepdims=True)
        gain = own if gain is None else gain + own
    cut = [gain[:, i:i + LANES] for i in range(0, gain.shape[1], LANES)]
    dgain_ref[...] = jnp.concatenate(cut + [jnp.zeros((8 - len(cut), LANES), f32)], axis=0)


def normed_term(dx, dgate, dstep, dbc, w_a, w_b, w_s, w_bct, hidden, inv_rms, rank, ranks, apart):
    tokens, channels = dx.shape
    depth = w_a.shape[0]
    rows = tokens // ranks
    whole = lambda i, rank_ref: (0, 0)
    return pl.pallas_call(
        functools.partial(term_kernel, apart=apart),
        grid_spec=pltpu.PrefetchScalarGridSpec(
        num_scalar_prefetch=1,
        grid=(depth // TILE_D,),
        in_specs=[
            pl.BlockSpec(dx.shape, whole),
            pl.BlockSpec((TILE_D, channels), lambda i, rank_ref: (i, 0)),
            pl.BlockSpec(dgate.shape, whole),
            pl.BlockSpec((TILE_D, channels), lambda i, rank_ref: (i, 0)),
            pl.BlockSpec(dstep.shape, whole),
            pl.BlockSpec((TILE_D, LANES), lambda i, rank_ref: (i, 0)),
            pl.BlockSpec(dbc.shape, whole),
            pl.BlockSpec(inv_rms.shape, whole),
        ]
        + [pl.BlockSpec((rows, TILE_D), functools.partial(lambda r, i, rank_ref: (rank_ref[0] ^ r, i), r)) for r in apart]
        + [pl.BlockSpec((w.shape[0], TILE_D), lambda i, rank_ref: (0, i)) for w in w_bct],
        out_specs=[pl.BlockSpec((rows, TILE_D), lambda i, rank_ref: (0, i))] * len(apart) + [pl.BlockSpec((8, LANES), lambda i, rank_ref: (i, 0))],
        ),
        out_shape=[jax.ShapeDtypeStruct((rows, depth), bf16)] * len(apart)
        + [jax.ShapeDtypeStruct((8 * (depth // TILE_D), LANES), f32)],
        compiler_params=params(32),
        cost_estimate=cost(5 if 2 in apart else 5),
        name="normed_term",
    )(
        rank, dx, from_hbm(w_a), dgate, from_hbm(w_b), dstep, from_hbm(w_s), dbc, inv_rms, *[from_hbm(hidden) for _ in apart], *w_bct
    )


def norm_back_kernel(rank_ref, a_ref, b_ref, hidden_ref, cot_ref, gain_ref, out_ref):
    grad = a_ref[...].astype(f32) + b_ref[...].astype(f32)
    inputs = hidden_ref[...].astype(f32)
    inv_rms = lax.rsqrt(jnp.mean(inputs * inputs, axis=1, keepdims=True) + EPSILON)
    normed = inputs * inv_rms
    scaled = grad * gain_ref[0:1, :]
    mean = jnp.mean(scaled * normed, axis=1, keepdims=True)
    out_ref[...] = (inv_rms * (scaled - normed * mean) + cot_ref[...].astype(f32)).astype(out_ref.dtype)


def norm_backward(a, b, hidden, cot, gain_rows, rank):
    rows, depth = a.shape
    mine = lambda i, rank_ref: (rank_ref[0], 0)
    whole = lambda i, rank_ref: (0, 0)
    return pl.pallas_call(
        norm_back_kernel,
        grid_spec=pltpu.PrefetchScalarGridSpec(
            num_scalar_prefetch=1,
            grid=(1,),
            in_specs=[
                pl.BlockSpec((rows, depth), whole),
                pl.BlockSpec((rows, depth), whole),
                pl.BlockSpec((rows, depth), mine),
                pl.BlockSpec((rows, depth), mine),
                pl.BlockSpec((8, depth), whole),
            ],
            out_specs=pl.BlockSpec((rows, depth), whole),
        ),
        out_shape=jax.ShapeDtypeStruct((rows, depth), bf16),
        compiler_params=params(),
        cost_estimate=cost(0.1),
        name="norm_backward",
    )(rank, a, b, from_hbm(hidden), from_hbm(cot), gain_rows)


def moved(weight, moment, grad):
    fresh = 0.5 * moment + 0.5 * grad
    return fresh, weight - LEARN_RATE * fresh - LEARN_RATE * DECAY_RATE * weight


def add_up(refs):
    total = refs[0][...].astype(f32)
    for ref in refs[1:]:
        total = total + ref[...].astype(f32)
    return total


def update_in_kernel(w_ref, m_ref, *refs, count):
    gate_refs, x_refs, (m_out, w_out) = refs[:count], refs[count:2 * count], refs[2 * count:]
    for at, parts in ((0, gate_refs), (1, x_refs)):
        fresh, weight = moved(w_ref[:, at, :], m_ref[:, at, :], add_up(parts))
        m_out[:, at, :] = fresh
        w_out[:, at, :] = weight


def update_in(weight, moment, gate_parts, x_parts):
    rows, _, channels = weight.shape
    size = min(rows, 96)
    full = pl.BlockSpec((size, 2, channels), lambda i: (i, 0, 0))
    parts = [*gate_parts, *x_parts]
    return pl.pallas_call(
        functools.partial(update_in_kernel, count=len(gate_parts)),
        grid=(rows // size,),
        in_specs=[full, full] + [pl.BlockSpec((size, channels), functools.partial(lambda at, i: (i, at), at)) for _, at in parts],
        out_specs=[full, full],
        out_shape=[jax.ShapeDtypeStruct(weight.shape, f32)] * 2,
        compiler_params=params(),
        cost_estimate=cost(0.1),
        name="update_in",
    )(from_hbm(weight), from_hbm(moment), *[part for part, _ in parts])


def update_small_kernel(w_ref, m_ref, sums_ref, own_ref, back_ref, *refs, share, order, shared):
    alone, late, (m_out, w_out, exchange, totals, scratch) = refs[:order[0]], refs[order[0]:-5], refs[-5:]
    heads, rows = w_ref.shape
    count = sums_ref.shape[0]
    last = late[0].shape[1] - LANES
    grad = own_ref[...].astype(f32) + back_ref[...].astype(f32)
    found = {0: sums_ref[...].astype(f32)}
    for at, ref in zip(order[1], alone):
        grad = grad + ref[0:rows, :].astype(f32)
        found[at] = ref[rows:, :].astype(f32)
    for at, ref in zip(order[2], late):
        grad = grad + ref[0:rows, last:].astype(f32)
        tail = ref[rows:, :].astype(f32)
        found[at] = jnp.concatenate([tail[:, i:i + LANES] for i in range(0, tail.shape[1], LANES)], axis=0)
    step = len(found) // 2
    while step >= 1:
        found = {i: found[i] + found[i + step] for i in range(step)}
        step //= 2
    totals[...] = found[0]
    exchange[0:rows, :] = grad
    exchange[rows:, :] = found[0][shared[0]:shared[1], :]
    scratch[0:rows, :] = grad
    turned = scratch[...].T[share:share + heads, 0:rows]
    fresh, weight = moved(w_ref[...], m_ref[...], turned)
    m_out[...] = fresh
    w_out[...] = weight


def update_small(weight_t, moment_t, sums, own, back, alone, late, order, shared, share):
    rows = weight_t.shape[1]
    count = sums.shape[0]
    whole = lambda i: (0, 0)
    spec = pl.BlockSpec(weight_t.shape, whole)
    return pl.pallas_call(
        functools.partial(update_small_kernel, share=share, order=order, shared=shared),
        grid=(1,),
        in_specs=[spec, spec, pl.BlockSpec(sums.shape, whole)] + [pl.BlockSpec((rows, LANES), whole)] * 2
        + [pl.BlockSpec(v.shape, whole) for v in (*alone, *late)],
        out_specs=[
            spec, spec,
            pl.BlockSpec((rows + shared[1] - shared[0], LANES), whole),
            pl.BlockSpec((count, LANES), whole),
        ],
        out_shape=[jax.ShapeDtypeStruct(weight_t.shape, f32)] * 2
        + [jax.ShapeDtypeStruct((rows + shared[1] - shared[0], LANES), f32), jax.ShapeDtypeStruct((count, LANES), f32)],
        scratch_shapes=[pltpu.VMEM((2 * LANES, LANES), f32)],
        compiler_params=params(),
        cost_estimate=cost(0.1),
        name="update_small",
    )(weight_t, moment_t, sums, own, back, *alone, *late)


def update_bc_kernel(rank_ref, w_ref, m_ref, *refs):
    pieces, (m_out, w_out, shared_out) = refs[:-3], refs[-3:]
    rows, width = w_ref.shape
    share = width // len(pieces)
    shared_out[...] = (pieces[0][rows:, :] + pieces[1][rows:, :]) + (pieces[2][rows:, :] + pieces[3][rows:, :])
    lane = lax.broadcasted_iota(jnp.int32, (rows, LANES), 1)
    for pair in range(width // LANES):
        halves = []
        for member in (2 * pair, 2 * pair + 1):
            own = pieces[0][0:rows, :]
            for r in range(1, len(pieces)):
                own = jnp.where((rank_ref[0] ^ r) == member, pieces[r][0:rows, :], own)
            halves.append(own)
        grad = jnp.where(lane < share, halves[0], pltpu.roll(halves[1], share, 1))
        span = slice(pair * LANES, (pair + 1) * LANES)
        fresh, weight = moved(w_ref[:, span], m_ref[:, span], grad)
        m_out[:, span] = fresh
        w_out[:, span] = weight


def update_bc(weight, moment, pieces, rank):
    vmem = pl.BlockSpec(memory_space=pltpu.VMEM)
    return pl.pallas_call(
        update_bc_kernel,
        in_specs=[pl.BlockSpec(memory_space=pltpu.SMEM)] + [vmem] * (2 + len(pieces)),
        out_specs=[vmem] * 3,
        out_shape=[jax.ShapeDtypeStruct(weight.shape, f32)] * 2
        + [jax.ShapeDtypeStruct((pieces[0].shape[0] - weight.shape[0], LANES), f32)],
        compiler_params=params(),
        cost_estimate=cost(0.1),
        name="update_bc",
    )(rank, weight, moment, *pieces)


def fence(*values):
    leaves, tree = jax.tree.flatten(values)
    return jax.tree.unflatten(tree, lax.optimization_barrier(leaves))


def outer_from(v, k):
    n = lax.axis_size("dp") // 2
    return lax.ppermute(v, "dp", [(((o + k) % n) * 2 + x, o * 2 + x) for o in range(n) for x in range(2)])


def outer_flip(v, bit):
    n = lax.axis_size("dp") // 2
    return lax.ppermute(v, "dp", [((o ^ bit) * 2 + x, o * 2 + x) for o in range(n) for x in range(2)])


def inner_flip(v):
    return lax.ppermute(v, "dp", [(d ^ 1, d) for d in range(lax.axis_size("dp"))])


def rank_flip(v, bit):
    return lax.ppermute(v, "mp", [(m ^ bit, m) for m in range(lax.axis_size("mp"))])


def hops(n):
    order = []
    for k in range(1, n // 2 + 1):
        order.append(k)
        if n - k != k:
            order.append(n - k)
    return order


def pair_sum(a, b):
    return (a.astype(f32) + b.astype(f32)).astype(bf16)


def outer_blocks(own, here, back, ks):
    rows = own.shape[0]
    back = [part[i:i + rows] for part in back for i in range(0, part.shape[0], rows)]
    return [
        (here[i * rows:(i + 1) * rows].astype(f32) + back[i].astype(f32)).astype(bf16) for i in range(len(ks))
    ]


def outer_send(blocks, ks):
    n = lax.axis_size("dp") // 2
    return [outer_from(block, n - k) for block, k in zip(blocks, ks)]


def outer_sum(v):
    bit = 1
    while bit < lax.axis_size("dp") // 2:
        v = v + outer_flip(v, bit)
        bit *= 2
    return v


def mp_sum(v):
    v = v + rank_flip(v, 1)
    return v + rank_flip(v, 2)


def mp_sum_direct(v):
    return (v + rank_flip(v, 1)) + (rank_flip(v, 2) + rank_flip(v, 3))


def mp_reduce(blocks):
    far = blocks[2].astype(f32) + rank_flip(blocks[3], 1).astype(f32)
    near = blocks[0].astype(f32) + rank_flip(blocks[1], 1).astype(f32)
    return near, rank_flip(far.astype(bf16), 2)


def mp_pieces(v):
    far = rank_flip(v, 2)
    return [v, rank_flip(v, 1), far, rank_flip(far, 1)]


def in_rank_order(pieces, rank, axis):
    odd, high = (rank & 1) == 1, (rank & 2) == 2
    join = lambda a, b: jnp.concatenate([a, b], axis=axis)
    low = jnp.where(odd, join(pieces[1], pieces[0]), join(pieces[0], pieces[1]))
    far = jnp.where(odd, join(pieces[3], pieces[2]), join(pieces[2], pieces[3]))
    return jnp.where(high, join(far, low), join(low, far))


def momentum(moment, grad):
    return 0.5 * moment + 0.5 * grad


def advance(weight, moment, grad):
    fresh = momentum(moment, grad)
    return (fresh, weight - LEARN_RATE * fresh - LEARN_RATE * DECAY_RATE * weight)


def body(
    hidden, segments, cotangent, in_weight, in_moment, bc_weight, bc_moment, step_weight, step_moment,
    out_weight, out_moment, conv_table, conv_moment, bc_table, bc_table_moment, head_table, head_moment,
    norm_gain, gain_moment,
):
    size = lax.axis_size("dp")
    ranks = lax.axis_size("mp")
    n = size // 2
    place, rank = lax.axis_index("dp"), lax.axis_index("mp")
    outer, inner = place // 2, place % 2
    rank1 = rank.reshape(1).astype(jnp.int32)
    rows, _, channels = in_weight.shape
    heads = head_table.shape[1]
    tokens, depth = hidden.shape
    share = bc_weight.shape[1] // ranks

    ks = hops(n)
    near_ks, far_k = ks[:-1], ks[-1]

    def members(order):
        return jnp.stack([((outer + k) % n) * 2 + (inner ^ j) for k, j in order]).astype(jnp.int32)

    first = [(0, 0), (0, 1)]
    idx = members(first + [(k, 0) for k in ks] + [(k, 1) for k in ks])
    idx_s = members([(0, 0)] + [(k, 0) for k in ks] + [(0, 1)] + [(k, 1) for k in ks])
    sizes = (1, 1, n - 1, n - 1)
    split_sizes = (1, 1, n - 1, n - 2, 1)
    width = depth // ranks

    set_a = pack(in_weight, bc_weight, step_weight.T, rank1)
    set_c = out_weight.T.astype(bf16)

    def blocks(own, z, x):
        return [own, x[0]] + [z[k] for k in ks] + [x[k] for k in ks]

    def block(v, i):
        return v[i * rows:(i + 1) * rows]

    def blocks(own, z, x):
        return [own, x[0]] + [z[k] for k in ks] + [x[k] for k in ks]

    def block(v, i):
        return v[i * rows:(i + 1) * rows]

    def total(own, own_got, got):
        value = own.astype(f32) + own_got.astype(f32)
        for part in got:
            value = value + part.astype(f32)
        return value

    def outer_all(v, some):
        return {k: outer_from(v, k) for k in some}

    def flip_all(z, some):
        return {k: inner_flip(z[k]) for k in some}

    a_z = outer_all(set_a, near_ks)
    a_x = {0: inner_flip(set_a)}
    far_a, a_x[0], hidden, segments, in_gate = fence(set_a, a_x[0], hidden, segments, in_weight)
    set_b = pack_gate(in_gate)
    a_z[far_k] = outer_from(far_a, far_k)
    cot_far = rank_flip(cotangent, 2)
    gain_rows = pad_rows(norm_gain[None])
    normed_low, normed_t, inv_rms = prepare(hidden, gain_rows)
    a_x.update(flip_all(a_z, near_ks))
    aux, seg_row = segment_facts(segments)
    head_rows = pad_lanes(pad_rows(head_table))
    facts = (aux, seg_row, pad_rows(conv_table), pad_rows(bc_table), head_rows, *head_expand(channels))
    set_a, set_b, set_c, a_z, a_x, cot_far, normed_low, normed_t, inv_rms, facts = fence(
        set_a, set_b, set_c, a_z, a_x, cot_far, normed_low, normed_t, inv_rms, facts
    )

    a_x[far_k] = inner_flip(a_z[far_k])
    b_x = {0: inner_flip(set_b)}
    b_z = outer_all(set_b, near_ks)
    cot, cot_t = join_columns([cotangent, rank_flip(cotangent, 1), cot_far, rank_flip(cot_far, 1)], rank1)
    set_b, set_c, b_z, b_x, a_z, a_x, cot, cot_t, normed_low = fence(
        set_b, set_c, b_z, b_x, a_z, a_x, cot, cot_t, normed_low
    )

    b_z[far_k] = outer_from(set_b, far_k)
    b_x.update(flip_all(b_z, near_ks[:1]))
    c_x = {0: inner_flip(set_c)}
    a_blocks = blocks(set_a, a_z, a_x)
    small, bc_share, w_s, w_bct_share = project_small(normed_low, a_blocks, idx, share)
    bc_far, bc_near = rank_flip(bc_share, 2), rank_flip(bc_share, 1)
    x_pre, w_a = project(normed_low, a_blocks, idx, channels)
    bc_far, x_pre, small, set_c, w_bct_share, w_s = fence(bc_far, x_pre, small, set_c, w_bct_share, w_s)
    bc_pieces = [bc_share, bc_near, bc_far, rank_flip(bc_far, 1)]
    bc_pre, step_pre = join_small(bc_pieces, small, rank1)
    set_c, b_z, b_x, c_x, x_pre, bc_pre, step_pre, w_bct_share = fence(
        set_c, b_z, b_x, c_x, x_pre, bc_pre, step_pre, w_bct_share
    )

    c_z = outer_all(set_c, near_ks)
    b_x.update(flip_all(b_z, ks[1:]))
    kept = ssd_forward(x_pre, bc_pre, step_pre, *facts[:-1])
    mixed = kept[0]
    mixed, b_x, b_z, c_z, c_x, w_bct_share, set_c = fence(mixed, b_x, b_z, c_z, c_x, w_bct_share, set_c)

    c_z[far_k] = outer_from(set_c, far_k)
    c_x.update(flip_all(c_z, near_ks))
    gate_pre, square, w_b = gate_forward(normed_low, mixed, blocks(set_b, b_z, b_x), idx)
    square = mp_sum_direct(square)
    mixed, gate_pre, square, w_b, w_bct_share, c_z, c_x = fence(mixed, gate_pre, square, w_b, w_bct_share, c_z, c_x)

    c_x[far_k] = inner_flip(c_z[far_k])
    w_bct = [w_bct_share, rank_flip(w_bct_share, 2)]
    conv_rows = facts[2]
    gated_out = gated_norm(gate_pre, mixed, square, conv_rows, channels * ranks)
    gc_own, gc_own1, gc_here, gc_near, gc_far = weight_grad(cot_t, gated_out, idx, split_sizes)
    c_x, square, gated_out, gc_own, gc_own1, gc_here, gc_near, gc_far, w_bct = fence(
        c_x, square, gated_out, gc_own, gc_own1, gc_here, gc_near, gc_far, w_bct
    )

    gc_far_back, gc_near_back = inner_flip(gc_far), inner_flip(gc_near)
    gout, inner_dot, w_c = grad_gout(cot, gate_pre, mixed, conv_rows, blocks(set_c, c_z, c_x), idx)
    gout, inner_dot, w_c = fence(gout, inner_dot, w_c)
    inner_dot = mp_sum_direct(inner_dot)
    partial = out_partial(gated_out, w_c, rank1, ranks)
    inner_dot, gout, partial, w_bct, gc_far_back = fence(inner_dot, gout, partial, w_bct, gc_far_back)
    c_far_got = outer_from(pair_sum(block(gc_here, n - 2), gc_far_back), n - far_k)
    out_back = rank_flip(partial[3], 1)
    w_bct = [w_bct[0], rank_flip(w_bct[0], 1), w_bct[1], rank_flip(w_bct[1], 1)]
    dmixed, dgate, dgain = gate_backward(gate_pre, gout, mixed, square, inner_dot, conv_rows, channels * ranks)
    gb_own, gb_own1, gb_here, gb_send = weight_grad(normed_t, dgate, idx, sizes)
    gc_near_back, c_far_got, w_bct, out_back, gb_own, gb_own1, gb_here, gb_send, partial, dmixed, dgain = fence(
        gc_near_back, c_far_got, w_bct, out_back, gb_own, gb_own1, gb_here, gb_send, partial, dmixed, dgain
    )
    c_blocks = [pair_sum(block(gc_here, i), block(gc_near_back, i)) for i in range(n - 2)]
    out_far = pair_sum(partial[2], out_back)
    c_blocks, out_far, w_bct, dmixed, gb_send = fence(c_blocks, out_far, w_bct, dmixed, gb_send)

    c_got = outer_send(c_blocks, near_ks) + [c_far_got]
    gb_back = inner_flip(gb_send)
    out_got = rank_flip(out_far, 2)
    dx, dbc, dbc_keep, dbc_send, dstep, dstep_t, dconv, dbct_part, dheads = ssd_backward(
        rank1, x_pre, bc_pre, step_pre, *facts, dmixed, kept
    )
    c_got, gb_back, out_got, dx, dbc, dbc_keep, dbc_send, dstep, dstep_t, dconv, dbct_part, dheads = fence(
        c_got, gb_back, out_got, dx, dbc, dbc_keep, dbc_send, dstep, dstep_t, dconv, dbct_part, dheads
    )

    b_got = {far_k: outer_from(pair_sum(block(gb_here, n - 2), block(gb_back, n - 2)), n - far_k)}
    dbc_back = rank_flip(dbc_send, 1)
    out_near_back = rank_flip(partial[1], 1)
    ga_own, ga_own1, ga_here, ga_send = weight_grad(normed_t, dx, idx, sizes, us=20)
    ga_own, ga_own1, ga_here, ga_send, dx, dbc_back, gb_back, gb_here, out_near_back = fence(
        ga_own, ga_own1, ga_here, ga_send, dx, dbc_back, gb_back, gb_here, out_near_back
    )

    b_near = [pair_sum(block(gb_here, i), block(gb_back, i)) for i in range(n - 2)]
    b_got.update(zip(near_ks, outer_send(b_near, near_ks)))
    ga_back = inner_flip(ga_send)
    dbc_pair = pair_sum(dbc_keep, dbc_back)
    dbc_got = rank_flip(dbc_pair[share:], 2)
    operands = (dx, dgate, dstep, dbc, w_a, w_b, w_s, w_bct, hidden, inv_rms, rank1, ranks)
    far_own, far_send, gain_far = normed_term(*operands, (2, 3))
    far_own, far_send, gain_far, dx, dbc_got, dbc_pair, dstep_t, b_got[far_k] = fence(
        far_own, far_send, gain_far, dx, dbc_got, dbc_pair, dstep_t, b_got[far_k]
    )
    far_back = rank_flip(far_send, 1)
    operands = (dx, *operands[1:])
    near_own, near_send, gain_near = normed_term(*operands, (0, 1))
    far_back, near_own, near_send, gain_near, ga_back = fence(far_back, near_own, near_send, gain_near, ga_back)
    near_back = rank_flip(near_send, 1)
    far = pair_sum(far_own, far_back)
    a_blocks = [pair_sum(block(ga_here, i), block(ga_back, i)) for i in range(n - 1)]
    dbc_share = pair_sum(dbc_pair[:share], dbc_got)
    dsmall_t = jnp.concatenate([dbc_share, dstep_t, jnp.zeros((LANES - share - 16, tokens), bf16)], axis=0)
    gs_own, gs_here, gs_send = weight_grad(normed_t, dsmall_t, idx_s, (1, n - 1, n), turned=True)
    far, a_blocks, near_back, gs_send, gc_own1, gb_own1, b_got = fence(
        far, a_blocks, near_back, gs_send, gc_own1, gb_own1, b_got
    )

    early, late = [], near_ks
    got = rank_flip(far, 2)
    a_got = dict(zip([far_k, *early], outer_send([a_blocks[-1], *a_blocks[:len(early)]], [far_k, *early])))
    cut = lambda v: [v[:, i:i + LANES] for i in range(0, v.shape[1], LANES)]
    alone = channels // LANES * 8 + 8
    sums = jnp.concatenate([*cut(dconv + dgain), dheads, *cut(dbct_part), gain_far + gain_near], axis=0)
    shared = (alone, sums.shape[0])
    wide = (channels + LANES) // LANES
    sums = pad_rows(sums, -(-sums.shape[0] // (16 * wide)) * 16 * wide).astype(bf16)
    small_back = inner_flip(jnp.concatenate([gs_send, sums], axis=0))
    own_got = inner_flip(jnp.concatenate([gc_own1, gb_own1], axis=1))
    near = near_own.astype(f32) + near_back.astype(f32)
    got, near, a_got, small_back, sums, own_got, ga_own1, a_late = fence(
        got, near, a_got, small_back, sums, own_got, ga_own1, a_blocks[len(early):-1]
    )

    mine = norm_backward(near, got, hidden, cot, gain_rows, rank1)
    mine, small_back, sums, ga_own1, a_late, gs_here, out_got, out_near_back = fence(
        mine, small_back, sums, ga_own1, a_late, gs_here, out_got, out_near_back
    )
    a_own_got = inner_flip(ga_own1)
    gs_back, sums_back = small_back[:n * rows], small_back[n * rows:]
    s_blocks = dict(zip(ks, outer_blocks(gs_own, gs_here, [gs_back[rows:]], ks)))
    sums = pair_sum(sums, sums_back)
    size = sums.shape[0] // wide
    sums_wide = jnp.concatenate([sums[i * size:(i + 1) * size] for i in range(wide)], axis=1)
    late_got = outer_send(
        [
            jnp.concatenate([jnp.concatenate([a_block, s_blocks[k]], axis=1), sums_wide], axis=0)
            for k, a_block in zip(late, a_late)
        ],
        late,
    )
    s_got = outer_send([jnp.concatenate([s_blocks[k], sums], axis=0) for k in (far_k, *early)], (far_k, *early))
    mine_far = rank_flip(mine, 2)
    mine_far, mine = fence(mine_far, mine)
    late_got, s_got, a_own_got, sums = fence(late_got, s_got, a_own_got, sums)

    mine_near, mine_far_near = rank_flip(mine, 1), rank_flip(mine_far, 1)
    step_m, step_w, exchange, totals = update_small(
        step_weight.T, step_moment.T, sums, gs_own, gs_back, s_got, late_got,
        (len(s_got), [n - k for k in (far_k, *early)], [n - k for k in late]), shared, share,
    )
    exchanged = [exchange] + [rank_flip(exchange, r) for r in (1, 2, 3)]
    in_m, in_w = update_in(
        in_weight, in_moment,
        [(gb_own, 0), (own_got, 1)] + [(b_got[k], 0) for k in ks],
        [(ga_own, 0), (a_own_got, 0)] + [(a_got[k], 0) for k in (far_k, *early)] + [(v, 0) for v in late_got],
    )
    input_grad = join_rows([mine, mine_near, mine_far, mine_far_near], rank1)
    exchanged, mine_far_near = fence(exchanged, mine_far_near)
    bc_m, bc_w, totals_shared = update_bc(bc_weight, bc_moment, exchanged, rank1)

    resid = lax.dynamic_slice_in_dim(hidden, rank * width, width, 1).astype(f32)
    output = (resid + partial[0].astype(f32) + out_near_back.astype(f32) + out_got.astype(f32)).astype(bf16)
    shard_c = total(gc_own, own_got[:, :channels], c_got)

    side_by_side = lambda v: jnp.concatenate([v[i:i + 8] for i in range(0, v.shape[0], 8)], axis=1)
    total_conv = side_by_side(totals[:alone - 8])[:6]
    total_head = totals[alone - 8:alone - 5, :heads]
    total_bct = side_by_side(totals_shared[:16])[:5]
    per = TILE_D // LANES
    total_gain = jnp.concatenate([totals_shared[i:i + per] for i in range(16, totals_shared.shape[0], 8)], axis=0).reshape(-1)

    out_m, out_w = advance(out_weight, out_moment, shard_c.T)
    return (
        output, input_grad, in_m, in_w, bc_m, bc_w, step_m.T, step_w.T, out_m, out_w,
        momentum(conv_moment, total_conv),
        momentum(bc_table_moment, total_bct),
        momentum(head_moment, total_head),
        momentum(gain_moment, total_gain),
    )


def solution(mesh):
    placed = (
        P("dp", None),
        P("dp", None),
        P("dp", "mp"),
        P("dp", None, "mp"),
        P("dp", None, "mp"),
        P("dp", None),
        P("dp", None),
        P("dp", "mp"),
        P("dp", "mp"),
        P("mp", "dp"),
        P("mp", "dp"),
        P(None, "mp"),
        P(None, "mp"),
        P(),
        P(),
        P(None, "mp"),
        P(None, "mp"),
        P(),
        P(),
    )
    return jax.shard_map(
        body,
        mesh=mesh,
        in_specs=placed,
        out_specs=(
            P("dp", "mp"),
            P("dp", None),
            P("dp", None, "mp"),
            P("dp", None, "mp"),
            P("dp", None),
            P("dp", None),
            P("dp", "mp"),
            P("dp", "mp"),
            P("mp", "dp"),
            P("mp", "dp"),
            P(None, "mp"),
            P(),
            P(None, "mp"),
            P(),
        ),
        check_vma=False,
    )
```
